32 devices in a mesh: section: 4 (over y, core), wide: 8 (over z, x).
Axes of the slice: x: 2, y: 2, z: 4, core: 2. Of those that a mesh axis runs over, the one named last changes fastest.
Arguments:
- token_ids: int32 [8, 2, 64], P('wide'), may hold values from 0 to 2047
- targets: int32 [8, 2, 64], P('wide'), may hold values from 0 to 2047
- slot_ids: int32 [2048, 8], P(('section', 'wide')), may hold values from 0 to 1023
- group_ids: int32 [2048], P(('section', 'wide')), may hold values from 0 to 3
- group_offsets: int32 [4], replicated, may hold values from 0 to 3072
- piece_table: bfloat16 [4096, 512], replicated, may hold values from -6 to 6
- prenorm_gain: float32 [512], P(('section', 'wide')), may hold values from 0.25 to 1.75
- prenorm_bias: float32 [512], P(('section', 'wide')), may hold values from -2 to 2
- query_map: float32 [512, 512], P(('section', 'wide')), may hold values from -0.25 to 0.25
- key_map: float32 [512, 512], P(('section', 'wide')), may hold values from -0.25 to 0.25
- value_map: float32 [512, 512], P(('section', 'wide')), may hold values from -0.25 to 0.25
- output_map: float32 [512, 512], P(('section', 'wide')), may hold values from -0.5 to 0.5
- midnorm_gain: float32 [512], P(('section', 'wide')), may hold values from 0.25 to 1.75
- midnorm_bias: float32 [512], P(('section', 'wide')), may hold values from -2 to 2
- expand_map: float32 [512, 2048], P(('section', 'wide')), may hold values from -0.25 to 0.25
- reduce_map: float32 [2048, 512], P(('section', 'wide')), may hold values from -0.1875 to 0.1875
- embed_map: float32 [512, 2048], P(('section', 'wide')), may hold values from -0.0234375 to 0.0234375
- attention_gain: bfloat16 [2, 2048], P(None, 'wide'), may hold values from 0.25 to 1.75
- query_weight: bfloat16 [2, 2048, 2048], P(None, 'wide'), may hold values from -0.125 to 0.125
- key_weight: bfloat16 [2, 2048, 256], P(None, 'wide'), may hold values from -0.125 to 0.125
- value_weight: bfloat16 [2, 2048, 256], P(None, 'wide'), may hold values from -0.125 to 0.125
- output_weight: bfloat16 [2, 2048, 2048], P(None, 'wide'), may hold values from -0.375 to 0.375
- feed_gain: bfloat16 [2, 2048], P(None, 'wide'), may hold values from 0.25 to 1.75
- gate_weight: bfloat16 [2, 2048, 5632], P(None, 'wide'), may hold values from -0.125 to 0.125
- up_weight: bfloat16 [2, 2048, 5632], P(None, 'wide'), may hold values from -0.125 to 0.125
- down_weight: bfloat16 [2, 5632, 2048], P(None, 'wide'), may hold values from -0.109375 to 0.109375
- final_gain: bfloat16 [2048], replicated, may hold values from 0.25 to 1.75
Outputs:
- mean_loss: float32 [], replicated
- grad_prescale: float32 [512], P(('section', 'wide'))
- prenorm_bias_gradient: float32 [512], P(('section', 'wide'))
- grad_query: float32 [512, 512], P(('section', 'wide'))
- grad_key: float32 [512, 512], P(('section', 'wide'))
- grad_value: float32 [512, 512], P(('section', 'wide'))
- grad_output: float32 [512, 512], P(('section', 'wide'))
- grad_midscale: float32 [512], P(('section', 'wide'))
- grad_midshift: float32 [512], P(('section', 'wide'))
- grad_expand: float32 [512, 2048], P(('section', 'wide'))
- grad_reduce: float32 [2048, 512], P(('section', 'wide'))
- grad_embed: float32 [512, 2048], P(('section', 'wide'))
The draws below stay inside these ranges and needn't reach their ends.
All inputs are finite; a program needn't handle non-finite values.
Results may differ from the reference program's by a relative error of at most 0.035.
The reference program's roundings to bfloat16 on the way count: a program that leaves them out, or rounds other values in their place, can miss the bound.
Values may be sent and summed in bfloat16 or wider, within the bound.
A program may use at most 448 MiB of HBM per device.

```python
import jax
import jax.numpy as jnp
from jax import lax

D = 2048
KV_HEADS = 4
HEAD_DIM = 64
FF = 5632
HW = 512
HYPER_HEAD_COUNT = 8
HFF = 2048
SLOTS = 8
GROUPS = 4
PIECES = 1024
PIECE_ROWS = 4096
MB = 2
LEN = 64
VOCAB = 2048
SEQS = 8


def set_ends(drawn, own_key, least, top_value):
    longest = drawn.shape.index(max(drawn.shape))
    spots = []
    for shift in (0, 1):
        where = [jax.random.randint(jax.random.fold_in(own_key, axis), (), 0, length) for axis, length in enumerate(drawn.shape)]
        where[longest] = (where[longest] + shift) % drawn.shape[longest]
        spots.append(tuple(where))
    return drawn.at[spots[0]].set(least).at[spots[1]].set(top_value)


def steps_of(stream_key, dims, cuts, least, top_value):
    loudness = 1.0
    for position, parts in cuts:
        draws = jax.random.uniform(jax.random.fold_in(jax.random.fold_in(stream_key, 6), position), (parts,), jnp.float32, least / len(cuts), top_value / len(cuts))
        loudness = loudness * jnp.repeat(jnp.exp(draws), dims[position] // parts).reshape((-1,) + (1,) * (len(dims) - 1 - position))
    return loudness


def scatter_about(own_key, shape, scale, most, cuts=(), held_as=jnp.bfloat16):
    values = scale * jax.random.normal(own_key, shape, jnp.float32)
    if cuts:
        values = values * steps_of(own_key, shape, cuts, -0.22, 0.18)
    return jnp.clip(values, -most, most).astype(held_as)


def setup_inputs(seed: int = 0) -> dict:
    key_list = jax.random.split(jax.random.key(seed), 28)
    token_ids = set_ends(jax.random.randint(key_list[0], (SEQS, MB, LEN), 0, VOCAB), jax.random.fold_in(key_list[0], 1), 0, VOCAB - 1).astype(jnp.int32)
    targets = set_ends(jax.random.randint(key_list[1], (SEQS, MB, LEN), 0, VOCAB), jax.random.fold_in(key_list[1], 1), 0, VOCAB - 1).astype(jnp.int32)
    slot_ids = set_ends(jax.random.randint(key_list[2], (VOCAB, SLOTS), 0, PIECES), jax.random.fold_in(key_list[2], 1), 0, PIECES - 1).astype(jnp.int32)
    group_ids = set_ends(jax.random.randint(key_list[3], (VOCAB,), 0, GROUPS), jax.random.fold_in(key_list[3], 1), 0, GROUPS - 1).astype(jnp.int32)
    group_offsets = set_ends(jax.random.randint(key_list[4], (GROUPS,), 0, PIECE_ROWS - PIECES + 1), jax.random.fold_in(key_list[4], 1), 0, PIECE_ROWS - PIECES).astype(jnp.int32)
    piece_table = scatter_about(key_list[5], (PIECE_ROWS, HW), 1.0, 6.0)
    prenorm_gain = jnp.clip(1.0 + 0.15 * jax.random.normal(key_list[6], (HW,), jnp.float32), 0.25, 1.75)
    prenorm_bias = scatter_about(key_list[7], (HW,), 0.3, 2.0, ((0, 32),), jnp.float32)
    query_map = scatter_about(key_list[8], (HW, HW), HW ** -0.5, 0.25, ((0, 32),), jnp.float32)
    key_map = scatter_about(key_list[9], (HW, HW), HW ** -0.5, 0.25, ((0, 32),), jnp.float32)
    value_map = scatter_about(key_list[10], (HW, HW), HW ** -0.5, 0.25, ((0, 32),), jnp.float32)
    output_map = scatter_about(key_list[11], (HW, HW), (HW // 4) ** -0.5, 0.5, ((0, 32),), jnp.float32)
    midnorm_gain = jnp.clip(1.0 + 0.15 * jax.random.normal(key_list[12], (HW,), jnp.float32), 0.25, 1.75)
    midnorm_bias = scatter_about(key_list[13], (HW,), 0.3, 2.0, ((0, 32),), jnp.float32)
    expand_map = scatter_about(key_list[14], (HW, HFF), HW ** -0.5, 0.25, ((0, 32),), jnp.float32)
    reduce_map = scatter_about(key_list[15], (HFF, HW), (HFF // 2) ** -0.5, 0.1875, ((0, 32),), jnp.float32)
    embed_map = scatter_about(key_list[16], (HW, D), (HW * D // 16) ** -0.5, 0.0234375, ((0, 32),), jnp.float32)
    attention_gain = jnp.clip(1.0 + 0.15 * jax.random.normal(key_list[17], (2, D), jnp.float32), 0.25, 1.75).astype(jnp.bfloat16)
    query_weight = scatter_about(key_list[18], (2, D, D), D ** -0.5, 0.125, ((1, 8),))
    key_weight = scatter_about(key_list[19], (2, D, KV_HEADS * HEAD_DIM), D ** -0.5, 0.125, ((1, 8),))
    value_weight = scatter_about(key_list[20], (2, D, KV_HEADS * HEAD_DIM), D ** -0.5, 0.125, ((1, 8),))
    output_weight = scatter_about(key_list[21], (2, D, D), (D // 8) ** -0.5, 0.375, ((1, 8),))
    feed_gain = jnp.clip(1.0 + 0.15 * jax.random.normal(key_list[22], (2, D), jnp.float32), 0.25, 1.75).astype(jnp.bfloat16)
    gate_weight = scatter_about(key_list[23], (2, D, FF), D ** -0.5, 0.125, ((1, 8),))
    up_weight = scatter_about(key_list[24], (2, D, FF), D ** -0.5, 0.125, ((1, 8),))
    down_weight = scatter_about(key_list[25], (2, FF, D), (FF // 2) ** -0.5, 0.109375, ((1, 8),))
    final_gain = jnp.clip(1.0 + 0.15 * jax.random.normal(key_list[26], (D,), jnp.float32), 0.25, 1.75).astype(jnp.bfloat16)
    return dict(token_ids=token_ids, targets=targets, slot_ids=slot_ids, group_ids=group_ids, group_offsets=group_offsets, piece_table=piece_table, prenorm_gain=prenorm_gain, prenorm_bias=prenorm_bias, query_map=query_map, key_map=key_map, value_map=value_map, output_map=output_map, midnorm_gain=midnorm_gain, midnorm_bias=midnorm_bias, expand_map=expand_map, reduce_map=reduce_map, embed_map=embed_map, attention_gain=attention_gain, query_weight=query_weight, key_weight=key_weight, value_weight=value_weight, output_weight=output_weight, feed_gain=feed_gain, gate_weight=gate_weight, up_weight=up_weight, down_weight=down_weight, final_gain=final_gain)


norm_eps = 1e-05
highest = lax.Precision.HIGHEST

@jax.custom_vjp
def low(v):
    return lax.optimization_barrier(v.astype(jnp.bfloat16)).astype(jnp.float32)

@jax.custom_vjp
def low_back(v):
    return v

def low_keep(v):
    return (low(v), None)

def low_pass(kept, grad):
    return (grad,)

def back_keep(v):
    return (v, None)

def back_low(kept, grad):
    return (low(grad),)
low.defvjp(low_keep, low_pass)
low_back.defvjp(back_keep, back_low)

def matmul(former, latter):
    return jnp.dot(former, latter, precision=highest, preferred_element_type=jnp.float32)

def center_norm(values, gain_vec, bias_vector):
    center = values - lax.optimization_barrier(jnp.mean(values, axis=-1, keepdims=True))
    inverse = lax.rsqrt(lax.optimization_barrier(jnp.mean(center * center, axis=-1, keepdims=True)) + norm_eps)
    return center * inverse * gain_vec + bias_vector

def root_norm(values, gain_vec):
    return values * lax.rsqrt(lax.optimization_barrier(jnp.mean(values * values, axis=-1, keepdims=True)) + norm_eps) * gain_vec

def rope_tables(positions, head_width):
    halfway = head_width // 2
    frequency = jnp.exp(-jnp.log(10000.0) * (2.0 * jnp.arange(halfway, dtype=jnp.float32) / head_width))
    angles = jnp.arange(positions, dtype=jnp.float32)[:, None] * frequency[None, :]
    angles = jnp.concatenate([angles, angles], axis=1)
    return (jnp.cos(angles), jnp.sin(angles))

def apply_rotary(values, cosines, sines):
    halfway = values.shape[-1] // 2
    turned = jnp.concatenate([-values[..., halfway:], values[..., :halfway]], axis=-1)
    return values * cosines[None, :, None, :] + turned * sines[None, :, None, :]

def hyper_table(params, pieces):
    working = [low(item) for item in params]
    gain_one, bias_one, query_mat, key_mat, value_mat, out_mat, second_gain, bias_two, expand_mat, reduce_mat, embed_mat = working
    entries, slot_count, model_width = pieces.shape
    head_width = model_width // HYPER_HEAD_COUNT
    score_scale = head_width ** (-0.5)
    flat_in = pieces.reshape(entries * slot_count, model_width)
    attn_in = low(center_norm(flat_in, gain_one, bias_one))
    queries = low(low_back(matmul(attn_in, query_mat))).reshape(entries, slot_count, HYPER_HEAD_COUNT, head_width)
    key_rows = low(low_back(matmul(attn_in, key_mat))).reshape(entries, slot_count, HYPER_HEAD_COUNT, head_width)
    value_rows = low(low_back(matmul(attn_in, value_mat))).reshape(entries, slot_count, HYPER_HEAD_COUNT, head_width)
    scores = low_back(jnp.einsum('eshd,ethd->ehst', queries, key_rows, precision=highest) * score_scale)
    weights_low = low(jax.nn.softmax(scores, axis=-1))
    mixed = low(low_back(jnp.einsum('ehst,ethd->eshd', weights_low, value_rows, precision=highest)))
    middle = flat_in + low_back(matmul(mixed.reshape(entries * slot_count, model_width), out_mat))
    ffn_in = low(center_norm(middle, second_gain, bias_two))
    activated = low(jax.nn.gelu(low_back(matmul(ffn_in, expand_mat)), approximate=False))
    outcome = middle + low_back(matmul(activated, reduce_mat))
    pooled = low(lax.optimization_barrier(jnp.mean(outcome.reshape(entries, slot_count, model_width), axis=1)))
    return low(low_back(matmul(pooled, embed_mat)))

def decoder(hidden, weights, cosines, sines):
    gain_attn, query_mat, key_mat, value_mat, out_mat, gain_ffn, gate_mat, up_mat, down_mat = weights
    sequences, positions, model_width = hidden.shape
    head_width = cosines.shape[1]
    head_count = query_mat.shape[1] // head_width
    key_heads = key_mat.shape[1] // head_width
    shared = head_count // key_heads
    score_scale = head_width ** (-0.5)
    flat_in = hidden.reshape(sequences * positions, model_width)
    normed_one = low(root_norm(flat_in, gain_attn))
    query_pre = low_back(matmul(normed_one, query_mat)).reshape(sequences, positions, head_count, head_width)
    key_pre = low_back(matmul(normed_one, key_mat)).reshape(sequences, positions, key_heads, head_width)
    value_rows = low(low_back(matmul(normed_one, value_mat))).reshape(sequences, positions, key_heads, head_width)
    queries = low(apply_rotary(query_pre, cosines, sines)).reshape(sequences, positions, key_heads, shared, head_width)
    key_rows = low(apply_rotary(key_pre, cosines, sines))
    causal = jnp.arange(positions)[:, None] >= jnp.arange(positions)[None, :]
    scores = jnp.einsum('blkgd,bmkd->bkglm', queries, key_rows, precision=highest) * score_scale
    scores = low_back(jnp.where(causal, scores, -1e+30))
    weights_low = low(jax.nn.softmax(scores, axis=-1))
    mixed = low(low_back(jnp.einsum('bkglm,bmkd->blkgd', weights_low, value_rows, precision=highest)))
    middle = flat_in + low_back(matmul(mixed.reshape(sequences * positions, model_width), out_mat))
    normed_two = low(root_norm(middle, gain_ffn))
    gate_pre = low_back(matmul(normed_two, gate_mat))
    up_pre = low_back(matmul(normed_two, up_mat))
    activated = low(jax.nn.silu(gate_pre) * up_pre)
    outcome = middle + low_back(matmul(activated, down_mat))
    return low(low_back(outcome)).reshape(sequences, positions, model_width)

def reference(token_ids, targets, slot_ids, group_ids, group_offsets, piece_table, prenorm_gain, prenorm_bias, query_map, key_map, value_map, output_map, midnorm_gain, midnorm_bias, expand_map, reduce_map, embed_map, attention_gain, query_weight, key_weight, value_weight, output_weight, feed_gain, gate_weight, up_weight, down_weight, final_gain):
    piece_rows = (group_offsets[group_ids][:, None] + slot_ids).astype(jnp.int32)
    pieces = jnp.take(piece_table, piece_rows, axis=0).astype(jnp.float32)
    stacks = (attention_gain, query_weight, key_weight, value_weight, output_weight, feed_gain, gate_weight, up_weight, down_weight)
    layers = [tuple((stack[level].astype(jnp.float32) for stack in stacks)) for level in range(2)]
    cosines, sines = rope_tables(LEN, HEAD_DIM)
    gain_end = final_gain.astype(jnp.float32)
    token_total = SEQS * MB * LEN

    def block_loss(table, block_ids, block_targets):
        hidden = low_back(jnp.take(table, block_ids.reshape(-1), axis=0)).reshape(MB, LEN, D)
        for weights in layers:
            hidden = decoder(hidden, weights, cosines, sines)
        flat = hidden.reshape(MB * LEN, D)
        normed = low(root_norm(flat, gain_end))
        logits = low_back(jnp.dot(normed, table.T, precision=highest, preferred_element_type=jnp.float32))
        log_norm = jax.nn.logsumexp(logits, axis=-1)
        picked = jnp.take_along_axis(logits, block_targets.reshape(-1, 1), axis=1)[:, 0]
        return jnp.sum(log_norm - picked)

    def total_loss(params):
        table = hyper_table(params, pieces)

        def advance(running, inputs):
            block_ids, block_targets = inputs
            return (running + jax.checkpoint(block_loss)(table, block_ids, block_targets), None)
        running, unused = lax.scan(advance, jnp.zeros((), jnp.float32), (token_ids, targets))
        return running / token_total
    params = (prenorm_gain, prenorm_bias, query_map, key_map, value_map, output_map, midnorm_gain, midnorm_bias, expand_map, reduce_map, embed_map)
    mean_loss, pullback = jax.vjp(total_loss, params)
    gradients = pullback(jnp.ones_like(mean_loss))[0]
    return (mean_loss, gradients[0], gradients[1], gradients[2], gradients[3], gradients[4], gradients[5], gradients[6], gradients[7], gradients[8], gradients[9], gradients[10])
```

```python
import functools

import jax
import jax.numpy as jnp
from jax import lax
from jax.experimental import pallas as pl
from jax.experimental.pallas import tpu as pltpu
from jax.sharding import PartitionSpec as P

HEAD_DIM = 64
HYPER_HEAD_COUNT = 8
MB = 2
LEN = 64
TEAM = 8
SECTIONS = 4
ROWS = MB * LEN * TEAM // SECTIONS
OWN = ROWS // TEAM
LANES = 128
MESH_IDS = pl.DeviceIdType.MESH
ANYWHERE = pl.BlockSpec(memory_space=pl.ANY)
IN_VMEM = pl.BlockSpec(memory_space=pltpu.VMEM)
VMEM_LIMIT = 56 * 1024 * 1024

norm_eps = 1e-05
inv_root_two = 0.7071067811865476
inv_root_tau = 0.3989422804014327


def matmul(former, latter):
    return jnp.dot(former, latter, preferred_element_type=jnp.float32)


def times_trans(former, latter):
    return lax.dot_general(
        former, latter, (((1,), (1,)), ((), ())), preferred_element_type=jnp.float32
    )


def trans_times(former, latter):
    return lax.dot_general(
        former, latter, (((0,), (0,)), ((), ())), preferred_element_type=jnp.float32
    )


def center_norm(values):
    center = values - jnp.mean(values, axis=-1, keepdims=True)
    inverse = lax.rsqrt(jnp.mean(center * center, axis=-1, keepdims=True) + norm_eps)
    return (center * inverse, inverse)


def center_back(normed, inverse, normed_grad):
    mean_grad = jnp.mean(normed_grad, axis=-1, keepdims=True)
    mean_mix = jnp.mean(normed_grad * normed, axis=-1, keepdims=True)
    return inverse * (normed_grad - mean_grad - normed * mean_mix)


def root_inverse(values):
    return lax.rsqrt(jnp.mean(values * values, axis=-1, keepdims=True) + norm_eps)


def reciprocal_root_backward(values, inverse, gain_vec, outer_grad):
    scaled = outer_grad * gain_vec
    mixing = jnp.mean(scaled * values, axis=-1, keepdims=True)
    return inverse * scaled - values * inverse * inverse * inverse * mixing


def rope_tables(positions, head_width):
    halfway = head_width // 2
    frequency = jnp.exp(
        -jnp.log(10000.0) * (2.0 * jnp.arange(halfway, dtype=jnp.float32) / head_width)
    )
    angles = jnp.arange(positions, dtype=jnp.float32)[:, None] * frequency[None, :]
    angles = jnp.concatenate([angles, angles], axis=1)
    return (jnp.cos(angles), jnp.sin(angles))


def apply_rotary(values, cosines, sines):
    halfway = values.shape[-1] // 2
    turned = jnp.concatenate([-values[..., halfway:], values[..., :halfway]], axis=-1)
    return values * cosines[None, :, None, :] + turned * sines[None, :, None, :]


def invert_rotary(gradient, cosines, sines):
    halfway = gradient.shape[-1] // 2
    scaled = gradient * sines[None, :, None, :]
    turned = jnp.concatenate([scaled[..., halfway:], -scaled[..., :halfway]], axis=-1)
    return gradient * cosines[None, :, None, :] + turned


def hyper_forward(pieces, params, head_count):
    (
        gain_one,
        bias_one,
        query_mat,
        key_mat,
        value_mat,
        out_mat,
        second_gain,
        bias_two,
        expand_mat,
        reduce_mat,
        embed_mat,
    ) = params
    entries, slot_count, model_width = pieces.shape
    head_width = model_width // head_count
    score_scale = head_width ** (-0.5)
    flat_in = pieces.reshape(entries * slot_count, model_width)
    normed_one, inverse_one = center_norm(flat_in)
    attn_in = (normed_one * gain_one.astype(jnp.float32) + bias_one.astype(jnp.float32)).astype(
        jnp.bfloat16
    )
    queries = (
        matmul(attn_in, query_mat)
        .astype(jnp.bfloat16)
        .reshape(entries, slot_count, head_count, head_width)
    )
    key_rows = (
        matmul(attn_in, key_mat)
        .astype(jnp.bfloat16)
        .reshape(entries, slot_count, head_count, head_width)
    )
    value_rows = (
        matmul(attn_in, value_mat)
        .astype(jnp.bfloat16)
        .reshape(entries, slot_count, head_count, head_width)
    )
    scores = (
        jnp.einsum("eshd,ethd->ehst", queries, key_rows, preferred_element_type=jnp.float32)
        * score_scale
    )
    weights_full = jax.nn.softmax(scores, axis=-1)
    weights_low = weights_full.astype(jnp.bfloat16)
    mixed = jnp.einsum(
        "ehst,ethd->eshd", weights_low, value_rows, preferred_element_type=jnp.float32
    )
    mixed = mixed.astype(jnp.bfloat16).reshape(entries * slot_count, model_width)
    middle = flat_in + matmul(mixed, out_mat)
    normed_two, inverse_two = center_norm(middle)
    ffn_in = (normed_two * second_gain.astype(jnp.float32) + bias_two.astype(jnp.float32)).astype(
        jnp.bfloat16
    )
    expanded = matmul(ffn_in, expand_mat)
    activated = jax.nn.gelu(expanded, approximate=False).astype(jnp.bfloat16)
    outcome = middle + matmul(activated, reduce_mat)
    pooled = jnp.mean(outcome.reshape(entries, slot_count, model_width), axis=1).astype(
        jnp.bfloat16
    )
    table_rows = matmul(pooled, embed_mat).astype(jnp.bfloat16)
    stored = (
        normed_one,
        inverse_one,
        attn_in,
        queries,
        key_rows,
        value_rows,
        weights_full,
        weights_low,
        mixed,
        normed_two,
        inverse_two,
        ffn_in,
        expanded,
        activated,
        pooled,
    )
    return (table_rows, stored)


def hyper_backward(params, stored, table_grad):
    (
        gain_one,
        bias_one,
        query_mat,
        key_mat,
        value_mat,
        out_mat,
        second_gain,
        bias_two,
        expand_mat,
        reduce_mat,
        embed_mat,
    ) = params
    (
        normed_one,
        inverse_one,
        attn_in,
        queries,
        key_rows,
        value_rows,
        weights_full,
        weights_low,
        mixed,
        normed_two,
        inverse_two,
        ffn_in,
        expanded,
        activated,
        pooled,
    ) = stored
    entries, slot_count, head_total, head_width = queries.shape
    model_width = head_total * head_width
    score_scale = head_width ** (-0.5)
    grad_low = table_grad.astype(jnp.bfloat16)
    grad_embed = trans_times(pooled, grad_low)
    pooled_grad = times_trans(grad_low, embed_mat) / slot_count
    outcome_grad = jnp.broadcast_to(pooled_grad[:, None, :], (entries, slot_count, model_width))
    outcome_grad = outcome_grad.reshape(entries * slot_count, model_width)
    outcome_low = outcome_grad.astype(jnp.bfloat16)
    grad_reduce = trans_times(activated, outcome_low)
    act_grad = times_trans(outcome_low, reduce_mat)
    slope = (
        0.5 * (1.0 + lax.erf(expanded * inv_root_two))
        + expanded * jnp.exp(-0.5 * expanded * expanded) * inv_root_tau
    )
    expanded_low = (act_grad * slope).astype(jnp.bfloat16)
    grad_expand = trans_times(ffn_in, expanded_low)
    ffn_grad = times_trans(expanded_low, expand_mat)
    grad_midscale = jnp.sum(ffn_grad * normed_two, axis=0)
    grad_midshift = jnp.sum(ffn_grad, axis=0)
    middle_grad = outcome_grad + center_back(
        normed_two, inverse_two, ffn_grad * second_gain.astype(jnp.float32)
    )
    middle_low = middle_grad.astype(jnp.bfloat16)
    grad_output = trans_times(mixed, middle_low)
    mixed_grad = times_trans(middle_low, out_mat).astype(jnp.bfloat16).reshape(queries.shape)
    weight_grad = jnp.einsum(
        "eshd,ethd->ehst", mixed_grad, value_rows, preferred_element_type=jnp.float32
    )
    value_grad = jnp.einsum(
        "ehst,eshd->ethd", weights_low, mixed_grad, preferred_element_type=jnp.float32
    )
    score_grad = weights_full * (
        weight_grad - jnp.sum(weights_full * weight_grad, axis=-1, keepdims=True)
    )
    score_grad = score_grad.astype(jnp.bfloat16)
    query_grad = (
        jnp.einsum("ehst,ethd->eshd", score_grad, key_rows, preferred_element_type=jnp.float32)
        * score_scale
    )
    key_grad = (
        jnp.einsum("ehst,eshd->ethd", score_grad, queries, preferred_element_type=jnp.float32)
        * score_scale
    )
    query_low = query_grad.astype(jnp.bfloat16).reshape(entries * slot_count, model_width)
    key_low = key_grad.astype(jnp.bfloat16).reshape(entries * slot_count, model_width)
    value_low = value_grad.astype(jnp.bfloat16).reshape(entries * slot_count, model_width)
    grad_query = trans_times(attn_in, query_low)
    grad_key = trans_times(attn_in, key_low)
    grad_value = trans_times(attn_in, value_low)
    attention_gradient = (
        times_trans(query_low, query_mat)
        + times_trans(key_low, key_mat)
        + times_trans(value_low, value_mat)
    )
    grad_prescale = jnp.sum(attention_gradient * normed_one, axis=0)
    prenorm_bias_gradient = jnp.sum(attention_gradient, axis=0)
    return (
        grad_prescale,
        prenorm_bias_gradient,
        grad_query,
        grad_key,
        grad_value,
        grad_output,
        grad_midscale,
        grad_midshift,
        grad_expand,
        grad_reduce,
        grad_embed,
    )


def greet(peers):
    barrier = pltpu.get_barrier_semaphore()
    for peer in peers:
        pl.semaphore_signal(barrier, inc=1, device_id=peer, device_id_type=MESH_IDS)
    pl.semaphore_wait(barrier, len(peers))


def remote(source, target, send, recv, peer):
    return pltpu.make_async_remote_copy(
        src_ref=source,
        dst_ref=target,
        send_sem=send,
        recv_sem=recv,
        device_id=peer,
        device_id_type=MESH_IDS,
    )


def settings(collective_id):
    return pltpu.CompilerParams(
        collective_id=collective_id, has_side_effects=True, vmem_limit_bytes=VMEM_LIMIT
    )


def dma_sems(*shape):
    return pltpu.SemaphoreType.DMA(shape)


def fold_kernel(finish, outer, n_in, n_out, *refs):
    partial, extras = refs[0], refs[1:n_in]
    gathered, outs = refs[n_in], refs[n_in + 1 : n_in + n_out]
    (
        own,
        side,
        pair,
        far,
        ready,
        load_sem,
        keep_sem,
        side_send,
        side_recv,
        far_send,
        far_recv,
        out_send,
        out_recv,
        over_send,
        over_recv,
    ) = refs[n_in + n_out :]
    wide = lax.axis_index("wide")
    rank, team = wide // outer, wide % outer
    line, column = rank // 2, rank % 2
    lines = TEAM // 2

    def at(some_line, some_column):
        return (some_line % lines) * 2 + some_column

    def member(some_line, some_column):
        return {"wide": at(some_line, some_column) * outer + team}

    beside = member(line, 1 - column)
    greet([beside] + [member(line + j, column) for j in range(1, lines)])
    order = (2, 1, 3, 0)
    loads = [
        pltpu.make_async_copy(partial.at[at(line + j, column)], own.at[j], load_sem.at[j])
        for j in range(lines)
    ]
    sides = [
        remote(
            partial.at[at(line + j, 1 - column)],
            side.at[j],
            side_send.at[j],
            side_recv.at[j],
            beside,
        )
        for j in range(lines)
    ]
    fars = [None] + [
        remote(pair.at[j], far.at[j], far_send.at[j], far_recv.at[j], member(line + j, column))
        for j in range(1, lines)
    ]
    for j in order:
        sides[j].start()
        loads[j].start()
    for j in order[:3]:
        loads[j].wait()
        sides[j].wait_recv()
        pair[j] = (own[j].astype(jnp.float32) + side[j].astype(jnp.float32)).astype(jnp.bfloat16)
        fars[j].start()
    loads[0].wait()
    sides[0].wait_recv()
    total = own[0].astype(jnp.float32) + side[0].astype(jnp.float32)
    for j in (1, 3, 2):
        fars[j].wait_recv()
        total = total + far[j].astype(jnp.float32)
    ready[...] = finish(total, extras, outs)
    mine = at(line, column)
    keep = pltpu.make_async_copy(ready, gathered.at[mine], keep_sem)
    pushes = [None] + [
        remote(ready, gathered.at[mine], out_send.at[j], out_recv.at[j], member(line + j, column))
        for j in range(1, lines)
    ]
    overs = [
        remote(
            ready if j == 0 else gathered.at[at(line - j, column)],
            gathered.at[at(line - j, column)],
            over_send.at[j],
            over_recv.at[j],
            beside,
        )
        for j in range(lines)
    ]
    for j in (2, 1, 3):
        pushes[j].start()
    overs[0].start()
    keep.start()
    for j in (1, 3, 2):
        pushes[j].wait_recv()
        overs[j].start()
    for j in range(lines):
        overs[j].wait()
        sides[j].wait_send()
        if j:
            fars[j].wait_send()
            pushes[j].wait_send()
    keep.wait()


def fold(finish, outer, collective_id, partial, extras, outs):
    width = partial.shape[-1]
    lines = TEAM // 2
    slots = pltpu.VMEM((lines, OWN, width), jnp.bfloat16)
    return pl.pallas_call(
        functools.partial(fold_kernel, finish, outer, 1 + len(extras), 1 + len(outs)),
        out_shape=(jax.ShapeDtypeStruct((TEAM, OWN, width), jnp.bfloat16),)
        + tuple(jax.ShapeDtypeStruct((OWN, width), kind) for kind in outs),
        in_specs=[ANYWHERE] + [IN_VMEM] * len(extras),
        out_specs=(ANYWHERE,) + (IN_VMEM,) * len(outs),
        scratch_shapes=[slots, slots, slots, slots, pltpu.VMEM((OWN, width), jnp.bfloat16)]
        + [dma_sems(lines), pltpu.SemaphoreType.DMA]
        + [dma_sems(lines)] * 8,
        compiler_params=settings(collective_id),
        name=finish.__name__,
    )(partial.reshape(TEAM, OWN, width), *extras)


def inject(total, extras, outs):
    (gain,) = extras
    hidden = total.astype(jnp.bfloat16)
    outs[0][...] = hidden
    wide = hidden.astype(jnp.float32)
    return (wide * root_inverse(wide) * gain[...]).astype(jnp.bfloat16)


def enter_feed(total, extras, outs):
    hidden, gain = extras
    middle = hidden[...].astype(jnp.float32) + total
    outs[0][...] = middle
    return (middle * root_inverse(middle) * gain[...]).astype(jnp.bfloat16)


def leave_layer(total, extras, outs):
    middle, gain = extras
    hidden = (middle[...] + total).astype(jnp.bfloat16)
    outs[0][...] = hidden
    wide = hidden.astype(jnp.float32)
    return (wide * root_inverse(wide) * gain[...]).astype(jnp.bfloat16)


def head_back(total, extras, outs):
    hidden, gain = extras
    wide = hidden[...].astype(jnp.float32)
    grad = reciprocal_root_backward(wide, root_inverse(wide), gain[...], total)
    grad = grad.astype(jnp.bfloat16)
    outs[0][...] = grad
    return grad


def feed_back(total, extras, outs):
    outer_grad, middle, gain = extras
    wide = middle[...]
    grad = outer_grad[...].astype(jnp.float32) + reciprocal_root_backward(
        wide, root_inverse(wide), gain[...], total
    )
    outs[0][...] = grad
    return grad.astype(jnp.bfloat16)


def layer_back(total, extras, outs):
    middle_grad, hidden, gain = extras
    wide = hidden[...].astype(jnp.float32)
    grad = middle_grad[...] + reciprocal_root_backward(wide, root_inverse(wide), gain[...], total)
    grad = grad.astype(jnp.bfloat16)
    outs[0][...] = grad
    return grad


def team_kernel(outer, block, gathered, send, recv):
    wide = lax.axis_index("wide")
    rank, team = wide // outer, wide % outer
    peers = [{"wide": ((rank + k) % TEAM) * outer + team} for k in range(1, TEAM)]
    greet(peers)
    copies = [
        remote(block, gathered.at[rank], send.at[k], recv.at[k], peer)
        for k, peer in enumerate(peers)
    ]
    for copy in copies:
        copy.start()
    gathered[rank] = block[...]
    for copy in copies:
        copy.wait()


def team_gather(outer, collective_id, block):
    return pl.pallas_call(
        functools.partial(team_kernel, outer),
        out_shape=jax.ShapeDtypeStruct((TEAM,) + block.shape, block.dtype),
        in_specs=[IN_VMEM],
        out_specs=IN_VMEM,
        scratch_shapes=[dma_sems(TEAM - 1), dma_sems(TEAM - 1)],
        compiler_params=settings(collective_id),
        name="team_gather",
    )(block)


def section_places():
    section = lax.axis_index("section")
    core = section % 2
    partner = section + 1 - 2 * core
    across = (section + 2) % SECTIONS
    return section, partner, across


def section_gather_kernel(block, gathered, keep_sem, send, recv):
    section, partner, across = section_places()
    greet([{"section": partner}, {"section": across}])
    keep = pltpu.make_async_copy(block, gathered.at[section], keep_sem)
    near = remote(block, gathered.at[section], send.at[0], recv.at[0], {"section": partner})
    far = remote(block, gathered.at[section], send.at[1], recv.at[1], {"section": across})
    on = remote(
        gathered.at[across], gathered.at[across], send.at[2], recv.at[2], {"section": partner}
    )
    far.start()
    near.start()
    keep.start()
    far.wait_recv()
    on.start()
    near.wait()
    on.wait()
    far.wait_send()
    keep.wait()


def section_gather(collective_id, block):
    return pl.pallas_call(
        section_gather_kernel,
        out_shape=jax.ShapeDtypeStruct((SECTIONS,) + block.shape, block.dtype),
        in_specs=[ANYWHERE],
        out_specs=ANYWHERE,
        scratch_shapes=[pltpu.SemaphoreType.DMA, dma_sems(3), dma_sems(3)],
        compiler_params=settings(collective_id),
        name="section_gather",
    )(block)


def section_sum_kernel(partial, loss, summed, loss_sum, own, near, pair, far, loss_near, loss_pair, loss_far, load_sem, send, recv):
    section, partner, across = section_places()
    beyond = (partner + 2) % SECTIONS
    greet([{"section": partner}, {"section": across}])
    loads = [
        pltpu.make_async_copy(partial.at[section], own.at[0], load_sem.at[0]),
        pltpu.make_async_copy(partial.at[across], own.at[1], load_sem.at[1]),
    ]
    nears = [
        remote(partial.at[partner], near.at[0], send.at[0], recv.at[0], {"section": partner}),
        remote(partial.at[beyond], near.at[1], send.at[1], recv.at[1], {"section": partner}),
        remote(loss, loss_near, send.at[2], recv.at[2], {"section": partner}),
    ]
    fars = [
        remote(pair, far, send.at[3], recv.at[3], {"section": across}),
        remote(loss_pair, loss_far, send.at[4], recv.at[4], {"section": across}),
    ]
    for j in (1, 2, 0):
        nears[j].start()
    loads[1].start()
    loads[0].start()
    loads[1].wait()
    nears[1].wait_recv()
    pair[...] = (own[1].astype(jnp.float32) + near[1].astype(jnp.float32)).astype(jnp.bfloat16)
    fars[0].start()
    nears[2].wait_recv()
    loss_pair[...] = loss[...] + loss_near[...]
    fars[1].start()
    loads[0].wait()
    nears[0].wait_recv()
    total = own[0].astype(jnp.float32) + near[0].astype(jnp.float32)
    fars[0].wait_recv()
    summed[...] = total + far[...].astype(jnp.float32)
    fars[1].wait_recv()
    loss_sum[...] = loss_pair[...] + loss_far[...]
    for copy in nears + fars:
        copy.wait_send()


def section_sum(collective_id, partial, loss):
    shape = partial.shape[1:]
    low, low_two = pltpu.VMEM(shape, jnp.bfloat16), pltpu.VMEM((2,) + shape, jnp.bfloat16)
    number = pltpu.VMEM(loss.shape, jnp.float32)
    return pl.pallas_call(
        section_sum_kernel,
        out_shape=(
            jax.ShapeDtypeStruct(shape, jnp.float32),
            jax.ShapeDtypeStruct(loss.shape, jnp.float32),
        ),
        in_specs=[ANYWHERE, IN_VMEM],
        out_specs=(IN_VMEM, IN_VMEM),
        scratch_shapes=[low_two, low_two, low, low, number, number, number]
        + [dma_sems(2), dma_sems(5), dma_sems(5)],
        compiler_params=settings(collective_id),
        name="section_sum",
    )(partial, loss)


def all_places(halves):
    section, partner, across = section_places()
    wide = lax.axis_index("wide")
    line, column = wide // 2, wide % 2

    def wide_at(j):
        return ((line + j) % halves) * 2 + column

    return section, partner, across, wide, wide_at


def steps_of(x_first, section, partner, across, wide):
    column_flip = wide + 1 - 2 * (wide % 2)
    x_step = ({"wide": column_flip}, False, True)
    y_step = ({"section": across}, True, False)
    return (x_step, y_step) if x_first else (y_step, x_step)


def owner_of(home, flips_y, flips_x, wide_block):
    section = (home + 2) % SECTIONS if flips_y else home
    return section, (wide_block + 1 - 2 * (wide_block % 2) if flips_x else wide_block)


def spread_kernel(count, halves, *refs):
    blocks, gathereds = refs[:count], refs[count : 2 * count]
    keep_sem, z_send, a_send, b_send, c_send, z_recv, a_recv, b_recv, c_recv = refs[2 * count :]
    section, partner, across, wide, wide_at = all_places(halves)
    beside = wide + 1 - 2 * (wide % 2)
    barrier = pltpu.get_barrier_semaphore()
    for peer in ({"section": partner}, {"section": across}, {"wide": beside}):
        pl.semaphore_signal(barrier, inc=1, device_id=peer, device_id_type=MESH_IDS)

    def hello(j, carry):
        peer = {"wide": wide_at(j)}
        pl.semaphore_signal(barrier, inc=1, device_id=peer, device_id_type=MESH_IDS)
        return carry

    lax.fori_loop(1, halves, hello, 0)
    pl.semaphore_wait(barrier, 3 + halves - 1)

    keeps = [
        pltpu.make_async_copy(blocks[n], gathereds[n].at[section, wide], keep_sem.at[n])
        for n in range(count)
    ]

    def z_copy(n, j):
        return remote(
            blocks[n],
            gathereds[n].at[section, wide],
            z_send.at[n, j],
            z_recv.at[n, j],
            {"wide": wide_at(j)},
        )

    def a_copy(n, j):
        (peer, _, _), _ = steps_of(n == 0, section, partner, across, wide)
        block = gathereds[n].at[section, wide_at(-j)]
        return remote(block, block, a_send.at[n, j], a_recv.at[n, j], peer)

    def b_copy(n, flip, j):
        (_, y_a, x_a), (peer, _, _) = steps_of(n == 0, section, partner, across, wide)
        place = owner_of(section, y_a and flip, x_a and flip, wide_at(-j))
        block = gathereds[n].at[place[0], place[1]]
        slot = j + (halves if flip else 0)
        return remote(block, block, b_send.at[n, slot], b_recv.at[n, slot], peer)

    def c_copy(n, which):
        home = (section + 2) % SECTIONS if which else section
        block = gathereds[n].at[home]
        return remote(
            block, block, c_send.at[n, which], c_recv.at[n, which], {"section": partner}
        )

    for keep in keeps:
        keep.start()

    def start_z(j, carry):
        for n in range(count):
            z_copy(n, j).start()
        return carry

    lax.fori_loop(1, halves, start_z, 0)
    for n in range(count):
        keeps[n].wait()
        a_copy(n, 0).start()
        b_copy(n, False, 0).start()

    def pass_z(j, carry):
        for n in range(count):
            z_copy(n, j).wait_recv()
            a_copy(n, j).start()
            b_copy(n, False, j).start()
        return carry

    lax.fori_loop(1, halves, pass_z, 0)

    def pass_a(j, carry):
        for n in range(count):
            a_copy(n, j).wait_recv()
            b_copy(n, True, j).start()
        return carry

    lax.fori_loop(0, halves, pass_a, 0)

    def settle_b(j, carry):
        for n in range(count):
            for flip in (False, True):
                b_copy(n, flip, j).wait_recv()
        return carry

    c_copy(0, 0).start()
    lax.fori_loop(0, halves, settle_b, 0)
    c_copy(0, 1).start()
    for n in range(1, count):
        c_copy(n, 0).start()
        c_copy(n, 1).start()
    for n in range(count):
        c_copy(n, 0).wait()
        c_copy(n, 1).wait()

    def drain(j, carry):
        for n in range(count):
            a_copy(n, j).wait_send()
            b_copy(n, False, j).wait_send()
            b_copy(n, True, j).wait_send()
        return carry

    lax.fori_loop(0, halves, drain, 0)

    def drain_z(j, carry):
        for n in range(count):
            z_copy(n, j).wait_send()
        return carry

    lax.fori_loop(1, halves, drain_z, 0)


def spread(collective_id, wides, blocks):
    count, halves = len(blocks), wides // 2
    return pl.pallas_call(
        functools.partial(spread_kernel, count, halves),
        out_shape=tuple(
            jax.ShapeDtypeStruct((SECTIONS, wides) + block.shape, block.dtype) for block in blocks
        ),
        in_specs=[ANYWHERE] * count,
        out_specs=(ANYWHERE,) * count,
        scratch_shapes=[dma_sems(count)]
        + [
            dma_sems(count, halves),
            dma_sems(count, halves),
            dma_sems(count, 2 * halves),
            dma_sems(count, 2),
        ]
        * 2,
        compiler_params=settings(collective_id),
        name="spread",
    )(*blocks)


def collect_kernel(count, halves, *refs):
    partials, sums = refs[:count], refs[count : 2 * count]
    keeps, c_in, b_in, a_in, z_in = (refs[(2 + k) * count : (3 + k) * count] for k in range(5))
    load_sem, c_send, b_send, a_send, z_send, c_recv, b_recv, a_recv, z_recv = refs[7 * count :]
    section, partner, across, wide, wide_at = all_places(halves)
    beside = wide + 1 - 2 * (wide % 2)
    barrier = pltpu.get_barrier_semaphore()
    for peer in ({"section": partner}, {"section": across}, {"wide": beside}):
        pl.semaphore_signal(barrier, inc=1, device_id=peer, device_id_type=MESH_IDS)

    def hello(j, carry):
        peer = {"wide": wide_at(j)}
        pl.semaphore_signal(barrier, inc=1, device_id=peer, device_id_type=MESH_IDS)
        return carry

    lax.fori_loop(1, halves, hello, 0)
    pl.semaphore_wait(barrier, 3 + halves - 1)

    def place(n, home, flip_b, flip_a, j):
        (_, y_a, x_a), (_, y_b, x_b) = steps_of(n == 0, section, partner, across, wide)
        flips_y = (y_a and flip_a) or (y_b and flip_b)
        flips_x = (x_a and flip_a) or (x_b and flip_b)
        return owner_of(home, flips_y, flips_x, wide_at(j))

    def load(n, fb, fa, j):
        owner = place(n, section, fb, fa, j)
        slot = (fb * 2 + fa) * halves + j
        return pltpu.make_async_copy(
            partials[n].at[owner[0], owner[1]], keeps[n].at[slot], load_sem.at[n, slot]
        )

    def c_copy(n, fb, fa, j):
        owner = place(n, partner, fb, fa, j)
        slot = (fb * 2 + fa) * halves + j
        return remote(
            partials[n].at[owner[0], owner[1]],
            c_in[n].at[slot],
            c_send.at[n, slot],
            c_recv.at[n, slot],
            {"section": partner},
        )

    def b_copy(n, fa, j):
        _, (peer, _, _) = steps_of(n == 0, section, partner, across, wide)
        slot = fa * halves + j
        return remote(
            keeps[n].at[2 * halves + slot],
            b_in[n].at[slot],
            b_send.at[n, slot],
            b_recv.at[n, slot],
            peer,
        )

    def a_copy(n, j):
        (peer, _, _), _ = steps_of(n == 0, section, partner, across, wide)
        return remote(
            keeps[n].at[halves + j], a_in[n].at[j], a_send.at[n, j], a_recv.at[n, j], peer
        )

    def z_copy(n, j):
        return remote(
            keeps[n].at[j],
            z_in[n].at[j],
            z_send.at[n, j],
            z_recv.at[n, j],
            {"wide": wide_at(j)},
        )

    def add(n, slot, more):
        keeps[n][slot] = (
            keeps[n][slot].astype(jnp.float32) + more.astype(jnp.float32)
        ).astype(jnp.bfloat16)

    groups = ((1, 1), (1, 0), (0, 1), (0, 0))
    for fb, fa in groups:

        def start_c(j, carry):
            for n in range(count):
                c_copy(n, fb, fa, j).start()
                load(n, fb, fa, j).start()
            return carry

        lax.fori_loop(0, halves, start_c, 0)

    for fb, fa in groups:

        def sum_c(j, carry):
            for n in range(count):
                slot = (fb * 2 + fa) * halves + j
                load(n, fb, fa, j).wait()
                c_copy(n, fb, fa, j).wait_recv()
                add(n, slot, c_in[n][slot])
                if fb:
                    b_copy(n, fa, j).start()
            return carry

        lax.fori_loop(0, halves, sum_c, 0)

    for fa in (1, 0):

        def sum_b(j, carry):
            for n in range(count):
                slot = fa * halves + j
                b_copy(n, fa, j).wait_recv()
                add(n, slot, b_in[n][slot])
                if fa:
                    a_copy(n, j).start()
            return carry

        lax.fori_loop(0, halves, sum_b, 0)

    def sum_a(j, carry):
        for n in range(count):
            a_copy(n, j).wait_recv()
            add(n, j, a_in[n][j])
            z_copy(n, j).start()
        return carry

    lax.fori_loop(1, halves, sum_a, 0)
    for n in range(count):
        a_copy(n, 0).wait_recv()
        sums[n][...] = keeps[n][0].astype(jnp.float32) + a_in[n][0].astype(jnp.float32)

    def sum_z(j, carry):
        for n in range(count):
            z_copy(n, j).wait_recv()
            sums[n][...] += z_in[n][j].astype(jnp.float32)
        return carry

    lax.fori_loop(1, halves, sum_z, 0)

    def drain(j, carry):
        for n in range(count):
            for fb, fa in groups:
                c_copy(n, fb, fa, j).wait_send()
            b_copy(n, 0, j).wait_send()
            b_copy(n, 1, j).wait_send()
            a_copy(n, j).wait_send()
        return carry

    lax.fori_loop(0, halves, drain, 0)

    def drain_z(j, carry):
        for n in range(count):
            z_copy(n, j).wait_send()
        return carry

    lax.fori_loop(1, halves, drain_z, 0)


def collect(collective_id, partials):
    count, halves = len(partials), partials[0].shape[1] // 2
    shapes = [partial.shape[2:] for partial in partials]

    def slots(number):
        return [pltpu.VMEM((number,) + shape, jnp.bfloat16) for shape in shapes]

    return pl.pallas_call(
        functools.partial(collect_kernel, count, halves),
        out_shape=tuple(jax.ShapeDtypeStruct(shape, jnp.float32) for shape in shapes),
        in_specs=[ANYWHERE] * count,
        out_specs=(IN_VMEM,) * count,
        scratch_shapes=slots(4 * halves)
        + slots(4 * halves)
        + slots(2 * halves)
        + slots(halves)
        + slots(halves)
        + [dma_sems(count, 4 * halves)]
        + [
            dma_sems(count, 4 * halves),
            dma_sems(count, 2 * halves),
            dma_sems(count, halves),
            dma_sems(count, halves),
        ]
        * 2,
        compiler_params=settings(collective_id),
        name="collect",
    )(*partials)


def column_starts(rank, feed_width):
    share = feed_width // TEAM
    return (rank * share) // LANES * LANES, (rank // 4) * LANES


def reshard_kernel(
    outer,
    span,
    query,
    key,
    value,
    gate,
    up,
    small,
    notes,
    heads_out,
    feed_out,
    small_out,
    notes_out,
    keep_sem,
    push_send,
    push_recv,
    y_send,
    y_recv,
    core_send,
    core_recv,
    small_send,
    small_recv,
    notes_send,
    notes_recv,
):
    section, partner, across = section_places()
    wide = lax.axis_index("wide")
    rank, team = wide // outer, wide % outer
    depth, rows = query.shape[0], query.shape[1]
    half = rows // 2
    mine = pl.ds(pl.multiple_of((section // 2) * half, half), half)
    q_width = query.shape[2] // TEAM

    def member(k):
        return {"wide": ((rank + k) % TEAM) * outer + team}

    greet([{"section": partner}, {"section": across}] + [member(k) for k in range(1, TEAM)])

    def pieces(core, target_rank):
        feed_start, head_start = column_starts(target_rank, gate.shape[2])
        feed_start = pl.multiple_of(feed_start, LANES)
        head_start = pl.multiple_of(head_start, LANES)
        if core == 0:
            return [
                (gate, pl.ds(feed_start, span), feed_out, pl.ds(0, span)),
                (
                    query,
                    pl.ds(pl.multiple_of(target_rank * q_width, LANES), q_width),
                    heads_out,
                    pl.ds(0, q_width),
                ),
            ]
        return [
            (up, pl.ds(feed_start, span), feed_out, pl.ds(span, span)),
            (key, pl.ds(head_start, LANES), heads_out, pl.ds(q_width, LANES)),
            (value, pl.ds(head_start, LANES), heads_out, pl.ds(q_width + LANES, LANES)),
        ]

    for k in range(1, TEAM):
        remote(
            small, small_out.at[rank], small_send.at[k], small_recv.at[k], member(k)
        ).start()
        remote(
            notes, notes_out.at[rank], notes_send.at[k], notes_recv.at[k], member(k)
        ).start()
    small_keep = pltpu.make_async_copy(small, small_out.at[rank], keep_sem.at[2])
    notes_keep = pltpu.make_async_copy(notes, notes_out.at[rank], keep_sem.at[3])
    small_keep.start()
    notes_keep.start()

    total = span + q_width

    def layer_bytes(layer, semaphores):
        block = feed_out.at[layer, :, :, pl.ds(0, total)]
        return pltpu.make_async_copy(block, block, semaphores.at[layer])

    def all_moves(core):
        def keep(layer):
            return [
                pltpu.make_async_copy(
                    source.at[layer, mine, columns],
                    target.at[layer, rank, mine, to],
                    keep_sem.at[layer],
                )
                for source, columns, target, to in pieces(core, rank)
            ]

        def push(layer, k):
            return [
                remote(
                    source.at[layer, mine, columns],
                    target.at[layer, rank, mine, to],
                    push_send.at[layer, k],
                    push_recv.at[layer, k],
                    member(k),
                )
                for source, columns, target, to in pieces(core, (rank + k) % TEAM)
            ]

        def over(layer, k):
            origin = (rank + TEAM - k) % TEAM
            return [
                remote(
                    target.at[layer, origin, mine, to],
                    target.at[layer, origin, mine, to],
                    y_send.at[layer, k],
                    y_recv.at[layer, k],
                    {"section": across},
                )
                for _, _, target, to in pieces(core, rank)
            ]

        def on(layer):
            return [
                remote(
                    target.at[layer, :, :, to],
                    target.at[layer, :, :, to],
                    core_send.at[layer],
                    core_recv.at[layer],
                    {"section": partner},
                )
                for _, _, target, to in pieces(core, rank)
            ]

        def bytes_of(semaphore):
            block = gate.at[0, mine, pl.ds(0, total)]
            return pltpu.make_async_copy(block, block, semaphore)

        order = (4, 3, 5, 2, 6, 1, 7)
        for layer in range(depth):
            for copy in keep(layer):
                copy.start()
            for k in order:
                for copy in push(layer, k):
                    copy.start()
        for layer in range(depth):
            bytes_of(keep_sem.at[layer]).wait()
            for copy in over(layer, 0):
                copy.start()
            for k in order[::-1]:
                bytes_of(push_recv.at[layer, k]).wait()
                for copy in over(layer, k):
                    copy.start()
        for layer in range(depth):
            for k in range(TEAM):
                bytes_of(y_recv.at[layer, k]).wait()
            for copy in on(layer):
                copy.start()
        for layer in range(depth):
            layer_bytes(layer, core_send).wait()
            for k in range(TEAM):
                bytes_of(y_send.at[layer, k]).wait()
                if k:
                    bytes_of(push_send.at[layer, k]).wait()

    core = section % 2

    @pl.when(core == 0)
    def _():
        all_moves(0)

    @pl.when(core == 1)
    def _():
        all_moves(1)

    for layer in range(depth):
        layer_bytes(layer, core_recv).wait()
    small_keep.wait()
    notes_keep.wait()
    for k in range(1, TEAM):
        remote(small, small_out.at[rank], small_send.at[k], small_recv.at[k], member(k)).wait()
        remote(notes, notes_out.at[rank], notes_send.at[k], notes_recv.at[k], member(k)).wait()


def reshard(outer, collective_id, query, key, value, gate, up, small, notes):
    depth, rows = query.shape[:2]
    share = gate.shape[2] // TEAM
    span = -(-(share + LANES // 2) // LANES) * LANES
    heads_width = query.shape[2] // TEAM + 2 * LANES
    return pl.pallas_call(
        functools.partial(reshard_kernel, outer, span),
        out_shape=(
            jax.ShapeDtypeStruct((depth, TEAM, rows, heads_width), jnp.bfloat16),
            jax.ShapeDtypeStruct((depth, TEAM, rows, 2 * span), jnp.bfloat16),
            jax.ShapeDtypeStruct((TEAM,) + small.shape, small.dtype),
            jax.ShapeDtypeStruct((TEAM,) + notes.shape, notes.dtype),
        ),
        in_specs=[ANYWHERE] * 7,
        out_specs=(ANYWHERE,) * 4,
        scratch_shapes=[dma_sems(4)]
        + [dma_sems(depth, TEAM)] * 4
        + [dma_sems(depth)] * 2
        + [dma_sems(TEAM)] * 4,
        compiler_params=settings(collective_id),
        name="reshard",
    )(query, key, value, gate, up, small, notes)
def team_groups(wides, outer):
    return [[rank * outer + team for team in range(outer)] for rank in range(wides // outer)]


def turn(values, cosines, sines):
    halfway = values.shape[-1] // 2
    turned = jnp.concatenate([-values[..., halfway:], values[..., :halfway]], axis=-1)
    return values * cosines[None, :, None, :] + turned * sines[None, :, None, :]


def attention_forward(normed, heads_weight, out_weight, offset, cosines, sines):
    width = HEAD_DIM
    rows = normed.shape[0] // LEN
    q_width = out_weight.shape[0]
    shared = q_width // width
    projected = matmul(normed, heads_weight)
    query_pre = projected[:, :q_width].reshape(rows, LEN, shared, width)
    key_pre = lax.dynamic_slice_in_dim(projected[:, q_width : q_width + LANES], offset, width, 1)
    value_rows = lax.dynamic_slice_in_dim(projected[:, q_width + LANES :], offset, width, 1)
    queries = turn(query_pre, cosines, sines).astype(jnp.bfloat16)
    key_rows = turn(key_pre.reshape(rows, LEN, 1, width), cosines, sines)[:, :, 0]
    key_rows = key_rows.astype(jnp.bfloat16)
    value_rows = value_rows.astype(jnp.bfloat16).reshape(rows, LEN, width)
    causal = jnp.arange(LEN)[:, None] >= jnp.arange(LEN)[None, :]
    scores = jnp.einsum(
        "blgd,bmd->bglm", queries, key_rows, preferred_element_type=jnp.float32
    ) * width ** (-0.5)
    scores = jnp.where(causal, scores, -1e30)
    weights_full = jax.nn.softmax(scores, axis=-1)
    weights_low = weights_full.astype(jnp.bfloat16)
    mixed = jnp.einsum("bglm,bmd->blgd", weights_low, value_rows, preferred_element_type=jnp.float32)
    mixed = mixed.astype(jnp.bfloat16).reshape(rows * LEN, q_width)
    partial = matmul(mixed, out_weight).astype(jnp.bfloat16)
    return partial, (queries, key_rows, value_rows, weights_full, weights_low)


def attention_backward(grad, stored, heads_weight, out_weight, offset, cosines, sines):
    queries, key_rows, value_rows, weights_full, weights_low = stored
    rows, _, shared, width = queries.shape
    count = rows * LEN
    scale = width ** (-0.5)
    mixed_grad = times_trans(grad, out_weight).astype(jnp.bfloat16).reshape(queries.shape)
    weight_grad = jnp.einsum(
        "blgd,bmd->bglm", mixed_grad, value_rows, preferred_element_type=jnp.float32
    )
    value_grad = jnp.einsum(
        "bglm,blgd->bmd", weights_low, mixed_grad, preferred_element_type=jnp.float32
    )
    score_grad = weights_full * (
        weight_grad - jnp.sum(weights_full * weight_grad, axis=-1, keepdims=True)
    )
    score_grad = score_grad.astype(jnp.bfloat16)
    query_grad = (
        jnp.einsum("bglm,bmd->blgd", score_grad, key_rows, preferred_element_type=jnp.float32)
        * scale
    )
    key_grad = (
        jnp.einsum("bglm,blgd->bmd", score_grad, queries, preferred_element_type=jnp.float32)
        * scale
    )
    query_low = turn(query_grad, cosines, -sines).astype(jnp.bfloat16).reshape(count, -1)
    key_low = turn(key_grad[:, :, None], cosines, -sines).astype(jnp.bfloat16)
    blank = jnp.zeros((count, LANES), jnp.bfloat16)
    key_low = lax.dynamic_update_slice_in_dim(blank, key_low.reshape(count, width), offset, 1)
    value_low = value_grad.astype(jnp.bfloat16).reshape(count, width)
    value_low = lax.dynamic_update_slice_in_dim(blank, value_low, offset, 1)
    all_low = jnp.concatenate([query_low, key_low, value_low], axis=1)
    return times_trans(all_low, heads_weight).astype(jnp.bfloat16)


def feed_forward(normed, feed_weight, down_weight, offset):
    span = feed_weight.shape[1] // 2
    share = down_weight.shape[0]
    both = matmul(normed, feed_weight)
    gate_pre = lax.dynamic_slice_in_dim(both[:, :span], offset, share, 1)
    up_pre = lax.dynamic_slice_in_dim(both[:, span:], offset, share, 1)
    activated = (jax.nn.silu(gate_pre) * up_pre).astype(jnp.bfloat16)
    return matmul(activated, down_weight).astype(jnp.bfloat16), (gate_pre, up_pre)


def feed_backward(grad, stored, feed_weight, down_weight, offset):
    gate_pre, up_pre = stored
    span = feed_weight.shape[1] // 2
    activated_grad = times_trans(grad, down_weight)
    gate_sig = jax.nn.sigmoid(gate_pre)
    gate_grad = activated_grad * up_pre * gate_sig * (1.0 + gate_pre * (1.0 - gate_sig))
    up_grad = activated_grad * gate_pre * gate_sig
    blank = jnp.zeros((grad.shape[0], 2 * span), jnp.bfloat16)
    both = lax.dynamic_update_slice_in_dim(blank, gate_grad.astype(jnp.bfloat16), offset, 1)
    both = lax.dynamic_update_slice_in_dim(both, up_grad.astype(jnp.bfloat16), span + offset, 1)
    return times_trans(both, feed_weight).astype(jnp.bfloat16)


def shards(
    token_ids,
    targets,
    slot_ids,
    group_ids,
    group_offsets,
    piece_table,
    prenorm_gain,
    prenorm_bias,
    query_map,
    key_map,
    value_map,
    output_map,
    midnorm_gain,
    midnorm_bias,
    expand_map,
    reduce_map,
    embed_map,
    attention_gain,
    query_weight,
    key_weight,
    value_weight,
    output_weight,
    feed_gain,
    gate_weight,
    up_weight,
    down_weight,
    final_gain,
):
    wides = lax.axis_size("wide")
    outer = wides // TEAM
    groups = team_groups(wides, outer)
    section_index = lax.axis_index("section")
    wide_index = lax.axis_index("wide")
    rank = wide_index // outer
    hyper_width, hyper_feed = piece_table.shape[1], expand_map.shape[1]
    model_width = embed_map.shape[1]
    total_tokens = wides * MB * LEN

    owned = query_map.shape[0]
    vectors = jnp.stack([prenorm_gain, prenorm_bias, midnorm_gain, midnorm_bias], axis=1)
    vectors = jnp.pad(vectors, ((0, 0), (0, LANES - 4)))
    first = jnp.concatenate([query_map, key_map, value_map, output_map, expand_map], axis=1)
    second = jnp.concatenate([embed_map, vectors], axis=1)
    first, second, third = spread(
        1,
        wides,
        (first.astype(jnp.bfloat16), second.astype(jnp.bfloat16), reduce_map.astype(jnp.bfloat16)),
    )
    first = first.reshape(hyper_width, -1)
    second = second.reshape(hyper_width, -1)
    reduce_low = third.reshape(hyper_feed, hyper_width)
    query_low, key_low, value_low, output_low = (
        first[:, n * hyper_width : (n + 1) * hyper_width] for n in range(4)
    )
    expand_low = first[:, 4 * hyper_width :]
    embed_low = second[:, :model_width]
    gain_one, bias_one, second_gain, bias_two = (second[:, model_width + n] for n in range(4))
    params = (
        gain_one,
        bias_one,
        query_low,
        key_low,
        value_low,
        output_low,
        second_gain,
        bias_two,
        expand_low,
        reduce_low,
        embed_low,
    )

    gains = jnp.concatenate([attention_gain, feed_gain], axis=0)
    gains = jnp.pad(gains, ((0, 16 - gains.shape[0]), (0, 0)))
    notes = jnp.concatenate([token_ids.reshape(1, -1), targets.reshape(1, -1)], axis=0)
    notes = jnp.pad(notes, ((0, 6), (0, 0)))
    heads_all, feed_all, gains, notes = reshard(
        outer,
        2,
        query_weight,
        key_weight,
        value_weight,
        gate_weight,
        up_weight,
        gains,
        notes,
    )
    if outer > 1:
        heads_all, feed_all = (
            lax.all_gather(item, "wide", axis=2, axis_index_groups=groups)
            for item in (heads_all, feed_all)
        )
        gains = lax.all_gather(gains, "wide", axis=1, axis_index_groups=groups)
        gains = gains.reshape(-1, gains.shape[2], gains.shape[3])
        output_weight, down_weight = (
            lax.all_gather(item, "wide", axis=1, axis_index_groups=groups, tiled=True)
            for item in (output_weight, down_weight)
        )
    heads_all = heads_all.reshape(2, model_width, -1)
    feed_all = feed_all.reshape(2, model_width, -1)
    gains = gains.astype(jnp.float32).transpose(1, 0, 2).reshape(-1, 1, model_width)
    attention_gains, feed_gains = gains[:2], gains[2:4]
    final_scale = final_gain.astype(jnp.float32).reshape(1, model_width)
    notes = lax.dynamic_slice_in_dim(notes, section_index * 2, 2, 0)
    ids, wanted = notes[:, 0].reshape(-1), notes[:, 1].reshape(-1)
    share = down_weight.shape[1]
    feed_offset = rank * share % LANES
    head_offset = rank // 2 % 2 * HEAD_DIM
    cosines, sines = rope_tables(LEN, HEAD_DIM)

    entries, slot_count = slot_ids.shape
    group_hits = (
        group_ids[:, None] == jnp.arange(group_offsets.shape[0], dtype=jnp.int32)[None, :]
    ).astype(jnp.int32)
    row_start = jnp.sum(group_hits * group_offsets[None, :], axis=1)
    piece_rows = (row_start[:, None] + slot_ids).reshape(-1)
    pieces = (
        jnp.take(piece_table, piece_rows, axis=0)
        .astype(jnp.float32)
        .reshape(entries, slot_count, hyper_width)
    )
    table_shard, hyper_stored = hyper_forward(pieces, params, HYPER_HEAD_COUNT)

    table_rows = section_gather(3, table_shard)
    if outer > 1:
        table_rows = lax.all_gather(table_rows, "wide", axis=1, axis_index_groups=groups)
    table_rows = table_rows.reshape(-1, model_width)
    wide_rows = rank * outer + jnp.arange(outer, dtype=jnp.int32)
    row_starts = (
        jnp.arange(SECTIONS, dtype=jnp.int32)[:, None] * wides + wide_rows[None, :]
    ) * entries
    own_rows = row_starts[:, :, None] + jnp.arange(entries, dtype=jnp.int32)[None, None, :]
    own_rows = own_rows.reshape(-1)
    hits = (ids[:, None] == own_rows[None, :]).astype(jnp.bfloat16)
    injected = matmul(hits, table_rows).astype(jnp.bfloat16)
    normed, hidden = fold(inject, outer, 4, injected, (attention_gains[0],), (jnp.bfloat16,))

    kept = []
    for layer in range(2):
        heads_weight, feed_weight = heads_all[layer], feed_all[layer]
        partial, attended = attention_forward(
            normed.reshape(ROWS, model_width),
            heads_weight,
            output_weight[layer],
            head_offset,
            cosines,
            sines,
        )
        normed, middle = fold(
            enter_feed, outer, 5, partial, (hidden, feed_gains[layer]), (jnp.float32,)
        )
        partial, fed = feed_forward(
            normed.reshape(ROWS, model_width), feed_weight, down_weight[layer], feed_offset
        )
        kept.append((hidden, attended, middle, fed))
        next_gain = attention_gains[1] if layer == 0 else final_scale
        normed, hidden = fold(
            leave_layer, outer, 6, partial, (middle, next_gain), (jnp.bfloat16,)
        )

    final_normed = normed.reshape(ROWS, model_width)
    logits = times_trans(final_normed, table_rows)
    row_peak = jnp.max(logits, axis=1)
    row_mass = jnp.sum(jnp.exp(logits - row_peak[:, None]), axis=1)
    wanted_hits = wanted[:, None] == own_rows[None, :]
    chosen = jnp.sum(jnp.where(wanted_hits, logits, 0.0), axis=1)
    blank = jnp.zeros_like(chosen)
    stats = jnp.stack([row_peak, row_mass, chosen] + [blank] * 5, axis=0)
    stats = team_gather(outer, 7, stats)
    peak = jnp.max(stats[:, 0], axis=0)
    mass = jnp.sum(stats[:, 1] * jnp.exp(stats[:, 0] - peak[None, :]), axis=0)
    log_norm = peak + jnp.log(mass)
    loss_part = jnp.sum(log_norm - jnp.sum(stats[:, 2], axis=0)) / total_tokens
    logit_grad = (
        (jnp.exp(logits - log_norm[:, None]) - wanted_hits.astype(jnp.float32)) / total_tokens
    ).astype(jnp.bfloat16)
    partial = matmul(logit_grad, table_rows).astype(jnp.bfloat16)
    grads, outer_grad = fold(
        head_back, outer, 8, partial, (hidden, final_scale), (jnp.bfloat16,)
    )

    for layer in (1, 0):
        heads_weight, feed_weight = heads_all[layer], feed_all[layer]
        hidden, attended, middle, fed = kept[layer]
        partial = feed_backward(
            grads.reshape(ROWS, model_width), fed, feed_weight, down_weight[layer], feed_offset
        )
        grads, middle_grad = fold(
            feed_back, outer, 9, partial, (outer_grad, middle, feed_gains[layer]), (jnp.float32,)
        )
        partial = attention_backward(
            grads.reshape(ROWS, model_width),
            attended,
            heads_weight,
            output_weight[layer],
            head_offset,
            cosines,
            sines,
        )
        grads, outer_grad = fold(
            layer_back,
            outer,
            10,
            partial,
            (middle_grad, hidden, attention_gains[layer]),
            (jnp.bfloat16,),
        )

    table_part = trans_times(logit_grad, final_normed) + trans_times(
        hits, grads.reshape(ROWS, model_width)
    )
    table_part = table_part.astype(jnp.bfloat16).reshape(SECTIONS, outer, entries, model_width)
    loss_block = jnp.full((8, LANES), loss_part, jnp.float32)
    if outer > 1:
        table_part = lax.psum_scatter(
            table_part.astype(jnp.float32),
            "wide",
            scatter_dimension=1,
            axis_index_groups=groups,
        ).astype(jnp.bfloat16)
        loss_block = lax.psum(loss_block, "wide", axis_index_groups=groups)
    table_grad, loss_block = section_sum(
        11, table_part.reshape(SECTIONS, entries, model_width), loss_block
    )
    mean_loss = loss_block[0, 0]
    (
        grad_prescale,
        prenorm_bias_gradient,
        grad_query,
        grad_key,
        grad_value,
        grad_output,
        grad_midscale,
        grad_midshift,
        grad_expand,
        grad_reduce,
        grad_embed,
    ) = hyper_backward(params, hyper_stored, table_grad)
    vectors = jnp.stack(
        [grad_prescale, prenorm_bias_gradient, grad_midscale, grad_midshift], axis=1
    )
    vectors = jnp.pad(vectors, ((0, 0), (0, LANES - 4)))
    first = jnp.concatenate([grad_query, grad_key, grad_value, grad_output, grad_expand], axis=1)
    second = jnp.concatenate([grad_embed, vectors], axis=1)
    first, second, third = (
        item.astype(jnp.bfloat16).reshape(SECTIONS, wides, -1, item.shape[1])
        for item in (first, second, grad_reduce)
    )
    first, second, third = collect(12, (first, second, third))
    grad_query, grad_key, grad_value, grad_output = (
        first[:, n * hyper_width : (n + 1) * hyper_width] for n in range(4)
    )
    return (
        mean_loss,
        second[:, model_width],
        second[:, model_width + 1],
        grad_query,
        grad_key,
        grad_value,
        grad_output,
        second[:, model_width + 2],
        second[:, model_width + 3],
        first[:, 4 * hyper_width :],
        third,
        second[:, :model_width],
    )


def solution(mesh):
    placed = (
        P("wide", None, None),
        P("wide", None, None),
        P(("section", "wide"), None),
        P(("section", "wide")),
        P(),
        P(),
        P(("section", "wide")),
        P(("section", "wide")),
        P(("section", "wide"), None),
        P(("section", "wide"), None),
        P(("section", "wide"), None),
        P(("section", "wide"), None),
        P(("section", "wide")),
        P(("section", "wide")),
        P(("section", "wide"), None),
        P(("section", "wide"), None),
        P(("section", "wide"), None),
        P(None, "wide"),
        P(None, "wide", None),
        P(None, "wide", None),
        P(None, "wide", None),
        P(None, "wide", None),
        P(None, "wide"),
        P(None, "wide", None),
        P(None, "wide", None),
        P(None, "wide", None),
        P(),
    )
    return jax.shard_map(
        shards,
        mesh=mesh,
        in_specs=placed,
        out_specs=(
            P(),
            P(("section", "wide")),
            P(("section", "wide")),
            P(("section", "wide"), None),
            P(("section", "wide"), None),
            P(("section", "wide"), None),
            P(("section", "wide"), None),
            P(("section", "wide")),
            P(("section", "wide")),
            P(("section", "wide"), None),
            P(("section", "wide"), None),
            P(("section", "wide"), None),
        ),
        check_vma=False,
    )
```

```python
import functools

import jax
import jax.numpy as jnp
from jax import lax
from jax.experimental import pallas as pl
from jax.experimental.pallas import tpu as pltpu
from jax.sharding import PartitionSpec as P

HEAD_DIM = 64
HYPER_HEAD_COUNT = 8
MB = 2
LEN = 64
TEAM = 8
SECTIONS = 4
ROWS = MB * LEN * TEAM // SECTIONS
OWN = ROWS // TEAM
LANES = 128
MESH_IDS = pl.DeviceIdType.MESH
ANYWHERE = pl.BlockSpec(memory_space=pl.ANY)
IN_VMEM = pl.BlockSpec(memory_space=pltpu.VMEM)
VMEM_LIMIT = 56 * 1024 * 1024

norm_eps = 1e-05
inv_root_two = 0.7071067811865476
inv_root_tau = 0.3989422804014327


def matmul(former, latter):
    return jnp.dot(former, latter, preferred_element_type=jnp.float32)


def times_trans(former, latter):
    return lax.dot_general(
        former, latter, (((1,), (1,)), ((), ())), preferred_element_type=jnp.float32
    )


def trans_times(former, latter):
    return lax.dot_general(
        former, latter, (((0,), (0,)), ((), ())), preferred_element_type=jnp.float32
    )


def center_norm(values):
    center = values - jnp.mean(values, axis=-1, keepdims=True)
    inverse = lax.rsqrt(jnp.mean(center * center, axis=-1, keepdims=True) + norm_eps)
    return (center * inverse, inverse)


def center_back(normed, inverse, normed_grad):
    mean_grad = jnp.mean(normed_grad, axis=-1, keepdims=True)
    mean_mix = jnp.mean(normed_grad * normed, axis=-1, keepdims=True)
    return inverse * (normed_grad - mean_grad - normed * mean_mix)


def root_inverse(values):
    return lax.rsqrt(jnp.mean(values * values, axis=-1, keepdims=True) + norm_eps)


def reciprocal_root_backward(values, inverse, gain_vec, outer_grad):
    scaled = outer_grad * gain_vec
    mixing = jnp.mean(scaled * values, axis=-1, keepdims=True)
    return inverse * scaled - values * inverse * inverse * inverse * mixing


def rope_tables(positions, head_width):
    halfway = head_width // 2
    frequency = jnp.exp(
        -jnp.log(10000.0) * (2.0 * jnp.arange(halfway, dtype=jnp.float32) / head_width)
    )
    angles = jnp.arange(positions, dtype=jnp.float32)[:, None] * frequency[None, :]
    angles = jnp.concatenate([angles, angles], axis=1)
    return (jnp.cos(angles), jnp.sin(angles))


def greet(peers):
    barrier = pltpu.get_barrier_semaphore()
    for peer in peers:
        pl.semaphore_signal(barrier, inc=1, device_id=peer, device_id_type=MESH_IDS)
    pl.semaphore_wait(barrier, len(peers))


def remote(source, target, send, recv, peer):
    return pltpu.make_async_remote_copy(
        src_ref=source,
        dst_ref=target,
        send_sem=send,
        recv_sem=recv,
        device_id=peer,
        device_id_type=MESH_IDS,
    )


def settings(collective_id):
    return pltpu.CompilerParams(
        collective_id=collective_id, has_side_effects=True, vmem_limit_bytes=VMEM_LIMIT
    )


def dma_sems(*shape):
    return pltpu.SemaphoreType.DMA(shape)


def fold_kernel(finish, outer, n_in, n_out, *refs):
    partial, extras = refs[0], refs[1:n_in]
    gathered, outs = refs[n_in], refs[n_in + 1 : n_in + n_out]
    (
        own,
        side,
        pair,
        far,
        ready,
        load_sem,
        keep_sem,
        side_send,
        side_recv,
        far_send,
        far_recv,
        out_send,
        out_recv,
        over_send,
        over_recv,
    ) = refs[n_in + n_out :]
    wide = lax.axis_index("wide")
    rank, team = wide // outer, wide % outer
    line, column = rank // 2, rank % 2
    lines = TEAM // 2

    def at(some_line, some_column):
        return (some_line % lines) * 2 + some_column

    def member(some_line, some_column):
        return {"wide": at(some_line, some_column) * outer + team}

    beside = member(line, 1 - column)
    greet([beside] + [member(line + j, column) for j in range(1, lines)])
    order = (2, 1, 3, 0)
    loads = [
        pltpu.make_async_copy(partial.at[at(line + j, column)], own.at[j], load_sem.at[j])
        for j in range(lines)
    ]
    sides = [
        remote(
            partial.at[at(line + j, 1 - column)],
            side.at[j],
            side_send.at[j],
            side_recv.at[j],
            beside,
        )
        for j in range(lines)
    ]
    fars = [None] + [
        remote(pair.at[j], far.at[j], far_send.at[j], far_recv.at[j], member(line + j, column))
        for j in range(1, lines)
    ]
    for j in order:
        sides[j].start()
        loads[j].start()
    for j in order[:3]:
        loads[j].wait()
        sides[j].wait_recv()
        pair[j] = (own[j].astype(jnp.float32) + side[j].astype(jnp.float32)).astype(jnp.bfloat16)
        fars[j].start()
    loads[0].wait()
    sides[0].wait_recv()
    total = own[0].astype(jnp.float32) + side[0].astype(jnp.float32)
    for j in (1, 3, 2):
        fars[j].wait_recv()
        total = total + far[j].astype(jnp.float32)
    ready[...] = finish(total, extras, outs)
    mine = at(line, column)
    keep = pltpu.make_async_copy(ready, gathered.at[mine], keep_sem)
    pushes = [None] + [
        remote(ready, gathered.at[mine], out_send.at[j], out_recv.at[j], member(line + j, column))
        for j in range(1, lines)
    ]
    overs = [
        remote(
            ready if j == 0 else gathered.at[at(line - j, column)],
            gathered.at[at(line - j, column)],
            over_send.at[j],
            over_recv.at[j],
            beside,
        )
        for j in range(lines)
    ]
    for j in (2, 1, 3):
        pushes[j].start()
    overs[0].start()
    keep.start()
    for j in (1, 3, 2):
        pushes[j].wait_recv()
        overs[j].start()
    for j in range(lines):
        overs[j].wait()
        sides[j].wait_send()
        if j:
            fars[j].wait_send()
            pushes[j].wait_send()
    keep.wait()


def fold(finish, outer, collective_id, partial, extras, outs):
    width = partial.shape[-1]
    lines = TEAM // 2
    slots = pltpu.VMEM((lines, OWN, width), jnp.bfloat16)
    return pl.pallas_call(
        functools.partial(fold_kernel, finish, outer, 1 + len(extras), 1 + len(outs)),
        out_shape=(jax.ShapeDtypeStruct((TEAM, OWN, width), jnp.bfloat16),)
        + tuple(jax.ShapeDtypeStruct((OWN, width), kind) for kind in outs),
        in_specs=[ANYWHERE] + [IN_VMEM] * len(extras),
        out_specs=(ANYWHERE,) + (IN_VMEM,) * len(outs),
        scratch_shapes=[slots, slots, slots, slots, pltpu.VMEM((OWN, width), jnp.bfloat16)]
        + [dma_sems(lines), pltpu.SemaphoreType.DMA]
        + [dma_sems(lines)] * 8,
        compiler_params=settings(collective_id),
        name=finish.__name__,
    )(partial.reshape(TEAM, OWN, width), *extras)


def inject(total, extras, outs):
    (gain,) = extras
    hidden = total.astype(jnp.bfloat16)
    outs[0][...] = hidden
    wide = hidden.astype(jnp.float32)
    return (wide * root_inverse(wide) * gain[...]).astype(jnp.bfloat16)


def enter_feed(total, extras, outs):
    hidden, gain = extras
    middle = hidden[...].astype(jnp.float32) + total
    outs[0][...] = middle
    return (middle * root_inverse(middle) * gain[...]).astype(jnp.bfloat16)


def leave_layer(total, extras, outs):
    middle, gain = extras
    hidden = (middle[...] + total).astype(jnp.bfloat16)
    outs[0][...] = hidden
    wide = hidden.astype(jnp.float32)
    return (wide * root_inverse(wide) * gain[...]).astype(jnp.bfloat16)


def head_back(total, extras, outs):
    hidden, gain = extras
    wide = hidden[...].astype(jnp.float32)
    grad = reciprocal_root_backward(wide, root_inverse(wide), gain[...], total)
    grad = grad.astype(jnp.bfloat16)
    outs[0][...] = grad
    return grad


def feed_back(total, extras, outs):
    outer_grad, middle, gain = extras
    wide = middle[...]
    grad = outer_grad[...].astype(jnp.float32) + reciprocal_root_backward(
        wide, root_inverse(wide), gain[...], total
    )
    outs[0][...] = grad
    return grad.astype(jnp.bfloat16)


def layer_back(total, extras, outs):
    middle_grad, hidden, gain = extras
    wide = hidden[...].astype(jnp.float32)
    grad = middle_grad[...] + reciprocal_root_backward(wide, root_inverse(wide), gain[...], total)
    grad = grad.astype(jnp.bfloat16)
    outs[0][...] = grad
    return grad


def team_kernel(outer, block, gathered, send, recv):
    wide = lax.axis_index("wide")
    rank, team = wide // outer, wide % outer
    peers = [{"wide": ((rank + k) % TEAM) * outer + team} for k in range(1, TEAM)]
    greet(peers)
    copies = [
        remote(block, gathered.at[rank], send.at[k], recv.at[k], peer)
        for k, peer in enumerate(peers)
    ]
    for copy in copies:
        copy.start()
    gathered[rank] = block[...]
    for copy in copies:
        copy.wait()


def team_gather(outer, collective_id, block):
    return pl.pallas_call(
        functools.partial(team_kernel, outer),
        out_shape=jax.ShapeDtypeStruct((TEAM,) + block.shape, block.dtype),
        in_specs=[IN_VMEM],
        out_specs=IN_VMEM,
        scratch_shapes=[dma_sems(TEAM - 1), dma_sems(TEAM - 1)],
        compiler_params=settings(collective_id),
        name="team_gather",
    )(block)


def section_places():
    section = lax.axis_index("section")
    core = section % 2
    partner = section + 1 - 2 * core
    across = (section + 2) % SECTIONS
    return section, partner, across


def section_gather_kernel(block, gathered, keep_sem, send, recv):
    section, partner, across = section_places()
    greet([{"section": partner}, {"section": across}])
    keep = pltpu.make_async_copy(block, gathered.at[section], keep_sem)
    near = remote(block, gathered.at[section], send.at[0], recv.at[0], {"section": partner})
    far = remote(block, gathered.at[section], send.at[1], recv.at[1], {"section": across})
    on = remote(
        gathered.at[across], gathered.at[across], send.at[2], recv.at[2], {"section": partner}
    )
    far.start()
    near.start()
    keep.start()
    far.wait_recv()
    on.start()
    near.wait()
    on.wait()
    far.wait_send()
    keep.wait()


def section_gather(collective_id, block):
    return pl.pallas_call(
        section_gather_kernel,
        out_shape=jax.ShapeDtypeStruct((SECTIONS,) + block.shape, block.dtype),
        in_specs=[ANYWHERE],
        out_specs=ANYWHERE,
        scratch_shapes=[pltpu.SemaphoreType.DMA, dma_sems(3), dma_sems(3)],
        compiler_params=settings(collective_id),
        name="section_gather",
    )(block)


def section_sum_kernel(partial, loss, summed, loss_sum, own, near, pair, far, loss_near, loss_pair, loss_far, load_sem, send, recv):
    section, partner, across = section_places()
    beyond = (partner + 2) % SECTIONS
    greet([{"section": partner}, {"section": across}])
    loads = [
        pltpu.make_async_copy(partial.at[section], own.at[0], load_sem.at[0]),
        pltpu.make_async_copy(partial.at[across], own.at[1], load_sem.at[1]),
    ]
    nears = [
        remote(partial.at[partner], near.at[0], send.at[0], recv.at[0], {"section": partner}),
        remote(partial.at[beyond], near.at[1], send.at[1], recv.at[1], {"section": partner}),
        remote(loss, loss_near, send.at[2], recv.at[2], {"section": partner}),
    ]
    fars = [
        remote(pair, far, send.at[3], recv.at[3], {"section": across}),
        remote(loss_pair, loss_far, send.at[4], recv.at[4], {"section": across}),
    ]
    for j in (1, 2, 0):
        nears[j].start()
    loads[1].start()
    loads[0].start()
    loads[1].wait()
    nears[1].wait_recv()
    pair[...] = (own[1].astype(jnp.float32) + near[1].astype(jnp.float32)).astype(jnp.bfloat16)
    fars[0].start()
    nears[2].wait_recv()
    loss_pair[...] = loss[...] + loss_near[...]
    fars[1].start()
    loads[0].wait()
    nears[0].wait_recv()
    total = own[0].astype(jnp.float32) + near[0].astype(jnp.float32)
    fars[0].wait_recv()
    summed[...] = total + far[...].astype(jnp.float32)
    fars[1].wait_recv()
    loss_sum[...] = loss_pair[...] + loss_far[...]
    for copy in nears + fars:
        copy.wait_send()


def section_sum(collective_id, partial, loss):
    shape = partial.shape[1:]
    low, low_two = pltpu.VMEM(shape, jnp.bfloat16), pltpu.VMEM((2,) + shape, jnp.bfloat16)
    number = pltpu.VMEM(loss.shape, jnp.float32)
    return pl.pallas_call(
        section_sum_kernel,
        out_shape=(
            jax.ShapeDtypeStruct(shape, jnp.float32),
            jax.ShapeDtypeStruct(loss.shape, jnp.float32),
        ),
        in_specs=[ANYWHERE, IN_VMEM],
        out_specs=(IN_VMEM, IN_VMEM),
        scratch_shapes=[low_two, low_two, low, low, number, number, number]
        + [dma_sems(2), dma_sems(5), dma_sems(5)],
        compiler_params=settings(collective_id),
        name="section_sum",
    )(partial, loss)


def all_places(halves):
    section, partner, across = section_places()
    wide = lax.axis_index("wide")
    line, column = wide // 2, wide % 2

    def wide_at(j):
        return ((line + j) % halves) * 2 + column

    return section, partner, across, wide, wide_at


def steps_of(x_first, section, partner, across, wide):
    column_flip = wide + 1 - 2 * (wide % 2)
    x_step = ({"wide": column_flip}, False, True)
    y_step = ({"section": across}, True, False)
    return (x_step, y_step) if x_first else (y_step, x_step)


def owner_of(home, flips_y, flips_x, wide_block):
    section = (home + 2) % SECTIONS if flips_y else home
    return section, (wide_block + 1 - 2 * (wide_block % 2) if flips_x else wide_block)


def spread_kernel(count, halves, outer, *refs):
    blocks, notes = refs[:count], refs[count : count + 2]
    gathereds, notes_out = refs[count + 2 : 2 * count + 2], refs[2 * count + 2 : 2 * count + 4]
    (
        keep_sem,
        note_keep,
        note_send,
        note_recv,
        z_send,
        a_send,
        b_send,
        c_send,
        z_recv,
        a_recv,
        b_recv,
        c_recv,
    ) = refs[2 * count + 4 :]
    section, partner, across, wide, wide_at = all_places(halves)
    rank, team = wide // outer, wide % outer
    members = [None] + [{"wide": (rank + k) % TEAM * outer + team} for k in range(1, TEAM)]
    beside = wide + 1 - 2 * (wide % 2)
    barrier = pltpu.get_barrier_semaphore()
    for peer in ({"section": partner}, {"section": across}, {"wide": beside}):
        pl.semaphore_signal(barrier, inc=1, device_id=peer, device_id_type=MESH_IDS)

    def hello(j, carry):
        peer = {"wide": wide_at(j)}
        pl.semaphore_signal(barrier, inc=1, device_id=peer, device_id_type=MESH_IDS)
        return carry

    lax.fori_loop(1, halves, hello, 0)
    for peer in members[1:]:
        pl.semaphore_signal(barrier, inc=1, device_id=peer, device_id_type=MESH_IDS)
    pl.semaphore_wait(barrier, 3 + halves - 1 + TEAM - 1)
    note_keeps = [
        pltpu.make_async_copy(notes[m], notes_out[m].at[rank], note_keep.at[m]) for m in range(2)
    ]
    note_copies = [
        remote(notes[m], notes_out[m].at[rank], note_send.at[m, k], note_recv.at[m, k], members[k])
        for m in range(2)
        for k in range(1, TEAM)
    ]
    for copy in note_keeps + note_copies:
        copy.start()

    keeps = [
        pltpu.make_async_copy(blocks[n], gathereds[n].at[section, wide], keep_sem.at[n])
        for n in range(count)
    ]

    def z_copy(n, j):
        return remote(
            blocks[n],
            gathereds[n].at[section, wide],
            z_send.at[n, j],
            z_recv.at[n, j],
            {"wide": wide_at(j)},
        )

    def a_copy(n, j):
        (peer, _, _), _ = steps_of(n == 0, section, partner, across, wide)
        block = gathereds[n].at[section, wide_at(-j)]
        return remote(block, block, a_send.at[n, j], a_recv.at[n, j], peer)

    def b_copy(n, flip, j):
        (_, y_a, x_a), (peer, _, _) = steps_of(n == 0, section, partner, across, wide)
        place = owner_of(section, y_a and flip, x_a and flip, wide_at(-j))
        block = gathereds[n].at[place[0], place[1]]
        slot = j + (halves if flip else 0)
        return remote(block, block, b_send.at[n, slot], b_recv.at[n, slot], peer)

    def c_copy(n, which):
        home = (section + 2) % SECTIONS if which else section
        block = gathereds[n].at[home]
        return remote(
            block, block, c_send.at[n, which], c_recv.at[n, which], {"section": partner}
        )

    for keep in keeps:
        keep.start()

    def start_z(j, carry):
        for n in range(count):
            z_copy(n, j).start()
        return carry

    lax.fori_loop(1, halves, start_z, 0)
    for n in range(count):
        keeps[n].wait()
        a_copy(n, 0).start()
        b_copy(n, False, 0).start()

    def pass_z(j, carry):
        for n in range(count):
            z_copy(n, j).wait_recv()
            a_copy(n, j).start()
            b_copy(n, False, j).start()
        return carry

    lax.fori_loop(1, halves, pass_z, 0)

    def pass_a(j, carry):
        for n in range(count):
            a_copy(n, j).wait_recv()
            b_copy(n, True, j).start()
        return carry

    lax.fori_loop(0, halves, pass_a, 0)

    def settle_b(j, carry):
        for n in range(count):
            for flip in (False, True):
                b_copy(n, flip, j).wait_recv()
        return carry

    c_copy(0, 0).start()
    lax.fori_loop(0, halves, settle_b, 0)
    c_copy(0, 1).start()
    for n in range(1, count):
        c_copy(n, 0).start()
        c_copy(n, 1).start()
    for n in range(count):
        c_copy(n, 0).wait()
        c_copy(n, 1).wait()

    def drain(j, carry):
        for n in range(count):
            a_copy(n, j).wait_send()
            b_copy(n, False, j).wait_send()
            b_copy(n, True, j).wait_send()
        return carry

    lax.fori_loop(0, halves, drain, 0)

    def drain_z(j, carry):
        for n in range(count):
            z_copy(n, j).wait_send()
        return carry

    lax.fori_loop(1, halves, drain_z, 0)
    for copy in note_keeps + note_copies:
        copy.wait()


def spread(collective_id, wides, outer, blocks, notes):
    count, halves = len(blocks), wides // 2
    return pl.pallas_call(
        functools.partial(spread_kernel, count, halves, outer),
        out_shape=tuple(
            jax.ShapeDtypeStruct((SECTIONS, wides) + block.shape, block.dtype) for block in blocks
        )
        + tuple(jax.ShapeDtypeStruct((TEAM,) + note.shape, note.dtype) for note in notes),
        in_specs=[ANYWHERE] * (count + 2),
        out_specs=(ANYWHERE,) * (count + 2),
        scratch_shapes=[dma_sems(count), dma_sems(2), dma_sems(2, TEAM), dma_sems(2, TEAM)]
        + [
            dma_sems(count, halves),
            dma_sems(count, halves),
            dma_sems(count, 2 * halves),
            dma_sems(count, 2),
        ]
        * 2,
        compiler_params=settings(collective_id),
        name="spread",
    )(*blocks, *notes)


def collect_kernel(count, halves, *refs):
    partials, sums = refs[:count], refs[count : 2 * count]
    keeps, c_in, b_in, a_in, z_in = (refs[(2 + k) * count : (3 + k) * count] for k in range(5))
    load_sem, c_send, b_send, a_send, z_send, c_recv, b_recv, a_recv, z_recv = refs[7 * count :]
    section, partner, across, wide, wide_at = all_places(halves)
    beside = wide + 1 - 2 * (wide % 2)
    barrier = pltpu.get_barrier_semaphore()
    for peer in ({"section": partner}, {"section": across}, {"wide": beside}):
        pl.semaphore_signal(barrier, inc=1, device_id=peer, device_id_type=MESH_IDS)

    def hello(j, carry):
        peer = {"wide": wide_at(j)}
        pl.semaphore_signal(barrier, inc=1, device_id=peer, device_id_type=MESH_IDS)
        return carry

    lax.fori_loop(1, halves, hello, 0)
    pl.semaphore_wait(barrier, 3 + halves - 1)

    def place(n, home, flip_b, flip_a, j):
        (_, y_a, x_a), (_, y_b, x_b) = steps_of(n == 0, section, partner, across, wide)
        flips_y = (y_a and flip_a) or (y_b and flip_b)
        flips_x = (x_a and flip_a) or (x_b and flip_b)
        return owner_of(home, flips_y, flips_x, wide_at(j))

    def load(n, fb, fa, j):
        owner = place(n, section, fb, fa, j)
        slot = (fb * 2 + fa) * halves + j
        return pltpu.make_async_copy(
            partials[n].at[owner[0], owner[1]], keeps[n].at[slot], load_sem.at[n, slot]
        )

    def c_copy(n, fb, fa, j):
        owner = place(n, partner, fb, fa, j)
        slot = (fb * 2 + fa) * halves + j
        return remote(
            partials[n].at[owner[0], owner[1]],
            c_in[n].at[slot],
            c_send.at[n, slot],
            c_recv.at[n, slot],
            {"section": partner},
        )

    def b_copy(n, fa, j):
        _, (peer, _, _) = steps_of(n == 0, section, partner, across, wide)
        slot = fa * halves + j
        return remote(
            keeps[n].at[2 * halves + slot],
            b_in[n].at[slot],
            b_send.at[n, slot],
            b_recv.at[n, slot],
            peer,
        )

    def a_copy(n, j):
        (peer, _, _), _ = steps_of(n == 0, section, partner, across, wide)
        return remote(
            keeps[n].at[halves + j], a_in[n].at[j], a_send.at[n, j], a_recv.at[n, j], peer
        )

    def z_copy(n, j):
        return remote(
            keeps[n].at[j],
            z_in[n].at[j],
            z_send.at[n, j],
            z_recv.at[n, j],
            {"wide": wide_at(j)},
        )

    def add(n, slot, more):
        keeps[n][slot] = (
            keeps[n][slot].astype(jnp.float32) + more.astype(jnp.float32)
        ).astype(jnp.bfloat16)

    groups = ((1, 1), (1, 0), (0, 1), (0, 0))
    for fb, fa in groups:

        def start_c(j, carry):
            for n in range(count):
                c_copy(n, fb, fa, j).start()
                load(n, fb, fa, j).start()
            return carry

        lax.fori_loop(0, halves, start_c, 0)

    for fb, fa in groups:

        def sum_c(j, carry):
            for n in range(count):
                slot = (fb * 2 + fa) * halves + j
                load(n, fb, fa, j).wait()
                c_copy(n, fb, fa, j).wait_recv()
                add(n, slot, c_in[n][slot])
                if fb:
                    b_copy(n, fa, j).start()
            return carry

        lax.fori_loop(0, halves, sum_c, 0)

    for fa in (1, 0):

        def sum_b(j, carry):
            for n in range(count):
                slot = fa * halves + j
                b_copy(n, fa, j).wait_recv()
                add(n, slot, b_in[n][slot])
                if fa:
                    a_copy(n, j).start()
            return carry

        lax.fori_loop(0, halves, sum_b, 0)

    def sum_a(j, carry):
        for n in range(count):
            a_copy(n, j).wait_recv()
            add(n, j, a_in[n][j])
            z_copy(n, j).start()
        return carry

    lax.fori_loop(1, halves, sum_a, 0)
    for n in range(count):
        a_copy(n, 0).wait_recv()
        sums[n][...] = keeps[n][0].astype(jnp.float32) + a_in[n][0].astype(jnp.float32)

    def sum_z(j, carry):
        for n in range(count):
            z_copy(n, j).wait_recv()
            sums[n][...] += z_in[n][j].astype(jnp.float32)
        return carry

    lax.fori_loop(1, halves, sum_z, 0)

    def drain(j, carry):
        for n in range(count):
            for fb, fa in groups:
                c_copy(n, fb, fa, j).wait_send()
            b_copy(n, 0, j).wait_send()
            b_copy(n, 1, j).wait_send()
            a_copy(n, j).wait_send()
        return carry

    lax.fori_loop(0, halves, drain, 0)

    def drain_z(j, carry):
        for n in range(count):
            z_copy(n, j).wait_send()
        return carry

    lax.fori_loop(1, halves, drain_z, 0)


def collect(collective_id, partials):
    count, halves = len(partials), partials[0].shape[1] // 2
    shapes = [partial.shape[2:] for partial in partials]

    def slots(number):
        return [pltpu.VMEM((number,) + shape, jnp.bfloat16) for shape in shapes]

    return pl.pallas_call(
        functools.partial(collect_kernel, count, halves),
        out_shape=tuple(jax.ShapeDtypeStruct(shape, jnp.float32) for shape in shapes),
        in_specs=[ANYWHERE] * count,
        out_specs=(IN_VMEM,) * count,
        scratch_shapes=slots(4 * halves)
        + slots(4 * halves)
        + slots(2 * halves)
        + slots(halves)
        + slots(halves)
        + [dma_sems(count, 4 * halves)]
        + [
            dma_sems(count, 4 * halves),
            dma_sems(count, 2 * halves),
            dma_sems(count, halves),
            dma_sems(count, halves),
        ]
        * 2,
        compiler_params=settings(collective_id),
        name="collect",
    )(*partials)


TILE = 256


def causal_blocks(count, length):
    row = lax.broadcasted_iota(jnp.int32, (count, count), 0)
    column = lax.broadcasted_iota(jnp.int32, (count, count), 1)
    return (row // length == column // length) & (column <= row)


def turn(values, tables):
    cosines, upper, lower = tables
    parts = []
    for start in range(0, values.shape[1], LANES):
        part = values[:, start : start + LANES]
        ahead = pltpu.roll(part, LANES - HEAD_DIM // 2, 1)
        behind = pltpu.roll(part, HEAD_DIM // 2, 1)
        parts.append(part * cosines + ahead * upper + behind * lower)
    return parts[0] if len(parts) == 1 else jnp.concatenate(parts, axis=1)


def turn_tables(back):
    cosines, sines = rope_tables(LEN, HEAD_DIM)
    sines = -sines if back else sines
    first = jnp.arange(HEAD_DIM) < HEAD_DIM // 2
    upper, lower = jnp.where(first, -sines, 0.0), jnp.where(first, 0.0, sines)
    blank = jnp.zeros_like(cosines)
    pairs = [(cosines, cosines), (upper, upper), (lower, lower)]
    pairs += [(cosines, blank + 1.0), (upper, blank), (lower, blank)]
    tables = jnp.stack([jnp.concatenate(pair, axis=1) for pair in pairs])
    return jnp.tile(tables, (1, ROWS // LEN, 1))


def load_weight(pieces, columns, scratch, sem):
    section = lax.axis_index("section")
    partner = section + 1 - 2 * (section % 2)
    places = (section, (section + 2) % SECTIONS, partner, (partner + 2) % SECTIONS)
    copies = [
        pltpu.make_async_copy(source.at[:, :, columns], scratch.at[:, place], sem.at[n])
        for n, (source, place) in enumerate(zip(pieces, places))
    ]
    for copy in copies:
        copy.start()
    return copies


def attend(queries, key, mask, scale):
    scores = times_trans(queries, key) * scale
    scores = jnp.where(mask, scores, -1e30)
    peak = jnp.max(scores, axis=1, keepdims=True)
    mass = jnp.exp(scores - peak)
    return mass / jnp.sum(mass, axis=1, keepdims=True)


def attention_kernel(
    normed, out_weight, tables, own, other_y, other_core, beyond, partial, queries_out, pairs_out, weight, sem
):
    heads_width = weight.shape[-1]
    q_width = heads_width - LANES
    copies = load_weight((own, other_y, other_core, beyond), pl.ds(0, heads_width), weight, sem)
    for copy in copies:
        copy.wait()
    rows = normed[...]
    projected = matmul(rows, weight[...].reshape(-1, heads_width))
    queries = turn(projected[:, :q_width], [tables[n] for n in range(3)]).astype(jnp.bfloat16)
    pairs = turn(projected[:, q_width:], [tables[n] for n in range(3, 6)]).astype(jnp.bfloat16)
    queries_out[...] = queries
    pairs_out[...] = pairs
    key, value = pairs[:, :HEAD_DIM], pairs[:, HEAD_DIM:]
    mask = causal_blocks(ROWS, LEN)
    mixed = []
    for start in range(0, q_width, HEAD_DIM):
        weights = attend(queries[:, start : start + HEAD_DIM], key, mask, HEAD_DIM ** (-0.5))
        mixed.append(matmul(weights.astype(jnp.bfloat16), value))
    mixed = jnp.concatenate(mixed, axis=1).astype(jnp.bfloat16)

    @pl.loop(0, partial.shape[1] // TILE)
    def _(n):
        columns = pl.ds(pl.multiple_of(n * TILE, TILE), TILE)
        partial[:, columns] = matmul(mixed, out_weight[:, columns]).astype(jnp.bfloat16)


def attention_back_kernel(
    grad, queries, pairs, out_weight, tables, own, other_y, other_core, beyond, partial, weight, sem
):
    heads_width = weight.shape[-1]
    q_width = heads_width - LANES
    scale = HEAD_DIM ** (-0.5)
    copies = load_weight((own, other_y, other_core, beyond), pl.ds(0, heads_width), weight, sem)
    mixed_grad = times_trans(grad[...], out_weight[...]).astype(jnp.bfloat16)
    key, value = pairs[:, :HEAD_DIM], pairs[:, HEAD_DIM:]
    mask = causal_blocks(ROWS, LEN)
    query_grads, key_grad, value_grad = [], 0.0, 0.0
    for start in range(0, q_width, HEAD_DIM):
        query = queries[:, start : start + HEAD_DIM]
        outer = mixed_grad[:, start : start + HEAD_DIM]
        weights = attend(query, key, mask, scale)
        weight_grad = times_trans(outer, value)
        score_grad = weights * (
            weight_grad - jnp.sum(weights * weight_grad, axis=1, keepdims=True)
        )
        score_grad = score_grad.astype(jnp.bfloat16)
        query_grads.append(matmul(score_grad, key) * scale)
        key_grad = key_grad + trans_times(score_grad, query) * scale
        value_grad = value_grad + trans_times(weights.astype(jnp.bfloat16), outer)
    query_grad = turn(jnp.concatenate(query_grads, axis=1), [tables[n] for n in range(3)])
    pair_grad = jnp.concatenate([key_grad, value_grad], axis=1)
    pair_grad = turn(pair_grad, [tables[n] for n in range(3, 6)])
    both = jnp.concatenate([query_grad, pair_grad], axis=1).astype(jnp.bfloat16)
    for copy in copies:
        copy.wait()
    tiles = partial.shape[1] // TILE
    each = weight.shape[0] // tiles

    @pl.loop(0, tiles)
    def _(n):
        columns = pl.ds(pl.multiple_of(n * TILE, TILE), TILE)
        block = weight[pl.ds(n * each, each)].reshape(TILE, heads_width)
        partial[:, columns] = times_trans(both, block).astype(jnp.bfloat16)


def feed_kernel(normed, down, own, other_y, other_core, beyond, partial, kept, weight, active, sem):
    width = weight.shape[-1]
    share = down.shape[0]
    edge = share // LANES * LANES
    tail = share - edge
    copies = load_weight(
        (own, other_y, other_core, beyond), pl.ds(own.shape[-1] - width, width), weight, sem
    )
    for copy in copies:
        copy.wait()
    depth = partial.shape[1]

    @pl.loop(0, width // LANES)
    def _(n):
        columns = pl.ds(pl.multiple_of(n * LANES, LANES), LANES)
        kept[:, columns] = matmul(normed[...], weight[:, :, :, columns].reshape(depth, LANES))

    def activate(gate, up):
        return (jax.nn.silu(gate) * up).astype(jnp.bfloat16)

    active[:, :edge] = activate(kept[:, :edge], kept[:, edge : 2 * edge])
    if tail:
        last = kept[:, 2 * edge :]
        active[:, edge:] = activate(last[:, :tail], last[:, tail:])

    @pl.loop(0, depth // TILE)
    def _(n):
        columns = pl.ds(pl.multiple_of(n * TILE, TILE), TILE)
        partial[:, columns] = matmul(active[...], down[:, columns]).astype(jnp.bfloat16)


def feed_back_kernel(grad, kept, down, own, other_y, other_core, beyond, partial, weight, both, sem):
    width = weight.shape[-1]
    share = down.shape[0]
    edge = share // LANES * LANES
    tail = share - edge
    copies = load_weight(
        (own, other_y, other_core, beyond), pl.ds(own.shape[-1] - width, width), weight, sem
    )
    active_grad = times_trans(grad[...], down[...])

    def back(outer, gate, up):
        sigmoid = jax.nn.sigmoid(gate)
        gate_grad = outer * up * sigmoid * (1.0 + gate * (1.0 - sigmoid))
        return gate_grad.astype(jnp.bfloat16), (outer * gate * sigmoid).astype(jnp.bfloat16)

    gate_grad, up_grad = back(active_grad[:, :edge], kept[:, :edge], kept[:, edge : 2 * edge])
    both[:, :edge] = gate_grad
    both[:, edge : 2 * edge] = up_grad
    if tail:
        last = kept[:, 2 * edge :]
        gate_grad, up_grad = back(active_grad[:, edge:], last[:, :tail], last[:, tail:])
        both[:, 2 * edge :] = jnp.concatenate([gate_grad, up_grad], axis=1)
    for copy in copies:
        copy.wait()
    tiles = partial.shape[1] // TILE
    each = weight.shape[0] // tiles

    @pl.loop(0, tiles)
    def _(n):
        columns = pl.ds(pl.multiple_of(n * TILE, TILE), TILE)
        block = weight[pl.ds(n * each, each)].reshape(TILE, width)
        partial[:, columns] = times_trans(both[...], block).astype(jnp.bfloat16)


class Layer:
    def __init__(self, stack, index):
        self.stack, self.index, self.shape = stack, index, stack.shape[1:]

    def spec(self):
        return pl.BlockSpec(
            (None,) + self.shape, lambda step: (self.index, 0, 0), memory_space=pltpu.VMEM
        )


def local(kernel, operands, weights, outs, scratch, name):
    specs = [item.spec() if isinstance(item, Layer) else IN_VMEM for item in operands]
    operands = [item.stack if isinstance(item, Layer) else item for item in operands]
    return pl.pallas_call(
        kernel,
        grid=(1,),
        out_shape=tuple(jax.ShapeDtypeStruct(shape, kind) for shape, kind in outs),
        in_specs=specs + [ANYWHERE] * len(weights),
        out_specs=(IN_VMEM,) * len(outs),
        scratch_shapes=list(scratch),
        compiler_params=pltpu.CompilerParams(vmem_limit_bytes=VMEM_LIMIT),
        name=name,
    )(*operands, *weights)


def weight_scratch(pieces, width):
    groups, rows = pieces[0].shape[:2]
    return pltpu.VMEM((groups, SECTIONS, rows, width), jnp.bfloat16)


def attention_forward(normed, pieces, out_weight, tables):
    q_width, depth = out_weight.shape
    partial, queries, pairs = local(
        attention_kernel,
        (normed, out_weight, tables),
        pieces,
        [
            ((ROWS, depth), jnp.bfloat16),
            ((ROWS, q_width), jnp.bfloat16),
            ((ROWS, LANES), jnp.bfloat16),
        ],
        [weight_scratch(pieces, q_width + LANES), dma_sems(4)],
        "attention",
    )
    return partial, (queries, pairs)


def attention_backward(grad, stored, pieces, out_weight, tables):
    q_width, depth = out_weight.shape
    (partial,) = local(
        attention_back_kernel,
        (grad, *stored, out_weight, tables),
        pieces,
        [((ROWS, depth), jnp.bfloat16)],
        [weight_scratch(pieces, q_width + LANES), dma_sems(4)],
        "attention_grad",
    )
    return partial


def feed_forward(normed, pieces, down):
    share, depth = down.shape
    partial, kept = local(
        feed_kernel,
        (normed, down),
        pieces,
        [((ROWS, depth), jnp.bfloat16), ((ROWS, 2 * share), jnp.float32)],
        [
            weight_scratch(pieces, 2 * share),
            pltpu.VMEM((ROWS, share), jnp.bfloat16),
            dma_sems(4),
        ],
        "feed",
    )
    return partial, kept


def feed_backward(grad, kept, pieces, down):
    share, depth = down.shape
    (partial,) = local(
        feed_back_kernel,
        (grad, kept, down),
        pieces,
        [((ROWS, depth), jnp.bfloat16)],
        [
            weight_scratch(pieces, 2 * share),
            pltpu.VMEM((ROWS, 2 * share), jnp.bfloat16),
            dma_sems(4),
        ],
        "feed_grad",
    )
    return partial


CHUNK = 128


def same_entry(count, slots):
    row = lax.broadcasted_iota(jnp.int32, (count, count), 0)
    column = lax.broadcasted_iota(jnp.int32, (count, count), 1)
    return row // slots == column // slots


def gelu(values):
    return 0.5 * values * (1.0 + lax.erf(values * inv_root_two))


def hyper_kernel(
    slots,
    pieces,
    first,
    second,
    third,
    vectors,
    table,
    heads_out,
    mixed_out,
    middle_out,
    expanded_out,
    pooled_out,
    entered,
    outcome,
):
    width = pieces.shape[1]
    count, feed = pieces.shape[0], third.shape[0]
    head = width // HYPER_HEAD_COUNT
    flat = pieces[...].astype(jnp.float32)
    normed, _ = center_norm(flat)
    entered[...] = (normed * vectors[0:1] + vectors[1:2]).astype(jnp.bfloat16)

    @pl.loop(0, 3 * width // TILE)
    def _(n):
        columns = pl.ds(pl.multiple_of(n * TILE, TILE), TILE)
        heads_out[:, columns] = matmul(entered[...], first[:, columns]).astype(jnp.bfloat16)

    mask = same_entry(CHUNK, slots)

    @pl.loop(0, count // CHUNK)
    def _(n):
        rows = pl.ds(pl.multiple_of(n * CHUNK, CHUNK), CHUNK)
        block = heads_out[rows, :]
        mixed = []
        for start in range(0, width, head):
            query, key, value = (
                block[:, part * width + start : part * width + start + head] for part in range(3)
            )
            weights = attend(query, key, mask, head ** (-0.5))
            mixed.append(matmul(weights.astype(jnp.bfloat16), value))
        mixed_out[rows, :] = jnp.concatenate(mixed, axis=1).astype(jnp.bfloat16)

    for start in range(0, width, TILE):
        columns = pl.ds(start, TILE)
        middle_out[:, columns] = pieces[:, columns].astype(jnp.float32) + matmul(
            mixed_out[...], first[:, pl.ds(3 * width + start, TILE)]
        )
    normed, _ = center_norm(middle_out[...])
    entered[...] = (normed * vectors[2:3] + vectors[3:4]).astype(jnp.bfloat16)
    outcome[...] = middle_out[...]

    @pl.loop(0, feed // TILE)
    def _(n):
        start = pl.multiple_of(n * TILE, TILE)
        columns = pl.ds(pl.multiple_of(4 * width + start, TILE), TILE)
        expanded = matmul(entered[...], first[:, columns])
        expanded_out[:, pl.ds(start, TILE)] = expanded
        outcome[...] += matmul(gelu(expanded).astype(jnp.bfloat16), third[pl.ds(start, TILE), :])

    pooled = jnp.mean(outcome[...].reshape(count // slots, slots, width), axis=1)
    pooled_out[...] = pooled.astype(jnp.bfloat16)

    @pl.loop(0, table.shape[1] // TILE)
    def _(n):
        columns = pl.ds(pl.multiple_of(n * TILE, TILE), TILE)
        table[:, columns] = matmul(pooled_out[...], second[:, columns]).astype(jnp.bfloat16)


def hyper_forward(pieces, slots, params):
    count, width = pieces.shape
    first, second, third, vectors = params
    feed = third.shape[0]
    depth = second.shape[1] - LANES
    entries = count // slots
    table, *stored = local(
        functools.partial(hyper_kernel, slots),
        (pieces, *params),
        (),
        [
            ((entries, depth), jnp.bfloat16),
            ((count, 3 * width), jnp.bfloat16),
            ((count, width), jnp.bfloat16),
            ((count, width), jnp.float32),
            ((count, feed), jnp.float32),
            ((entries, width), jnp.bfloat16),
        ],
        [pltpu.VMEM((count, width), jnp.bfloat16), pltpu.VMEM((count, width), jnp.float32)],
        "hyper",
    )
    return table, stored


def hyper_back_kernel(
    slots,
    table_grad,
    pieces,
    first,
    second,
    third,
    vectors,
    heads,
    mixed,
    middle,
    expanded,
    pooled,
    first_grad,
    second_grad,
    third_grad,
    entered,
    outcome_low,
    feed_grad,
    heads_grad,
    mixed_grad,
):
    width = pieces.shape[1]
    count, feed = pieces.shape[0], third.shape[0]
    depth = table_grad.shape[1]
    head = width // HYPER_HEAD_COUNT
    scale = head ** (-0.5)
    grad_low = table_grad[...].astype(jnp.bfloat16)
    pooled_turned = jnp.transpose(pooled[...].astype(jnp.float32)).astype(jnp.bfloat16)

    for start in range(0, depth, TILE):
        columns = pl.ds(start, TILE)
        second_grad[:, columns] = matmul(
            pooled_turned, grad_low[:, start : start + TILE]
        ).astype(jnp.bfloat16)
    pooled_grad = times_trans(grad_low, second[:, pl.ds(0, depth)]) / slots
    outcome_grad = jnp.broadcast_to(pooled_grad[:, None, :], (count // slots, slots, width))
    outcome_grad = outcome_grad.reshape(count, width)
    outcome_low[...] = outcome_grad.astype(jnp.bfloat16)
    normed, inverse = center_norm(middle[...])
    entered[...] = jnp.transpose(normed * vectors[2:3] + vectors[3:4]).astype(jnp.bfloat16)
    feed_grad[...] = jnp.zeros_like(feed_grad)

    @pl.loop(0, feed // TILE)
    def _(n):
        start = pl.multiple_of(n * TILE, TILE)
        tile = pl.ds(start, TILE)
        columns = pl.ds(pl.multiple_of(4 * width + start, TILE), TILE)
        values = expanded[:, tile]
        erf = 0.5 * (1.0 + lax.erf(values * inv_root_two))
        active = (values * erf).astype(jnp.bfloat16)
        third_grad[tile, :] = trans_times(active, outcome_low[...]).astype(jnp.bfloat16)
        active_grad = times_trans(outcome_low[...], third[tile, :])
        slope = erf + values * jnp.exp(-0.5 * values * values) * inv_root_tau
        low = (active_grad * slope).astype(jnp.bfloat16)
        first_grad[:, columns] = matmul(entered[...], low).astype(jnp.bfloat16)
        feed_grad[...] += times_trans(low, first[:, columns])

    grad = feed_grad[...]
    scale_two = jnp.sum(grad * normed, axis=0, keepdims=True)
    shift_two = jnp.sum(grad, axis=0, keepdims=True)
    middle_grad = outcome_grad + center_back(normed, inverse, grad * vectors[2:3])
    middle_low = middle_grad.astype(jnp.bfloat16)
    out_columns = pl.ds(3 * width, width)
    first_grad[:, out_columns] = trans_times(mixed[...], middle_low).astype(jnp.bfloat16)
    mixed_grad[...] = times_trans(middle_low, first[:, out_columns]).astype(jnp.bfloat16)
    mask = same_entry(CHUNK, slots)

    @pl.loop(0, count // CHUNK)
    def _(n):
        rows = pl.ds(pl.multiple_of(n * CHUNK, CHUNK), CHUNK)
        block = heads[rows, :]
        outer_block = mixed_grad[rows, :]
        grads = [[], [], []]
        for start in range(0, width, head):
            query, key, value = (
                block[:, part * width + start : part * width + start + head] for part in range(3)
            )
            outer = outer_block[:, start : start + head]
            weights = attend(query, key, mask, scale)
            weight_grad = times_trans(outer, value)
            score_grad = weights * (
                weight_grad - jnp.sum(weights * weight_grad, axis=1, keepdims=True)
            )
            score_grad = score_grad.astype(jnp.bfloat16)
            grads[0].append(matmul(score_grad, key) * scale)
            grads[1].append(trans_times(score_grad, query) * scale)
            grads[2].append(trans_times(weights.astype(jnp.bfloat16), outer))
        for part in range(3):
            heads_grad[rows, pl.ds(part * width, width)] = jnp.concatenate(
                grads[part], axis=1
            ).astype(jnp.bfloat16)

    normed, _ = center_norm(pieces[...].astype(jnp.float32))
    entered[...] = jnp.transpose(normed * vectors[0:1] + vectors[1:2]).astype(jnp.bfloat16)
    feed_grad[...] = jnp.zeros_like(feed_grad)

    @pl.loop(0, 3 * width // TILE)
    def _(n):
        columns = pl.ds(pl.multiple_of(n * TILE, TILE), TILE)
        low = heads_grad[:, columns]
        first_grad[:, columns] = matmul(entered[...], low).astype(jnp.bfloat16)
        feed_grad[...] += times_trans(low, first[:, columns])

    grad = feed_grad[...]
    scale_one = jnp.sum(grad * normed, axis=0, keepdims=True)
    shift_one = jnp.sum(grad, axis=0, keepdims=True)
    row = lax.broadcasted_iota(jnp.int32, (LANES, width), 0)
    summed = jnp.zeros((LANES, width), jnp.float32)
    for n, item in enumerate((scale_one, shift_one, scale_two, shift_two)):
        summed = jnp.where(row == n, item, summed)
    second_grad[:, pl.ds(depth, LANES)] = jnp.transpose(summed).astype(jnp.bfloat16)


def hyper_backward(pieces, slots, params, stored, table_grad):
    count, width = pieces.shape
    first, second, third, _ = params
    return local(
        functools.partial(hyper_back_kernel, slots),
        (table_grad, pieces, *params, *stored),
        (),
        [(item.shape, jnp.bfloat16) for item in (first, second, third)],
        [
            pltpu.VMEM((width, count), jnp.bfloat16),
            pltpu.VMEM((count, width), jnp.bfloat16),
            pltpu.VMEM((count, width), jnp.float32),
            pltpu.VMEM((count, 3 * width), jnp.bfloat16),
            pltpu.VMEM((count, width), jnp.bfloat16),
        ],
        "hyper_back",
    )


def column_plan(q_columns, kv_columns, ff_columns):
    share = ff_columns // TEAM
    edge = share // LANES * LANES
    tail = share - edge
    heads = kv_columns // HEAD_DIM
    q_share = q_columns // TEAM
    plan = []
    for rank in range(TEAM):
        kv = rank * heads // TEAM * HEAD_DIM
        widths = [
            (0, rank * q_share, q_share),
            (1, kv, HEAD_DIM),
            (2, kv, HEAD_DIM),
            (3, rank * share, edge),
            (4, rank * share, edge),
            (3, rank * share + edge, tail),
            (4, rank * share + edge, tail),
        ]
        moves, start = [], 0
        for item, source, size in widths:
            moves.append((item, source, start, size))
            start += size
        plan.append(moves)
    return plan, start


def pack_kernel(plan, rows, *refs):
    sources, targets = refs[:5], refs[5:7]
    blocks, sem = refs[7:12], refs[12]
    section = lax.axis_index("section")
    mine = pl.ds(pl.multiple_of(section * rows, rows), rows)
    copies = [
        [
            pltpu.make_async_copy(source.at[layer, mine], block.at[layer], sem.at[layer, n])
            for n, (source, block) in enumerate(zip(sources, blocks))
        ]
        for layer in range(2)
    ]
    for layer in range(2):
        for copy in copies[layer]:
            copy.start()
    for layer in range(2):
        for copy in copies[layer]:
            copy.wait()
        for rank, moves in enumerate(plan):
            parts = [
                blocks[item][layer, :, source : source + size] for item, source, _, size in moves
            ]
            heads = jnp.concatenate(parts[1:3], axis=1)
            ends = jnp.concatenate(parts[5:7], axis=1)
            for part, start in zip(
                (parts[0], heads, parts[3], parts[4], ends),
                (moves[0][2], moves[1][2], moves[3][2], moves[4][2], moves[5][2]),
            ):
                if part.shape[1]:
                    targets[layer][rank, :, start : start + part.shape[1]] = part


def pack(weights):
    rows = weights[0].shape[1] // SECTIONS
    plan, width = column_plan(weights[0].shape[2], weights[1].shape[2], weights[3].shape[2])
    if rows % 16:
        section = lax.axis_index("section")
        mine = [lax.dynamic_slice_in_dim(item, section * rows, rows, 1) for item in weights]
        return tuple(
            jnp.stack(
                [
                    jnp.concatenate(
                        [mine[item][layer, :, at : at + size] for item, at, _, size in moves], axis=1
                    )
                    for moves in plan
                ]
            )
            for layer in range(2)
        )
    return pl.pallas_call(
        functools.partial(pack_kernel, plan, rows),
        out_shape=(jax.ShapeDtypeStruct((TEAM, rows, width), jnp.bfloat16),) * 2,
        in_specs=[ANYWHERE] * 5,
        out_specs=(IN_VMEM,) * 2,
        scratch_shapes=[pltpu.VMEM((2, rows, item.shape[2]), jnp.bfloat16) for item in weights]
        + [dma_sems(2, 5)],
        compiler_params=pltpu.CompilerParams(vmem_limit_bytes=VMEM_LIMIT),
        name="pack",
    )(*weights)


def team_groups(wides, outer):
    return [[rank * outer + team for team in range(outer)] for rank in range(wides // outer)]


SWAP_Y = [(source, (source + 2) % SECTIONS) for source in range(SECTIONS)]
SWAP_CORE = [(source, source + 1 - 2 * (source % 2)) for source in range(SECTIONS)]


def together(*items):
    return lax.optimization_barrier(items)


def all_teams(pieces, outer, groups):
    if outer == 1:
        return pieces
    pieces = [
        lax.all_gather(piece, "wide", axis=1, axis_index_groups=groups) for piece in pieces
    ]
    return [piece.reshape((-1,) + piece.shape[2:]) for piece in pieces]


def shards(
    token_ids,
    targets,
    slot_ids,
    group_ids,
    group_offsets,
    piece_table,
    prenorm_gain,
    prenorm_bias,
    query_map,
    key_map,
    value_map,
    output_map,
    midnorm_gain,
    midnorm_bias,
    expand_map,
    reduce_map,
    embed_map,
    attention_gain,
    query_weight,
    key_weight,
    value_weight,
    output_weight,
    feed_gain,
    gate_weight,
    up_weight,
    down_weight,
    final_gain,
):
    wides = lax.axis_size("wide")
    outer = wides // TEAM
    groups = team_groups(wides, outer)
    section_index = lax.axis_index("section")
    wide_index = lax.axis_index("wide")
    rank = wide_index // outer
    hyper_width, hyper_feed = piece_table.shape[1], expand_map.shape[1]
    model_width = embed_map.shape[1]
    total_tokens = wides * MB * LEN

    rank_groups = [[rank * outer + team for rank in range(TEAM)] for team in range(outer)]

    def to_ranks(block):
        return lax.all_to_all(
            block, "wide", 0, 0, axis_index_groups=rank_groups if outer > 1 else None, tiled=True
        )

    blocks = pack((query_weight, key_weight, value_weight, gate_weight, up_weight))
    own_one = to_ranks(blocks[0])

    vectors = jnp.stack([prenorm_gain, prenorm_bias, midnorm_gain, midnorm_bias], axis=1)
    vectors = jnp.pad(vectors, ((0, 0), (0, LANES - 4)))
    first = jnp.concatenate([query_map, key_map, value_map, output_map, expand_map], axis=1)
    second = jnp.concatenate([embed_map, vectors], axis=1)
    gains = jnp.concatenate([attention_gain, feed_gain], axis=0)
    gains = jnp.pad(gains, ((0, 16 - gains.shape[0]), (0, 0)))
    notes = jnp.concatenate([token_ids.reshape(1, -1), targets.reshape(1, -1)], axis=0)
    notes = jnp.pad(notes, ((0, 6), (0, 0)))
    first, second, third, gains, notes = spread(
        1,
        wides,
        outer,
        (first.astype(jnp.bfloat16), second.astype(jnp.bfloat16), reduce_map.astype(jnp.bfloat16)),
        (gains, notes),
    )
    first, own_one, block = together(first, own_one, blocks[1])
    own_two = to_ranks(block)
    y_one = lax.ppermute(own_one, "section", SWAP_Y)
    core_one = lax.ppermute(own_one, "section", SWAP_CORE)
    first = first.reshape(hyper_width, -1)
    second = second.reshape(hyper_width, -1)
    third = third.reshape(hyper_feed, hyper_width)
    vectors = second[:, model_width : model_width + 8].astype(jnp.float32).T
    params = (first, second, third, vectors)
    if outer > 1:
        gains = lax.all_gather(gains, "wide", axis=1, axis_index_groups=groups)
        gains = gains.reshape(-1, gains.shape[2], gains.shape[3])
        output_weight, down_weight = (
            lax.all_gather(item, "wide", axis=1, axis_index_groups=groups, tiled=True)
            for item in (output_weight, down_weight)
        )
    gains = gains.astype(jnp.float32).transpose(1, 0, 2).reshape(-1, 1, model_width)
    attention_gains, feed_gains = gains[:2], gains[2:4]
    final_scale = final_gain.astype(jnp.float32).reshape(1, model_width)
    notes = lax.dynamic_slice_in_dim(notes, section_index * 2, 2, 0)
    ids, wanted = notes[:, 0].reshape(-1), notes[:, 1].reshape(-1)
    tables, back_tables = turn_tables(False), turn_tables(True)

    entries, slot_count = slot_ids.shape
    group_hits = (
        group_ids[:, None] == jnp.arange(group_offsets.shape[0], dtype=jnp.int32)[None, :]
    ).astype(jnp.int32)
    row_start = jnp.sum(group_hits * group_offsets[None, :], axis=1)
    piece_rows = (row_start[:, None] + slot_ids).reshape(-1)
    pieces = jnp.take(piece_table, piece_rows, axis=0)
    table_shard, hyper_stored = hyper_forward(pieces, slot_count, params)
    table_shard, y_one = together(table_shard, y_one)
    beyond_one = lax.ppermute(y_one, "section", SWAP_CORE)
    table_rows = section_gather(3, table_shard)
    table_rows, own_two = together(table_rows, own_two)
    y_two = lax.ppermute(own_two, "section", SWAP_Y)
    core_two = lax.ppermute(own_two, "section", SWAP_CORE)
    if outer > 1:
        table_rows = lax.all_gather(table_rows, "wide", axis=1, axis_index_groups=groups)
    table_rows = table_rows.reshape(-1, model_width)
    wide_rows = rank * outer + jnp.arange(outer, dtype=jnp.int32)
    row_starts = (
        jnp.arange(SECTIONS, dtype=jnp.int32)[:, None] * wides + wide_rows[None, :]
    ) * entries
    own_rows = row_starts[:, :, None] + jnp.arange(entries, dtype=jnp.int32)[None, None, :]
    own_rows = own_rows.reshape(-1)
    hits = (ids[:, None] == own_rows[None, :]).astype(jnp.bfloat16)
    injected = matmul(hits, table_rows).astype(jnp.bfloat16)
    normed, hidden = fold(inject, outer, 4, injected, (attention_gains[0],), (jnp.bfloat16,))

    weights = [all_teams((own_one, y_one, core_one, beyond_one), outer, groups)]
    kept = []
    for layer in range(2):
        partial, attended = attention_forward(
            normed.reshape(ROWS, model_width), weights[layer], Layer(output_weight, layer), tables
        )
        normed, middle = fold(
            enter_feed, outer, 5, partial, (hidden, feed_gains[layer]), (jnp.float32,)
        )
        partial, fed = feed_forward(
            normed.reshape(ROWS, model_width), weights[layer], Layer(down_weight, layer)
        )
        if layer == 0:
            partial, y_two = together(partial, y_two)
            beyond_two = lax.ppermute(y_two, "section", SWAP_CORE)
            weights.append(all_teams((own_two, y_two, core_two, beyond_two), outer, groups))
        kept.append((hidden, attended, middle, fed))
        next_gain = attention_gains[1] if layer == 0 else final_scale
        normed, hidden = fold(
            leave_layer, outer, 6, partial, (middle, next_gain), (jnp.bfloat16,)
        )

    final_normed = normed.reshape(ROWS, model_width)
    logits = times_trans(final_normed, table_rows)
    row_peak = jnp.max(logits, axis=1)
    row_mass = jnp.sum(jnp.exp(logits - row_peak[:, None]), axis=1)
    wanted_hits = wanted[:, None] == own_rows[None, :]
    chosen = jnp.sum(jnp.where(wanted_hits, logits, 0.0), axis=1)
    blank = jnp.zeros_like(chosen)
    stats = jnp.stack([row_peak, row_mass, chosen] + [blank] * 5, axis=0)
    stats = team_gather(outer, 7, stats)
    peak = jnp.max(stats[:, 0], axis=0)
    mass = jnp.sum(stats[:, 1] * jnp.exp(stats[:, 0] - peak[None, :]), axis=0)
    log_norm = peak + jnp.log(mass)
    loss_part = jnp.sum(log_norm - jnp.sum(stats[:, 2], axis=0)) / total_tokens
    logit_grad = (
        (jnp.exp(logits - log_norm[:, None]) - wanted_hits.astype(jnp.float32)) / total_tokens
    ).astype(jnp.bfloat16)
    partial = matmul(logit_grad, table_rows).astype(jnp.bfloat16)
    grads, outer_grad = fold(
        head_back, outer, 8, partial, (hidden, final_scale), (jnp.bfloat16,)
    )

    for layer in (1, 0):
        hidden, attended, middle, fed = kept[layer]
        partial = feed_backward(
            grads.reshape(ROWS, model_width), fed, weights[layer], Layer(down_weight, layer)
        )
        grads, middle_grad = fold(
            feed_back, outer, 9, partial, (outer_grad, middle, feed_gains[layer]), (jnp.float32,)
        )
        partial = attention_backward(
            grads.reshape(ROWS, model_width),
            attended,
            weights[layer],
            Layer(output_weight, layer),
            back_tables,
        )
        grads, outer_grad = fold(
            layer_back,
            outer,
            10,
            partial,
            (middle_grad, hidden, attention_gains[layer]),
            (jnp.bfloat16,),
        )

    table_part = trans_times(logit_grad, final_normed) + trans_times(
        hits, grads.reshape(ROWS, model_width)
    )
    table_part = table_part.astype(jnp.bfloat16).reshape(SECTIONS, outer, entries, model_width)
    loss_block = jnp.full((8, LANES), loss_part, jnp.float32)
    if outer > 1:
        table_part = lax.psum_scatter(
            table_part.astype(jnp.float32),
            "wide",
            scatter_dimension=1,
            axis_index_groups=groups,
        ).astype(jnp.bfloat16)
        loss_block = lax.psum(loss_block, "wide", axis_index_groups=groups)
    table_grad, loss_block = section_sum(
        11, table_part.reshape(SECTIONS, entries, model_width), loss_block
    )
    mean_loss = loss_block[0, 0]
    grads = hyper_backward(pieces, slot_count, params, hyper_stored, table_grad)
    first, second, third = (
        item.reshape(SECTIONS, wides, -1, item.shape[1]) for item in grads
    )
    first, second, third = collect(12, (first, second, third))
    grad_query, grad_key, grad_value, grad_output = (
        first[:, n * hyper_width : (n + 1) * hyper_width] for n in range(4)
    )
    return (
        mean_loss,
        second[:, model_width],
        second[:, model_width + 1],
        grad_query,
        grad_key,
        grad_value,
        grad_output,
        second[:, model_width + 2],
        second[:, model_width + 3],
        first[:, 4 * hyper_width :],
        third,
        second[:, :model_width],
    )


def solution(mesh):
    placed = (
        P("wide", None, None),
        P("wide", None, None),
        P(("section", "wide"), None),
        P(("section", "wide")),
        P(),
        P(),
        P(("section", "wide")),
        P(("section", "wide")),
        P(("section", "wide"), None),
        P(("section", "wide"), None),
        P(("section", "wide"), None),
        P(("section", "wide"), None),
        P(("section", "wide")),
        P(("section", "wide")),
        P(("section", "wide"), None),
        P(("section", "wide"), None),
        P(("section", "wide"), None),
        P(None, "wide"),
        P(None, "wide", None),
        P(None, "wide", None),
        P(None, "wide", None),
        P(None, "wide", None),
        P(None, "wide"),
        P(None, "wide", None),
        P(None, "wide", None),
        P(None, "wide", None),
        P(),
    )
    return jax.shard_map(
        shards,
        mesh=mesh,
        in_specs=placed,
        out_specs=(
            P(),
            P(("section", "wide")),
            P(("section", "wide")),
            P(("section", "wide"), None),
            P(("section", "wide"), None),
            P(("section", "wide"), None),
            P(("section", "wide"), None),
            P(("section", "wide")),
            P(("section", "wide")),
            P(("section", "wide"), None),
            P(("section", "wide"), None),
            P(("section", "wide"), None),
        ),
        check_vma=False,
    )
```

```python
import functools

import jax
import jax.numpy as jnp
from jax import lax
from jax.experimental import pallas as pl
from jax.experimental.pallas import tpu as pltpu
from jax.sharding import PartitionSpec as P

HEAD_DIM = 64
HYPER_HEAD_COUNT = 8
MB = 2
LEN = 64
TEAM = 8
SECTIONS = 4
ROWS = MB * LEN * TEAM // SECTIONS
HALF = ROWS // 2
EACH = HALF // TEAM
LINES = TEAM // 2
FIRST, SECOND = 0, 1
LANES = 128
MESH_IDS = pl.DeviceIdType.MESH
ANYWHERE = pl.BlockSpec(memory_space=pl.ANY)
IN_VMEM = pl.BlockSpec(memory_space=pltpu.VMEM)
VMEM_LIMIT = 56 * 1024 * 1024

norm_eps = 1e-05
inv_root_two = 0.7071067811865476
inv_root_tau = 0.3989422804014327


def matmul(former, latter):
    return jnp.dot(former, latter, preferred_element_type=jnp.float32)


def times_trans(former, latter):
    return lax.dot_general(
        former, latter, (((1,), (1,)), ((), ())), preferred_element_type=jnp.float32
    )


def trans_times(former, latter):
    return lax.dot_general(
        former, latter, (((0,), (0,)), ((), ())), preferred_element_type=jnp.float32
    )


def center_norm(values):
    center = values - jnp.mean(values, axis=-1, keepdims=True)
    inverse = lax.rsqrt(jnp.mean(center * center, axis=-1, keepdims=True) + norm_eps)
    return (center * inverse, inverse)


def center_back(normed, inverse, normed_grad):
    mean_grad = jnp.mean(normed_grad, axis=-1, keepdims=True)
    mean_mix = jnp.mean(normed_grad * normed, axis=-1, keepdims=True)
    return inverse * (normed_grad - mean_grad - normed * mean_mix)


def root_inverse(values):
    return lax.rsqrt(jnp.mean(values * values, axis=-1, keepdims=True) + norm_eps)


def reciprocal_root_backward(values, inverse, gain_vec, outer_grad):
    scaled = outer_grad * gain_vec
    mixing = jnp.mean(scaled * values, axis=-1, keepdims=True)
    return inverse * scaled - values * inverse * inverse * inverse * mixing


def rope_tables(positions, head_width):
    halfway = head_width // 2
    frequency = jnp.exp(
        -jnp.log(10000.0) * (2.0 * jnp.arange(halfway, dtype=jnp.float32) / head_width)
    )
    angles = jnp.arange(positions, dtype=jnp.float32)[:, None] * frequency[None, :]
    angles = jnp.concatenate([angles, angles], axis=1)
    return (jnp.cos(angles), jnp.sin(angles))


def greet(peers):
    barrier = pltpu.get_barrier_semaphore()
    for peer in peers:
        pl.semaphore_signal(barrier, inc=1, device_id=peer, device_id_type=MESH_IDS)
    pl.semaphore_wait(barrier, len(peers))


def remote(source, target, send, recv, peer):
    return pltpu.make_async_remote_copy(
        src_ref=source,
        dst_ref=target,
        send_sem=send,
        recv_sem=recv,
        device_id=peer,
        device_id_type=MESH_IDS,
    )


def settings(collective_id):
    return pltpu.CompilerParams(
        collective_id=collective_id, has_side_effects=True, vmem_limit_bytes=VMEM_LIMIT
    )


def dma_sems(*shape):
    return pltpu.SemaphoreType.DMA(shape)


def section_places():
    section = lax.axis_index("section")
    core = section % 2
    partner = section + 1 - 2 * core
    across = (section + 2) % SECTIONS
    return section, partner, across


def section_gather_kernel(block, gathered, keep_sem, send, recv):
    section, partner, across = section_places()
    greet([{"section": partner}, {"section": across}])
    keep = pltpu.make_async_copy(block, gathered.at[section], keep_sem)
    near = remote(block, gathered.at[section], send.at[0], recv.at[0], {"section": partner})
    far = remote(block, gathered.at[section], send.at[1], recv.at[1], {"section": across})
    on = remote(
        gathered.at[across], gathered.at[across], send.at[2], recv.at[2], {"section": partner}
    )
    far.start()
    near.start()
    keep.start()
    far.wait_recv()
    on.start()
    near.wait()
    on.wait()
    far.wait_send()
    keep.wait()


def section_gather(collective_id, block):
    return pl.pallas_call(
        section_gather_kernel,
        out_shape=jax.ShapeDtypeStruct((SECTIONS,) + block.shape, block.dtype),
        in_specs=[ANYWHERE],
        out_specs=ANYWHERE,
        scratch_shapes=[pltpu.SemaphoreType.DMA, dma_sems(3), dma_sems(3)],
        compiler_params=settings(collective_id),
        name="section_gather",
    )(block)


def section_sum_kernel(partial, loss, summed, loss_sum, own, near, pair, far, loss_near, loss_pair, loss_far, load_sem, send, recv):
    section, partner, across = section_places()
    beyond = (partner + 2) % SECTIONS
    greet([{"section": partner}, {"section": across}])
    loads = [
        pltpu.make_async_copy(partial.at[section], own.at[0], load_sem.at[0]),
        pltpu.make_async_copy(partial.at[across], own.at[1], load_sem.at[1]),
    ]
    nears = [
        remote(partial.at[partner], near.at[0], send.at[0], recv.at[0], {"section": partner}),
        remote(partial.at[beyond], near.at[1], send.at[1], recv.at[1], {"section": partner}),
        remote(loss, loss_near, send.at[2], recv.at[2], {"section": partner}),
    ]
    fars = [
        remote(pair, far, send.at[3], recv.at[3], {"section": across}),
        remote(loss_pair, loss_far, send.at[4], recv.at[4], {"section": across}),
    ]
    for j in (1, 2, 0):
        nears[j].start()
    loads[1].start()
    loads[0].start()
    loads[1].wait()
    nears[1].wait_recv()
    pair[...] = (own[1].astype(jnp.float32) + near[1].astype(jnp.float32)).astype(jnp.bfloat16)
    fars[0].start()
    nears[2].wait_recv()
    loss_pair[...] = loss[...] + loss_near[...]
    fars[1].start()
    loads[0].wait()
    nears[0].wait_recv()
    total = own[0].astype(jnp.float32) + near[0].astype(jnp.float32)
    fars[0].wait_recv()
    summed[...] = total + far[...].astype(jnp.float32)
    fars[1].wait_recv()
    loss_sum[...] = loss_pair[...] + loss_far[...]
    for copy in nears + fars:
        copy.wait_send()


def section_sum(collective_id, partial, loss):
    shape = partial.shape[1:]
    low, low_two = pltpu.VMEM(shape, jnp.bfloat16), pltpu.VMEM((2,) + shape, jnp.bfloat16)
    number = pltpu.VMEM(loss.shape, jnp.float32)
    return pl.pallas_call(
        section_sum_kernel,
        out_shape=(
            jax.ShapeDtypeStruct(shape, jnp.float32),
            jax.ShapeDtypeStruct(loss.shape, jnp.float32),
        ),
        in_specs=[ANYWHERE, IN_VMEM],
        out_specs=(IN_VMEM, IN_VMEM),
        scratch_shapes=[low_two, low_two, low, low, number, number, number]
        + [dma_sems(2), dma_sems(5), dma_sems(5)],
        compiler_params=settings(collective_id),
        name="section_sum",
    )(partial, loss)


def all_places(halves):
    section, partner, across = section_places()
    wide = lax.axis_index("wide")
    line, column = wide // 2, wide % 2

    def wide_at(j):
        return ((line + j) % halves) * 2 + column

    return section, partner, across, wide, wide_at


def steps_of(x_first, section, partner, across, wide):
    column_flip = wide + 1 - 2 * (wide % 2)
    x_step = ({"wide": column_flip}, False, True)
    y_step = ({"section": across}, True, False)
    return (x_step, y_step) if x_first else (y_step, x_step)


def owner_of(home, flips_y, flips_x, wide_block):
    section = (home + 2) % SECTIONS if flips_y else home
    return section, (wide_block + 1 - 2 * (wide_block % 2) if flips_x else wide_block)


def spread_kernel(count, halves, outer, *refs):
    blocks, notes = refs[:count], refs[count : count + 2]
    gathereds, notes_out = refs[count + 2 : 2 * count + 2], refs[2 * count + 2 : 2 * count + 4]
    (
        keep_sem,
        note_keep,
        note_send,
        note_recv,
        z_send,
        a_send,
        b_send,
        c_send,
        z_recv,
        a_recv,
        b_recv,
        c_recv,
    ) = refs[2 * count + 4 :]
    section, partner, across, wide, wide_at = all_places(halves)
    rank, team = wide // outer, wide % outer
    members = [None] + [{"wide": (rank + k) % TEAM * outer + team} for k in range(1, TEAM)]
    beside = wide + 1 - 2 * (wide % 2)
    barrier = pltpu.get_barrier_semaphore()
    for peer in ({"section": partner}, {"section": across}, {"wide": beside}):
        pl.semaphore_signal(barrier, inc=1, device_id=peer, device_id_type=MESH_IDS)

    def hello(j, carry):
        peer = {"wide": wide_at(j)}
        pl.semaphore_signal(barrier, inc=1, device_id=peer, device_id_type=MESH_IDS)
        return carry

    lax.fori_loop(1, halves, hello, 0)
    for peer in members[1:]:
        pl.semaphore_signal(barrier, inc=1, device_id=peer, device_id_type=MESH_IDS)
    pl.semaphore_wait(barrier, 3 + halves - 1 + TEAM - 1)
    note_keeps = [
        pltpu.make_async_copy(notes[m], notes_out[m].at[rank], note_keep.at[m]) for m in range(2)
    ]
    note_copies = [
        remote(notes[m], notes_out[m].at[rank], note_send.at[m, k], note_recv.at[m, k], members[k])
        for m in range(2)
        for k in range(1, TEAM)
    ]
    for copy in note_keeps + note_copies:
        copy.start()

    keeps = [
        pltpu.make_async_copy(blocks[n], gathereds[n].at[section, wide], keep_sem.at[n])
        for n in range(count)
    ]

    def z_copy(n, j):
        return remote(
            blocks[n],
            gathereds[n].at[section, wide],
            z_send.at[n, j],
            z_recv.at[n, j],
            {"wide": wide_at(j)},
        )

    def a_copy(n, j):
        (peer, _, _), _ = steps_of(n == 0, section, partner, across, wide)
        block = gathereds[n].at[section, wide_at(-j)]
        return remote(block, block, a_send.at[n, j], a_recv.at[n, j], peer)

    def b_copy(n, flip, j):
        (_, y_a, x_a), (peer, _, _) = steps_of(n == 0, section, partner, across, wide)
        place = owner_of(section, y_a and flip, x_a and flip, wide_at(-j))
        block = gathereds[n].at[place[0], place[1]]
        slot = j + (halves if flip else 0)
        return remote(block, block, b_send.at[n, slot], b_recv.at[n, slot], peer)

    def c_copy(n, which):
        home = (section + 2) % SECTIONS if which else section
        block = gathereds[n].at[home]
        return remote(
            block, block, c_send.at[n, which], c_recv.at[n, which], {"section": partner}
        )

    for keep in keeps:
        keep.start()

    def start_z(j, carry):
        for n in range(count):
            z_copy(n, j).start()
        return carry

    lax.fori_loop(1, halves, start_z, 0)
    for n in range(count):
        keeps[n].wait()
        a_copy(n, 0).start()
        b_copy(n, False, 0).start()

    def pass_z(j, carry):
        for n in range(count):
            z_copy(n, j).wait_recv()
            a_copy(n, j).start()
            b_copy(n, False, j).start()
        return carry

    lax.fori_loop(1, halves, pass_z, 0)

    def pass_a(j, carry):
        for n in range(count):
            a_copy(n, j).wait_recv()
            b_copy(n, True, j).start()
        return carry

    lax.fori_loop(0, halves, pass_a, 0)

    def settle_b(j, carry):
        for n in range(count):
            for flip in (False, True):
                b_copy(n, flip, j).wait_recv()
        return carry

    c_copy(0, 0).start()
    lax.fori_loop(0, halves, settle_b, 0)
    c_copy(0, 1).start()
    for n in range(1, count):
        c_copy(n, 0).start()
        c_copy(n, 1).start()
    for n in range(count):
        c_copy(n, 0).wait()
        c_copy(n, 1).wait()

    def drain(j, carry):
        for n in range(count):
            a_copy(n, j).wait_send()
            b_copy(n, False, j).wait_send()
            b_copy(n, True, j).wait_send()
        return carry

    lax.fori_loop(0, halves, drain, 0)

    def drain_z(j, carry):
        for n in range(count):
            z_copy(n, j).wait_send()
        return carry

    lax.fori_loop(1, halves, drain_z, 0)
    for copy in note_keeps + note_copies:
        copy.wait()


def spread(collective_id, wides, outer, blocks, notes):
    count, halves = len(blocks), wides // 2
    return pl.pallas_call(
        functools.partial(spread_kernel, count, halves, outer),
        out_shape=tuple(
            jax.ShapeDtypeStruct((SECTIONS, wides) + block.shape, block.dtype) for block in blocks
        )
        + tuple(jax.ShapeDtypeStruct((TEAM,) + note.shape, note.dtype) for note in notes),
        in_specs=[ANYWHERE] * (count + 2),
        out_specs=(ANYWHERE,) * (count + 2),
        scratch_shapes=[dma_sems(count), dma_sems(2), dma_sems(2, TEAM), dma_sems(2, TEAM)]
        + [
            dma_sems(count, halves),
            dma_sems(count, halves),
            dma_sems(count, 2 * halves),
            dma_sems(count, 2),
        ]
        * 2,
        compiler_params=settings(collective_id),
        name="spread",
    )(*blocks, *notes)


def collect_kernel(count, halves, *refs):
    partials, sums = refs[:count], refs[count : 2 * count]
    keeps, c_in, b_in, a_in, z_in = (refs[(2 + k) * count : (3 + k) * count] for k in range(5))
    load_sem, c_send, b_send, a_send, z_send, c_recv, b_recv, a_recv, z_recv = refs[7 * count :]
    section, partner, across, wide, wide_at = all_places(halves)
    beside = wide + 1 - 2 * (wide % 2)
    barrier = pltpu.get_barrier_semaphore()
    for peer in ({"section": partner}, {"section": across}, {"wide": beside}):
        pl.semaphore_signal(barrier, inc=1, device_id=peer, device_id_type=MESH_IDS)

    def hello(j, carry):
        peer = {"wide": wide_at(j)}
        pl.semaphore_signal(barrier, inc=1, device_id=peer, device_id_type=MESH_IDS)
        return carry

    lax.fori_loop(1, halves, hello, 0)
    pl.semaphore_wait(barrier, 3 + halves - 1)

    def place(n, home, flip_b, flip_a, j):
        (_, y_a, x_a), (_, y_b, x_b) = steps_of(n == 0, section, partner, across, wide)
        flips_y = (y_a and flip_a) or (y_b and flip_b)
        flips_x = (x_a and flip_a) or (x_b and flip_b)
        return owner_of(home, flips_y, flips_x, wide_at(j))

    def load(n, fb, fa, j):
        owner = place(n, section, fb, fa, j)
        slot = (fb * 2 + fa) * halves + j
        return pltpu.make_async_copy(
            partials[n].at[owner[0], owner[1]], keeps[n].at[slot], load_sem.at[n, slot]
        )

    def c_copy(n, fb, fa, j):
        owner = place(n, partner, fb, fa, j)
        slot = (fb * 2 + fa) * halves + j
        return remote(
            partials[n].at[owner[0], owner[1]],
            c_in[n].at[slot],
            c_send.at[n, slot],
            c_recv.at[n, slot],
            {"section": partner},
        )

    def b_copy(n, fa, j):
        _, (peer, _, _) = steps_of(n == 0, section, partner, across, wide)
        slot = fa * halves + j
        return remote(
            keeps[n].at[2 * halves + slot],
            b_in[n].at[slot],
            b_send.at[n, slot],
            b_recv.at[n, slot],
            peer,
        )

    def a_copy(n, j):
        (peer, _, _), _ = steps_of(n == 0, section, partner, across, wide)
        return remote(
            keeps[n].at[halves + j], a_in[n].at[j], a_send.at[n, j], a_recv.at[n, j], peer
        )

    def z_copy(n, j):
        return remote(
            keeps[n].at[j],
            z_in[n].at[j],
            z_send.at[n, j],
            z_recv.at[n, j],
            {"wide": wide_at(j)},
        )

    def add(n, slot, more):
        keeps[n][slot] = (
            keeps[n][slot].astype(jnp.float32) + more.astype(jnp.float32)
        ).astype(jnp.bfloat16)

    groups = ((1, 1), (1, 0), (0, 1), (0, 0))
    for fb, fa in groups:

        def start_c(j, carry):
            for n in range(count):
                c_copy(n, fb, fa, j).start()
                load(n, fb, fa, j).start()
            return carry

        lax.fori_loop(0, halves, start_c, 0)

    for fb, fa in groups:

        def sum_c(j, carry):
            for n in range(count):
                slot = (fb * 2 + fa) * halves + j
                load(n, fb, fa, j).wait()
                c_copy(n, fb, fa, j).wait_recv()
                add(n, slot, c_in[n][slot])
                if fb:
                    b_copy(n, fa, j).start()
            return carry

        lax.fori_loop(0, halves, sum_c, 0)

    for fa in (1, 0):

        def sum_b(j, carry):
            for n in range(count):
                slot = fa * halves + j
                b_copy(n, fa, j).wait_recv()
                add(n, slot, b_in[n][slot])
                if fa:
                    a_copy(n, j).start()
            return carry

        lax.fori_loop(0, halves, sum_b, 0)

    def sum_a(j, carry):
        for n in range(count):
            a_copy(n, j).wait_recv()
            add(n, j, a_in[n][j])
            z_copy(n, j).start()
        return carry

    lax.fori_loop(1, halves, sum_a, 0)
    for n in range(count):
        a_copy(n, 0).wait_recv()
        sums[n][...] = keeps[n][0].astype(jnp.float32) + a_in[n][0].astype(jnp.float32)

    def sum_z(j, carry):
        for n in range(count):
            z_copy(n, j).wait_recv()
            sums[n][...] += z_in[n][j].astype(jnp.float32)
        return carry

    lax.fori_loop(1, halves, sum_z, 0)

    def drain(j, carry):
        for n in range(count):
            for fb, fa in groups:
                c_copy(n, fb, fa, j).wait_send()
            b_copy(n, 0, j).wait_send()
            b_copy(n, 1, j).wait_send()
            a_copy(n, j).wait_send()
        return carry

    lax.fori_loop(0, halves, drain, 0)

    def drain_z(j, carry):
        for n in range(count):
            z_copy(n, j).wait_send()
        return carry

    lax.fori_loop(1, halves, drain_z, 0)


def collect(collective_id, partials):
    count, halves = len(partials), partials[0].shape[1] // 2
    shapes = [partial.shape[2:] for partial in partials]

    def slots(number):
        return [pltpu.VMEM((number,) + shape, jnp.bfloat16) for shape in shapes]

    return pl.pallas_call(
        functools.partial(collect_kernel, count, halves),
        out_shape=tuple(jax.ShapeDtypeStruct(shape, jnp.float32) for shape in shapes),
        in_specs=[ANYWHERE] * count,
        out_specs=(IN_VMEM,) * count,
        scratch_shapes=slots(4 * halves)
        + slots(4 * halves)
        + slots(2 * halves)
        + slots(halves)
        + slots(halves)
        + [dma_sems(count, 4 * halves)]
        + [
            dma_sems(count, 4 * halves),
            dma_sems(count, 2 * halves),
            dma_sems(count, halves),
            dma_sems(count, halves),
        ]
        * 2,
        compiler_params=settings(collective_id),
        name="collect",
    )(*partials)


TILE = 256


def causal_blocks(count, length):
    row = lax.broadcasted_iota(jnp.int32, (count, count), 0)
    column = lax.broadcasted_iota(jnp.int32, (count, count), 1)
    return (row // length == column // length) & (column <= row)


def turn(values, tables):
    cosines, upper, lower = tables
    parts = []
    for start in range(0, values.shape[1], LANES):
        part = values[:, start : start + LANES]
        ahead = pltpu.roll(part, LANES - HEAD_DIM // 2, 1)
        behind = pltpu.roll(part, HEAD_DIM // 2, 1)
        parts.append(part * cosines + ahead * upper + behind * lower)
    return parts[0] if len(parts) == 1 else jnp.concatenate(parts, axis=1)


def turn_tables(back):
    cosines, sines = rope_tables(LEN, HEAD_DIM)
    sines = -sines if back else sines
    first = jnp.arange(HEAD_DIM) < HEAD_DIM // 2
    upper, lower = jnp.where(first, -sines, 0.0), jnp.where(first, 0.0, sines)
    blank = jnp.zeros_like(cosines)
    pairs = [(cosines, cosines), (upper, upper), (lower, lower)]
    pairs += [(cosines, blank + 1.0), (upper, blank), (lower, blank)]
    tables = jnp.stack([jnp.concatenate(pair, axis=1) for pair in pairs])
    return jnp.tile(tables, (1, HALF // LEN, 1))


def attend(queries, key, mask, scale):
    scores = times_trans(queries, key) * scale
    scores = jnp.where(mask, scores, -1e30)
    peak = jnp.max(scores, axis=1, keepdims=True)
    mass = jnp.exp(scores - peak)
    return mass / jnp.sum(mass, axis=1, keepdims=True)


def local(kernel, operands, outs, scratch, name):
    return pl.pallas_call(
        kernel,
        out_shape=tuple(jax.ShapeDtypeStruct(shape, kind) for shape, kind in outs),
        in_specs=[IN_VMEM] * len(operands),
        out_specs=(IN_VMEM,) * len(outs),
        scratch_shapes=list(scratch),
        compiler_params=pltpu.CompilerParams(vmem_limit_bytes=VMEM_LIMIT),
        name=name,
    )(*operands)


CHUNK = 128


def same_entry(count, slots):
    row = lax.broadcasted_iota(jnp.int32, (count, count), 0)
    column = lax.broadcasted_iota(jnp.int32, (count, count), 1)
    return row // slots == column // slots


def gelu(values):
    return 0.5 * values * (1.0 + lax.erf(values * inv_root_two))


def hyper_kernel(
    slots,
    pieces,
    first,
    second,
    third,
    vectors,
    table,
    heads_out,
    mixed_out,
    middle_out,
    expanded_out,
    pooled_out,
    entered,
    outcome,
):
    width = pieces.shape[1]
    count, feed = pieces.shape[0], third.shape[0]
    head = width // HYPER_HEAD_COUNT
    flat = pieces[...].astype(jnp.float32)
    normed, _ = center_norm(flat)
    entered[...] = (normed * vectors[0:1] + vectors[1:2]).astype(jnp.bfloat16)

    @pl.loop(0, 3 * width // TILE)
    def _(n):
        columns = pl.ds(pl.multiple_of(n * TILE, TILE), TILE)
        heads_out[:, columns] = matmul(entered[...], first[:, columns]).astype(jnp.bfloat16)

    mask = same_entry(CHUNK, slots)

    @pl.loop(0, count // CHUNK)
    def _(n):
        rows = pl.ds(pl.multiple_of(n * CHUNK, CHUNK), CHUNK)
        block = heads_out[rows, :]
        mixed = []
        for start in range(0, width, head):
            query, key, value = (
                block[:, part * width + start : part * width + start + head] for part in range(3)
            )
            weights = attend(query, key, mask, head ** (-0.5))
            mixed.append(matmul(weights.astype(jnp.bfloat16), value))
        mixed_out[rows, :] = jnp.concatenate(mixed, axis=1).astype(jnp.bfloat16)

    for start in range(0, width, TILE):
        columns = pl.ds(start, TILE)
        middle_out[:, columns] = pieces[:, columns].astype(jnp.float32) + matmul(
            mixed_out[...], first[:, pl.ds(3 * width + start, TILE)]
        )
    normed, _ = center_norm(middle_out[...])
    entered[...] = (normed * vectors[2:3] + vectors[3:4]).astype(jnp.bfloat16)
    outcome[...] = middle_out[...]

    @pl.loop(0, feed // TILE)
    def _(n):
        start = pl.multiple_of(n * TILE, TILE)
        columns = pl.ds(pl.multiple_of(4 * width + start, TILE), TILE)
        expanded = matmul(entered[...], first[:, columns])
        expanded_out[:, pl.ds(start, TILE)] = expanded
        outcome[...] += matmul(gelu(expanded).astype(jnp.bfloat16), third[pl.ds(start, TILE), :])

    pooled = jnp.mean(outcome[...].reshape(count // slots, slots, width), axis=1)
    pooled_out[...] = pooled.astype(jnp.bfloat16)

    @pl.loop(0, table.shape[1] // TILE)
    def _(n):
        columns = pl.ds(pl.multiple_of(n * TILE, TILE), TILE)
        table[:, columns] = matmul(pooled_out[...], second[:, columns]).astype(jnp.bfloat16)


def hyper_forward(pieces, slots, params):
    count, width = pieces.shape
    first, second, third, vectors = params
    feed = third.shape[0]
    depth = second.shape[1] - LANES
    entries = count // slots
    table, *stored = local(
        functools.partial(hyper_kernel, slots),
        (pieces, *params),
        [
            ((entries, depth), jnp.bfloat16),
            ((count, 3 * width), jnp.bfloat16),
            ((count, width), jnp.bfloat16),
            ((count, width), jnp.float32),
            ((count, feed), jnp.float32),
            ((entries, width), jnp.bfloat16),
        ],
        [pltpu.VMEM((count, width), jnp.bfloat16), pltpu.VMEM((count, width), jnp.float32)],
        "hyper",
    )
    return table, stored


def hyper_back_kernel(
    slots,
    table_grad,
    pieces,
    first,
    second,
    third,
    vectors,
    heads,
    mixed,
    middle,
    expanded,
    pooled,
    first_grad,
    second_grad,
    third_grad,
    entered,
    outcome_low,
    feed_grad,
    heads_grad,
    mixed_grad,
):
    width = pieces.shape[1]
    count, feed = pieces.shape[0], third.shape[0]
    depth = table_grad.shape[1]
    head = width // HYPER_HEAD_COUNT
    scale = head ** (-0.5)
    grad_low = table_grad[...].astype(jnp.bfloat16)
    pooled_turned = jnp.transpose(pooled[...].astype(jnp.float32)).astype(jnp.bfloat16)

    for start in range(0, depth, TILE):
        columns = pl.ds(start, TILE)
        second_grad[:, columns] = matmul(
            pooled_turned, grad_low[:, start : start + TILE]
        ).astype(jnp.bfloat16)
    pooled_grad = times_trans(grad_low, second[:, pl.ds(0, depth)]) / slots
    outcome_grad = jnp.broadcast_to(pooled_grad[:, None, :], (count // slots, slots, width))
    outcome_grad = outcome_grad.reshape(count, width)
    outcome_low[...] = outcome_grad.astype(jnp.bfloat16)
    normed, inverse = center_norm(middle[...])
    entered[...] = jnp.transpose(normed * vectors[2:3] + vectors[3:4]).astype(jnp.bfloat16)
    feed_grad[...] = jnp.zeros_like(feed_grad)

    @pl.loop(0, feed // TILE)
    def _(n):
        start = pl.multiple_of(n * TILE, TILE)
        tile = pl.ds(start, TILE)
        columns = pl.ds(pl.multiple_of(4 * width + start, TILE), TILE)
        values = expanded[:, tile]
        erf = 0.5 * (1.0 + lax.erf(values * inv_root_two))
        active = (values * erf).astype(jnp.bfloat16)
        third_grad[tile, :] = trans_times(active, outcome_low[...]).astype(jnp.bfloat16)
        active_grad = times_trans(outcome_low[...], third[tile, :])
        slope = erf + values * jnp.exp(-0.5 * values * values) * inv_root_tau
        low = (active_grad * slope).astype(jnp.bfloat16)
        first_grad[:, columns] = matmul(entered[...], low).astype(jnp.bfloat16)
        feed_grad[...] += times_trans(low, first[:, columns])

    grad = feed_grad[...]
    scale_two = jnp.sum(grad * normed, axis=0, keepdims=True)
    shift_two = jnp.sum(grad, axis=0, keepdims=True)
    middle_grad = outcome_grad + center_back(normed, inverse, grad * vectors[2:3])
    middle_low = middle_grad.astype(jnp.bfloat16)
    out_columns = pl.ds(3 * width, width)
    first_grad[:, out_columns] = trans_times(mixed[...], middle_low).astype(jnp.bfloat16)
    mixed_grad[...] = times_trans(middle_low, first[:, out_columns]).astype(jnp.bfloat16)
    mask = same_entry(CHUNK, slots)

    @pl.loop(0, count // CHUNK)
    def _(n):
        rows = pl.ds(pl.multiple_of(n * CHUNK, CHUNK), CHUNK)
        block = heads[rows, :]
        outer_block = mixed_grad[rows, :]
        grads = [[], [], []]
        for start in range(0, width, head):
            query, key, value = (
                block[:, part * width + start : part * width + start + head] for part in range(3)
            )
            outer = outer_block[:, start : start + head]
            weights = attend(query, key, mask, scale)
            weight_grad = times_trans(outer, value)
            score_grad = weights * (
                weight_grad - jnp.sum(weights * weight_grad, axis=1, keepdims=True)
            )
            score_grad = score_grad.astype(jnp.bfloat16)
            grads[0].append(matmul(score_grad, key) * scale)
            grads[1].append(trans_times(score_grad, query) * scale)
            grads[2].append(trans_times(weights.astype(jnp.bfloat16), outer))
        for part in range(3):
            heads_grad[rows, pl.ds(part * width, width)] = jnp.concatenate(
                grads[part], axis=1
            ).astype(jnp.bfloat16)

    normed, _ = center_norm(pieces[...].astype(jnp.float32))
    entered[...] = jnp.transpose(normed * vectors[0:1] + vectors[1:2]).astype(jnp.bfloat16)
    feed_grad[...] = jnp.zeros_like(feed_grad)

    @pl.loop(0, 3 * width // TILE)
    def _(n):
        columns = pl.ds(pl.multiple_of(n * TILE, TILE), TILE)
        low = heads_grad[:, columns]
        first_grad[:, columns] = matmul(entered[...], low).astype(jnp.bfloat16)
        feed_grad[...] += times_trans(low, first[:, columns])

    grad = feed_grad[...]
    scale_one = jnp.sum(grad * normed, axis=0, keepdims=True)
    shift_one = jnp.sum(grad, axis=0, keepdims=True)
    row = lax.broadcasted_iota(jnp.int32, (LANES, width), 0)
    summed = jnp.zeros((LANES, width), jnp.float32)
    for n, item in enumerate((scale_one, shift_one, scale_two, shift_two)):
        summed = jnp.where(row == n, item, summed)
    second_grad[:, pl.ds(depth, LANES)] = jnp.transpose(summed).astype(jnp.bfloat16)


def hyper_backward(pieces, slots, params, stored, table_grad):
    count, width = pieces.shape
    first, second, third, _ = params
    return local(
        functools.partial(hyper_back_kernel, slots),
        (table_grad, pieces, *params, *stored),
        [(item.shape, jnp.bfloat16) for item in (first, second, third)],
        [
            pltpu.VMEM((width, count), jnp.bfloat16),
            pltpu.VMEM((count, width), jnp.bfloat16),
            pltpu.VMEM((count, width), jnp.float32),
            pltpu.VMEM((count, 3 * width), jnp.bfloat16),
            pltpu.VMEM((count, width), jnp.bfloat16),
        ],
        "hyper_back",
    )


def column_plan(q_columns, kv_columns, ff_columns):
    share = ff_columns // TEAM
    edge = share // LANES * LANES
    tail = share - edge
    heads = kv_columns // HEAD_DIM
    q_share = q_columns // TEAM
    plan = []
    for rank in range(TEAM):
        kv = rank * heads // TEAM * HEAD_DIM
        widths = [
            (0, rank * q_share, q_share),
            (1, kv, HEAD_DIM),
            (2, kv, HEAD_DIM),
            (3, rank * share, edge),
            (4, rank * share, edge),
            (3, rank * share + edge, tail),
            (4, rank * share + edge, tail),
        ]
        moves, start = [], 0
        for item, source, size in widths:
            moves.append((item, source, start, size))
            start += size
        plan.append(moves)
    return plan, start


def pack_kernel(plan, rows, *refs):
    sources, targets = refs[:5], refs[5:7]
    blocks, sem = refs[7:12], refs[12]
    section = lax.axis_index("section")
    mine = pl.ds(pl.multiple_of(section * rows, rows), rows)
    copies = [
        [
            pltpu.make_async_copy(source.at[layer, mine], block.at[layer], sem.at[layer, n])
            for n, (source, block) in enumerate(zip(sources, blocks))
        ]
        for layer in range(2)
    ]
    for layer in range(2):
        for copy in copies[layer]:
            copy.start()
    for layer in range(2):
        for copy in copies[layer]:
            copy.wait()
        for rank, moves in enumerate(plan):
            parts = [
                blocks[item][layer, :, source : source + size] for item, source, _, size in moves
            ]
            heads = jnp.concatenate(parts[1:3], axis=1)
            ends = jnp.concatenate(parts[5:7], axis=1)
            for part, start in zip(
                (parts[0], heads, parts[3], parts[4], ends),
                (moves[0][2], moves[1][2], moves[3][2], moves[4][2], moves[5][2]),
            ):
                if part.shape[1]:
                    targets[layer][rank, :, start : start + part.shape[1]] = part


def pack(weights):
    rows = weights[0].shape[1] // SECTIONS
    plan, width = column_plan(weights[0].shape[2], weights[1].shape[2], weights[3].shape[2])
    if rows % 16:
        section = lax.axis_index("section")
        mine = [lax.dynamic_slice_in_dim(item, section * rows, rows, 1) for item in weights]
        return tuple(
            jnp.stack(
                [
                    jnp.concatenate(
                        [mine[item][layer, :, at : at + size] for item, at, _, size in moves], axis=1
                    )
                    for moves in plan
                ]
            )
            for layer in range(2)
        )
    return pl.pallas_call(
        functools.partial(pack_kernel, plan, rows),
        out_shape=(jax.ShapeDtypeStruct((TEAM, rows, width), jnp.bfloat16),) * 2,
        in_specs=[ANYWHERE] * 5,
        out_specs=(IN_VMEM,) * 2,
        scratch_shapes=[pltpu.VMEM((2, rows, item.shape[2]), jnp.bfloat16) for item in weights]
        + [dma_sems(2, 5)],
        compiler_params=pltpu.CompilerParams(vmem_limit_bytes=VMEM_LIMIT),
        name="pack",
    )(*weights)


def run(main, beside, most):
    for count, _ in enumerate(main):
        if beside is not None and count < most:
            next(beside, None)


def finish(*steps):
    steps = list(steps)
    while steps:
        steps = [step for step in steps if next(step, steps) is not steps]


class Decoder:
    def __init__(self, shape, refs):
        self.outer, self.tokens, self.share, self.q_width, self.depth = shape
        for name, ref in refs.items():
            setattr(self, name, ref)
        self.section, self.partner, self.across = section_places()
        self.beyond = (self.partner + 2) % SECTIONS
        wide = lax.axis_index("wide")
        self.rank, self.team = wide // self.outer, wide % self.outer
        self.line, self.column = self.rank // 2, self.rank % 2
        self.mine = self.rank
        self.beside = self.member(self.line, 1 - self.column)
        self.edge = self.share // LANES * LANES
        self.tail = self.share - self.edge

    def at(self, line, column):
        return (line % LINES) * 2 + column

    def member(self, line, column):
        return {"wide": self.at(line, column) * self.outer + self.team}

    def ranked(self, step):
        return {"wide": (self.rank + step) % TEAM * self.outer + self.team}

    def greet(self):
        sections = [{"section": place} for place in (self.partner, self.across, self.beyond)]
        greet(sections + [self.ranked(k) for k in range(1, TEAM)])

    def weight_copies(self):
        heads, feed = pl.ds(0, self.q_width + LANES), pl.ds(self.q_width + LANES, 2 * self.share)
        places = (self.section, self.across, self.partner, self.beyond)
        self.head_loads = [[], []]
        self.feed_loads = [[], []]
        for n, (piece, place) in enumerate(zip(self.pieces, places)):
            self.head_loads[0].append(
                pltpu.make_async_copy(
                    piece.at[:, :, heads], self.head_weight.at[0, :, place], self.load_sem.at[0, n]
                )
            )
            self.feed_loads[0].append(
                pltpu.make_async_copy(
                    piece.at[:, :, feed], self.feed_weight.at[0, :, place], self.load_sem.at[1, n]
                )
            )
        self.head_loads[1].append(
            pltpu.make_async_copy(
                self.own_two.at[:, :, heads],
                self.head_weight.at[1, :, self.section],
                self.load_sem.at[2, 0],
            )
        )
        self.feed_loads[1].append(
            pltpu.make_async_copy(
                self.own_two.at[:, :, feed],
                self.feed_weight.at[1, :, self.section],
                self.load_sem.at[3, 0],
            )
        )
        for n, place in enumerate((self.across, self.beyond, self.partner)):
            peer = {"section": place}
            self.head_loads[1].append(
                remote(
                    self.own_two.at[:, :, heads],
                    self.head_weight.at[1, :, self.section],
                    self.share_send.at[0, n],
                    self.share_recv.at[0, n],
                    peer,
                )
            )
            self.feed_loads[1].append(
                remote(
                    self.own_two.at[:, :, feed],
                    self.feed_weight.at[1, :, self.section],
                    self.share_send.at[1, n],
                    self.share_recv.at[1, n],
                    peer,
                )
            )
        for layer in range(2):
            self.head_loads[layer].append(
                pltpu.make_async_copy(
                    self.out_source.at[layer], self.out_weight.at[layer], self.load_sem.at[4, layer]
                )
            )
            self.feed_loads[layer].append(
                pltpu.make_async_copy(
                    self.down_source.at[layer],
                    self.down_weight.at[layer],
                    self.load_sem.at[5, layer],
                )
            )
        for layer in range(2):
            for copy in self.head_loads[layer] + self.feed_loads[layer]:
                copy.start()

    def send(self, half):
        self.sides = getattr(self, "sides", {})
        self.sides[half] = [
            remote(
                self.partial.at[half, self.at(self.line + j, 1 - self.column)],
                self.side.at[half, j],
                self.side_send.at[half, j],
                self.side_recv.at[half, j],
                self.beside,
            )
            for j in range(LINES)
        ]
        for j in (2, 1, 3, 0):
            self.sides[half][j].start()

    def reduce(self, half, close):
        sides = self.sides[half]
        fars = [None] + [
            remote(
                self.pair.at[half, j],
                self.far.at[half, j],
                self.far_send.at[half, j],
                self.far_recv.at[half, j],
                self.member(self.line + j, self.column),
            )
            for j in range(1, LINES)
        ]

        def pair_sum(j):
            sides[j].wait_recv()
            own = self.partial[half, self.at(self.line + j, self.column)]
            return own.astype(jnp.float32) + self.side[half, j].astype(jnp.float32)

        for j in (2, 1, 3):
            self.pair[half, j] = pair_sum(j).astype(jnp.bfloat16)
            fars[j].start()
            yield
        total = pair_sum(0)
        for j in (1, 3, 2):
            fars[j].wait_recv()
            total = total + self.far[half, j].astype(jnp.float32)
        self.gathered[half, self.mine] = close(half, total)
        for j in range(LINES):
            sides[j].wait_send()
            if j:
                fars[j].wait_send()
        pushes = [None] + [
            remote(
                self.gathered.at[half, self.mine],
                self.gathered.at[half, self.mine],
                self.out_send.at[half, j],
                self.out_recv.at[half, j],
                self.member(self.line + j, self.column),
            )
            for j in range(1, LINES)
        ]
        overs = []
        for j in range(LINES):
            block = self.gathered.at[half, self.at(self.line - j, self.column)]
            overs.append(
                remote(
                    block, block, self.over_send.at[half, j], self.over_recv.at[half, j], self.beside
                )
            )
        for j in (2, 1, 3):
            pushes[j].start()
        overs[0].start()
        self.moving[half] = (pushes, overs)
        yield

    def gather(self, half):
        pushes, overs = self.moving[half]
        for j in (1, 3, 2):
            pushes[j].wait_recv()
            overs[j].start()
            yield
        for j in range(LINES):
            overs[j].wait()
            if j:
                pushes[j].wait_send()
        yield

    def rows(self, half):
        return self.gathered[half].reshape(HALF, self.depth)

    def store_partial(self, half, columns, values):
        self.partial[half, :, :, columns] = values.astype(jnp.bfloat16).reshape(
            TEAM, EACH, values.shape[1]
        )

    def tiles(self, count, parts):
        bounds = [count * n // parts for n in range(parts + 1)]
        return [(low, high) for low, high in zip(bounds[:-1], bounds[1:]) if high > low]

    def inject(self, half):
        hits = self.own_rows[...] == self.ids[half : half + 1, :]
        hits = jnp.where(hits, 1.0, 0.0).astype(jnp.bfloat16)

        @pl.loop(0, self.depth // TILE)
        def _(n):
            columns = pl.ds(pl.multiple_of(n * TILE, TILE), TILE)
            self.store_partial(half, columns, trans_times(hits, self.table[:, columns]))

        yield

    def attention(self, layer, half):
        if half == FIRST:
            for copy in self.head_loads[layer]:
                copy.wait()
        own = pl.ds(half * HALF, HALF)
        width = self.q_width + LANES
        projected = matmul(self.rows(half), self.head_weight[layer].reshape(self.depth, width))
        yield
        queries = turn(projected[:, : self.q_width], [self.tables[n] for n in range(3)])
        pairs = turn(projected[:, self.q_width :], [self.tables[n] for n in range(3, 6)])
        queries, pairs = queries.astype(jnp.bfloat16), pairs.astype(jnp.bfloat16)
        self.queries[layer, own, :] = queries
        self.pairs[layer, own, :] = pairs
        key, value = pairs[:, :HEAD_DIM], pairs[:, HEAD_DIM:]
        mask = causal_blocks(HALF, LEN)
        mixed = []
        for start in range(0, self.q_width, HEAD_DIM):
            weights = attend(queries[:, start : start + HEAD_DIM], key, mask, HEAD_DIM ** (-0.5))
            mixed.append(matmul(weights.astype(jnp.bfloat16), value))
        mixed = jnp.concatenate(mixed, axis=1).astype(jnp.bfloat16)
        yield

        @pl.loop(0, self.depth // TILE)
        def _(n):
            columns = pl.ds(pl.multiple_of(n * TILE, TILE), TILE)
            self.store_partial(half, columns, matmul(mixed, self.out_weight[layer, :, columns]))

        yield

    def feed(self, layer, half):
        if half == FIRST:
            for copy in self.feed_loads[layer]:
                copy.wait()
        own = pl.ds(half * HALF, HALF)
        edge, tail = self.edge, self.tail
        for low, high in self.tiles(2 * self.share // LANES, 3):

            @pl.loop(low, high)
            def _(n):
                columns = pl.ds(pl.multiple_of(n * LANES, LANES), LANES)
                block = self.feed_weight[layer, :, :, :, columns].reshape(self.depth, LANES)
                self.kept[layer, own, columns] = matmul(self.rows(half), block)

            yield

        def activate(gate, up):
            return (jax.nn.silu(gate) * up).astype(jnp.bfloat16)

        self.active[:, :edge] = activate(
            self.kept[layer, own, :edge], self.kept[layer, own, edge : 2 * edge]
        )
        if tail:
            last = self.kept[layer, own, 2 * edge :]
            self.active[:, edge:] = activate(last[:, :tail], last[:, tail:])
        for low, high in self.tiles(self.depth // TILE, 2):

            @pl.loop(low, high)
            def _(n):
                columns = pl.ds(pl.multiple_of(n * TILE, TILE), TILE)
                block = self.down_weight[layer, :, columns]
                self.store_partial(half, columns, matmul(self.active[...], block))

            yield

    def head(self, half):
        keep = pltpu.make_async_copy(
            self.gathered.at[half], self.normed_out.at[half], self.keep_sem.at[half]
        )
        keep.start()
        logits = times_trans(self.table[...], self.rows(half))
        peak = jnp.max(logits, axis=0, keepdims=True)
        mass = jnp.sum(jnp.exp(logits - peak), axis=0, keepdims=True)
        wanted = self.own_rows[...] == self.wanted[half : half + 1, :]
        chosen = jnp.sum(jnp.where(wanted, logits, 0.0), axis=0, keepdims=True)
        row = lax.broadcasted_iota(jnp.int32, (8, HALF), 0)
        stats = jnp.where(row == 0, peak, jnp.where(row == 1, mass, chosen))
        self.stats[half, self.rank] = stats
        copies = [
            remote(
                self.stats.at[half, self.rank],
                self.stats.at[half, self.rank],
                self.stats_send.at[half, k],
                self.stats_recv.at[half, k],
                self.ranked(k),
            )
            for k in range(1, TEAM)
        ]
        for copy in copies:
            copy.start()
        yield
        yield
        for copy in copies:
            copy.wait()
        peaks = [self.stats[half, n, 0:1, :] for n in range(TEAM)]
        top = functools.reduce(jnp.maximum, peaks)
        mass = sum(self.stats[half, n, 1:2, :] * jnp.exp(peaks[n] - top) for n in range(TEAM))
        chosen = sum(self.stats[half, n, 2:3, :] for n in range(TEAM))
        log_norm = top + jnp.log(mass)
        loss = jnp.sum(log_norm - chosen, axis=1, keepdims=True) / self.tokens
        loss = jnp.broadcast_to(loss, self.loss_out.shape)
        if half == FIRST:
            self.loss_out[...] = loss
        else:
            self.loss_out[...] += loss
        grad = (jnp.exp(logits - log_norm) - jnp.where(wanted, 1.0, 0.0)) / self.tokens
        grad = grad.astype(jnp.bfloat16)
        self.logit_grad[:, pl.ds(half * HALF, HALF)] = grad
        yield

        @pl.loop(0, self.depth // TILE)
        def _(n):
            columns = pl.ds(pl.multiple_of(n * TILE, TILE), TILE)
            self.store_partial(half, columns, trans_times(grad, self.table[:, columns]))

        keep.wait()
        yield

    def feed_back(self, layer, half):
        own = pl.ds(half * HALF, HALF)
        edge, tail = self.edge, self.tail
        active_grad = times_trans(self.rows(half), self.down_weight[layer])
        yield

        def back(outer, gate, up):
            sigmoid = jax.nn.sigmoid(gate)
            gate_grad = outer * up * sigmoid * (1.0 + gate * (1.0 - sigmoid))
            return gate_grad.astype(jnp.bfloat16), (outer * gate * sigmoid).astype(jnp.bfloat16)

        gate_grad, up_grad = back(
            active_grad[:, :edge],
            self.kept[layer, own, :edge],
            self.kept[layer, own, edge : 2 * edge],
        )
        self.both[:, :edge] = gate_grad
        self.both[:, edge : 2 * edge] = up_grad
        if tail:
            last = self.kept[layer, own, 2 * edge :]
            gate_grad, up_grad = back(active_grad[:, edge:], last[:, :tail], last[:, tail:])
            self.both[:, 2 * edge :] = jnp.concatenate([gate_grad, up_grad], axis=1)
        yield
        tiles = self.depth // TILE
        each = self.feed_weight.shape[1] // tiles
        for low, high in self.tiles(tiles, 3):

            @pl.loop(low, high)
            def _(n):
                columns = pl.ds(pl.multiple_of(n * TILE, TILE), TILE)
                block = self.feed_weight[layer, pl.ds(n * each, each)].reshape(TILE, -1)
                self.store_partial(half, columns, times_trans(self.both[...], block))

            yield

    def attention_back(self, layer, half):
        own = pl.ds(half * HALF, HALF)
        scale = HEAD_DIM ** (-0.5)
        mixed_grad = times_trans(self.rows(half), self.out_weight[layer]).astype(jnp.bfloat16)
        yield
        queries, pairs = self.queries[layer, own, :], self.pairs[layer, own, :]
        key, value = pairs[:, :HEAD_DIM], pairs[:, HEAD_DIM:]
        mask = causal_blocks(HALF, LEN)
        query_grads, key_grad, value_grad = [], 0.0, 0.0
        for start in range(0, self.q_width, HEAD_DIM):
            query = queries[:, start : start + HEAD_DIM]
            outer = mixed_grad[:, start : start + HEAD_DIM]
            weights = attend(query, key, mask, scale)
            weight_grad = times_trans(outer, value)
            score_grad = weights * (
                weight_grad - jnp.sum(weights * weight_grad, axis=1, keepdims=True)
            )
            score_grad = score_grad.astype(jnp.bfloat16)
            query_grads.append(matmul(score_grad, key) * scale)
            key_grad = key_grad + trans_times(score_grad, query) * scale
            value_grad = value_grad + trans_times(weights.astype(jnp.bfloat16), outer)
        query_grad = jnp.concatenate(query_grads, axis=1)
        query_grad = turn(query_grad, [self.back_tables[n] for n in range(3)])
        pair_grad = jnp.concatenate([key_grad, value_grad], axis=1)
        pair_grad = turn(pair_grad, [self.back_tables[n] for n in range(3, 6)])
        both = jnp.concatenate([query_grad, pair_grad], axis=1).astype(jnp.bfloat16)
        yield
        tiles = self.depth // TILE
        each = self.head_weight.shape[1] // tiles

        @pl.loop(0, tiles)
        def _(n):
            columns = pl.ds(pl.multiple_of(n * TILE, TILE), TILE)
            block = self.head_weight[layer, pl.ds(n * each, each)].reshape(TILE, -1)
            self.store_partial(half, columns, times_trans(both, block))

        yield

    def normed(self, values, gain):
        return (values * root_inverse(values) * gain[...]).astype(jnp.bfloat16)

    def close_inject(self, half, total):
        hidden = total.astype(jnp.bfloat16)
        self.hidden[0, half] = hidden
        return self.normed(hidden.astype(jnp.float32), self.gains[0])

    def close_attention(self, layer):
        def close(half, total):
            middle = self.hidden[layer, half].astype(jnp.float32) + total
            self.middle[layer, half] = middle
            return self.normed(middle, self.gains[2 + layer])

        return close

    def close_feed(self, layer):
        def close(half, total):
            hidden = (self.middle[layer, half] + total).astype(jnp.bfloat16)
            self.hidden[layer + 1, half] = hidden
            gain = self.gains[4] if layer else self.gains[1]
            return self.normed(hidden.astype(jnp.float32), gain)

        return close

    def close_head(self, half, total):
        hidden = self.hidden[2, half].astype(jnp.float32)
        grad = reciprocal_root_backward(hidden, root_inverse(hidden), self.gains[4][...], total)
        grad = grad.astype(jnp.bfloat16)
        self.grad[half] = grad.astype(jnp.float32)
        return grad

    def close_feed_back(self, layer):
        def close(half, total):
            middle = self.middle[layer, half]
            grad = self.grad[half] + reciprocal_root_backward(
                middle, root_inverse(middle), self.gains[2 + layer][...], total
            )
            self.grad[half] = grad
            return grad.astype(jnp.bfloat16)

        return close

    def close_attention_back(self, layer):
        def close(half, total):
            hidden = self.hidden[layer, half].astype(jnp.float32)
            grad = self.grad[half] + reciprocal_root_backward(
                hidden, root_inverse(hidden), self.gains[layer][...], total
            )
            grad = grad.astype(jnp.bfloat16)
            self.grad[half] = grad.astype(jnp.float32)
            return grad

        return close


def decode_kernel(shape, names, *refs):
    refs = dict(zip(names, refs))
    refs["pieces"] = [refs.pop(name) for name in ("own_one", "y_one", "core_one", "beyond_one")]
    refs["gains"] = [refs["gain_rows"].at[pl.ds(n, 1)] for n in range(5)]
    this = Decoder(shape, refs)
    this.greet()
    this.moving = {}
    this.weight_copies()
    phases = [(this.inject, this.close_inject)]
    for layer in range(2):
        phases.append((functools.partial(this.attention, layer), this.close_attention(layer)))
        phases.append((functools.partial(this.feed, layer), this.close_feed(layer)))
    phases.append((this.head, this.close_head))
    for layer in (1, 0):
        phases.append((functools.partial(this.feed_back, layer), this.close_feed_back(layer)))
        phases.append(
            (functools.partial(this.attention_back, layer), this.close_attention_back(layer))
        )
    reduces, gathers = {}, {}

    def settle(half, *beside):
        if half in reduces:
            finish(*beside, reduces.pop(half))
            gathers[half] = this.gather(half)
        else:
            finish(*beside)

    for work, close in phases:
        for half in (FIRST, SECOND):
            other = 1 - half
            settle(other, gathers.pop(half, iter(())))
            run(work(half), gathers.get(other), LINES - 1)
            this.send(half)
            reduces[half] = this.reduce(half, close)
    settle(SECOND, gathers.pop(FIRST))
    finish(gathers.pop(SECOND))
    outs = [
        pltpu.make_async_copy(
            this.gathered.at[half], this.grad_out.at[half], this.keep_sem.at[half]
        )
        for half in (FIRST, SECOND)
    ]
    for copy in outs:
        copy.start()
    for copy in outs:
        copy.wait()


def decode(outer, collective_id, tokens, weights, out_source, down_source, gains, tables, table, own_rows, ids, wanted):
    q_width, depth = out_source.shape[1:]
    share = down_source.shape[1]
    groups, quarter = weights[0].shape[:2]
    entries = table.shape[0]
    low, full = jnp.bfloat16, jnp.float32
    block = (2, TEAM, EACH, depth)
    slots = pltpu.VMEM((2, LINES, EACH, depth), low)
    inputs = dict(
        own_rows=own_rows,
        ids=ids,
        wanted=wanted,
        table=table,
        gain_rows=gains,
        tables=tables[0],
        back_tables=tables[1],
    )
    far_inputs = dict(
        zip(("own_one", "y_one", "core_one", "beyond_one", "own_two"), weights),
        out_source=out_source,
        down_source=down_source,
    )
    outputs = dict(
        normed_out=(jax.ShapeDtypeStruct(block, low), ANYWHERE),
        grad_out=(jax.ShapeDtypeStruct(block, low), ANYWHERE),
        logit_grad=(jax.ShapeDtypeStruct((entries, ROWS), low), IN_VMEM),
        loss_out=(jax.ShapeDtypeStruct((8, LANES), full), IN_VMEM),
    )
    scratch = dict(
        head_weight=pltpu.VMEM((2, groups, SECTIONS, quarter, q_width + LANES), low),
        feed_weight=pltpu.VMEM((2, groups, SECTIONS, quarter, 2 * share), low),
        out_weight=pltpu.VMEM((2, q_width, depth), low),
        down_weight=pltpu.VMEM((2, share, depth), low),
        gathered=pltpu.VMEM(block, low),
        partial=pltpu.VMEM(block, low),
        side=slots,
        pair=slots,
        far=slots,
        kept=pltpu.VMEM((2, ROWS, 2 * share), full),
        queries=pltpu.VMEM((2, ROWS, q_width), low),
        pairs=pltpu.VMEM((2, ROWS, LANES), low),
        active=pltpu.VMEM((HALF, share), low),
        both=pltpu.VMEM((HALF, 2 * share), low),
        hidden=pltpu.VMEM((3, 2, EACH, depth), low),
        middle=pltpu.VMEM((2, 2, EACH, depth), full),
        grad=pltpu.VMEM((2, EACH, depth), full),
        stats=pltpu.VMEM((2, TEAM, 8, HALF), full),
        load_sem=dma_sems(6, 4),
        share_send=dma_sems(2, 3),
        share_recv=dma_sems(2, 3),
        stats_send=dma_sems(2, TEAM),
        stats_recv=dma_sems(2, TEAM),
        keep_sem=dma_sems(2),
    )
    for name in ("side", "far", "out", "over"):
        scratch[name + "_send"] = dma_sems(2, LINES)
        scratch[name + "_recv"] = dma_sems(2, LINES)
    names = (*inputs, *far_inputs, *outputs, *scratch)
    return pl.pallas_call(
        functools.partial(decode_kernel, (outer, tokens, share, q_width, depth), names),
        out_shape=tuple(shape for shape, _ in outputs.values()),
        in_specs=[IN_VMEM] * len(inputs) + [ANYWHERE] * len(far_inputs),
        out_specs=tuple(spec for _, spec in outputs.values()),
        scratch_shapes=list(scratch.values()),
        compiler_params=settings(collective_id),
        name="decode",
    )(*inputs.values(), *far_inputs.values())


def team_groups(wides, outer):
    return [[rank * outer + team for team in range(outer)] for rank in range(wides // outer)]


SWAP_Y = [(source, (source + 2) % SECTIONS) for source in range(SECTIONS)]
SWAP_CORE = [(source, source + 1 - 2 * (source % 2)) for source in range(SECTIONS)]


def together(*items):
    return lax.optimization_barrier(items)


def all_teams(pieces, outer, groups):
    if outer == 1:
        return pieces
    pieces = [
        lax.all_gather(piece, "wide", axis=1, axis_index_groups=groups) for piece in pieces
    ]
    return [piece.reshape((-1,) + piece.shape[2:]) for piece in pieces]


def shards(
    token_ids,
    targets,
    slot_ids,
    group_ids,
    group_offsets,
    piece_table,
    prenorm_gain,
    prenorm_bias,
    query_map,
    key_map,
    value_map,
    output_map,
    midnorm_gain,
    midnorm_bias,
    expand_map,
    reduce_map,
    embed_map,
    attention_gain,
    query_weight,
    key_weight,
    value_weight,
    output_weight,
    feed_gain,
    gate_weight,
    up_weight,
    down_weight,
    final_gain,
):
    wides = lax.axis_size("wide")
    outer = wides // TEAM
    groups = team_groups(wides, outer)
    section_index = lax.axis_index("section")
    wide_index = lax.axis_index("wide")
    rank = wide_index // outer
    hyper_width, hyper_feed = piece_table.shape[1], expand_map.shape[1]
    model_width = embed_map.shape[1]
    total_tokens = wides * MB * LEN

    rank_groups = [[rank * outer + team for rank in range(TEAM)] for team in range(outer)]

    def to_ranks(block):
        return lax.all_to_all(
            block, "wide", 0, 0, axis_index_groups=rank_groups if outer > 1 else None, tiled=True
        )

    blocks = pack((query_weight, key_weight, value_weight, gate_weight, up_weight))
    own_one = to_ranks(blocks[0])

    vectors = jnp.stack([prenorm_gain, prenorm_bias, midnorm_gain, midnorm_bias], axis=1)
    vectors = jnp.pad(vectors, ((0, 0), (0, LANES - 4)))
    first = jnp.concatenate([query_map, key_map, value_map, output_map, expand_map], axis=1)
    second = jnp.concatenate([embed_map, vectors], axis=1)
    gains = jnp.concatenate([attention_gain, feed_gain], axis=0)
    gains = jnp.pad(gains, ((0, 16 - gains.shape[0]), (0, 0)))
    notes = jnp.concatenate([token_ids.reshape(1, -1), targets.reshape(1, -1)], axis=0)
    notes = jnp.pad(notes, ((0, 6), (0, 0)))
    first, second, third, gains, notes = spread(
        1,
        wides,
        outer,
        (first.astype(jnp.bfloat16), second.astype(jnp.bfloat16), reduce_map.astype(jnp.bfloat16)),
        (gains, notes),
    )
    first, own_one, block = together(first, own_one, blocks[1])
    own_two = to_ranks(block)
    y_one = lax.ppermute(own_one, "section", SWAP_Y)
    core_one = lax.ppermute(own_one, "section", SWAP_CORE)
    first = first.reshape(hyper_width, -1)
    second = second.reshape(hyper_width, -1)
    third = third.reshape(hyper_feed, hyper_width)
    vectors = second[:, model_width : model_width + 8].astype(jnp.float32).T
    params = (first, second, third, vectors)
    if outer > 1:
        gains = lax.all_gather(gains, "wide", axis=1, axis_index_groups=groups)
        gains = gains.reshape(-1, gains.shape[2], gains.shape[3])
        output_weight, down_weight = (
            lax.all_gather(item, "wide", axis=1, axis_index_groups=groups, tiled=True)
            for item in (output_weight, down_weight)
        )
    gains = gains.astype(jnp.float32).transpose(1, 0, 2).reshape(-1, model_width)
    final_scale = final_gain.astype(jnp.float32).reshape(1, model_width)
    gains = jnp.concatenate([gains[:4], final_scale, gains[:3]], axis=0)
    notes = lax.dynamic_slice_in_dim(notes, section_index * 2, 2, 0)
    ids, wanted = notes[:, 0].reshape(-1), notes[:, 1].reshape(-1)

    entries, slot_count = slot_ids.shape
    group_hits = (
        group_ids[:, None] == jnp.arange(group_offsets.shape[0], dtype=jnp.int32)[None, :]
    ).astype(jnp.int32)
    row_start = jnp.sum(group_hits * group_offsets[None, :], axis=1)
    piece_rows = (row_start[:, None] + slot_ids).reshape(-1)
    pieces = jnp.take(piece_table, piece_rows, axis=0)
    table_shard, hyper_stored = hyper_forward(pieces, slot_count, params)
    table_shard, y_one = together(table_shard, y_one)
    beyond_one = lax.ppermute(y_one, "section", SWAP_CORE)
    table_rows = section_gather(3, table_shard)
    if outer > 1:
        table_rows = lax.all_gather(table_rows, "wide", axis=1, axis_index_groups=groups)
    table_rows = table_rows.reshape(-1, model_width)
    wide_rows = rank * outer + jnp.arange(outer, dtype=jnp.int32)
    row_starts = (
        jnp.arange(SECTIONS, dtype=jnp.int32)[:, None] * wides + wide_rows[None, :]
    ) * entries
    own_rows = row_starts[:, :, None] + jnp.arange(entries, dtype=jnp.int32)[None, None, :]
    own_rows = own_rows.reshape(-1)
    own_rows = own_rows.reshape(-1, 1)

    def by_halves(numbers):
        return jnp.pad(numbers.reshape(2, -1), ((0, 6), (0, 0)))

    normed, grads, logit_grad, loss_block = decode(
        outer,
        4,
        total_tokens,
        all_teams((own_one, y_one, core_one, beyond_one, own_two), outer, groups),
        output_weight,
        down_weight,
        gains,
        (turn_tables(False), turn_tables(True)),
        table_rows,
        own_rows,
        by_halves(ids),
        by_halves(wanted),
    )

    hits = (own_rows == ids[None, :]).astype(jnp.bfloat16)
    table_part = matmul(logit_grad, normed.reshape(ROWS, model_width)) + matmul(
        hits, grads.reshape(ROWS, model_width)
    )
    table_part = table_part.astype(jnp.bfloat16).reshape(SECTIONS, outer, entries, model_width)
    if outer > 1:
        table_part = lax.psum_scatter(
            table_part.astype(jnp.float32),
            "wide",
            scatter_dimension=1,
            axis_index_groups=groups,
        ).astype(jnp.bfloat16)
        loss_block = lax.psum(loss_block, "wide", axis_index_groups=groups)
    table_grad, loss_block = section_sum(
        11, table_part.reshape(SECTIONS, entries, model_width), loss_block
    )
    mean_loss = loss_block[0, 0]
    grads = hyper_backward(pieces, slot_count, params, hyper_stored, table_grad)
    first, second, third = (
        item.reshape(SECTIONS, wides, -1, item.shape[1]) for item in grads
    )
    first, second, third = collect(12, (first, second, third))
    grad_query, grad_key, grad_value, grad_output = (
        first[:, n * hyper_width : (n + 1) * hyper_width] for n in range(4)
    )
    return (
        mean_loss,
        second[:, model_width],
        second[:, model_width + 1],
        grad_query,
        grad_key,
        grad_value,
        grad_output,
        second[:, model_width + 2],
        second[:, model_width + 3],
        first[:, 4 * hyper_width :],
        third,
        second[:, :model_width],
    )


def solution(mesh):
    placed = (
        P("wide", None, None),
        P("wide", None, None),
        P(("section", "wide"), None),
        P(("section", "wide")),
        P(),
        P(),
        P(("section", "wide")),
        P(("section", "wide")),
        P(("section", "wide"), None),
        P(("section", "wide"), None),
        P(("section", "wide"), None),
        P(("section", "wide"), None),
        P(("section", "wide")),
        P(("section", "wide")),
        P(("section", "wide"), None),
        P(("section", "wide"), None),
        P(("section", "wide"), None),
        P(None, "wide"),
        P(None, "wide", None),
        P(None, "wide", None),
        P(None, "wide", None),
        P(None, "wide", None),
        P(None, "wide"),
        P(None, "wide", None),
        P(None, "wide", None),
        P(None, "wide", None),
        P(),
    )
    return jax.shard_map(
        shards,
        mesh=mesh,
        in_specs=placed,
        out_specs=(
            P(),
            P(("section", "wide")),
            P(("section", "wide")),
            P(("section", "wide"), None),
            P(("section", "wide"), None),
            P(("section", "wide"), None),
            P(("section", "wide"), None),
            P(("section", "wide")),
            P(("section", "wide")),
            P(("section", "wide"), None),
            P(("section", "wide"), None),
            P(("section", "wide"), None),
        ),
        check_vma=False,
    )
```

```python
import functools

import jax
import jax.numpy as jnp
from jax import lax
from jax.experimental import pallas as pl
from jax.experimental.pallas import tpu as pltpu
from jax.sharding import PartitionSpec as P

HEAD_DIM = 64
HYPER_HEAD_COUNT = 8
MB = 2
LEN = 64
TEAM = 8
SECTIONS = 4
ROWS = MB * LEN * TEAM // SECTIONS
HALF = ROWS // 2
EACH = HALF // TEAM
LINES = TEAM // 2
FIRST, SECOND = 0, 1
LANES = 128
MESH_IDS = pl.DeviceIdType.MESH
ANYWHERE = pl.BlockSpec(memory_space=pl.ANY)
IN_VMEM = pl.BlockSpec(memory_space=pltpu.VMEM)
VMEM_LIMIT = 56 * 1024 * 1024

norm_eps = 1e-05
inv_root_two = 0.7071067811865476
inv_root_tau = 0.3989422804014327


def matmul(former, latter):
    return jnp.dot(former, latter, preferred_element_type=jnp.float32)


def times_trans(former, latter):
    return lax.dot_general(
        former, latter, (((1,), (1,)), ((), ())), preferred_element_type=jnp.float32
    )


def trans_times(former, latter):
    return lax.dot_general(
        former, latter, (((0,), (0,)), ((), ())), preferred_element_type=jnp.float32
    )


def center_norm(values):
    center = values - jnp.mean(values, axis=-1, keepdims=True)
    inverse = lax.rsqrt(jnp.mean(center * center, axis=-1, keepdims=True) + norm_eps)
    return (center * inverse, inverse)


def center_back(normed, inverse, normed_grad):
    mean_grad = jnp.mean(normed_grad, axis=-1, keepdims=True)
    mean_mix = jnp.mean(normed_grad * normed, axis=-1, keepdims=True)
    return inverse * (normed_grad - mean_grad - normed * mean_mix)


def root_inverse(values):
    return lax.rsqrt(jnp.mean(values * values, axis=-1, keepdims=True) + norm_eps)


def reciprocal_root_backward(values, inverse, gain_vec, outer_grad):
    scaled = outer_grad * gain_vec
    mixing = jnp.mean(scaled * values, axis=-1, keepdims=True)
    return inverse * scaled - values * inverse * inverse * inverse * mixing


def rope_tables(positions, head_width):
    halfway = head_width // 2
    frequency = jnp.exp(
        -jnp.log(10000.0) * (2.0 * jnp.arange(halfway, dtype=jnp.float32) / head_width)
    )
    angles = jnp.arange(positions, dtype=jnp.float32)[:, None] * frequency[None, :]
    angles = jnp.concatenate([angles, angles], axis=1)
    return (jnp.cos(angles), jnp.sin(angles))


def greet(peers):
    barrier = pltpu.get_barrier_semaphore()
    for peer in peers:
        pl.semaphore_signal(barrier, inc=1, device_id=peer, device_id_type=MESH_IDS)
    pl.semaphore_wait(barrier, len(peers))


def remote(source, target, send, recv, peer):
    return pltpu.make_async_remote_copy(
        src_ref=source,
        dst_ref=target,
        send_sem=send,
        recv_sem=recv,
        device_id=peer,
        device_id_type=MESH_IDS,
    )


def settings(collective_id):
    return pltpu.CompilerParams(
        collective_id=collective_id, has_side_effects=True, vmem_limit_bytes=VMEM_LIMIT
    )


def dma_sems(*shape):
    return pltpu.SemaphoreType.DMA(shape)


def section_places():
    section = lax.axis_index("section")
    core = section % 2
    partner = section + 1 - 2 * core
    across = (section + 2) % SECTIONS
    return section, partner, across


def section_gather_kernel(block, gathered, keep_sem, send, recv):
    section, partner, across = section_places()
    greet([{"section": partner}, {"section": across}])
    keep = pltpu.make_async_copy(block, gathered.at[section], keep_sem)
    near = remote(block, gathered.at[section], send.at[0], recv.at[0], {"section": partner})
    far = remote(block, gathered.at[section], send.at[1], recv.at[1], {"section": across})
    on = remote(
        gathered.at[across], gathered.at[across], send.at[2], recv.at[2], {"section": partner}
    )
    far.start()
    near.start()
    keep.start()
    far.wait_recv()
    on.start()
    near.wait()
    on.wait()
    far.wait_send()
    keep.wait()


def section_gather(collective_id, block):
    return pl.pallas_call(
        section_gather_kernel,
        out_shape=jax.ShapeDtypeStruct((SECTIONS,) + block.shape, block.dtype),
        in_specs=[ANYWHERE],
        out_specs=ANYWHERE,
        scratch_shapes=[pltpu.SemaphoreType.DMA, dma_sems(3), dma_sems(3)],
        compiler_params=settings(collective_id),
        name="section_gather",
    )(block)


def section_sum_kernel(partial, loss, summed, loss_sum, own, near, pair, far, loss_near, loss_pair, loss_far, load_sem, send, recv):
    section, partner, across = section_places()
    beyond = (partner + 2) % SECTIONS
    greet([{"section": partner}, {"section": across}])
    loads = [
        pltpu.make_async_copy(partial.at[section], own.at[0], load_sem.at[0]),
        pltpu.make_async_copy(partial.at[across], own.at[1], load_sem.at[1]),
    ]
    nears = [
        remote(partial.at[partner], near.at[0], send.at[0], recv.at[0], {"section": partner}),
        remote(partial.at[beyond], near.at[1], send.at[1], recv.at[1], {"section": partner}),
        remote(loss, loss_near, send.at[2], recv.at[2], {"section": partner}),
    ]
    fars = [
        remote(pair, far, send.at[3], recv.at[3], {"section": across}),
        remote(loss_pair, loss_far, send.at[4], recv.at[4], {"section": across}),
    ]
    for j in (1, 2, 0):
        nears[j].start()
    loads[1].start()
    loads[0].start()
    loads[1].wait()
    nears[1].wait_recv()
    pair[...] = (own[1].astype(jnp.float32) + near[1].astype(jnp.float32)).astype(jnp.bfloat16)
    fars[0].start()
    nears[2].wait_recv()
    loss_pair[...] = loss[...] + loss_near[...]
    fars[1].start()
    loads[0].wait()
    nears[0].wait_recv()
    total = own[0].astype(jnp.float32) + near[0].astype(jnp.float32)
    fars[0].wait_recv()
    summed[...] = total + far[...].astype(jnp.float32)
    fars[1].wait_recv()
    loss_sum[...] = loss_pair[...] + loss_far[...]
    for copy in nears + fars:
        copy.wait_send()


def section_sum(collective_id, partial, loss):
    shape = partial.shape[1:]
    low, low_two = pltpu.VMEM(shape, jnp.bfloat16), pltpu.VMEM((2,) + shape, jnp.bfloat16)
    number = pltpu.VMEM(loss.shape, jnp.float32)
    return pl.pallas_call(
        section_sum_kernel,
        out_shape=(
            jax.ShapeDtypeStruct(shape, jnp.float32),
            jax.ShapeDtypeStruct(loss.shape, jnp.float32),
        ),
        in_specs=[ANYWHERE, IN_VMEM],
        out_specs=(IN_VMEM, IN_VMEM),
        scratch_shapes=[low_two, low_two, low, low, number, number, number]
        + [dma_sems(2), dma_sems(5), dma_sems(5)],
        compiler_params=settings(collective_id),
        name="section_sum",
    )(partial, loss)


def all_places(halves):
    section, partner, across = section_places()
    wide = lax.axis_index("wide")
    line, column = wide // 2, wide % 2

    def wide_at(j):
        return ((line + j) % halves) * 2 + column

    return section, partner, across, wide, wide_at


def steps_of(x_first, section, partner, across, wide):
    column_flip = wide + 1 - 2 * (wide % 2)
    x_step = ({"wide": column_flip}, False, True)
    y_step = ({"section": across}, True, False)
    return (x_step, y_step) if x_first else (y_step, x_step)


def owner_of(home, flips_y, flips_x, wide_block):
    section = (home + 2) % SECTIONS if flips_y else home
    return section, (wide_block + 1 - 2 * (wide_block % 2) if flips_x else wide_block)


def spread_kernel(count, halves, outer, *refs):
    blocks, notes = refs[:count], refs[count : count + 2]
    gathereds, notes_out = refs[count + 2 : 2 * count + 2], refs[2 * count + 2 : 2 * count + 4]
    (
        keep_sem,
        note_keep,
        note_send,
        note_recv,
        z_send,
        a_send,
        b_send,
        c_send,
        z_recv,
        a_recv,
        b_recv,
        c_recv,
    ) = refs[2 * count + 4 :]
    section, partner, across, wide, wide_at = all_places(halves)
    rank, team = wide // outer, wide % outer
    members = [None] + [{"wide": (rank + k) % TEAM * outer + team} for k in range(1, TEAM)]
    beside = wide + 1 - 2 * (wide % 2)
    barrier = pltpu.get_barrier_semaphore()
    for peer in ({"section": partner}, {"section": across}, {"wide": beside}):
        pl.semaphore_signal(barrier, inc=1, device_id=peer, device_id_type=MESH_IDS)

    def hello(j, carry):
        peer = {"wide": wide_at(j)}
        pl.semaphore_signal(barrier, inc=1, device_id=peer, device_id_type=MESH_IDS)
        return carry

    lax.fori_loop(1, halves, hello, 0)
    for peer in members[1:]:
        pl.semaphore_signal(barrier, inc=1, device_id=peer, device_id_type=MESH_IDS)
    pl.semaphore_wait(barrier, 3 + halves - 1 + TEAM - 1)
    note_keeps = [
        pltpu.make_async_copy(notes[m], notes_out[m].at[rank], note_keep.at[m]) for m in range(2)
    ]
    note_copies = [
        remote(notes[m], notes_out[m].at[rank], note_send.at[m, k], note_recv.at[m, k], members[k])
        for m in range(2)
        for k in range(1, TEAM)
    ]
    for copy in note_keeps + note_copies:
        copy.start()

    keeps = [
        pltpu.make_async_copy(blocks[n], gathereds[n].at[section, wide], keep_sem.at[n])
        for n in range(count)
    ]

    def z_copy(n, j):
        return remote(
            blocks[n],
            gathereds[n].at[section, wide],
            z_send.at[n, j],
            z_recv.at[n, j],
            {"wide": wide_at(j)},
        )

    def a_copy(n, j):
        (peer, _, _), _ = steps_of(n == 0, section, partner, across, wide)
        block = gathereds[n].at[section, wide_at(-j)]
        return remote(block, block, a_send.at[n, j], a_recv.at[n, j], peer)

    def b_copy(n, flip, j):
        (_, y_a, x_a), (peer, _, _) = steps_of(n == 0, section, partner, across, wide)
        place = owner_of(section, y_a and flip, x_a and flip, wide_at(-j))
        block = gathereds[n].at[place[0], place[1]]
        slot = j + (halves if flip else 0)
        return remote(block, block, b_send.at[n, slot], b_recv.at[n, slot], peer)

    def c_copy(n, which):
        home = (section + 2) % SECTIONS if which else section
        block = gathereds[n].at[home]
        return remote(
            block, block, c_send.at[n, which], c_recv.at[n, which], {"section": partner}
        )

    for keep in keeps:
        keep.start()

    def start_z(j, carry):
        for n in range(count):
            z_copy(n, j).start()
        return carry

    lax.fori_loop(1, halves, start_z, 0)
    for n in range(count):
        keeps[n].wait()
        a_copy(n, 0).start()
        b_copy(n, False, 0).start()

    def pass_z(j, carry):
        for n in range(count):
            z_copy(n, j).wait_recv()
            a_copy(n, j).start()
            b_copy(n, False, j).start()
        return carry

    lax.fori_loop(1, halves, pass_z, 0)

    def pass_a(j, carry):
        for n in range(count):
            a_copy(n, j).wait_recv()
            b_copy(n, True, j).start()
        return carry

    lax.fori_loop(0, halves, pass_a, 0)

    def settle_b(j, carry):
        for n in range(count):
            for flip in (False, True):
                b_copy(n, flip, j).wait_recv()
        return carry

    c_copy(0, 0).start()
    lax.fori_loop(0, halves, settle_b, 0)
    c_copy(0, 1).start()
    for n in range(1, count):
        c_copy(n, 0).start()
        c_copy(n, 1).start()
    for n in range(count):
        c_copy(n, 0).wait()
        c_copy(n, 1).wait()

    def drain(j, carry):
        for n in range(count):
            a_copy(n, j).wait_send()
            b_copy(n, False, j).wait_send()
            b_copy(n, True, j).wait_send()
        return carry

    lax.fori_loop(0, halves, drain, 0)

    def drain_z(j, carry):
        for n in range(count):
            z_copy(n, j).wait_send()
        return carry

    lax.fori_loop(1, halves, drain_z, 0)
    for copy in note_keeps + note_copies:
        copy.wait()


def spread(collective_id, wides, outer, blocks, notes):
    count, halves = len(blocks), wides // 2
    return pl.pallas_call(
        functools.partial(spread_kernel, count, halves, outer),
        out_shape=tuple(
            jax.ShapeDtypeStruct((SECTIONS, wides) + block.shape, block.dtype) for block in blocks
        )
        + tuple(jax.ShapeDtypeStruct((TEAM,) + note.shape, note.dtype) for note in notes),
        in_specs=[ANYWHERE] * (count + 2),
        out_specs=(ANYWHERE,) * (count + 2),
        scratch_shapes=[dma_sems(count), dma_sems(2), dma_sems(2, TEAM), dma_sems(2, TEAM)]
        + [
            dma_sems(count, halves),
            dma_sems(count, halves),
            dma_sems(count, 2 * halves),
            dma_sems(count, 2),
        ]
        * 2,
        compiler_params=settings(collective_id),
        name="spread",
    )(*blocks, *notes)


def collect_kernel(count, halves, *refs):
    partials, sums = refs[:count], refs[count : 2 * count]
    keeps, c_in, b_in, a_in, z_in = (refs[(2 + k) * count : (3 + k) * count] for k in range(5))
    load_sem, c_send, b_send, a_send, z_send, c_recv, b_recv, a_recv, z_recv = refs[7 * count :]
    section, partner, across, wide, wide_at = all_places(halves)
    beside = wide + 1 - 2 * (wide % 2)
    barrier = pltpu.get_barrier_semaphore()
    for peer in ({"section": partner}, {"section": across}, {"wide": beside}):
        pl.semaphore_signal(barrier, inc=1, device_id=peer, device_id_type=MESH_IDS)

    def hello(j, carry):
        peer = {"wide": wide_at(j)}
        pl.semaphore_signal(barrier, inc=1, device_id=peer, device_id_type=MESH_IDS)
        return carry

    lax.fori_loop(1, halves, hello, 0)
    pl.semaphore_wait(barrier, 3 + halves - 1)

    def place(n, home, flip_b, flip_a, j):
        (_, y_a, x_a), (_, y_b, x_b) = steps_of(n == 0, section, partner, across, wide)
        flips_y = (y_a and flip_a) or (y_b and flip_b)
        flips_x = (x_a and flip_a) or (x_b and flip_b)
        return owner_of(home, flips_y, flips_x, wide_at(j))

    def load(n, fb, fa, j):
        owner = place(n, section, fb, fa, j)
        slot = (fb * 2 + fa) * halves + j
        return pltpu.make_async_copy(
            partials[n].at[owner[0], owner[1]], keeps[n].at[slot], load_sem.at[n, slot]
        )

    def c_copy(n, fb, fa, j):
        owner = place(n, partner, fb, fa, j)
        slot = (fb * 2 + fa) * halves + j
        return remote(
            partials[n].at[owner[0], owner[1]],
            c_in[n].at[slot],
            c_send.at[n, slot],
            c_recv.at[n, slot],
            {"section": partner},
        )

    def b_copy(n, fa, j):
        _, (peer, _, _) = steps_of(n == 0, section, partner, across, wide)
        slot = fa * halves + j
        return remote(
            keeps[n].at[2 * halves + slot],
            b_in[n].at[slot],
            b_send.at[n, slot],
            b_recv.at[n, slot],
            peer,
        )

    def a_copy(n, j):
        (peer, _, _), _ = steps_of(n == 0, section, partner, across, wide)
        return remote(
            keeps[n].at[halves + j], a_in[n].at[j], a_send.at[n, j], a_recv.at[n, j], peer
        )

    def z_copy(n, j):
        return remote(
            keeps[n].at[j],
            z_in[n].at[j],
            z_send.at[n, j],
            z_recv.at[n, j],
            {"wide": wide_at(j)},
        )

    def add(n, slot, more):
        keeps[n][slot] = (
            keeps[n][slot].astype(jnp.float32) + more.astype(jnp.float32)
        ).astype(jnp.bfloat16)

    groups = ((1, 1), (1, 0), (0, 1), (0, 0))
    for fb, fa in groups:

        def start_c(j, carry):
            for n in range(count):
                c_copy(n, fb, fa, j).start()
                load(n, fb, fa, j).start()
            return carry

        lax.fori_loop(0, halves, start_c, 0)

    for fb, fa in groups:

        def sum_c(j, carry):
            for n in range(count):
                slot = (fb * 2 + fa) * halves + j
                load(n, fb, fa, j).wait()
                c_copy(n, fb, fa, j).wait_recv()
                add(n, slot, c_in[n][slot])
                if fb:
                    b_copy(n, fa, j).start()
            return carry

        lax.fori_loop(0, halves, sum_c, 0)

    for fa in (1, 0):

        def sum_b(j, carry):
            for n in range(count):
                slot = fa * halves + j
                b_copy(n, fa, j).wait_recv()
                add(n, slot, b_in[n][slot])
                if fa:
                    a_copy(n, j).start()
            return carry

        lax.fori_loop(0, halves, sum_b, 0)

    def sum_a(j, carry):
        for n in range(count):
            a_copy(n, j).wait_recv()
            add(n, j, a_in[n][j])
            z_copy(n, j).start()
        return carry

    lax.fori_loop(1, halves, sum_a, 0)
    for n in range(count):
        a_copy(n, 0).wait_recv()
        sums[n][...] = keeps[n][0].astype(jnp.float32) + a_in[n][0].astype(jnp.float32)

    def sum_z(j, carry):
        for n in range(count):
            z_copy(n, j).wait_recv()
            sums[n][...] += z_in[n][j].astype(jnp.float32)
        return carry

    lax.fori_loop(1, halves, sum_z, 0)

    def drain(j, carry):
        for n in range(count):
            for fb, fa in groups:
                c_copy(n, fb, fa, j).wait_send()
            b_copy(n, 0, j).wait_send()
            b_copy(n, 1, j).wait_send()
            a_copy(n, j).wait_send()
        return carry

    lax.fori_loop(0, halves, drain, 0)

    def drain_z(j, carry):
        for n in range(count):
            z_copy(n, j).wait_send()
        return carry

    lax.fori_loop(1, halves, drain_z, 0)


def collect(collective_id, partials):
    count, halves = len(partials), partials[0].shape[1] // 2
    shapes = [partial.shape[2:] for partial in partials]

    def slots(number):
        return [pltpu.VMEM((number,) + shape, jnp.bfloat16) for shape in shapes]

    return pl.pallas_call(
        functools.partial(collect_kernel, count, halves),
        out_shape=tuple(jax.ShapeDtypeStruct(shape, jnp.float32) for shape in shapes),
        in_specs=[ANYWHERE] * count,
        out_specs=(IN_VMEM,) * count,
        scratch_shapes=slots(4 * halves)
        + slots(4 * halves)
        + slots(2 * halves)
        + slots(halves)
        + slots(halves)
        + [dma_sems(count, 4 * halves)]
        + [
            dma_sems(count, 4 * halves),
            dma_sems(count, 2 * halves),
            dma_sems(count, halves),
            dma_sems(count, halves),
        ]
        * 2,
        compiler_params=settings(collective_id),
        name="collect",
    )(*partials)


TILE = 256


def causal_blocks(count, length):
    row = lax.broadcasted_iota(jnp.int32, (count, count), 0)
    column = lax.broadcasted_iota(jnp.int32, (count, count), 1)
    return (row // length == column // length) & (column <= row)


def turn(values, tables):
    cosines, upper, lower = tables
    parts = []
    for start in range(0, values.shape[1], LANES):
        part = values[:, start : start + LANES]
        ahead = pltpu.roll(part, LANES - HEAD_DIM // 2, 1)
        behind = pltpu.roll(part, HEAD_DIM // 2, 1)
        parts.append(part * cosines + ahead * upper + behind * lower)
    return parts[0] if len(parts) == 1 else jnp.concatenate(parts, axis=1)


def turn_tables(back):
    cosines, sines = rope_tables(LEN, HEAD_DIM)
    sines = -sines if back else sines
    first = jnp.arange(HEAD_DIM) < HEAD_DIM // 2
    upper, lower = jnp.where(first, -sines, 0.0), jnp.where(first, 0.0, sines)
    blank = jnp.zeros_like(cosines)
    pairs = [(cosines, cosines), (upper, upper), (lower, lower)]
    pairs += [(cosines, blank + 1.0), (upper, blank), (lower, blank)]
    tables = jnp.stack([jnp.concatenate(pair, axis=1) for pair in pairs])
    return jnp.tile(tables, (1, HALF // LEN, 1))


def attend(queries, key, mask, scale):
    scores = times_trans(queries, key) * scale
    scores = jnp.where(mask, scores, -1e30)
    peak = jnp.max(scores, axis=1, keepdims=True)
    mass = jnp.exp(scores - peak)
    return mass / jnp.sum(mass, axis=1, keepdims=True)


def local(kernel, operands, outs, scratch, name):
    return pl.pallas_call(
        kernel,
        out_shape=tuple(jax.ShapeDtypeStruct(shape, kind) for shape, kind in outs),
        in_specs=[IN_VMEM] * len(operands),
        out_specs=(IN_VMEM,) * len(outs),
        scratch_shapes=list(scratch),
        compiler_params=pltpu.CompilerParams(vmem_limit_bytes=VMEM_LIMIT),
        name=name,
    )(*operands)


CHUNK = 128


def same_entry(count, slots):
    row = lax.broadcasted_iota(jnp.int32, (count, count), 0)
    column = lax.broadcasted_iota(jnp.int32, (count, count), 1)
    return row // slots == column // slots


def gelu(values):
    return 0.5 * values * (1.0 + lax.erf(values * inv_root_two))


def hyper_kernel(
    slots,
    pieces,
    first,
    second,
    third,
    vectors,
    table,
    heads_out,
    mixed_out,
    middle_out,
    expanded_out,
    pooled_out,
    entered,
    outcome,
):
    width = pieces.shape[1]
    count, feed = pieces.shape[0], third.shape[0]
    head = width // HYPER_HEAD_COUNT
    flat = pieces[...].astype(jnp.float32)
    normed, _ = center_norm(flat)
    entered[...] = (normed * vectors[0:1] + vectors[1:2]).astype(jnp.bfloat16)

    @pl.loop(0, 3 * width // TILE)
    def _(n):
        columns = pl.ds(pl.multiple_of(n * TILE, TILE), TILE)
        heads_out[:, columns] = matmul(entered[...], first[:, columns]).astype(jnp.bfloat16)

    mask = same_entry(CHUNK, slots)

    @pl.loop(0, count // CHUNK)
    def _(n):
        rows = pl.ds(pl.multiple_of(n * CHUNK, CHUNK), CHUNK)
        block = heads_out[rows, :]
        mixed = []
        for start in range(0, width, head):
            query, key, value = (
                block[:, part * width + start : part * width + start + head] for part in range(3)
            )
            weights = attend(query, key, mask, head ** (-0.5))
            mixed.append(matmul(weights.astype(jnp.bfloat16), value))
        mixed_out[rows, :] = jnp.concatenate(mixed, axis=1).astype(jnp.bfloat16)

    for start in range(0, width, TILE):
        columns = pl.ds(start, TILE)
        middle_out[:, columns] = pieces[:, columns].astype(jnp.float32) + matmul(
            mixed_out[...], first[:, pl.ds(3 * width + start, TILE)]
        )
    normed, _ = center_norm(middle_out[...])
    entered[...] = (normed * vectors[2:3] + vectors[3:4]).astype(jnp.bfloat16)
    outcome[...] = middle_out[...]

    @pl.loop(0, feed // TILE)
    def _(n):
        start = pl.multiple_of(n * TILE, TILE)
        columns = pl.ds(pl.multiple_of(4 * width + start, TILE), TILE)
        expanded = matmul(entered[...], first[:, columns])
        expanded_out[:, pl.ds(start, TILE)] = expanded
        outcome[...] += matmul(gelu(expanded).astype(jnp.bfloat16), third[pl.ds(start, TILE), :])

    pooled = jnp.mean(outcome[...].reshape(count // slots, slots, width), axis=1)
    pooled_out[...] = pooled.astype(jnp.bfloat16)

    @pl.loop(0, table.shape[1] // TILE)
    def _(n):
        columns = pl.ds(pl.multiple_of(n * TILE, TILE), TILE)
        table[:, columns] = matmul(pooled_out[...], second[:, columns]).astype(jnp.bfloat16)


def hyper_forward(pieces, slots, params):
    count, width = pieces.shape
    first, second, third, vectors = params
    feed = third.shape[0]
    depth = second.shape[1] - LANES
    entries = count // slots
    table, *stored = local(
        functools.partial(hyper_kernel, slots),
        (pieces, *params),
        [
            ((entries, depth), jnp.bfloat16),
            ((count, 3 * width), jnp.bfloat16),
            ((count, width), jnp.bfloat16),
            ((count, width), jnp.float32),
            ((count, feed), jnp.float32),
            ((entries, width), jnp.bfloat16),
        ],
        [pltpu.VMEM((count, width), jnp.bfloat16), pltpu.VMEM((count, width), jnp.float32)],
        "hyper",
    )
    return table, stored


def hyper_back_kernel(
    slots,
    table_grad,
    pieces,
    first,
    second,
    third,
    vectors,
    heads,
    mixed,
    middle,
    expanded,
    pooled,
    first_grad,
    second_grad,
    third_grad,
    entered,
    outcome_low,
    feed_grad,
    heads_grad,
    mixed_grad,
):
    width = pieces.shape[1]
    count, feed = pieces.shape[0], third.shape[0]
    depth = table_grad.shape[1]
    head = width // HYPER_HEAD_COUNT
    scale = head ** (-0.5)
    grad_low = table_grad[...].astype(jnp.bfloat16)
    pooled_turned = jnp.transpose(pooled[...].astype(jnp.float32)).astype(jnp.bfloat16)

    for start in range(0, depth, TILE):
        columns = pl.ds(start, TILE)
        second_grad[:, columns] = matmul(
            pooled_turned, grad_low[:, start : start + TILE]
        ).astype(jnp.bfloat16)
    pooled_grad = times_trans(grad_low, second[:, pl.ds(0, depth)]) / slots
    outcome_grad = jnp.broadcast_to(pooled_grad[:, None, :], (count // slots, slots, width))
    outcome_grad = outcome_grad.reshape(count, width)
    outcome_low[...] = outcome_grad.astype(jnp.bfloat16)
    normed, inverse = center_norm(middle[...])
    entered[...] = jnp.transpose(normed * vectors[2:3] + vectors[3:4]).astype(jnp.bfloat16)
    feed_grad[...] = jnp.zeros_like(feed_grad)

    @pl.loop(0, feed // TILE)
    def _(n):
        start = pl.multiple_of(n * TILE, TILE)
        tile = pl.ds(start, TILE)
        columns = pl.ds(pl.multiple_of(4 * width + start, TILE), TILE)
        values = expanded[:, tile]
        erf = 0.5 * (1.0 + lax.erf(values * inv_root_two))
        active = (values * erf).astype(jnp.bfloat16)
        third_grad[tile, :] = trans_times(active, outcome_low[...]).astype(jnp.bfloat16)
        active_grad = times_trans(outcome_low[...], third[tile, :])
        slope = erf + values * jnp.exp(-0.5 * values * values) * inv_root_tau
        low = (active_grad * slope).astype(jnp.bfloat16)
        first_grad[:, columns] = matmul(entered[...], low).astype(jnp.bfloat16)
        feed_grad[...] += times_trans(low, first[:, columns])

    grad = feed_grad[...]
    scale_two = jnp.sum(grad * normed, axis=0, keepdims=True)
    shift_two = jnp.sum(grad, axis=0, keepdims=True)
    middle_grad = outcome_grad + center_back(normed, inverse, grad * vectors[2:3])
    middle_low = middle_grad.astype(jnp.bfloat16)
    out_columns = pl.ds(3 * width, width)
    first_grad[:, out_columns] = trans_times(mixed[...], middle_low).astype(jnp.bfloat16)
    mixed_grad[...] = times_trans(middle_low, first[:, out_columns]).astype(jnp.bfloat16)
    mask = same_entry(CHUNK, slots)

    @pl.loop(0, count // CHUNK)
    def _(n):
        rows = pl.ds(pl.multiple_of(n * CHUNK, CHUNK), CHUNK)
        block = heads[rows, :]
        outer_block = mixed_grad[rows, :]
        grads = [[], [], []]
        for start in range(0, width, head):
            query, key, value = (
                block[:, part * width + start : part * width + start + head] for part in range(3)
            )
            outer = outer_block[:, start : start + head]
            weights = attend(query, key, mask, scale)
            weight_grad = times_trans(outer, value)
            score_grad = weights * (
                weight_grad - jnp.sum(weights * weight_grad, axis=1, keepdims=True)
            )
            score_grad = score_grad.astype(jnp.bfloat16)
            grads[0].append(matmul(score_grad, key) * scale)
            grads[1].append(trans_times(score_grad, query) * scale)
            grads[2].append(trans_times(weights.astype(jnp.bfloat16), outer))
        for part in range(3):
            heads_grad[rows, pl.ds(part * width, width)] = jnp.concatenate(
                grads[part], axis=1
            ).astype(jnp.bfloat16)

    normed, _ = center_norm(pieces[...].astype(jnp.float32))
    entered[...] = jnp.transpose(normed * vectors[0:1] + vectors[1:2]).astype(jnp.bfloat16)
    feed_grad[...] = jnp.zeros_like(feed_grad)

    @pl.loop(0, 3 * width // TILE)
    def _(n):
        columns = pl.ds(pl.multiple_of(n * TILE, TILE), TILE)
        low = heads_grad[:, columns]
        first_grad[:, columns] = matmul(entered[...], low).astype(jnp.bfloat16)
        feed_grad[...] += times_trans(low, first[:, columns])

    grad = feed_grad[...]
    scale_one = jnp.sum(grad * normed, axis=0, keepdims=True)
    shift_one = jnp.sum(grad, axis=0, keepdims=True)
    row = lax.broadcasted_iota(jnp.int32, (LANES, width), 0)
    summed = jnp.zeros((LANES, width), jnp.float32)
    for n, item in enumerate((scale_one, shift_one, scale_two, shift_two)):
        summed = jnp.where(row == n, item, summed)
    second_grad[:, pl.ds(depth, LANES)] = jnp.transpose(summed).astype(jnp.bfloat16)


def hyper_backward(pieces, slots, params, stored, table_grad):
    count, width = pieces.shape
    first, second, third, _ = params
    return local(
        functools.partial(hyper_back_kernel, slots),
        (table_grad, pieces, *params, *stored),
        [(item.shape, jnp.bfloat16) for item in (first, second, third)],
        [
            pltpu.VMEM((width, count), jnp.bfloat16),
            pltpu.VMEM((count, width), jnp.bfloat16),
            pltpu.VMEM((count, width), jnp.float32),
            pltpu.VMEM((count, 3 * width), jnp.bfloat16),
            pltpu.VMEM((count, width), jnp.bfloat16),
        ],
        "hyper_back",
    )


def column_plan(q_columns, kv_columns, ff_columns):
    share = ff_columns // TEAM
    edge = share // LANES * LANES
    tail = share - edge
    heads = kv_columns // HEAD_DIM
    q_share = q_columns // TEAM
    plan = []
    for rank in range(TEAM):
        kv = rank * heads // TEAM * HEAD_DIM
        widths = [
            (0, rank * q_share, q_share),
            (1, kv, HEAD_DIM),
            (2, kv, HEAD_DIM),
            (3, rank * share, edge),
            (4, rank * share, edge),
            (3, rank * share + edge, tail),
            (4, rank * share + edge, tail),
        ]
        moves, start = [], 0
        for item, source, size in widths:
            moves.append((item, source, start, size))
            start += size
        plan.append(moves)
    return plan, start


def pack_kernel(plan, rows, *refs):
    sources, targets = refs[:5], refs[5:7]
    blocks, sem = refs[7:12], refs[12]
    section = lax.axis_index("section")
    mine = pl.ds(pl.multiple_of(section * rows, rows), rows)
    copies = [
        [
            pltpu.make_async_copy(source.at[layer, mine], block.at[layer], sem.at[layer, n])
            for n, (source, block) in enumerate(zip(sources, blocks))
        ]
        for layer in range(2)
    ]
    for layer in range(2):
        for copy in copies[layer]:
            copy.start()
    for layer in range(2):
        for copy in copies[layer]:
            copy.wait()
        for rank, moves in enumerate(plan):
            parts = [
                blocks[item][layer, :, source : source + size] for item, source, _, size in moves
            ]
            heads = jnp.concatenate(parts[1:3], axis=1)
            ends = jnp.concatenate(parts[5:7], axis=1)
            for part, start in zip(
                (parts[0], heads, parts[3], parts[4], ends),
                (moves[0][2], moves[1][2], moves[3][2], moves[4][2], moves[5][2]),
            ):
                if part.shape[1]:
                    targets[layer][rank, :, start : start + part.shape[1]] = part


def pack(weights):
    rows = weights[0].shape[1] // SECTIONS
    plan, width = column_plan(weights[0].shape[2], weights[1].shape[2], weights[3].shape[2])
    if rows % 16:
        section = lax.axis_index("section")
        mine = [lax.dynamic_slice_in_dim(item, section * rows, rows, 1) for item in weights]
        return tuple(
            jnp.stack(
                [
                    jnp.concatenate(
                        [mine[item][layer, :, at : at + size] for item, at, _, size in moves], axis=1
                    )
                    for moves in plan
                ]
            )
            for layer in range(2)
        )
    return pl.pallas_call(
        functools.partial(pack_kernel, plan, rows),
        out_shape=(jax.ShapeDtypeStruct((TEAM, rows, width), jnp.bfloat16),) * 2,
        in_specs=[ANYWHERE] * 5,
        out_specs=(IN_VMEM,) * 2,
        scratch_shapes=[pltpu.VMEM((2, rows, item.shape[2]), jnp.bfloat16) for item in weights]
        + [dma_sems(2, 5)],
        compiler_params=pltpu.CompilerParams(vmem_limit_bytes=VMEM_LIMIT),
        name="pack",
    )(*weights)


ORDER = "grgrrgg"


def finish(*steps):
    steps = list(steps)
    while steps:
        steps = [step for step in steps if next(step, steps) is not steps]


class Decoder:
    def __init__(self, shape, refs):
        self.outer, self.tokens, self.share, self.q_width, self.depth = shape
        for name, ref in refs.items():
            setattr(self, name, ref)
        self.section, self.partner, self.across = section_places()
        self.beyond = (self.partner + 2) % SECTIONS
        wide = lax.axis_index("wide")
        self.rank, self.team = wide // self.outer, wide % self.outer
        self.line, self.column = self.rank // 2, self.rank % 2
        self.mine = self.rank
        self.beside = self.member(self.line, 1 - self.column)
        self.edge = self.share // LANES * LANES
        self.tail = self.share - self.edge

    def at(self, line, column):
        return (line % LINES) * 2 + column

    def member(self, line, column):
        return {"wide": self.at(line, column) * self.outer + self.team}

    def ranked(self, step):
        return {"wide": (self.rank + step) % TEAM * self.outer + self.team}

    def greet(self):
        sections = [{"section": place} for place in (self.partner, self.across, self.beyond)]
        greet(sections + [self.ranked(k) for k in range(1, TEAM)])

    def weight_copies(self):
        heads, feed = pl.ds(0, self.q_width + LANES), pl.ds(self.q_width + LANES, 2 * self.share)
        places = (self.section, self.across, self.partner, self.beyond)
        self.head_loads = [[], []]
        self.feed_loads = [[], []]
        for n, (piece, place) in enumerate(zip(self.pieces, places)):
            self.head_loads[0].append(
                pltpu.make_async_copy(
                    piece.at[:, :, heads], self.head_weight.at[0, :, place], self.load_sem.at[0, n]
                )
            )
            self.feed_loads[0].append(
                pltpu.make_async_copy(
                    piece.at[:, :, feed], self.feed_weight.at[0, :, place], self.load_sem.at[1, n]
                )
            )
        self.head_loads[1].append(
            pltpu.make_async_copy(
                self.own_two.at[:, :, heads],
                self.head_weight.at[1, :, self.section],
                self.load_sem.at[2, 0],
            )
        )
        self.feed_loads[1].append(
            pltpu.make_async_copy(
                self.own_two.at[:, :, feed],
                self.feed_weight.at[1, :, self.section],
                self.load_sem.at[3, 0],
            )
        )
        for n, place in enumerate((self.across, self.beyond, self.partner)):
            peer = {"section": place}
            self.head_loads[1].append(
                remote(
                    self.own_two.at[:, :, heads],
                    self.head_weight.at[1, :, self.section],
                    self.share_send.at[0, n],
                    self.share_recv.at[0, n],
                    peer,
                )
            )
            self.feed_loads[1].append(
                remote(
                    self.own_two.at[:, :, feed],
                    self.feed_weight.at[1, :, self.section],
                    self.share_send.at[1, n],
                    self.share_recv.at[1, n],
                    peer,
                )
            )
        for layer in range(2):
            self.head_loads[layer].append(
                pltpu.make_async_copy(
                    self.out_source.at[layer], self.out_weight.at[layer], self.load_sem.at[4, layer]
                )
            )
            self.feed_loads[layer].append(
                pltpu.make_async_copy(
                    self.down_source.at[layer],
                    self.down_weight.at[layer],
                    self.load_sem.at[5, layer],
                )
            )
        for layer in range(2):
            for copy in self.head_loads[layer] + self.feed_loads[layer]:
                copy.start()

    def send(self, half):
        self.sides = getattr(self, "sides", {})
        self.sides[half] = [
            remote(
                self.partial.at[half, self.at(self.line + j, 1 - self.column)],
                self.side.at[half, j],
                self.side_send.at[half, j],
                self.side_recv.at[half, j],
                self.beside,
            )
            for j in range(LINES)
        ]
        for j in (2, 1, 3, 0):
            self.sides[half][j].start()

    def reduce(self, half, close):
        sides = self.sides[half]
        fars = [None] + [
            remote(
                self.pair.at[half, j],
                self.far.at[half, j],
                self.far_send.at[half, j],
                self.far_recv.at[half, j],
                self.member(self.line + j, self.column),
            )
            for j in range(1, LINES)
        ]

        def pair_sum(j):
            sides[j].wait_recv()
            own = self.partial[half, self.at(self.line + j, self.column)]
            return own.astype(jnp.float32) + self.side[half, j].astype(jnp.float32)

        for j in (2, 1, 3):
            self.pair[half, j] = pair_sum(j).astype(jnp.bfloat16)
            fars[j].start()
            yield
        total = pair_sum(0)
        for j in (1, 3, 2):
            fars[j].wait_recv()
            total = total + self.far[half, j].astype(jnp.float32)
        self.gathered[half, self.mine] = close(half, total)
        for j in range(LINES):
            sides[j].wait_send()
            if j:
                fars[j].wait_send()
        pushes = [None] + [
            remote(
                self.gathered.at[half, self.mine],
                self.gathered.at[half, self.mine],
                self.out_send.at[half, j],
                self.out_recv.at[half, j],
                self.member(self.line + j, self.column),
            )
            for j in range(1, LINES)
        ]
        overs = []
        for j in range(LINES):
            block = self.gathered.at[half, self.at(self.line - j, self.column)]
            overs.append(
                remote(
                    block, block, self.over_send.at[half, j], self.over_recv.at[half, j], self.beside
                )
            )
        for j in (2, 1, 3):
            pushes[j].start()
        overs[0].start()
        self.moving[half] = (pushes, overs)
        yield

    def gather(self, half):
        pushes, overs = self.moving[half]
        for j in (1, 3, 2):
            pushes[j].wait_recv()
            overs[j].start()
            yield
        for j in range(LINES):
            overs[j].wait()
            if j:
                pushes[j].wait_send()
        yield

    def rows(self, half):
        return self.gathered[half].reshape(HALF, self.depth)

    def store_partial(self, half, columns, values):
        self.partial[half, :, :, columns] = values.astype(jnp.bfloat16).reshape(
            TEAM, EACH, values.shape[1]
        )

    def tiles(self, count, parts):
        bounds = [count * n // parts for n in range(parts + 1)]
        return [(low, high) for low, high in zip(bounds[:-1], bounds[1:]) if high > low]

    def inject(self, half):
        hits = self.own_rows[...] == self.ids[half : half + 1, :]
        hits = jnp.where(hits, 1.0, 0.0).astype(jnp.bfloat16)

        @pl.loop(0, self.depth // TILE)
        def _(n):
            columns = pl.ds(pl.multiple_of(n * TILE, TILE), TILE)
            self.store_partial(half, columns, trans_times(hits, self.table[:, columns]))

        yield

    def attention(self, layer, half):
        if half == FIRST:
            for copy in self.head_loads[layer]:
                copy.wait()
        own = pl.ds(half * HALF, HALF)
        width = self.q_width + LANES
        projected = matmul(self.rows(half), self.head_weight[layer].reshape(self.depth, width))
        yield
        queries = turn(projected[:, : self.q_width], [self.tables[n] for n in range(3)])
        pairs = turn(projected[:, self.q_width :], [self.tables[n] for n in range(3, 6)])
        queries, pairs = queries.astype(jnp.bfloat16), pairs.astype(jnp.bfloat16)
        self.queries[layer, own, :] = queries
        self.pairs[layer, own, :] = pairs
        key, value = pairs[:, :HEAD_DIM], pairs[:, HEAD_DIM:]
        mask = causal_blocks(HALF, LEN)
        mixed = []
        for start in range(0, self.q_width, HEAD_DIM):
            weights = attend(queries[:, start : start + HEAD_DIM], key, mask, HEAD_DIM ** (-0.5))
            mixed.append(matmul(weights.astype(jnp.bfloat16), value))
        mixed = jnp.concatenate(mixed, axis=1).astype(jnp.bfloat16)
        yield

        @pl.loop(0, self.depth // TILE)
        def _(n):
            columns = pl.ds(pl.multiple_of(n * TILE, TILE), TILE)
            self.store_partial(half, columns, matmul(mixed, self.out_weight[layer, :, columns]))

        yield

    def feed(self, layer, half):
        if half == FIRST:
            for copy in self.feed_loads[layer]:
                copy.wait()
        own = pl.ds(half * HALF, HALF)
        edge, tail = self.edge, self.tail
        for low, high in self.tiles(2 * self.share // LANES, 3):

            @pl.loop(low, high)
            def _(n):
                columns = pl.ds(pl.multiple_of(n * LANES, LANES), LANES)
                block = self.feed_weight[layer, :, :, :, columns].reshape(self.depth, LANES)
                self.kept[layer, own, columns] = matmul(self.rows(half), block)

            yield

        def activate(gate, up):
            return (jax.nn.silu(gate) * up).astype(jnp.bfloat16)

        self.active[:, :edge] = activate(
            self.kept[layer, own, :edge], self.kept[layer, own, edge : 2 * edge]
        )
        if tail:
            last = self.kept[layer, own, 2 * edge :]
            self.active[:, edge:] = activate(last[:, :tail], last[:, tail:])
        for low, high in self.tiles(self.depth // TILE, 2):

            @pl.loop(low, high)
            def _(n):
                columns = pl.ds(pl.multiple_of(n * TILE, TILE), TILE)
                block = self.down_weight[layer, :, columns]
                self.store_partial(half, columns, matmul(self.active[...], block))

            yield

    def head(self, half):
        keep = pltpu.make_async_copy(
            self.gathered.at[half], self.normed_out.at[half], self.keep_sem.at[half]
        )
        keep.start()
        logits = times_trans(self.table[...], self.rows(half))
        peak = jnp.max(logits, axis=0, keepdims=True)
        mass = jnp.sum(jnp.exp(logits - peak), axis=0, keepdims=True)
        wanted = self.own_rows[...] == self.wanted[half : half + 1, :]
        chosen = jnp.sum(jnp.where(wanted, logits, 0.0), axis=0, keepdims=True)
        row = lax.broadcasted_iota(jnp.int32, (8, HALF), 0)
        stats = jnp.where(row == 0, peak, jnp.where(row == 1, mass, chosen))
        self.stats[half, self.rank] = stats
        copies = [
            remote(
                self.stats.at[half, self.rank],
                self.stats.at[half, self.rank],
                self.stats_send.at[half, k],
                self.stats_recv.at[half, k],
                self.ranked(k),
            )
            for k in range(1, TEAM)
        ]
        for copy in copies:
            copy.start()
        yield
        yield
        for copy in copies:
            copy.wait()
        peaks = [self.stats[half, n, 0:1, :] for n in range(TEAM)]
        top = functools.reduce(jnp.maximum, peaks)
        mass = sum(self.stats[half, n, 1:2, :] * jnp.exp(peaks[n] - top) for n in range(TEAM))
        chosen = sum(self.stats[half, n, 2:3, :] for n in range(TEAM))
        log_norm = top + jnp.log(mass)
        loss = jnp.sum(log_norm - chosen, axis=1, keepdims=True) / self.tokens
        loss = jnp.broadcast_to(loss, self.loss_out.shape)
        if half == FIRST:
            self.loss_out[...] = loss
        else:
            self.loss_out[...] += loss
        grad = (jnp.exp(logits - log_norm) - jnp.where(wanted, 1.0, 0.0)) / self.tokens
        grad = grad.astype(jnp.bfloat16)
        self.logit_grad[:, pl.ds(half * HALF, HALF)] = grad
        yield

        @pl.loop(0, self.depth // TILE)
        def _(n):
            columns = pl.ds(pl.multiple_of(n * TILE, TILE), TILE)
            self.store_partial(half, columns, trans_times(grad, self.table[:, columns]))

        keep.wait()
        yield

    def feed_back(self, layer, half):
        own = pl.ds(half * HALF, HALF)
        edge, tail = self.edge, self.tail
        active_grad = times_trans(self.rows(half), self.down_weight[layer])
        yield

        def back(outer, gate, up):
            sigmoid = jax.nn.sigmoid(gate)
            gate_grad = outer * up * sigmoid * (1.0 + gate * (1.0 - sigmoid))
            return gate_grad.astype(jnp.bfloat16), (outer * gate * sigmoid).astype(jnp.bfloat16)

        gate_grad, up_grad = back(
            active_grad[:, :edge],
            self.kept[layer, own, :edge],
            self.kept[layer, own, edge : 2 * edge],
        )
        self.both[:, :edge] = gate_grad
        self.both[:, edge : 2 * edge] = up_grad
        if tail:
            last = self.kept[layer, own, 2 * edge :]
            gate_grad, up_grad = back(active_grad[:, edge:], last[:, :tail], last[:, tail:])
            self.both[:, 2 * edge :] = jnp.concatenate([gate_grad, up_grad], axis=1)
        yield
        tiles = self.depth // TILE
        each = self.feed_weight.shape[1] // tiles
        for low, high in self.tiles(tiles, 3):

            @pl.loop(low, high)
            def _(n):
                columns = pl.ds(pl.multiple_of(n * TILE, TILE), TILE)
                block = self.feed_weight[layer, pl.ds(n * each, each)].reshape(TILE, -1)
                self.store_partial(half, columns, times_trans(self.both[...], block))

            yield

    def attention_back(self, layer, half):
        own = pl.ds(half * HALF, HALF)
        scale = HEAD_DIM ** (-0.5)
        mixed_grad = times_trans(self.rows(half), self.out_weight[layer]).astype(jnp.bfloat16)
        yield
        queries, pairs = self.queries[layer, own, :], self.pairs[layer, own, :]
        key, value = pairs[:, :HEAD_DIM], pairs[:, HEAD_DIM:]
        mask = causal_blocks(HALF, LEN)
        query_grads, key_grad, value_grad = [], 0.0, 0.0
        for start in range(0, self.q_width, HEAD_DIM):
            query = queries[:, start : start + HEAD_DIM]
            outer = mixed_grad[:, start : start + HEAD_DIM]
            weights = attend(query, key, mask, scale)
            weight_grad = times_trans(outer, value)
            score_grad = weights * (
                weight_grad - jnp.sum(weights * weight_grad, axis=1, keepdims=True)
            )
            score_grad = score_grad.astype(jnp.bfloat16)
            query_grads.append(matmul(score_grad, key) * scale)
            key_grad = key_grad + trans_times(score_grad, query) * scale
            value_grad = value_grad + trans_times(weights.astype(jnp.bfloat16), outer)
        query_grad = jnp.concatenate(query_grads, axis=1)
        query_grad = turn(query_grad, [self.back_tables[n] for n in range(3)])
        pair_grad = jnp.concatenate([key_grad, value_grad], axis=1)
        pair_grad = turn(pair_grad, [self.back_tables[n] for n in range(3, 6)])
        both = jnp.concatenate([query_grad, pair_grad], axis=1).astype(jnp.bfloat16)
        yield
        tiles = self.depth // TILE
        each = self.head_weight.shape[1] // tiles

        @pl.loop(0, tiles)
        def _(n):
            columns = pl.ds(pl.multiple_of(n * TILE, TILE), TILE)
            block = self.head_weight[layer, pl.ds(n * each, each)].reshape(TILE, -1)
            self.store_partial(half, columns, times_trans(both, block))

        yield

    def normed(self, values, gain):
        return (values * root_inverse(values) * gain[...]).astype(jnp.bfloat16)

    def close_inject(self, half, total):
        hidden = total.astype(jnp.bfloat16)
        self.hidden[0, half] = hidden
        return self.normed(hidden.astype(jnp.float32), self.gains[0])

    def close_attention(self, layer):
        def close(half, total):
            middle = self.hidden[layer, half].astype(jnp.float32) + total
            self.middle[layer, half] = middle
            return self.normed(middle, self.gains[2 + layer])

        return close

    def close_feed(self, layer):
        def close(half, total):
            hidden = (self.middle[layer, half] + total).astype(jnp.bfloat16)
            self.hidden[layer + 1, half] = hidden
            gain = self.gains[4] if layer else self.gains[1]
            return self.normed(hidden.astype(jnp.float32), gain)

        return close

    def close_head(self, half, total):
        hidden = self.hidden[2, half].astype(jnp.float32)
        grad = reciprocal_root_backward(hidden, root_inverse(hidden), self.gains[4][...], total)
        grad = grad.astype(jnp.bfloat16)
        self.grad[half] = grad.astype(jnp.float32)
        return grad

    def close_feed_back(self, layer):
        def close(half, total):
            middle = self.middle[layer, half]
            grad = self.grad[half] + reciprocal_root_backward(
                middle, root_inverse(middle), self.gains[2 + layer][...], total
            )
            self.grad[half] = grad
            return grad.astype(jnp.bfloat16)

        return close

    def close_attention_back(self, layer):
        def close(half, total):
            hidden = self.hidden[layer, half].astype(jnp.float32)
            grad = self.grad[half] + reciprocal_root_backward(
                hidden, root_inverse(hidden), self.gains[layer][...], total
            )
            grad = grad.astype(jnp.bfloat16)
            self.grad[half] = grad.astype(jnp.float32)
            return grad

        return close


def decode_kernel(shape, names, *refs):
    refs = dict(zip(names, refs))
    refs["pieces"] = [refs.pop(name) for name in ("own_one", "y_one", "core_one", "beyond_one")]
    refs["gains"] = [refs["gain_rows"].at[pl.ds(n, 1)] for n in range(5)]
    this = Decoder(shape, refs)
    this.greet()
    this.moving = {}
    this.weight_copies()
    phases = [(this.inject, this.close_inject, 1)]
    for layer in range(2):
        phases.append((functools.partial(this.attention, layer), this.close_attention(layer), 1))
        phases.append((functools.partial(this.feed, layer), this.close_feed(layer), 2))
    phases.append((this.head, this.close_head, 2))
    for layer in (1, 0):
        phases.append((functools.partial(this.feed_back, layer), this.close_feed_back(layer), 2))
        phases.append(
            (functools.partial(this.attention_back, layer), this.close_attention_back(layer), 1)
        )
    gathers = {}
    sent = None
    for work, close, parts in phases:
        for half in (FIRST, SECOND):
            gather = gathers.pop(half, iter(()))
            reduce = sent or iter(())
            for kind in ORDER:
                next(gather if kind == "g" else reduce, None)
            for count, _ in enumerate(work(half)):
                if count + 1 == parts:
                    finish(reduce)
            finish(reduce)
            if sent is not None:
                gathers[1 - half] = this.gather(1 - half)
            this.send(half)
            sent = this.reduce(half, close)
    finish(gathers.pop(FIRST), sent)
    finish(this.gather(SECOND))
    outs = [
        pltpu.make_async_copy(
            this.gathered.at[half], this.grad_out.at[half], this.keep_sem.at[half]
        )
        for half in (FIRST, SECOND)
    ]
    for copy in outs:
        copy.start()
    for copy in outs:
        copy.wait()


def decode(outer, collective_id, tokens, weights, out_source, down_source, gains, tables, table, own_rows, ids, wanted):
    q_width, depth = out_source.shape[1:]
    share = down_source.shape[1]
    groups, quarter = weights[0].shape[:2]
    entries = table.shape[0]
    low, full = jnp.bfloat16, jnp.float32
    block = (2, TEAM, EACH, depth)
    slots = pltpu.VMEM((2, LINES, EACH, depth), low)
    inputs = dict(
        own_rows=own_rows,
        ids=ids,
        wanted=wanted,
        table=table,
        gain_rows=gains,
        tables=tables[0],
        back_tables=tables[1],
    )
    far_inputs = dict(
        zip(("own_one", "y_one", "core_one", "beyond_one", "own_two"), weights),
        out_source=out_source,
        down_source=down_source,
    )
    outputs = dict(
        normed_out=(jax.ShapeDtypeStruct(block, low), ANYWHERE),
        grad_out=(jax.ShapeDtypeStruct(block, low), ANYWHERE),
        logit_grad=(jax.ShapeDtypeStruct((entries, ROWS), low), IN_VMEM),
        loss_out=(jax.ShapeDtypeStruct((8, LANES), full), IN_VMEM),
    )
    scratch = dict(
        head_weight=pltpu.VMEM((2, groups, SECTIONS, quarter, q_width + LANES), low),
        feed_weight=pltpu.VMEM((2, groups, SECTIONS, quarter, 2 * share), low),
        out_weight=pltpu.VMEM((2, q_width, depth), low),
        down_weight=pltpu.VMEM((2, share, depth), low),
        gathered=pltpu.VMEM(block, low),
        partial=pltpu.VMEM(block, low),
        side=slots,
        pair=slots,
        far=slots,
        kept=pltpu.VMEM((2, ROWS, 2 * share), full),
        queries=pltpu.VMEM((2, ROWS, q_width), low),
        pairs=pltpu.VMEM((2, ROWS, LANES), low),
        active=pltpu.VMEM((HALF, share), low),
        both=pltpu.VMEM((HALF, 2 * share), low),
        hidden=pltpu.VMEM((3, 2, EACH, depth), low),
        middle=pltpu.VMEM((2, 2, EACH, depth), full),
        grad=pltpu.VMEM((2, EACH, depth), full),
        stats=pltpu.VMEM((2, TEAM, 8, HALF), full),
        load_sem=dma_sems(6, 4),
        share_send=dma_sems(2, 3),
        share_recv=dma_sems(2, 3),
        stats_send=dma_sems(2, TEAM),
        stats_recv=dma_sems(2, TEAM),
        keep_sem=dma_sems(2),
    )
    for name in ("side", "far", "out", "over"):
        scratch[name + "_send"] = dma_sems(2, LINES)
        scratch[name + "_recv"] = dma_sems(2, LINES)
    names = (*inputs, *far_inputs, *outputs, *scratch)
    return pl.pallas_call(
        functools.partial(decode_kernel, (outer, tokens, share, q_width, depth), names),
        out_shape=tuple(shape for shape, _ in outputs.values()),
        in_specs=[IN_VMEM] * len(inputs) + [ANYWHERE] * len(far_inputs),
        out_specs=tuple(spec for _, spec in outputs.values()),
        scratch_shapes=list(scratch.values()),
        compiler_params=settings(collective_id),
        name="decode",
    )(*inputs.values(), *far_inputs.values())


class Collector:
    def __init__(self, halves, refs):
        for name, ref in refs.items():
            setattr(self, name, ref)
        self.halves = halves
        self.section, self.partner, self.across, self.wide, self.wide_at = all_places(halves)
        self.groups = ((1, 1), (1, 0), (0, 1), (0, 0))

    def greet(self):
        beside = self.wide + 1 - 2 * (self.wide % 2)
        peers = [{"section": self.partner}, {"section": self.across}, {"wide": beside}]
        greet(peers + [{"wide": self.wide_at(j)} for j in range(1, self.halves)])

    def steps(self, n):
        return steps_of(n % 2 == 0, self.section, self.partner, self.across, self.wide)

    def block(self, n, home, flip_b, flip_a, j):
        (_, y_a, x_a), (_, y_b, x_b) = self.steps(n)
        flips_y = (y_a and flip_a) or (y_b and flip_b)
        flips_x = (x_a and flip_a) or (x_b and flip_b)
        section, wide = owner_of(home, flips_y, flips_x, self.wide_at(j))
        return self.partials[n].at[section * (2 * self.halves) + wide]

    def core_copy(self, n, fb, fa, j):
        slot = (fb * 2 + fa) * self.halves + j
        return remote(
            self.block(n, self.partner, fb, fa, j),
            self.core_in[n].at[slot],
            self.core_send.at[n, slot],
            self.core_recv.at[n, slot],
            {"section": self.partner},
        )

    def b_copy(self, n, fa, j):
        _, (peer, _, _) = self.steps(n)
        slot = fa * self.halves + j
        return remote(
            self.block(n, self.section, 1, fa, j),
            self.b_in[n].at[slot],
            self.b_send.at[n, slot],
            self.b_recv.at[n, slot],
            peer,
        )

    def a_copy(self, n, j):
        (peer, _, _), _ = self.steps(n)
        return remote(
            self.block(n, self.section, 0, 1, j),
            self.a_in[n].at[j],
            self.a_send.at[n, j],
            self.a_recv.at[n, j],
            peer,
        )

    def z_copy(self, n, j):
        return remote(
            self.block(n, self.section, 0, 0, j),
            self.z_in[n].at[j],
            self.z_send.at[n, j],
            self.z_recv.at[n, j],
            {"wide": self.wide_at(j)},
        )

    def add(self, block, more):
        block[...] = (block[...].astype(jnp.float32) + more.astype(jnp.float32)).astype(jnp.bfloat16)

    def over(self, first, body):
        def step(j, carry):
            body(j)
            return carry

        lax.fori_loop(first, self.halves, step, 0)

    def start(self, n):
        for fb, fa in self.groups:
            self.over(0, lambda j: self.core_copy(n, fb, fa, j).start())

    def sum_core(self, n):
        for fb, fa in self.groups:

            def body(j):
                slot = (fb * 2 + fa) * self.halves + j
                self.core_copy(n, fb, fa, j).wait_recv()
                self.add(self.block(n, self.section, fb, fa, j), self.core_in[n][slot])
                if fb:
                    self.b_copy(n, fa, j).start()

            self.over(0, body)

    def sum_b(self, n):
        for fa in (1, 0):

            def body(j):
                self.b_copy(n, fa, j).wait_recv()
                block = self.block(n, self.section, 0, fa, j)
                self.add(block, self.b_in[n][fa * self.halves + j])
                if fa:
                    self.a_copy(n, j).start()

            self.over(0, body)

    def sum_a(self, n):
        def body(j):
            self.a_copy(n, j).wait_recv()
            self.add(self.block(n, self.section, 0, 0, j), self.a_in[n][j])
            self.z_copy(n, j).start()

        self.over(1, body)
        self.a_copy(n, 0).wait_recv()
        own = self.block(n, self.section, 0, 0, 0)[...]
        self.sums[n][...] = own.astype(jnp.float32) + self.a_in[n][0].astype(jnp.float32)

    def sum_lines(self, n):
        def body(j):
            self.z_copy(n, j).wait_recv()
            self.sums[n][...] += self.z_in[n][j].astype(jnp.float32)

        self.over(1, body)

    def drain(self, n):
        def body(j):
            for fb, fa in self.groups:
                self.core_copy(n, fb, fa, j).wait_send()
            self.b_copy(n, 0, j).wait_send()
            self.b_copy(n, 1, j).wait_send()
            self.a_copy(n, j).wait_send()

        self.over(0, body)
        self.over(1, lambda j: self.z_copy(n, j).wait_send())


EMBED, EXPAND, REDUCE, FRONT, REAR = range(5)


def hyper_collect_kernel(slots, halves, names, *refs):
    refs = dict(zip(names, refs))
    for name in ("sums", "partials", "core_in", "b_in", "a_in", "z_in"):
        refs[name] = [refs.pop(f"{name}{n}") for n in range(5)]
    this = Collector(halves, refs)
    first, second, third, vectors = this.first, this.second, this.third, this.vectors
    entered, outcome_low, feed_grad = this.entered, this.outcome_low, this.feed_grad
    width = this.pieces.shape[1]
    count, feed = this.pieces.shape[0], third.shape[0]
    depth = this.table_grad.shape[1]
    head = width // HYPER_HEAD_COUNT
    scale = head ** (-0.5)
    this.greet()

    def store(n, columns, values):
        block = this.partials[n]
        block[:, :, columns] = values.astype(jnp.bfloat16).reshape(
            block.shape[0], block.shape[1], values.shape[1]
        )

    grad_low = this.table_grad[...].astype(jnp.bfloat16)
    pooled_turned = jnp.transpose(this.pooled[...].astype(jnp.float32)).astype(jnp.bfloat16)
    for start in range(0, depth, TILE):
        store(EMBED, pl.ds(start, TILE), matmul(pooled_turned, grad_low[:, start : start + TILE]))
    this.start(EMBED)
    pooled_grad = times_trans(grad_low, second[:, pl.ds(0, depth)]) / slots
    outcome_grad = jnp.broadcast_to(pooled_grad[:, None, :], (count // slots, slots, width))
    outcome_grad = outcome_grad.reshape(count, width)
    outcome_low[...] = outcome_grad.astype(jnp.bfloat16)
    normed, inverse = center_norm(this.middle[...])
    entered[...] = jnp.transpose(normed * vectors[2:3] + vectors[3:4]).astype(jnp.bfloat16)
    feed_grad[...] = jnp.zeros_like(feed_grad)
    this.sum_core(EMBED)

    def feed_tiles(low, high):
        @pl.loop(low, high)
        def _(n):
            start = pl.multiple_of(n * TILE, TILE)
            tile = pl.ds(start, TILE)
            columns = pl.ds(pl.multiple_of(4 * width + start, TILE), TILE)
            values = this.expanded[:, tile]
            erf = 0.5 * (1.0 + lax.erf(values * inv_root_two))
            active = (values * erf).astype(jnp.bfloat16)
            block = this.partials[REDUCE]
            owners = TILE // block.shape[1]
            turned = trans_times(active, outcome_low[...]).astype(jnp.bfloat16)
            block[pl.ds(n * owners, owners)] = turned.reshape(owners, block.shape[1], width)
            active_grad = times_trans(outcome_low[...], third[tile, :])
            slope = erf + values * jnp.exp(-0.5 * values * values) * inv_root_tau
            low_grad = (active_grad * slope).astype(jnp.bfloat16)
            store(EXPAND, tile, matmul(entered[...], low_grad))
            feed_grad[...] += times_trans(low_grad, first[:, columns])

    tiles = feed // TILE
    feed_tiles(0, tiles // 2)
    this.sum_b(EMBED)
    feed_tiles(tiles // 2, tiles)
    this.start(EXPAND)
    this.start(REDUCE)
    this.sum_a(EMBED)

    grad = feed_grad[...]
    scale_two = jnp.sum(grad * normed, axis=0, keepdims=True)
    shift_two = jnp.sum(grad, axis=0, keepdims=True)
    middle_grad = outcome_grad + center_back(normed, inverse, grad * vectors[2:3])
    middle_low = middle_grad.astype(jnp.bfloat16)
    out_columns = pl.ds(3 * width, width)
    store(REAR, pl.ds(width, width), trans_times(this.mixed[...], middle_low))
    this.mixed_grad[...] = times_trans(middle_low, first[:, out_columns]).astype(jnp.bfloat16)
    mask = same_entry(CHUNK, slots)
    this.sum_core(EXPAND)

    def attention_chunks(low, high):
        @pl.loop(low, high)
        def _(n):
            rows = pl.ds(pl.multiple_of(n * CHUNK, CHUNK), CHUNK)
            block = this.heads[rows, :]
            outer_block = this.mixed_grad[rows, :]
            grads = [[], [], []]
            for start in range(0, width, head):
                query, key, value = (
                    block[:, part * width + start : part * width + start + head]
                    for part in range(3)
                )
                outer = outer_block[:, start : start + head]
                weights = attend(query, key, mask, scale)
                weight_grad = times_trans(outer, value)
                score_grad = weights * (
                    weight_grad - jnp.sum(weights * weight_grad, axis=1, keepdims=True)
                )
                score_grad = score_grad.astype(jnp.bfloat16)
                grads[0].append(matmul(score_grad, key) * scale)
                grads[1].append(trans_times(score_grad, query) * scale)
                grads[2].append(trans_times(weights.astype(jnp.bfloat16), outer))
            for part in range(3):
                this.heads_grad[rows, pl.ds(part * width, width)] = jnp.concatenate(
                    grads[part], axis=1
                ).astype(jnp.bfloat16)

    chunks = count // CHUNK
    attention_chunks(0, chunks // 2)
    this.sum_core(REDUCE)
    this.sum_b(EXPAND)
    attention_chunks(chunks // 2, chunks)
    this.sum_b(REDUCE)

    normed, _ = center_norm(this.pieces[...].astype(jnp.float32))
    entered[...] = jnp.transpose(normed * vectors[0:1] + vectors[1:2]).astype(jnp.bfloat16)
    feed_grad[...] = jnp.zeros_like(feed_grad)
    for start in range(0, 3 * width, TILE):
        columns = pl.ds(start, TILE)
        low_grad = this.heads_grad[:, columns]
        target = (FRONT, start) if start < 2 * width else (REAR, start - 2 * width)
        store(target[0], pl.ds(target[1], TILE), matmul(entered[...], low_grad))
        feed_grad[...] += times_trans(low_grad, first[:, columns])
        if start + TILE == 2 * width:
            this.start(FRONT)
            this.sum_a(EXPAND)
            this.sum_a(REDUCE)

    grad = feed_grad[...]
    scale_one = jnp.sum(grad * normed, axis=0, keepdims=True)
    shift_one = jnp.sum(grad, axis=0, keepdims=True)
    row = lax.broadcasted_iota(jnp.int32, (LANES, width), 0)
    summed = jnp.zeros((LANES, width), jnp.float32)
    for n, item in enumerate((scale_one, shift_one, scale_two, shift_two)):
        summed = jnp.where(row == n, item, summed)
    store(REAR, pl.ds(2 * width, LANES), jnp.transpose(summed))
    this.start(REAR)
    this.sum_core(FRONT)
    this.sum_core(REAR)
    for n in (EMBED, EXPAND, REDUCE):
        this.sum_lines(n)
    this.sum_b(FRONT)
    this.sum_b(REAR)
    this.sum_a(FRONT)
    this.sum_a(REAR)
    this.sum_lines(FRONT)
    this.sum_lines(REAR)
    for n in range(5):
        this.drain(n)


def hyper_collect(collective_id, wides, pieces, slots, params, stored, table_grad):
    count, width = pieces.shape
    first, second, third, vectors = params
    depth, feed = table_grad.shape[1], third.shape[0]
    devices, halves = SECTIONS * wides, wides // 2
    low, full = jnp.bfloat16, jnp.float32
    rows = width // devices
    shapes = [
        (rows, depth),
        (rows, feed),
        (feed // devices, width),
        (rows, 2 * width),
        (rows, 2 * width + LANES),
    ]
    inputs = dict(
        table_grad=table_grad,
        pieces=pieces,
        first=first,
        second=second,
        third=third,
        vectors=vectors,
    )
    inputs.update(zip(("heads", "mixed", "middle", "expanded", "pooled"), stored))
    outputs = {f"sums{n}": jax.ShapeDtypeStruct(shape, full) for n, shape in enumerate(shapes)}
    scratch = dict(
        entered=pltpu.VMEM((width, count), low),
        outcome_low=pltpu.VMEM((count, width), low),
        feed_grad=pltpu.VMEM((count, width), full),
        heads_grad=pltpu.VMEM((count, 3 * width), low),
        mixed_grad=pltpu.VMEM((count, width), low),
    )
    for name, number in (
        ("partials", devices),
        ("core_in", 4 * halves),
        ("b_in", 2 * halves),
        ("a_in", halves),
        ("z_in", halves),
    ):
        for n, shape in enumerate(shapes):
            scratch[f"{name}{n}"] = pltpu.VMEM((number,) + shape, low)
    for name, number in (("core", 4), ("b", 2), ("a", 1), ("z", 1)):
        scratch[name + "_send"] = dma_sems(5, number * halves)
        scratch[name + "_recv"] = dma_sems(5, number * halves)
    return pl.pallas_call(
        functools.partial(hyper_collect_kernel, slots, halves, (*inputs, *outputs, *scratch)),
        out_shape=tuple(outputs.values()),
        in_specs=[IN_VMEM] * len(inputs),
        out_specs=(IN_VMEM,) * len(outputs),
        scratch_shapes=list(scratch.values()),
        compiler_params=settings(collective_id),
        name="hyper_collect",
    )(*inputs.values())


def team_groups(wides, outer):
    return [[rank * outer + team for team in range(outer)] for rank in range(wides // outer)]


SWAP_Y = [(source, (source + 2) % SECTIONS) for source in range(SECTIONS)]
SWAP_CORE = [(source, source + 1 - 2 * (source % 2)) for source in range(SECTIONS)]


def together(*items):
    return lax.optimization_barrier(items)


def all_teams(pieces, outer, groups):
    if outer == 1:
        return pieces
    pieces = [
        lax.all_gather(piece, "wide", axis=1, axis_index_groups=groups) for piece in pieces
    ]
    return [piece.reshape((-1,) + piece.shape[2:]) for piece in pieces]


def shards(
    token_ids,
    targets,
    slot_ids,
    group_ids,
    group_offsets,
    piece_table,
    prenorm_gain,
    prenorm_bias,
    query_map,
    key_map,
    value_map,
    output_map,
    midnorm_gain,
    midnorm_bias,
    expand_map,
    reduce_map,
    embed_map,
    attention_gain,
    query_weight,
    key_weight,
    value_weight,
    output_weight,
    feed_gain,
    gate_weight,
    up_weight,
    down_weight,
    final_gain,
):
    wides = lax.axis_size("wide")
    outer = wides // TEAM
    groups = team_groups(wides, outer)
    section_index = lax.axis_index("section")
    wide_index = lax.axis_index("wide")
    rank = wide_index // outer
    hyper_width, hyper_feed = piece_table.shape[1], expand_map.shape[1]
    model_width = embed_map.shape[1]
    total_tokens = wides * MB * LEN

    rank_groups = [[rank * outer + team for rank in range(TEAM)] for team in range(outer)]

    def to_ranks(block):
        return lax.all_to_all(
            block, "wide", 0, 0, axis_index_groups=rank_groups if outer > 1 else None, tiled=True
        )

    blocks = pack((query_weight, key_weight, value_weight, gate_weight, up_weight))
    own_one = to_ranks(blocks[0])

    vectors = jnp.stack([prenorm_gain, prenorm_bias, midnorm_gain, midnorm_bias], axis=1)
    vectors = jnp.pad(vectors, ((0, 0), (0, LANES - 4)))
    first = jnp.concatenate([query_map, key_map, value_map, output_map, expand_map], axis=1)
    second = jnp.concatenate([embed_map, vectors], axis=1)
    gains = jnp.concatenate([attention_gain, feed_gain], axis=0)
    gains = jnp.pad(gains, ((0, 16 - gains.shape[0]), (0, 0)))
    notes = jnp.concatenate([token_ids.reshape(1, -1), targets.reshape(1, -1)], axis=0)
    notes = jnp.pad(notes, ((0, 6), (0, 0)))
    first, second, third, gains, notes = spread(
        1,
        wides,
        outer,
        (first.astype(jnp.bfloat16), second.astype(jnp.bfloat16), reduce_map.astype(jnp.bfloat16)),
        (gains, notes),
    )
    first, own_one, block = together(first, own_one, blocks[1])
    own_two = to_ranks(block)
    y_one = lax.ppermute(own_one, "section", SWAP_Y)
    core_one = lax.ppermute(own_one, "section", SWAP_CORE)
    first = first.reshape(hyper_width, -1)
    second = second.reshape(hyper_width, -1)
    third = third.reshape(hyper_feed, hyper_width)
    vectors = second[:, model_width : model_width + 8].astype(jnp.float32).T
    params = (first, second, third, vectors)
    if outer > 1:
        gains = lax.all_gather(gains, "wide", axis=1, axis_index_groups=groups)
        gains = gains.reshape(-1, gains.shape[2], gains.shape[3])
        output_weight, down_weight = (
            lax.all_gather(item, "wide", axis=1, axis_index_groups=groups, tiled=True)
            for item in (output_weight, down_weight)
        )
    gains = gains.astype(jnp.float32).transpose(1, 0, 2).reshape(-1, model_width)
    final_scale = final_gain.astype(jnp.float32).reshape(1, model_width)
    gains = jnp.concatenate([gains[:4], final_scale, gains[:3]], axis=0)
    notes = lax.dynamic_slice_in_dim(notes, section_index * 2, 2, 0)
    ids, wanted = notes[:, 0].reshape(-1), notes[:, 1].reshape(-1)

    entries, slot_count = slot_ids.shape
    group_hits = (
        group_ids[:, None] == jnp.arange(group_offsets.shape[0], dtype=jnp.int32)[None, :]
    ).astype(jnp.int32)
    row_start = jnp.sum(group_hits * group_offsets[None, :], axis=1)
    piece_rows = (row_start[:, None] + slot_ids).reshape(-1)
    pieces = jnp.take(piece_table, piece_rows, axis=0)
    table_shard, hyper_stored = hyper_forward(pieces, slot_count, params)
    table_shard, y_one = together(table_shard, y_one)
    beyond_one = lax.ppermute(y_one, "section", SWAP_CORE)
    table_rows = section_gather(3, table_shard)
    if outer > 1:
        table_rows = lax.all_gather(table_rows, "wide", axis=1, axis_index_groups=groups)
    table_rows = table_rows.reshape(-1, model_width)
    wide_rows = rank * outer + jnp.arange(outer, dtype=jnp.int32)
    row_starts = (
        jnp.arange(SECTIONS, dtype=jnp.int32)[:, None] * wides + wide_rows[None, :]
    ) * entries
    own_rows = row_starts[:, :, None] + jnp.arange(entries, dtype=jnp.int32)[None, None, :]
    own_rows = own_rows.reshape(-1)
    own_rows = own_rows.reshape(-1, 1)

    def by_halves(numbers):
        return jnp.pad(numbers.reshape(2, -1), ((0, 6), (0, 0)))

    normed, grads, logit_grad, loss_block = decode(
        outer,
        4,
        total_tokens,
        all_teams((own_one, y_one, core_one, beyond_one, own_two), outer, groups),
        output_weight,
        down_weight,
        gains,
        (turn_tables(False), turn_tables(True)),
        table_rows,
        own_rows,
        by_halves(ids),
        by_halves(wanted),
    )

    hits = (own_rows == ids[None, :]).astype(jnp.bfloat16)
    table_part = matmul(logit_grad, normed.reshape(ROWS, model_width)) + matmul(
        hits, grads.reshape(ROWS, model_width)
    )
    table_part = table_part.astype(jnp.bfloat16).reshape(SECTIONS, outer, entries, model_width)
    if outer > 1:
        table_part = lax.psum_scatter(
            table_part.astype(jnp.float32),
            "wide",
            scatter_dimension=1,
            axis_index_groups=groups,
        ).astype(jnp.bfloat16)
        loss_block = lax.psum(loss_block, "wide", axis_index_groups=groups)
    table_grad, loss_block = section_sum(
        11, table_part.reshape(SECTIONS, entries, model_width), loss_block
    )
    mean_loss = loss_block[0, 0]
    if hyper_width // (SECTIONS * wides) % 16 == 0:
        grad_embed, grad_expand, grad_reduce, front, rear = hyper_collect(
            12, wides, pieces, slot_count, params, hyper_stored, table_grad
        )
    else:
        grads = hyper_backward(pieces, slot_count, params, hyper_stored, table_grad)
        grads = [item.reshape(SECTIONS, wides, -1, item.shape[1]) for item in grads]
        first, second, grad_reduce = collect(12, grads)
        grad_embed, grad_expand = second[:, :model_width], first[:, 4 * hyper_width :]
        front = first[:, : 2 * hyper_width]
        rear = jnp.concatenate(
            [first[:, 2 * hyper_width : 4 * hyper_width], second[:, model_width:]], axis=1
        )
    vectors = rear[:, 2 * hyper_width : 2 * hyper_width + 4]
    return (
        mean_loss,
        vectors[:, 0],
        vectors[:, 1],
        front[:, :hyper_width],
        front[:, hyper_width:],
        rear[:, :hyper_width],
        rear[:, hyper_width : 2 * hyper_width],
        vectors[:, 2],
        vectors[:, 3],
        grad_expand,
        grad_reduce,
        grad_embed,
    )


def solution(mesh):
    placed = (
        P("wide", None, None),
        P("wide", None, None),
        P(("section", "wide"), None),
        P(("section", "wide")),
        P(),
        P(),
        P(("section", "wide")),
        P(("section", "wide")),
        P(("section", "wide"), None),
        P(("section", "wide"), None),
        P(("section", "wide"), None),
        P(("section", "wide"), None),
        P(("section", "wide")),
        P(("section", "wide")),
        P(("section", "wide"), None),
        P(("section", "wide"), None),
        P(("section", "wide"), None),
        P(None, "wide"),
        P(None, "wide", None),
        P(None, "wide", None),
        P(None, "wide", None),
        P(None, "wide", None),
        P(None, "wide"),
        P(None, "wide", None),
        P(None, "wide", None),
        P(None, "wide", None),
        P(),
    )
    return jax.shard_map(
        shards,
        mesh=mesh,
        in_specs=placed,
        out_specs=(
            P(),
            P(("section", "wide")),
            P(("section", "wide")),
            P(("section", "wide"), None),
            P(("section", "wide"), None),
            P(("section", "wide"), None),
            P(("section", "wide"), None),
            P(("section", "wide")),
            P(("section", "wide")),
            P(("section", "wide"), None),
            P(("section", "wide"), None),
            P(("section", "wide"), None),
        ),
        check_vma=False,
    )
```

```python
import functools

import jax
import jax.numpy as jnp
from jax import lax
from jax.experimental import pallas as pl
from jax.experimental.pallas import tpu as pltpu
from jax.sharding import PartitionSpec as P

HEAD_DIM = 64
HYPER_HEAD_COUNT = 8
MB = 2
LEN = 64
TEAM = 8
SECTIONS = 4
ROWS = MB * LEN * TEAM // SECTIONS
HALF = ROWS // 2
EACH = HALF // TEAM
LINES = TEAM // 2
FIRST, SECOND = 0, 1
LANES = 128
MESH_IDS = pl.DeviceIdType.MESH
ANYWHERE = pl.BlockSpec(memory_space=pl.ANY)
IN_VMEM = pl.BlockSpec(memory_space=pltpu.VMEM)
VMEM_LIMIT = 56 * 1024 * 1024

norm_eps = 1e-05
inv_root_two = 0.7071067811865476
inv_root_tau = 0.3989422804014327


def matmul(former, latter):
    return jnp.dot(former, latter, preferred_element_type=jnp.float32)


def times_trans(former, latter):
    return lax.dot_general(
        former, latter, (((1,), (1,)), ((), ())), preferred_element_type=jnp.float32
    )


def trans_times(former, latter):
    return lax.dot_general(
        former, latter, (((0,), (0,)), ((), ())), preferred_element_type=jnp.float32
    )


def center_norm(values):
    center = values - jnp.mean(values, axis=-1, keepdims=True)
    inverse = lax.rsqrt(jnp.mean(center * center, axis=-1, keepdims=True) + norm_eps)
    return (center * inverse, inverse)


def center_back(normed, inverse, normed_grad):
    mean_grad = jnp.mean(normed_grad, axis=-1, keepdims=True)
    mean_mix = jnp.mean(normed_grad * normed, axis=-1, keepdims=True)
    return inverse * (normed_grad - mean_grad - normed * mean_mix)


def root_inverse(values):
    return lax.rsqrt(jnp.mean(values * values, axis=-1, keepdims=True) + norm_eps)


def reciprocal_root_backward(values, inverse, gain_vec, outer_grad):
    scaled = outer_grad * gain_vec
    mixing = jnp.mean(scaled * values, axis=-1, keepdims=True)
    return inverse * scaled - values * inverse * inverse * inverse * mixing


def rope_tables(positions, head_width):
    halfway = head_width // 2
    frequency = jnp.exp(
        -jnp.log(10000.0) * (2.0 * jnp.arange(halfway, dtype=jnp.float32) / head_width)
    )
    angles = jnp.arange(positions, dtype=jnp.float32)[:, None] * frequency[None, :]
    angles = jnp.concatenate([angles, angles], axis=1)
    return (jnp.cos(angles), jnp.sin(angles))


def greet(peers):
    barrier = pltpu.get_barrier_semaphore()
    for peer in peers:
        pl.semaphore_signal(barrier, inc=1, device_id=peer, device_id_type=MESH_IDS)
    pl.semaphore_wait(barrier, len(peers))


def remote(source, target, send, recv, peer):
    return pltpu.make_async_remote_copy(
        src_ref=source,
        dst_ref=target,
        send_sem=send,
        recv_sem=recv,
        device_id=peer,
        device_id_type=MESH_IDS,
    )


def settings(collective_id):
    return pltpu.CompilerParams(
        collective_id=collective_id, has_side_effects=True, vmem_limit_bytes=VMEM_LIMIT
    )


def dma_sems(*shape):
    return pltpu.SemaphoreType.DMA(shape)


def section_places():
    section = lax.axis_index("section")
    core = section % 2
    partner = section + 1 - 2 * core
    across = (section + 2) % SECTIONS
    return section, partner, across


def section_gather_kernel(block, gathered, keep_sem, send, recv):
    section, partner, across = section_places()
    greet([{"section": partner}, {"section": across}])
    keep = pltpu.make_async_copy(block, gathered.at[section], keep_sem)
    near = remote(block, gathered.at[section], send.at[0], recv.at[0], {"section": partner})
    far = remote(block, gathered.at[section], send.at[1], recv.at[1], {"section": across})
    on = remote(
        gathered.at[across], gathered.at[across], send.at[2], recv.at[2], {"section": partner}
    )
    far.start()
    near.start()
    keep.start()
    far.wait_recv()
    on.start()
    near.wait()
    on.wait()
    far.wait_send()
    keep.wait()


def section_gather(collective_id, block):
    return pl.pallas_call(
        section_gather_kernel,
        out_shape=jax.ShapeDtypeStruct((SECTIONS,) + block.shape, block.dtype),
        in_specs=[ANYWHERE],
        out_specs=ANYWHERE,
        scratch_shapes=[pltpu.SemaphoreType.DMA, dma_sems(3), dma_sems(3)],
        compiler_params=settings(collective_id),
        name="section_gather",
    )(block)


def section_sum_kernel(partial, loss, summed, loss_sum, own, near, pair, far, loss_near, loss_pair, loss_far, load_sem, send, recv):
    section, partner, across = section_places()
    beyond = (partner + 2) % SECTIONS
    greet([{"section": partner}, {"section": across}])
    loads = [
        pltpu.make_async_copy(partial.at[section], own.at[0], load_sem.at[0]),
        pltpu.make_async_copy(partial.at[across], own.at[1], load_sem.at[1]),
    ]
    nears = [
        remote(partial.at[partner], near.at[0], send.at[0], recv.at[0], {"section": partner}),
        remote(partial.at[beyond], near.at[1], send.at[1], recv.at[1], {"section": partner}),
        remote(loss, loss_near, send.at[2], recv.at[2], {"section": partner}),
    ]
    fars = [
        remote(pair, far, send.at[3], recv.at[3], {"section": across}),
        remote(loss_pair, loss_far, send.at[4], recv.at[4], {"section": across}),
    ]
    for j in (1, 2, 0):
        nears[j].start()
    loads[1].start()
    loads[0].start()
    loads[1].wait()
    nears[1].wait_recv()
    pair[...] = (own[1].astype(jnp.float32) + near[1].astype(jnp.float32)).astype(jnp.bfloat16)
    fars[0].start()
    nears[2].wait_recv()
    loss_pair[...] = loss[...] + loss_near[...]
    fars[1].start()
    loads[0].wait()
    nears[0].wait_recv()
    total = own[0].astype(jnp.float32) + near[0].astype(jnp.float32)
    fars[0].wait_recv()
    summed[...] = total + far[...].astype(jnp.float32)
    fars[1].wait_recv()
    loss_sum[...] = loss_pair[...] + loss_far[...]
    for copy in nears + fars:
        copy.wait_send()


def section_sum(collective_id, partial, loss):
    shape = partial.shape[1:]
    low, low_two = pltpu.VMEM(shape, jnp.bfloat16), pltpu.VMEM((2,) + shape, jnp.bfloat16)
    number = pltpu.VMEM(loss.shape, jnp.float32)
    return pl.pallas_call(
        section_sum_kernel,
        out_shape=(
            jax.ShapeDtypeStruct(shape, jnp.float32),
            jax.ShapeDtypeStruct(loss.shape, jnp.float32),
        ),
        in_specs=[ANYWHERE, IN_VMEM],
        out_specs=(IN_VMEM, IN_VMEM),
        scratch_shapes=[low_two, low_two, low, low, number, number, number]
        + [dma_sems(2), dma_sems(5), dma_sems(5)],
        compiler_params=settings(collective_id),
        name="section_sum",
    )(partial, loss)


def all_places(halves):
    section, partner, across = section_places()
    wide = lax.axis_index("wide")
    line, column = wide // 2, wide % 2

    def wide_at(j):
        return ((line + j) % halves) * 2 + column

    return section, partner, across, wide, wide_at


def steps_of(x_first, section, partner, across, wide):
    column_flip = wide + 1 - 2 * (wide % 2)
    x_step = ({"wide": column_flip}, False, True)
    y_step = ({"section": across}, True, False)
    return (x_step, y_step) if x_first else (y_step, x_step)


def owner_of(home, flips_y, flips_x, wide_block):
    section = (home + 2) % SECTIONS if flips_y else home
    return section, (wide_block + 1 - 2 * (wide_block % 2) if flips_x else wide_block)


def spread_kernel(count, halves, outer, work, *refs):
    blocks, notes, columns = refs[:count], refs[count : count + 2], refs[count + 2 : count + 4]
    refs = refs[count + 4 :]
    extra, refs = refs[: work.inputs], refs[work.inputs :]
    gathereds, notes_out, columns_out = refs[:count], refs[count : count + 2], refs[count + 2 : count + 4]
    refs = refs[count + 4 :]
    extra, refs = extra + refs[: work.outputs], refs[work.outputs :]
    (
        keep_sem,
        note_keep,
        note_send,
        note_recv,
        z_send,
        a_send,
        b_send,
        c_send,
        z_recv,
        a_recv,
        b_recv,
        c_recv,
    ) = refs[:12]
    section, partner, across, wide, wide_at = all_places(halves)
    rank, team = wide // outer, wide % outer
    members = [None] + [{"wide": (rank + k) % TEAM * outer + team} for k in range(1, TEAM)]
    beside = wide + 1 - 2 * (wide % 2)
    barrier = pltpu.get_barrier_semaphore()
    for peer in ({"section": partner}, {"section": across}, {"wide": beside}):
        pl.semaphore_signal(barrier, inc=1, device_id=peer, device_id_type=MESH_IDS)

    def hello(j, carry):
        peer = {"wide": wide_at(j)}
        pl.semaphore_signal(barrier, inc=1, device_id=peer, device_id_type=MESH_IDS)
        return carry

    lax.fori_loop(1, halves, hello, 0)
    for peer in members[1:]:
        pl.semaphore_signal(barrier, inc=1, device_id=peer, device_id_type=MESH_IDS)
    pl.semaphore_wait(barrier, 3 + halves - 1 + TEAM - 1)
    note_keeps = [
        pltpu.make_async_copy(notes[m], notes_out[m].at[rank], note_keep.at[m]) for m in range(2)
    ]
    note_copies = [
        remote(notes[m], notes_out[m].at[rank], note_send.at[m, k], note_recv.at[m, k], members[k])
        for m in range(2)
        for k in range(1, TEAM)
    ]
    column_copies = []
    for layer in range(2):
        column_copies.append(
            pltpu.make_async_copy(
                columns[layer].at[rank], columns_out[layer].at[rank], note_keep.at[2 + layer]
            )
        )
        column_copies += [
            remote(
                columns[layer].at[(rank + k) % TEAM],
                columns_out[layer].at[rank],
                note_send.at[2 + layer, k],
                note_recv.at[2 + layer, k],
                members[k],
            )
            for k in (4, 3, 5, 2, 6, 1, 7)
        ]
    for copy in note_keeps + note_copies:
        copy.start()

    keeps = [
        pltpu.make_async_copy(blocks[n], gathereds[n].at[section, wide], keep_sem.at[n])
        for n in range(count)
    ]

    def z_copy(n, j):
        return remote(
            blocks[n],
            gathereds[n].at[section, wide],
            z_send.at[n, j],
            z_recv.at[n, j],
            {"wide": wide_at(j)},
        )

    def a_copy(n, j):
        (peer, _, _), _ = steps_of(n == 0, section, partner, across, wide)
        block = gathereds[n].at[section, wide_at(-j)]
        return remote(block, block, a_send.at[n, j], a_recv.at[n, j], peer)

    def b_copy(n, flip, j):
        (_, y_a, x_a), (peer, _, _) = steps_of(n == 0, section, partner, across, wide)
        place = owner_of(section, y_a and flip, x_a and flip, wide_at(-j))
        block = gathereds[n].at[place[0], place[1]]
        slot = j + (halves if flip else 0)
        return remote(block, block, b_send.at[n, slot], b_recv.at[n, slot], peer)

    def c_copy(n, which):
        home = (section + 2) % SECTIONS if which else section
        block = gathereds[n].at[home]
        return remote(
            block, block, c_send.at[n, which], c_recv.at[n, which], {"section": partner}
        )

    for keep in keeps:
        keep.start()

    def start_z(j, carry):
        for n in range(count):
            z_copy(n, j).start()
        return carry

    lax.fori_loop(1, halves, start_z, 0)
    for n in range(count):
        keeps[n].wait()
        a_copy(n, 0).start()
        b_copy(n, False, 0).start()

    def pass_z(j, carry):
        for n in range(count):
            z_copy(n, j).wait_recv()
            a_copy(n, j).start()
            b_copy(n, False, j).start()
        return carry

    lax.fori_loop(1, halves, pass_z, 0)
    for copy in column_copies:
        copy.start()

    def pass_a(j, carry):
        for n in range(count):
            a_copy(n, j).wait_recv()
            b_copy(n, True, j).start()
        return carry

    lax.fori_loop(0, halves, pass_a, 0)

    def settle_b(j, carry):
        for n in range(count):
            for flip in (False, True):
                b_copy(n, flip, j).wait_recv()
        return carry

    c_copy(0, 0).start()
    lax.fori_loop(0, halves, settle_b, 0)
    c_copy(0, 1).start()
    for n in range(1, count):
        c_copy(n, 0).start()
        c_copy(n, 1).start()
    for n in range(count):
        c_copy(n, 0).wait()
        c_copy(n, 1).wait()

    def drain(j, carry):
        for n in range(count):
            a_copy(n, j).wait_send()
            b_copy(n, False, j).wait_send()
            b_copy(n, True, j).wait_send()
        return carry

    lax.fori_loop(0, halves, drain, 0)

    def drain_z(j, carry):
        for n in range(count):
            z_copy(n, j).wait_send()
        return carry

    lax.fori_loop(1, halves, drain_z, 0)
    work.run(gathereds, extra + refs[12:])
    for copy in note_keeps + note_copies + column_copies:
        copy.wait()


class Work:
    def __init__(self, run=None, operands=(), outs=(), scratch=()):
        self.body, self.operands, self.outs, self.scratch = run, operands, outs, scratch
        self.inputs, self.outputs = len(operands), len(outs)

    def run(self, gathereds, refs):
        if self.body is not None:
            self.body(gathereds, *refs)


def spread(collective_id, wides, outer, blocks, notes, columns, work):
    count, halves = len(blocks), wides // 2
    place = ANYWHERE if work.body is None else IN_VMEM
    return pl.pallas_call(
        functools.partial(spread_kernel, count, halves, outer, work),
        out_shape=tuple(
            jax.ShapeDtypeStruct((SECTIONS, wides) + block.shape, block.dtype) for block in blocks
        )
        + tuple(jax.ShapeDtypeStruct((TEAM,) + note.shape, note.dtype) for note in notes)
        + tuple(jax.ShapeDtypeStruct(item.shape, item.dtype) for item in columns)
        + tuple(jax.ShapeDtypeStruct(shape, kind) for shape, kind in work.outs),
        in_specs=[ANYWHERE] * (count + 4) + [IN_VMEM] * work.inputs,
        out_specs=(place,) * count + (ANYWHERE,) * 4 + (IN_VMEM,) * work.outputs,
        scratch_shapes=[dma_sems(count), dma_sems(4), dma_sems(4, TEAM), dma_sems(4, TEAM)]
        + [
            dma_sems(count, halves),
            dma_sems(count, halves),
            dma_sems(count, 2 * halves),
            dma_sems(count, 2),
        ]
        * 2
        + list(work.scratch),
        compiler_params=settings(collective_id),
        name="spread",
    )(*blocks, *notes, *columns, *work.operands)


def collect_kernel(count, halves, *refs):
    partials, sums = refs[:count], refs[count : 2 * count]
    keeps, c_in, b_in, a_in, z_in = (refs[(2 + k) * count : (3 + k) * count] for k in range(5))
    load_sem, c_send, b_send, a_send, z_send, c_recv, b_recv, a_recv, z_recv = refs[7 * count :]
    section, partner, across, wide, wide_at = all_places(halves)
    beside = wide + 1 - 2 * (wide % 2)
    barrier = pltpu.get_barrier_semaphore()
    for peer in ({"section": partner}, {"section": across}, {"wide": beside}):
        pl.semaphore_signal(barrier, inc=1, device_id=peer, device_id_type=MESH_IDS)

    def hello(j, carry):
        peer = {"wide": wide_at(j)}
        pl.semaphore_signal(barrier, inc=1, device_id=peer, device_id_type=MESH_IDS)
        return carry

    lax.fori_loop(1, halves, hello, 0)
    pl.semaphore_wait(barrier, 3 + halves - 1)

    def place(n, home, flip_b, flip_a, j):
        (_, y_a, x_a), (_, y_b, x_b) = steps_of(n == 0, section, partner, across, wide)
        flips_y = (y_a and flip_a) or (y_b and flip_b)
        flips_x = (x_a and flip_a) or (x_b and flip_b)
        return owner_of(home, flips_y, flips_x, wide_at(j))

    def load(n, fb, fa, j):
        owner = place(n, section, fb, fa, j)
        slot = (fb * 2 + fa) * halves + j
        return pltpu.make_async_copy(
            partials[n].at[owner[0], owner[1]], keeps[n].at[slot], load_sem.at[n, slot]
        )

    def c_copy(n, fb, fa, j):
        owner = place(n, partner, fb, fa, j)
        slot = (fb * 2 + fa) * halves + j
        return remote(
            partials[n].at[owner[0], owner[1]],
            c_in[n].at[slot],
            c_send.at[n, slot],
            c_recv.at[n, slot],
            {"section": partner},
        )

    def b_copy(n, fa, j):
        _, (peer, _, _) = steps_of(n == 0, section, partner, across, wide)
        slot = fa * halves + j
        return remote(
            keeps[n].at[2 * halves + slot],
            b_in[n].at[slot],
            b_send.at[n, slot],
            b_recv.at[n, slot],
            peer,
        )

    def a_copy(n, j):
        (peer, _, _), _ = steps_of(n == 0, section, partner, across, wide)
        return remote(
            keeps[n].at[halves + j], a_in[n].at[j], a_send.at[n, j], a_recv.at[n, j], peer
        )

    def z_copy(n, j):
        return remote(
            keeps[n].at[j],
            z_in[n].at[j],
            z_send.at[n, j],
            z_recv.at[n, j],
            {"wide": wide_at(j)},
        )

    def add(n, slot, more):
        keeps[n][slot] = (
            keeps[n][slot].astype(jnp.float32) + more.astype(jnp.float32)
        ).astype(jnp.bfloat16)

    groups = ((1, 1), (1, 0), (0, 1), (0, 0))
    for fb, fa in groups:

        def start_c(j, carry):
            for n in range(count):
                c_copy(n, fb, fa, j).start()
                load(n, fb, fa, j).start()
            return carry

        lax.fori_loop(0, halves, start_c, 0)

    for fb, fa in groups:

        def sum_c(j, carry):
            for n in range(count):
                slot = (fb * 2 + fa) * halves + j
                load(n, fb, fa, j).wait()
                c_copy(n, fb, fa, j).wait_recv()
                add(n, slot, c_in[n][slot])
                if fb:
                    b_copy(n, fa, j).start()
            return carry

        lax.fori_loop(0, halves, sum_c, 0)

    for fa in (1, 0):

        def sum_b(j, carry):
            for n in range(count):
                slot = fa * halves + j
                b_copy(n, fa, j).wait_recv()
                add(n, slot, b_in[n][slot])
                if fa:
                    a_copy(n, j).start()
            return carry

        lax.fori_loop(0, halves, sum_b, 0)

    def sum_a(j, carry):
        for n in range(count):
            a_copy(n, j).wait_recv()
            add(n, j, a_in[n][j])
            z_copy(n, j).start()
        return carry

    lax.fori_loop(1, halves, sum_a, 0)
    for n in range(count):
        a_copy(n, 0).wait_recv()
        sums[n][...] = keeps[n][0].astype(jnp.float32) + a_in[n][0].astype(jnp.float32)

    def sum_z(j, carry):
        for n in range(count):
            z_copy(n, j).wait_recv()
            sums[n][...] += z_in[n][j].astype(jnp.float32)
        return carry

    lax.fori_loop(1, halves, sum_z, 0)

    def drain(j, carry):
        for n in range(count):
            for fb, fa in groups:
                c_copy(n, fb, fa, j).wait_send()
            b_copy(n, 0, j).wait_send()
            b_copy(n, 1, j).wait_send()
            a_copy(n, j).wait_send()
        return carry

    lax.fori_loop(0, halves, drain, 0)

    def drain_z(j, carry):
        for n in range(count):
            z_copy(n, j).wait_send()
        return carry

    lax.fori_loop(1, halves, drain_z, 0)


def collect(collective_id, partials):
    count, halves = len(partials), partials[0].shape[1] // 2
    shapes = [partial.shape[2:] for partial in partials]

    def slots(number):
        return [pltpu.VMEM((number,) + shape, jnp.bfloat16) for shape in shapes]

    return pl.pallas_call(
        functools.partial(collect_kernel, count, halves),
        out_shape=tuple(jax.ShapeDtypeStruct(shape, jnp.float32) for shape in shapes),
        in_specs=[ANYWHERE] * count,
        out_specs=(IN_VMEM,) * count,
        scratch_shapes=slots(4 * halves)
        + slots(4 * halves)
        + slots(2 * halves)
        + slots(halves)
        + slots(halves)
        + [dma_sems(count, 4 * halves)]
        + [
            dma_sems(count, 4 * halves),
            dma_sems(count, 2 * halves),
            dma_sems(count, halves),
            dma_sems(count, halves),
        ]
        * 2,
        compiler_params=settings(collective_id),
        name="collect",
    )(*partials)


TILE = 256


def causal_blocks(count, length):
    row = lax.broadcasted_iota(jnp.int32, (count, count), 0)
    column = lax.broadcasted_iota(jnp.int32, (count, count), 1)
    return (row // length == column // length) & (column <= row)


def turn(values, tables):
    cosines, upper, lower = tables
    parts = []
    for start in range(0, values.shape[1], LANES):
        part = values[:, start : start + LANES]
        ahead = pltpu.roll(part, LANES - HEAD_DIM // 2, 1)
        behind = pltpu.roll(part, HEAD_DIM // 2, 1)
        parts.append(part * cosines + ahead * upper + behind * lower)
    return parts[0] if len(parts) == 1 else jnp.concatenate(parts, axis=1)


def turn_tables(back):
    cosines, sines = rope_tables(LEN, HEAD_DIM)
    sines = -sines if back else sines
    first = jnp.arange(HEAD_DIM) < HEAD_DIM // 2
    upper, lower = jnp.where(first, -sines, 0.0), jnp.where(first, 0.0, sines)
    blank = jnp.zeros_like(cosines)
    pairs = [(cosines, cosines), (upper, upper), (lower, lower)]
    pairs += [(cosines, blank + 1.0), (upper, blank), (lower, blank)]
    tables = jnp.stack([jnp.concatenate(pair, axis=1) for pair in pairs])
    return jnp.tile(tables, (1, HALF // LEN, 1))


def attend(queries, key, mask, scale):
    scores = times_trans(queries, key) * scale
    scores = jnp.where(mask, scores, -1e30)
    peak = jnp.max(scores, axis=1, keepdims=True)
    mass = jnp.exp(scores - peak)
    return mass / jnp.sum(mass, axis=1, keepdims=True)


def local(kernel, operands, outs, scratch, name):
    return pl.pallas_call(
        kernel,
        out_shape=tuple(jax.ShapeDtypeStruct(shape, kind) for shape, kind in outs),
        in_specs=[IN_VMEM] * len(operands),
        out_specs=(IN_VMEM,) * len(outs),
        scratch_shapes=list(scratch),
        compiler_params=pltpu.CompilerParams(vmem_limit_bytes=VMEM_LIMIT),
        name=name,
    )(*operands)


CHUNK = 128


def same_entry(count, slots):
    entry = lax.broadcasted_iota(jnp.int32, (count // slots, slots, count), 0)
    column = lax.broadcasted_iota(jnp.int32, (count // slots, slots, count), 2)
    return entry == column // slots


def gathered_slots(products, mask):
    return jnp.sum(jnp.where(mask, products.reshape(mask.shape), 0.0), axis=0)


def spread_slots(values, mask):
    spread = jnp.where(mask, values[None], 0.0)
    return spread.reshape(mask.shape[0] * mask.shape[1], mask.shape[2])


def slot_weights(query, key, mask, scale):
    scores = gathered_slots(times_trans(key, query), mask) * scale
    mass = jnp.exp(scores - jnp.max(scores, axis=0, keepdims=True))
    return mass / jnp.sum(mass, axis=0, keepdims=True)


def gelu(values):
    return 0.5 * values * (1.0 + lax.erf(values * inv_root_two))


def hyper_kernel(
    slots,
    pieces,
    first,
    second,
    third,
    vectors,
    table,
    heads_out,
    mixed_out,
    middle_out,
    expanded_out,
    pooled_out,
    entered,
    outcome,
):
    width = pieces.shape[1]
    count, feed = pieces.shape[0], third.shape[0]
    head = width // HYPER_HEAD_COUNT
    flat = pieces[...].astype(jnp.float32)
    normed, _ = center_norm(flat)
    entered[...] = (normed * vectors[0:1] + vectors[1:2]).astype(jnp.bfloat16)

    @pl.loop(0, 3 * width // TILE)
    def _(n):
        columns = pl.ds(pl.multiple_of(n * TILE, TILE), TILE)
        heads_out[:, columns] = matmul(entered[...], first[:, columns]).astype(jnp.bfloat16)

    mask = same_entry(CHUNK, slots)

    @pl.loop(0, count // CHUNK)
    def _(n):
        rows = pl.ds(pl.multiple_of(n * CHUNK, CHUNK), CHUNK)
        block = heads_out[rows, :]
        mixed = []
        for start in range(0, width, head):
            query, key, value = (
                block[:, part * width + start : part * width + start + head] for part in range(3)
            )
            weights = slot_weights(query, key, mask, head ** (-0.5))
            weights = spread_slots(weights, mask).astype(jnp.bfloat16)
            mixed.append(trans_times(weights, value))
        mixed_out[rows, :] = jnp.concatenate(mixed, axis=1).astype(jnp.bfloat16)

    for start in range(0, width, TILE):
        columns = pl.ds(start, TILE)
        middle_out[:, columns] = pieces[:, columns].astype(jnp.float32) + matmul(
            mixed_out[...], first[:, pl.ds(3 * width + start, TILE)]
        )
    normed, _ = center_norm(middle_out[...])
    entered[...] = (normed * vectors[2:3] + vectors[3:4]).astype(jnp.bfloat16)
    outcome[...] = middle_out[...]

    @pl.loop(0, feed // TILE)
    def _(n):
        start = pl.multiple_of(n * TILE, TILE)
        columns = pl.ds(pl.multiple_of(4 * width + start, TILE), TILE)
        expanded = matmul(entered[...], first[:, columns])
        expanded_out[:, pl.ds(start, TILE)] = expanded
        outcome[...] += matmul(gelu(expanded).astype(jnp.bfloat16), third[pl.ds(start, TILE), :])

    pooled = jnp.mean(outcome[...].reshape(count // slots, slots, width), axis=1)
    pooled_out[...] = pooled.astype(jnp.bfloat16)

    @pl.loop(0, table.shape[1] // TILE)
    def _(n):
        columns = pl.ds(pl.multiple_of(n * TILE, TILE), TILE)
        table[:, columns] = matmul(pooled_out[...], second[:, columns]).astype(jnp.bfloat16)


class Rows:
    def __init__(self, blocks):
        self.blocks = blocks
        sections, wides, rows, columns = blocks.shape
        self.wides, self.rows, self.shape = wides, rows, (sections * wides * rows, columns)

    def __getitem__(self, index):
        rows, columns = index
        if rows == slice(None):
            values = self.blocks[:, :, :, columns]
        else:
            first = rows.start // self.rows
            owners = pl.ds(first % self.wides, rows.size // self.rows)
            values = self.blocks[first // self.wides, owners]
        return values.reshape(-1, values.shape[-1])


def hyper_outs(count, slots, width, feed, depth):
    entries = count // slots
    return [
        ((entries, depth), jnp.bfloat16),
        ((count, 3 * width), jnp.bfloat16),
        ((count, width), jnp.bfloat16),
        ((count, width), jnp.float32),
        ((count, feed), jnp.float32),
        ((entries, width), jnp.bfloat16),
    ]


def hyper_scratch(count, width):
    return [pltpu.VMEM((count, width), jnp.bfloat16), pltpu.VMEM((count, width), jnp.float32)]


def hyper_work(pieces, slots, feed, depth):
    count, width = pieces.shape

    def run(gathereds, pieces_ref, vectors, *refs):
        first, second, third = (Rows(blocks) for blocks in gathereds)
        turned = jnp.transpose(second[:, pl.ds(depth, LANES)].astype(jnp.float32))
        vectors[...] = turned[: vectors.shape[0]]
        hyper_kernel(slots, pieces_ref, first, second, third, vectors, *refs)

    outs = [((8, width), jnp.float32)] + hyper_outs(count, slots, width, feed, depth)
    return Work(run, (pieces,), outs, hyper_scratch(count, width))


def hyper_forward(pieces, slots, params):
    count, width = pieces.shape
    _, second, third, _ = params
    table, *stored = local(
        functools.partial(hyper_kernel, slots),
        (pieces, *params),
        hyper_outs(count, slots, width, third.shape[0], second.shape[1] - LANES),
        hyper_scratch(count, width),
        "hyper",
    )
    return table, stored


def hyper_back_kernel(
    slots,
    table_grad,
    pieces,
    first,
    second,
    third,
    vectors,
    heads,
    mixed,
    middle,
    expanded,
    pooled,
    first_grad,
    second_grad,
    third_grad,
    entered,
    outcome_low,
    feed_grad,
    heads_grad,
    mixed_grad,
):
    width = pieces.shape[1]
    count, feed = pieces.shape[0], third.shape[0]
    depth = table_grad.shape[1]
    head = width // HYPER_HEAD_COUNT
    scale = head ** (-0.5)
    grad_low = table_grad[...].astype(jnp.bfloat16)
    pooled_turned = jnp.transpose(pooled[...].astype(jnp.float32)).astype(jnp.bfloat16)

    for start in range(0, depth, TILE):
        columns = pl.ds(start, TILE)
        second_grad[:, columns] = matmul(
            pooled_turned, grad_low[:, start : start + TILE]
        ).astype(jnp.bfloat16)
    pooled_grad = times_trans(grad_low, second[:, pl.ds(0, depth)]) / slots
    outcome_grad = jnp.broadcast_to(pooled_grad[:, None, :], (count // slots, slots, width))
    outcome_grad = outcome_grad.reshape(count, width)
    outcome_low[...] = outcome_grad.astype(jnp.bfloat16)
    normed, inverse = center_norm(middle[...])
    entered[...] = jnp.transpose(normed * vectors[2:3] + vectors[3:4]).astype(jnp.bfloat16)
    feed_grad[...] = jnp.zeros_like(feed_grad)

    @pl.loop(0, feed // TILE)
    def _(n):
        start = pl.multiple_of(n * TILE, TILE)
        tile = pl.ds(start, TILE)
        columns = pl.ds(pl.multiple_of(4 * width + start, TILE), TILE)
        values = expanded[:, tile]
        erf = 0.5 * (1.0 + lax.erf(values * inv_root_two))
        active = (values * erf).astype(jnp.bfloat16)
        third_grad[tile, :] = trans_times(active, outcome_low[...]).astype(jnp.bfloat16)
        active_grad = times_trans(outcome_low[...], third[tile, :])
        slope = erf + values * jnp.exp(-0.5 * values * values) * inv_root_tau
        low = (active_grad * slope).astype(jnp.bfloat16)
        first_grad[:, columns] = matmul(entered[...], low).astype(jnp.bfloat16)
        feed_grad[...] += times_trans(low, first[:, columns])

    grad = feed_grad[...]
    scale_two = jnp.sum(grad * normed, axis=0, keepdims=True)
    shift_two = jnp.sum(grad, axis=0, keepdims=True)
    middle_grad = outcome_grad + center_back(normed, inverse, grad * vectors[2:3])
    middle_low = middle_grad.astype(jnp.bfloat16)
    out_columns = pl.ds(3 * width, width)
    first_grad[:, out_columns] = trans_times(mixed[...], middle_low).astype(jnp.bfloat16)
    mixed_grad[...] = times_trans(middle_low, first[:, out_columns]).astype(jnp.bfloat16)
    mask = same_entry(CHUNK, slots)

    @pl.loop(0, count // CHUNK)
    def _(n):
        rows = pl.ds(pl.multiple_of(n * CHUNK, CHUNK), CHUNK)
        block = heads[rows, :]
        outer_block = mixed_grad[rows, :]
        grads = [[], [], []]
        for start in range(0, width, head):
            query, key, value = (
                block[:, part * width + start : part * width + start + head] for part in range(3)
            )
            outer = outer_block[:, start : start + head]
            weights = slot_weights(query, key, mask, scale)
            weight_grad = gathered_slots(times_trans(value, outer), mask)
            score_grad = weights * (
                weight_grad - jnp.sum(weights * weight_grad, axis=0, keepdims=True)
            )
            score_grad = spread_slots(score_grad, mask).astype(jnp.bfloat16)
            weights = spread_slots(weights, mask).astype(jnp.bfloat16)
            grads[0].append(trans_times(score_grad, key) * scale)
            grads[1].append(matmul(score_grad, query) * scale)
            grads[2].append(matmul(weights, outer))
        for part in range(3):
            heads_grad[rows, pl.ds(part * width, width)] = jnp.concatenate(
                grads[part], axis=1
            ).astype(jnp.bfloat16)

    normed, _ = center_norm(pieces[...].astype(jnp.float32))
    entered[...] = jnp.transpose(normed * vectors[0:1] + vectors[1:2]).astype(jnp.bfloat16)
    feed_grad[...] = jnp.zeros_like(feed_grad)

    @pl.loop(0, 3 * width // TILE)
    def _(n):
        columns = pl.ds(pl.multiple_of(n * TILE, TILE), TILE)
        low = heads_grad[:, columns]
        first_grad[:, columns] = matmul(entered[...], low).astype(jnp.bfloat16)
        feed_grad[...] += times_trans(low, first[:, columns])

    grad = feed_grad[...]
    scale_one = jnp.sum(grad * normed, axis=0, keepdims=True)
    shift_one = jnp.sum(grad, axis=0, keepdims=True)
    row = lax.broadcasted_iota(jnp.int32, (LANES, width), 0)
    summed = jnp.zeros((LANES, width), jnp.float32)
    for n, item in enumerate((scale_one, shift_one, scale_two, shift_two)):
        summed = jnp.where(row == n, item, summed)
    second_grad[:, pl.ds(depth, LANES)] = jnp.transpose(summed).astype(jnp.bfloat16)


def hyper_backward(pieces, slots, params, stored, table_grad):
    count, width = pieces.shape
    first, second, third, _ = params
    return local(
        functools.partial(hyper_back_kernel, slots),
        (table_grad, pieces, *params, *stored),
        [(item.shape, jnp.bfloat16) for item in (first, second, third)],
        [
            pltpu.VMEM((width, count), jnp.bfloat16),
            pltpu.VMEM((count, width), jnp.bfloat16),
            pltpu.VMEM((count, width), jnp.float32),
            pltpu.VMEM((count, 3 * width), jnp.bfloat16),
            pltpu.VMEM((count, width), jnp.bfloat16),
        ],
        "hyper_back",
    )


def column_plan(q_columns, kv_columns, ff_columns):
    share = ff_columns // TEAM
    edge = share // LANES * LANES
    tail = share - edge
    heads = kv_columns // HEAD_DIM
    q_share = q_columns // TEAM
    plan = []
    for rank in range(TEAM):
        kv = rank * heads // TEAM * HEAD_DIM
        widths = [
            (0, rank * q_share, q_share),
            (1, kv, HEAD_DIM),
            (2, kv, HEAD_DIM),
            (3, rank * share, edge),
            (4, rank * share, edge),
            (3, rank * share + edge, tail),
            (4, rank * share + edge, tail),
        ]
        moves, start = [], 0
        for item, source, size in widths:
            moves.append((item, source, start, size))
            start += size
        plan.append(moves)
    return plan, start


def pack_kernel(plan, rows, *refs):
    sources, maps, targets = refs[:5], refs[5:16], refs[16:23]
    blocks, sem, square = refs[23:28], refs[28], refs[29]
    section = lax.axis_index("section")
    mine = pl.ds(pl.multiple_of(section * rows, rows), rows)
    copies = [
        [
            pltpu.make_async_copy(source.at[layer, mine], block.at[layer], sem.at[layer, n])
            for n, (source, block) in enumerate(zip(sources, blocks))
        ]
        for layer in range(2)
    ]
    for layer in range(2):
        for copy in copies[layer]:
            copy.start()
    *heads, expand, embed, reduce, vectors, norms, feeds, tokens = maps
    first, second, third, gains, notes = targets[2:]
    width = heads[0].shape[1]
    for n, item in enumerate(heads):
        first[:, n * width : (n + 1) * width] = item[...].astype(jnp.bfloat16)
    first[:, 4 * width :] = expand[...].astype(jnp.bfloat16)
    depth = embed.shape[1]
    second[:, :depth] = embed[...].astype(jnp.bfloat16)
    square[...] = jnp.zeros_like(square)
    square[: vectors.shape[0], : vectors.shape[1]] = vectors[...]
    second[:, depth:] = jnp.transpose(square[...])[: second.shape[0]].astype(jnp.bfloat16)
    third[...] = reduce[...].astype(jnp.bfloat16)
    gains[...] = jnp.zeros_like(gains)
    gains[0:2, :] = norms[...].astype(jnp.float32)
    gains[2:4, :] = feeds[...].astype(jnp.float32)
    notes[...] = jnp.zeros_like(notes)
    for n in range(2):
        for batch in range(MB):
            own = pl.ds(n * MB + batch, 1)
            notes[n : n + 1, batch * LEN : (batch + 1) * LEN] = tokens[own, :]
    for layer in range(2):
        for copy in copies[layer]:
            copy.wait()
        for rank, moves in enumerate(plan):
            parts = [
                blocks[item][layer, :, source : source + size] for item, source, _, size in moves
            ]
            heads = jnp.concatenate(parts[1:3], axis=1)
            ends = jnp.concatenate(parts[5:7], axis=1)
            for part, start in zip(
                (parts[0], heads, parts[3], parts[4], ends),
                (moves[0][2], moves[1][2], moves[3][2], moves[4][2], moves[5][2]),
            ):
                if part.shape[1]:
                    targets[layer][rank, :, start : start + part.shape[1]] = part


def pack(weights, maps, vectors, norms, tokens):
    rows = weights[0].shape[1] // SECTIONS
    plan, width = column_plan(weights[0].shape[2], weights[1].shape[2], weights[3].shape[2])
    low = jnp.bfloat16
    owned, hyper_width = maps[0].shape
    feed, depth = maps[4].shape[1], maps[5].shape[1]
    if rows % 16 or owned % 16:
        section = lax.axis_index("section")
        mine = [lax.dynamic_slice_in_dim(item, section * rows, rows, 1) for item in weights]
        columns = tuple(
            jnp.stack(
                [
                    jnp.concatenate(
                        [mine[item][layer, :, at : at + size] for item, at, _, size in moves], axis=1
                    )
                    for moves in plan
                ]
            )
            for layer in range(2)
        )
        first = jnp.concatenate(maps[:5], axis=1).astype(low)
        padded = jnp.pad(vectors.T, ((0, 0), (0, LANES - vectors.shape[0])))
        second = jnp.concatenate([maps[5], padded], axis=1).astype(low)
        gains = jnp.pad(jnp.concatenate(norms, axis=0).astype(jnp.float32), ((0, 4), (0, 0)))
        notes = jnp.pad(tokens.reshape(2, -1), ((0, 6), (0, 0)))
        return (*columns, first, second, maps[6].astype(low), gains, notes)
    shapes = [((TEAM, rows, width), low)] * 2 + [
        ((owned, 4 * hyper_width + feed), low),
        ((owned, depth + LANES), low),
        (maps[6].shape, low),
        ((8, norms[0].shape[1]), jnp.float32),
        ((8, MB * LEN), jnp.int32),
    ]
    return pl.pallas_call(
        functools.partial(pack_kernel, plan, rows),
        out_shape=tuple(jax.ShapeDtypeStruct(shape, kind) for shape, kind in shapes),
        in_specs=[ANYWHERE] * 5 + [IN_VMEM] * 11,
        out_specs=(IN_VMEM,) * 7,
        scratch_shapes=[pltpu.VMEM((2, rows, item.shape[2]), low) for item in weights]
        + [dma_sems(2, 5), pltpu.VMEM((LANES, LANES), jnp.float32)],
        compiler_params=pltpu.CompilerParams(vmem_limit_bytes=VMEM_LIMIT),
        name="pack",
    )(*weights, *maps, vectors, *norms, tokens)


def deliver_kernel(embed, expand, reduce, front, rear, *refs):
    outs, square = refs[:11], refs[11]
    width = front.shape[1] // 2
    square[...] = jnp.zeros_like(square)
    square[: rear.shape[0], :] = rear[:, 2 * width :]
    vectors = jnp.transpose(square[...])
    for n in range(4):
        outs[n][...] = vectors[n, : rear.shape[0]]
    outs[4][...] = front[:, :width]
    outs[5][...] = front[:, width:]
    outs[6][...] = rear[:, :width]
    outs[7][...] = rear[:, width : 2 * width]
    outs[8][...] = expand[...]
    outs[9][...] = reduce[...]
    outs[10][...] = embed[...]


def deliver(embed, expand, reduce, front, rear):
    rows, width = front.shape[0], front.shape[1] // 2
    shapes = [(rows,)] * 4 + [(rows, width)] * 4 + [expand.shape, reduce.shape, embed.shape]
    return local(
        deliver_kernel,
        (embed, expand, reduce, front, rear),
        [(shape, jnp.float32) for shape in shapes],
        [pltpu.VMEM((LANES, LANES), jnp.float32)],
        "deliver",
    )


ORDER = "grgrrgg"


def finish(*steps):
    steps = list(steps)
    while steps:
        steps = [step for step in steps if next(step, steps) is not steps]


class Decoder:
    def __init__(self, shape, refs):
        self.outer, self.tokens, self.share, self.q_width, self.depth = shape
        for name, ref in refs.items():
            setattr(self, name, ref)
        self.section, self.partner, self.across = section_places()
        wide = lax.axis_index("wide")
        self.rank, self.team = wide // self.outer, wide % self.outer
        self.line, self.column = self.rank // 2, self.rank % 2
        self.mine = self.rank
        self.beside = self.member(self.line, 1 - self.column)
        self.edge = self.share // LANES * LANES
        self.tail = self.share - self.edge

    def at(self, line, column):
        return (line % LINES) * 2 + column

    def member(self, line, column):
        return {"wide": self.at(line, column) * self.outer + self.team}

    def ranked(self, step):
        return {"wide": (self.rank + step) % TEAM * self.outer + self.team}

    def greet(self):
        sections = [{"section": place} for place in (self.partner, self.across)]
        greet(sections + [self.ranked(k) for k in range(1, TEAM)])

    def share_copy(self, layer, part, kind):
        split = self.q_width + LANES
        columns = pl.ds(split, 2 * self.share) if part else pl.ds(0, split)
        weight = self.feed_weight if part else self.head_weight
        source = self.own[layer].at[:, :, columns]
        target = weight.at[layer, :, self.section]
        if kind == "keep":
            return pltpu.make_async_copy(source, target, self.load_sem.at[layer, part, 0])
        if kind == "whole":
            source = self.down_source if part else self.out_source
            target = self.down_weight if part else self.out_weight
            return pltpu.make_async_copy(
                source.at[layer], target.at[layer], self.load_sem.at[layer, part, 1]
            )
        n = ("far", "near", "on").index(kind)
        if kind == "on":
            source = target = weight.at[layer, :, self.across]
        return remote(
            source,
            target,
            self.share_send.at[layer, part, n],
            self.share_recv.at[layer, part, n],
            {"section": self.across if kind == "far" else self.partner},
        )

    def share_start(self, layer):
        for part in range(2):
            for kind in ("far", "near", "keep", "whole"):
                self.share_copy(layer, part, kind).start()

    def share_on(self, layer, part):
        self.share_copy(layer, part, "far").wait_recv()
        self.share_copy(layer, part, "on").start()

    def share_end(self, layer, part):
        for kind in ("keep", "whole", "near", "on"):
            self.share_copy(layer, part, kind).wait()
        self.share_copy(layer, part, "far").wait_send()

    def send(self, half):
        self.sides = getattr(self, "sides", {})
        self.sides[half] = [
            remote(
                self.partial.at[half, self.at(self.line + j, 1 - self.column)],
                self.side.at[half, j],
                self.side_send.at[half, j],
                self.side_recv.at[half, j],
                self.beside,
            )
            for j in range(LINES)
        ]
        for j in (2, 1, 3, 0):
            self.sides[half][j].start()

    def reduce(self, half, close):
        sides = self.sides[half]
        fars = [None] + [
            remote(
                self.pair.at[half, j],
                self.far.at[half, j],
                self.far_send.at[half, j],
                self.far_recv.at[half, j],
                self.member(self.line + j, self.column),
            )
            for j in range(1, LINES)
        ]

        def pair_sum(j):
            sides[j].wait_recv()
            own = self.partial[half, self.at(self.line + j, self.column)]
            return own.astype(jnp.float32) + self.side[half, j].astype(jnp.float32)

        for j in (2, 1, 3):
            self.pair[half, j] = pair_sum(j).astype(jnp.bfloat16)
            fars[j].start()
            yield
        total = pair_sum(0)
        for j in (1, 3, 2):
            fars[j].wait_recv()
            total = total + self.far[half, j].astype(jnp.float32)
        self.gathered[half, self.mine] = close(half, total)
        for j in range(LINES):
            sides[j].wait_send()
            if j:
                fars[j].wait_send()
        pushes = [None] + [
            remote(
                self.gathered.at[half, self.mine],
                self.gathered.at[half, self.mine],
                self.out_send.at[half, j],
                self.out_recv.at[half, j],
                self.member(self.line + j, self.column),
            )
            for j in range(1, LINES)
        ]
        overs = []
        for j in range(LINES):
            block = self.gathered.at[half, self.at(self.line - j, self.column)]
            overs.append(
                remote(
                    block, block, self.over_send.at[half, j], self.over_recv.at[half, j], self.beside
                )
            )
        for j in (2, 1, 3):
            pushes[j].start()
        overs[0].start()
        self.moving[half] = (pushes, overs)
        yield

    def gather(self, half):
        pushes, overs = self.moving[half]
        for j in (1, 3, 2):
            pushes[j].wait_recv()
            overs[j].start()
            yield
        for j in range(LINES):
            overs[j].wait()
            if j:
                pushes[j].wait_send()
        yield

    def rows(self, half):
        return self.gathered[half].reshape(HALF, self.depth)

    def store_partial(self, half, columns, values):
        self.partial[half, :, :, columns] = values.astype(jnp.bfloat16).reshape(
            TEAM, EACH, values.shape[1]
        )

    def tiles(self, count, parts):
        bounds = [count * n // parts for n in range(parts + 1)]
        return [(low, high) for low, high in zip(bounds[:-1], bounds[1:]) if high > low]

    def inject(self, half):
        hits = self.own_rows[...] == self.ids[half : half + 1, :]
        hits = jnp.where(hits, 1.0, 0.0).astype(jnp.bfloat16)

        @pl.loop(0, self.depth // TILE)
        def _(n):
            columns = pl.ds(pl.multiple_of(n * TILE, TILE), TILE)
            self.store_partial(half, columns, trans_times(hits, self.table[:, columns]))

        if half == SECOND:
            self.share_on(0, 0)
        yield

    def attention(self, layer, half):
        if half == FIRST:
            self.share_end(layer, 0)
        own = pl.ds(half * HALF, HALF)
        width = self.q_width + LANES
        projected = matmul(self.rows(half), self.head_weight[layer].reshape(self.depth, width))
        yield
        queries = turn(projected[:, : self.q_width], [self.tables[n] for n in range(3)])
        pairs = turn(projected[:, self.q_width :], [self.tables[n] for n in range(3, 6)])
        queries, pairs = queries.astype(jnp.bfloat16), pairs.astype(jnp.bfloat16)
        self.queries[layer, own, :] = queries
        self.pairs[layer, own, :] = pairs
        key, value = pairs[:, :HEAD_DIM], pairs[:, HEAD_DIM:]
        mask = causal_blocks(HALF, LEN)
        mixed = []
        for start in range(0, self.q_width, HEAD_DIM):
            weights = attend(queries[:, start : start + HEAD_DIM], key, mask, HEAD_DIM ** (-0.5))
            mixed.append(matmul(weights.astype(jnp.bfloat16), value))
        mixed = jnp.concatenate(mixed, axis=1).astype(jnp.bfloat16)
        yield

        @pl.loop(0, self.depth // TILE)
        def _(n):
            columns = pl.ds(pl.multiple_of(n * TILE, TILE), TILE)
            self.store_partial(half, columns, matmul(mixed, self.out_weight[layer, :, columns]))

        if half == SECOND:
            self.share_on(layer, 1)
            if layer == 0:
                self.share_start(1)
        yield

    def feed(self, layer, half):
        if half == FIRST:
            self.share_end(layer, 1)
        own = pl.ds(half * HALF, HALF)
        edge, tail = self.edge, self.tail
        def project(columns, width):
            block = self.feed_weight[layer, :, :, :, columns].reshape(self.depth, width)
            self.kept[layer, own, columns] = matmul(self.rows(half), block)

        full, rest = 2 * self.share // TILE, 2 * self.share % TILE
        for low, high in self.tiles(full, 3):

            @pl.loop(low, high)
            def _(n):
                project(pl.ds(pl.multiple_of(n * TILE, TILE), TILE), TILE)

            if high == full and rest:
                project(pl.ds(full * TILE, rest), rest)
            yield

        def activate(gate, up):
            return (jax.nn.silu(gate) * up).astype(jnp.bfloat16)

        self.active[:, :edge] = activate(
            self.kept[layer, own, :edge], self.kept[layer, own, edge : 2 * edge]
        )
        if tail:
            last = self.kept[layer, own, 2 * edge :]
            self.active[:, edge:] = activate(last[:, :tail], last[:, tail:])
        for low, high in self.tiles(self.depth // TILE, 2):

            @pl.loop(low, high)
            def _(n):
                columns = pl.ds(pl.multiple_of(n * TILE, TILE), TILE)
                block = self.down_weight[layer, :, columns]
                self.store_partial(half, columns, matmul(self.active[...], block))

            if half == SECOND and layer == 0 and low:
                self.share_on(1, 0)
            yield

    def head(self, half):
        keep = pltpu.make_async_copy(
            self.gathered.at[half], self.normed_out.at[half], self.keep_sem.at[half]
        )
        keep.start()
        logits = times_trans(self.table[...], self.rows(half))
        peak = jnp.max(logits, axis=0, keepdims=True)
        mass = jnp.sum(jnp.exp(logits - peak), axis=0, keepdims=True)
        wanted = self.own_rows[...] == self.wanted[half : half + 1, :]
        chosen = jnp.sum(jnp.where(wanted, logits, 0.0), axis=0, keepdims=True)
        row = lax.broadcasted_iota(jnp.int32, (8, HALF), 0)
        stats = jnp.where(row == 0, peak, jnp.where(row == 1, mass, chosen))
        self.stats[half, self.rank] = stats
        copies = [
            remote(
                self.stats.at[half, self.rank],
                self.stats.at[half, self.rank],
                self.stats_send.at[half, k],
                self.stats_recv.at[half, k],
                self.ranked(k),
            )
            for k in range(1, TEAM)
        ]
        for copy in copies:
            copy.start()
        yield
        yield
        for copy in copies:
            copy.wait()
        peaks = [self.stats[half, n, 0:1, :] for n in range(TEAM)]
        top = functools.reduce(jnp.maximum, peaks)
        mass = sum(self.stats[half, n, 1:2, :] * jnp.exp(peaks[n] - top) for n in range(TEAM))
        chosen = sum(self.stats[half, n, 2:3, :] for n in range(TEAM))
        log_norm = top + jnp.log(mass)
        loss = jnp.sum(log_norm - chosen, axis=1, keepdims=True) / self.tokens
        loss = jnp.broadcast_to(loss, self.loss_out.shape)
        if half == FIRST:
            self.loss_out[...] = loss
        else:
            self.loss_out[...] += loss
        grad = (jnp.exp(logits - log_norm) - jnp.where(wanted, 1.0, 0.0)) / self.tokens
        grad = grad.astype(jnp.bfloat16)
        self.logit_grad[:, pl.ds(half * HALF, HALF)] = grad
        yield

        @pl.loop(0, self.depth // TILE)
        def _(n):
            columns = pl.ds(pl.multiple_of(n * TILE, TILE), TILE)
            self.store_partial(half, columns, trans_times(grad, self.table[:, columns]))

        keep.wait()
        yield

    def feed_back(self, layer, half):
        own = pl.ds(half * HALF, HALF)
        edge, tail = self.edge, self.tail
        active_grad = times_trans(self.rows(half), self.down_weight[layer])
        yield

        def back(outer, gate, up):
            sigmoid = jax.nn.sigmoid(gate)
            gate_grad = outer * up * sigmoid * (1.0 + gate * (1.0 - sigmoid))
            return gate_grad.astype(jnp.bfloat16), (outer * gate * sigmoid).astype(jnp.bfloat16)

        gate_grad, up_grad = back(
            active_grad[:, :edge],
            self.kept[layer, own, :edge],
            self.kept[layer, own, edge : 2 * edge],
        )
        self.both[:, :edge] = gate_grad
        self.both[:, edge : 2 * edge] = up_grad
        if tail:
            last = self.kept[layer, own, 2 * edge :]
            gate_grad, up_grad = back(active_grad[:, edge:], last[:, :tail], last[:, tail:])
            self.both[:, 2 * edge :] = jnp.concatenate([gate_grad, up_grad], axis=1)
        yield
        tiles = self.depth // TILE
        each = self.feed_weight.shape[1] // tiles
        for low, high in self.tiles(tiles, 3):

            @pl.loop(low, high)
            def _(n):
                columns = pl.ds(pl.multiple_of(n * TILE, TILE), TILE)
                block = self.feed_weight[layer, pl.ds(n * each, each)].reshape(TILE, -1)
                self.store_partial(half, columns, times_trans(self.both[...], block))

            yield

    def attention_back(self, layer, half):
        own = pl.ds(half * HALF, HALF)
        scale = HEAD_DIM ** (-0.5)
        mixed_grad = times_trans(self.rows(half), self.out_weight[layer]).astype(jnp.bfloat16)
        yield
        queries, pairs = self.queries[layer, own, :], self.pairs[layer, own, :]
        key, value = pairs[:, :HEAD_DIM], pairs[:, HEAD_DIM:]
        mask = causal_blocks(HALF, LEN)
        query_grads, key_grad, value_grad = [], 0.0, 0.0
        for start in range(0, self.q_width, HEAD_DIM):
            query = queries[:, start : start + HEAD_DIM]
            outer = mixed_grad[:, start : start + HEAD_DIM]
            weights = attend(query, key, mask, scale)
            weight_grad = times_trans(outer, value)
            score_grad = weights * (
                weight_grad - jnp.sum(weights * weight_grad, axis=1, keepdims=True)
            )
            score_grad = score_grad.astype(jnp.bfloat16)
            query_grads.append(matmul(score_grad, key) * scale)
            key_grad = key_grad + trans_times(score_grad, query) * scale
            value_grad = value_grad + trans_times(weights.astype(jnp.bfloat16), outer)
        query_grad = jnp.concatenate(query_grads, axis=1)
        query_grad = turn(query_grad, [self.back_tables[n] for n in range(3)])
        pair_grad = jnp.concatenate([key_grad, value_grad], axis=1)
        pair_grad = turn(pair_grad, [self.back_tables[n] for n in range(3, 6)])
        both = jnp.concatenate([query_grad, pair_grad], axis=1).astype(jnp.bfloat16)
        yield
        tiles = self.depth // TILE
        each = self.head_weight.shape[1] // tiles

        @pl.loop(0, tiles)
        def _(n):
            columns = pl.ds(pl.multiple_of(n * TILE, TILE), TILE)
            block = self.head_weight[layer, pl.ds(n * each, each)].reshape(TILE, -1)
            self.store_partial(half, columns, times_trans(both, block))

        yield

    def normed(self, values, gain):
        return (values * root_inverse(values) * gain[...]).astype(jnp.bfloat16)

    def close_inject(self, half, total):
        hidden = total.astype(jnp.bfloat16)
        self.hidden[0, half] = hidden
        return self.normed(hidden.astype(jnp.float32), self.gains[0])

    def close_attention(self, layer):
        def close(half, total):
            middle = self.hidden[layer, half].astype(jnp.float32) + total
            self.middle[layer, half] = middle
            return self.normed(middle, self.gains[2 + layer])

        return close

    def close_feed(self, layer):
        def close(half, total):
            hidden = (self.middle[layer, half] + total).astype(jnp.bfloat16)
            self.hidden[layer + 1, half] = hidden
            gain = self.gains[4] if layer else self.gains[1]
            return self.normed(hidden.astype(jnp.float32), gain)

        return close

    def close_head(self, half, total):
        hidden = self.hidden[2, half].astype(jnp.float32)
        grad = reciprocal_root_backward(hidden, root_inverse(hidden), self.gains[4][...], total)
        grad = grad.astype(jnp.bfloat16)
        self.grad[half] = grad.astype(jnp.float32)
        return grad

    def close_feed_back(self, layer):
        def close(half, total):
            middle = self.middle[layer, half]
            grad = self.grad[half] + reciprocal_root_backward(
                middle, root_inverse(middle), self.gains[2 + layer][...], total
            )
            self.grad[half] = grad
            return grad.astype(jnp.bfloat16)

        return close

    def close_attention_back(self, layer):
        def close(half, total):
            hidden = self.hidden[layer, half].astype(jnp.float32)
            grad = self.grad[half] + reciprocal_root_backward(
                hidden, root_inverse(hidden), self.gains[layer][...], total
            )
            grad = grad.astype(jnp.bfloat16)
            self.grad[half] = grad.astype(jnp.float32)
            return grad

        return close


def decode_kernel(shape, names, *refs):
    refs = dict(zip(names, refs))
    refs["own"] = [refs.pop(name) for name in ("own_one", "own_two")]
    refs["gains"] = [refs["gain_rows"].at[pl.ds(n, 1)] for n in range(5)]
    this = Decoder(shape, refs)
    this.greet()
    this.moving = {}
    this.share_start(0)
    phases = [(this.inject, this.close_inject, 1)]
    for layer in range(2):
        phases.append((functools.partial(this.attention, layer), this.close_attention(layer), 1))
        phases.append((functools.partial(this.feed, layer), this.close_feed(layer), 2))
    phases.append((this.head, this.close_head, 2))
    for layer in (1, 0):
        phases.append((functools.partial(this.feed_back, layer), this.close_feed_back(layer), 2))
        phases.append(
            (functools.partial(this.attention_back, layer), this.close_attention_back(layer), 1)
        )
    gathers = {}
    sent = None
    for work, close, parts in phases:
        for half in (FIRST, SECOND):
            gather = gathers.pop(half, iter(()))
            reduce = sent or iter(())
            for kind in ORDER:
                next(gather if kind == "g" else reduce, None)
            for count, _ in enumerate(work(half)):
                if count + 1 == parts:
                    finish(reduce)
            finish(reduce)
            if sent is not None:
                gathers[1 - half] = this.gather(1 - half)
            this.send(half)
            sent = this.reduce(half, close)
    finish(gathers.pop(FIRST), sent)
    finish(this.gather(SECOND))
    outs = [
        pltpu.make_async_copy(
            this.gathered.at[half], this.grad_out.at[half], this.keep_sem.at[half]
        )
        for half in (FIRST, SECOND)
    ]
    for copy in outs:
        copy.start()
    for copy in outs:
        copy.wait()


def decode(outer, collective_id, tokens, weights, out_source, down_source, gains, tables, table, own_rows, ids, wanted):
    q_width, depth = out_source.shape[1:]
    share = down_source.shape[1]
    groups, quarter = weights[0].shape[:2]
    entries = table.shape[0]
    low, full = jnp.bfloat16, jnp.float32
    block = (2, TEAM, EACH, depth)
    slots = pltpu.VMEM((2, LINES, EACH, depth), low)
    inputs = dict(
        own_rows=own_rows,
        ids=ids,
        wanted=wanted,
        table=table,
        gain_rows=gains,
        tables=tables[0],
        back_tables=tables[1],
    )
    far_inputs = dict(
        zip(("own_one", "own_two"), weights),
        out_source=out_source,
        down_source=down_source,
    )
    outputs = dict(
        normed_out=(jax.ShapeDtypeStruct(block, low), ANYWHERE),
        grad_out=(jax.ShapeDtypeStruct(block, low), ANYWHERE),
        logit_grad=(jax.ShapeDtypeStruct((entries, ROWS), low), IN_VMEM),
        loss_out=(jax.ShapeDtypeStruct((8, LANES), full), IN_VMEM),
    )
    scratch = dict(
        head_weight=pltpu.VMEM((2, groups, SECTIONS, quarter, q_width + LANES), low),
        feed_weight=pltpu.VMEM((2, groups, SECTIONS, quarter, 2 * share), low),
        out_weight=pltpu.VMEM((2, q_width, depth), low),
        down_weight=pltpu.VMEM((2, share, depth), low),
        gathered=pltpu.VMEM(block, low),
        partial=pltpu.VMEM(block, low),
        side=slots,
        pair=slots,
        far=slots,
        kept=pltpu.VMEM((2, ROWS, 2 * share), full),
        queries=pltpu.VMEM((2, ROWS, q_width), low),
        pairs=pltpu.VMEM((2, ROWS, LANES), low),
        active=pltpu.VMEM((HALF, share), low),
        both=pltpu.VMEM((HALF, 2 * share), low),
        hidden=pltpu.VMEM((3, 2, EACH, depth), low),
        middle=pltpu.VMEM((2, 2, EACH, depth), full),
        grad=pltpu.VMEM((2, EACH, depth), full),
        stats=pltpu.VMEM((2, TEAM, 8, HALF), full),
        load_sem=dma_sems(2, 2, 2),
        share_send=dma_sems(2, 2, 3),
        share_recv=dma_sems(2, 2, 3),
        stats_send=dma_sems(2, TEAM),
        stats_recv=dma_sems(2, TEAM),
        keep_sem=dma_sems(2),
    )
    for name in ("side", "far", "out", "over"):
        scratch[name + "_send"] = dma_sems(2, LINES)
        scratch[name + "_recv"] = dma_sems(2, LINES)
    names = (*inputs, *far_inputs, *outputs, *scratch)
    return pl.pallas_call(
        functools.partial(decode_kernel, (outer, tokens, share, q_width, depth), names),
        out_shape=tuple(shape for shape, _ in outputs.values()),
        in_specs=[IN_VMEM] * len(inputs) + [ANYWHERE] * len(far_inputs),
        out_specs=tuple(spec for _, spec in outputs.values()),
        scratch_shapes=list(scratch.values()),
        compiler_params=settings(collective_id),
        name="decode",
    )(*inputs.values(), *far_inputs.values())


class Collector:
    def __init__(self, halves, refs):
        for name, ref in refs.items():
            setattr(self, name, ref)
        self.halves = halves
        self.section, self.partner, self.across, self.wide, self.wide_at = all_places(halves)
        self.groups = ((1, 1), (1, 0), (0, 1), (0, 0))

    def greet(self):
        beside = self.wide + 1 - 2 * (self.wide % 2)
        peers = [{"section": self.partner}, {"section": self.across}, {"wide": beside}]
        greet(peers + [{"wide": self.wide_at(j)} for j in range(1, self.halves)])

    def steps(self, n):
        return steps_of(n % 2 == 0, self.section, self.partner, self.across, self.wide)

    def lines(self, n, home, flip_b, flip_a):
        (_, y_a, x_a), (_, y_b, x_b) = self.steps(n)
        flips_y = (y_a and flip_a) or (y_b and flip_b)
        flips_x = (x_a and flip_a) or (x_b and flip_b)
        section, wide = owner_of(home, flips_y, flips_x, self.wide)
        return self.partials[n].at[section, :, wide % 2]

    def line_block(self, n, j):
        return self.partials[n].at[self.section, (self.wide // 2 + j) % self.halves, self.wide % 2]

    def core_copy(self, n, fb, fa):
        return remote(
            self.lines(n, self.partner, fb, fa),
            self.core_in[n].at[fb, fa],
            self.core_send.at[n, fb, fa],
            self.core_recv.at[n, fb, fa],
            {"section": self.partner},
        )

    def b_copy(self, n, fa):
        _, (peer, _, _) = self.steps(n)
        return remote(
            self.lines(n, self.section, 1, fa),
            self.b_in[n].at[fa],
            self.b_send.at[n, fa],
            self.b_recv.at[n, fa],
            peer,
        )

    def a_copy(self, n):
        (peer, _, _), _ = self.steps(n)
        return remote(
            self.lines(n, self.section, 0, 1),
            self.a_in[n],
            self.a_send.at[n],
            self.a_recv.at[n],
            peer,
        )

    def z_copy(self, n, j):
        return remote(
            self.line_block(n, j),
            self.z_in[n].at[j],
            self.z_send.at[n, j],
            self.z_recv.at[n, j],
            {"wide": self.wide_at(j)},
        )

    def add(self, block, more):
        block[...] = (block[...].astype(jnp.float32) + more.astype(jnp.float32)).astype(jnp.bfloat16)

    def start(self, n):
        for fb, fa in self.groups:
            self.core_copy(n, fb, fa).start()

    def sum_core(self, n):
        for fb, fa in self.groups:
            self.core_copy(n, fb, fa).wait_recv()
            self.add(self.lines(n, self.section, fb, fa), self.core_in[n][fb, fa])
            if fb:
                self.b_copy(n, fa).start()

    def sum_b(self, n):
        for fa in (1, 0):
            self.b_copy(n, fa).wait_recv()
            self.add(self.lines(n, self.section, 0, fa), self.b_in[n][fa])
            if fa:
                self.a_copy(n).start()

    def sum_a(self, n):
        self.a_copy(n).wait_recv()
        self.add(self.lines(n, self.section, 0, 0), self.a_in[n][...])
        for j in range(1, self.halves):
            self.z_copy(n, j).start()

    def sum_lines(self, n):
        total = self.line_block(n, 0)[...].astype(jnp.float32)
        for j in range(1, self.halves):
            self.z_copy(n, j).wait_recv()
            total = total + self.z_in[n][j].astype(jnp.float32)
        self.sums[n][...] = total

    def drain(self, n):
        for fb, fa in self.groups:
            self.core_copy(n, fb, fa).wait_send()
        for fa in (0, 1):
            self.b_copy(n, fa).wait_send()
        self.a_copy(n).wait_send()
        for j in range(1, self.halves):
            self.z_copy(n, j).wait_send()


EMBED, EXPAND, REDUCE, FRONT, REAR = range(5)


def hyper_collect_kernel(slots, halves, names, *refs):
    refs = dict(zip(names, refs))
    for name in ("sums", "partials", "core_in", "b_in", "a_in", "z_in"):
        refs[name] = [refs.pop(f"{name}{n}") for n in range(5)]
    this = Collector(halves, refs)
    first, second, third, vectors = this.first, this.second, this.third, this.vectors
    entered, outcome_low, feed_grad = this.entered, this.outcome_low, this.feed_grad
    width = this.pieces.shape[1]
    count, feed = this.pieces.shape[0], third.shape[0]
    depth = this.table_grad.shape[1]
    head = width // HYPER_HEAD_COUNT
    scale = head ** (-0.5)
    this.greet()

    def store(n, columns, values):
        block = this.partials[n]
        block[:, :, :, :, columns] = values.astype(jnp.bfloat16).reshape(
            block.shape[:4] + (values.shape[1],)
        )

    grad_low = this.table_grad[...].astype(jnp.bfloat16)
    pooled_turned = jnp.transpose(this.pooled[...].astype(jnp.float32)).astype(jnp.bfloat16)
    for start in range(0, depth, TILE):
        store(EMBED, pl.ds(start, TILE), matmul(pooled_turned, grad_low[:, start : start + TILE]))
    this.start(EMBED)
    pooled_grad = times_trans(grad_low, second[:, pl.ds(0, depth)]) / slots
    outcome_grad = jnp.broadcast_to(pooled_grad[:, None, :], (count // slots, slots, width))
    outcome_grad = outcome_grad.reshape(count, width)
    outcome_low[...] = outcome_grad.astype(jnp.bfloat16)
    normed, inverse = center_norm(this.middle[...])
    entered[...] = jnp.transpose(normed * vectors[2:3] + vectors[3:4]).astype(jnp.bfloat16)
    feed_grad[...] = jnp.zeros_like(feed_grad)
    this.sum_core(EMBED)

    def feed_tiles(low, high):
        @pl.loop(low, high)
        def _(n):
            start = pl.multiple_of(n * TILE, TILE)
            tile = pl.ds(start, TILE)
            columns = pl.ds(pl.multiple_of(4 * width + start, TILE), TILE)
            values = this.expanded[:, tile]
            erf = 0.5 * (1.0 + lax.erf(values * inv_root_two))
            active = (values * erf).astype(jnp.bfloat16)
            block = this.partials[REDUCE]
            owned = block.shape[3]
            lines = TILE // (2 * owned)
            at = n * lines
            turned = trans_times(active, outcome_low[...]).astype(jnp.bfloat16)
            block[at // halves, pl.ds(at % halves, lines)] = turned.reshape(lines, 2, owned, width)
            active_grad = times_trans(outcome_low[...], third[tile, :])
            slope = erf + values * jnp.exp(-0.5 * values * values) * inv_root_tau
            low_grad = (active_grad * slope).astype(jnp.bfloat16)
            store(EXPAND, tile, matmul(entered[...], low_grad))
            feed_grad[...] += times_trans(low_grad, first[:, columns])

    tiles = feed // TILE
    feed_tiles(0, tiles // 2)
    this.sum_b(EMBED)
    feed_tiles(tiles // 2, tiles)
    this.start(EXPAND)
    this.start(REDUCE)
    this.sum_a(EMBED)

    grad = feed_grad[...]
    scale_two = jnp.sum(grad * normed, axis=0, keepdims=True)
    shift_two = jnp.sum(grad, axis=0, keepdims=True)
    middle_grad = outcome_grad + center_back(normed, inverse, grad * vectors[2:3])
    middle_low = middle_grad.astype(jnp.bfloat16)
    out_columns = pl.ds(3 * width, width)
    store(REAR, pl.ds(width, width), trans_times(this.mixed[...], middle_low))
    this.mixed_grad[...] = times_trans(middle_low, first[:, out_columns]).astype(jnp.bfloat16)
    mask = same_entry(CHUNK, slots)
    this.sum_core(EXPAND)

    def attention_chunks(low, high):
        @pl.loop(low, high)
        def _(n):
            rows = pl.ds(pl.multiple_of(n * CHUNK, CHUNK), CHUNK)
            block = this.heads[rows, :]
            outer_block = this.mixed_grad[rows, :]
            grads = [[], [], []]
            for start in range(0, width, head):
                query, key, value = (
                    block[:, part * width + start : part * width + start + head]
                    for part in range(3)
                )
                outer = outer_block[:, start : start + head]
                weights = slot_weights(query, key, mask, scale)
                weight_grad = gathered_slots(times_trans(value, outer), mask)
                score_grad = weights * (
                    weight_grad - jnp.sum(weights * weight_grad, axis=0, keepdims=True)
                )
                score_grad = spread_slots(score_grad, mask).astype(jnp.bfloat16)
                weights = spread_slots(weights, mask).astype(jnp.bfloat16)
                grads[0].append(trans_times(score_grad, key) * scale)
                grads[1].append(matmul(score_grad, query) * scale)
                grads[2].append(matmul(weights, outer))
            for part in range(3):
                this.heads_grad[rows, pl.ds(part * width, width)] = jnp.concatenate(
                    grads[part], axis=1
                ).astype(jnp.bfloat16)

    chunks = count // CHUNK
    attention_chunks(0, chunks // 2)
    this.sum_core(REDUCE)
    this.sum_b(EXPAND)
    attention_chunks(chunks // 2, chunks)
    this.sum_b(REDUCE)

    normed, _ = center_norm(this.pieces[...].astype(jnp.float32))
    entered[...] = jnp.transpose(normed * vectors[0:1] + vectors[1:2]).astype(jnp.bfloat16)
    feed_grad[...] = jnp.zeros_like(feed_grad)
    for start in range(0, 3 * width, TILE):
        columns = pl.ds(start, TILE)
        low_grad = this.heads_grad[:, columns]
        target = (FRONT, start) if start < 2 * width else (REAR, start - 2 * width)
        store(target[0], pl.ds(target[1], TILE), matmul(entered[...], low_grad))
        feed_grad[...] += times_trans(low_grad, first[:, columns])
        if start + TILE == 2 * width:
            this.start(FRONT)
            this.sum_a(EXPAND)
            this.sum_a(REDUCE)

    grad = feed_grad[...]
    scale_one = jnp.sum(grad * normed, axis=0, keepdims=True)
    shift_one = jnp.sum(grad, axis=0, keepdims=True)
    row = lax.broadcasted_iota(jnp.int32, (LANES, width), 0)
    summed = jnp.zeros((LANES, width), jnp.float32)
    for n, item in enumerate((scale_one, shift_one, scale_two, shift_two)):
        summed = jnp.where(row == n, item, summed)
    store(REAR, pl.ds(2 * width, LANES), jnp.transpose(summed))
    this.start(REAR)
    this.sum_core(FRONT)
    this.sum_core(REAR)
    for n in (EMBED, EXPAND, REDUCE):
        this.sum_lines(n)
    this.sum_b(FRONT)
    this.sum_b(REAR)
    this.sum_a(FRONT)
    this.sum_a(REAR)
    this.sum_lines(FRONT)
    this.sum_lines(REAR)
    for n in range(5):
        this.drain(n)


def hyper_collect(collective_id, wides, pieces, slots, params, stored, table_grad):
    count, width = pieces.shape
    first, second, third, vectors = params
    depth, feed = table_grad.shape[1], third.shape[0]
    devices, halves = SECTIONS * wides, wides // 2
    low, full = jnp.bfloat16, jnp.float32
    rows = width // devices
    shapes = [
        (rows, depth),
        (rows, feed),
        (feed // devices, width),
        (rows, 2 * width),
        (rows, 2 * width + LANES),
    ]
    inputs = dict(
        table_grad=table_grad,
        pieces=pieces,
        first=first,
        second=second,
        third=third,
        vectors=vectors,
    )
    inputs.update(zip(("heads", "mixed", "middle", "expanded", "pooled"), stored))
    outputs = {f"sums{n}": jax.ShapeDtypeStruct(shape, full) for n, shape in enumerate(shapes)}
    scratch = dict(
        entered=pltpu.VMEM((width, count), low),
        outcome_low=pltpu.VMEM((count, width), low),
        feed_grad=pltpu.VMEM((count, width), full),
        heads_grad=pltpu.VMEM((count, 3 * width), low),
        mixed_grad=pltpu.VMEM((count, width), low),
    )
    for name, slots_of in (
        ("partials", (SECTIONS, halves, 2)),
        ("core_in", (2, 2, halves)),
        ("b_in", (2, halves)),
        ("a_in", (halves,)),
        ("z_in", (halves,)),
    ):
        for n, shape in enumerate(shapes):
            scratch[f"{name}{n}"] = pltpu.VMEM(slots_of + shape, low)
    for name, numbers in (("core", (2, 2)), ("b", (2,)), ("a", ()), ("z", (halves,))):
        scratch[name + "_send"] = dma_sems(5, *numbers)
        scratch[name + "_recv"] = dma_sems(5, *numbers)
    return pl.pallas_call(
        functools.partial(hyper_collect_kernel, slots, halves, (*inputs, *outputs, *scratch)),
        out_shape=tuple(outputs.values()),
        in_specs=[IN_VMEM] * len(inputs),
        out_specs=(IN_VMEM,) * len(outputs),
        scratch_shapes=list(scratch.values()),
        compiler_params=settings(collective_id),
        name="hyper_collect",
    )(*inputs.values())


def team_groups(wides, outer):
    return [[rank * outer + team for team in range(outer)] for rank in range(wides // outer)]


def all_teams(pieces, outer, groups):
    if outer == 1:
        return pieces
    pieces = [
        lax.all_gather(piece, "wide", axis=1, axis_index_groups=groups) for piece in pieces
    ]
    return [piece.reshape((-1,) + piece.shape[2:]) for piece in pieces]


def shards(
    token_ids,
    targets,
    slot_ids,
    group_ids,
    group_offsets,
    piece_table,
    prenorm_gain,
    prenorm_bias,
    query_map,
    key_map,
    value_map,
    output_map,
    midnorm_gain,
    midnorm_bias,
    expand_map,
    reduce_map,
    embed_map,
    attention_gain,
    query_weight,
    key_weight,
    value_weight,
    output_weight,
    feed_gain,
    gate_weight,
    up_weight,
    down_weight,
    final_gain,
):
    wides = lax.axis_size("wide")
    outer = wides // TEAM
    groups = team_groups(wides, outer)
    section_index = lax.axis_index("section")
    wide_index = lax.axis_index("wide")
    rank = wide_index // outer
    hyper_width, hyper_feed = piece_table.shape[1], expand_map.shape[1]
    model_width = embed_map.shape[1]
    total_tokens = wides * MB * LEN

    entries, slot_count = slot_ids.shape
    group_hits = (
        group_ids[:, None] == jnp.arange(group_offsets.shape[0], dtype=jnp.int32)[None, :]
    ).astype(jnp.int32)
    row_start = jnp.sum(group_hits * group_offsets[None, :], axis=1)
    piece_rows = (row_start[:, None] + slot_ids).reshape(-1)
    pieces = jnp.take(piece_table, piece_rows, axis=0)

    *columns, first, second, third, gains, notes = pack(
        (query_weight, key_weight, value_weight, gate_weight, up_weight),
        (query_map, key_map, value_map, output_map, expand_map, embed_map, reduce_map),
        jnp.stack([prenorm_gain, prenorm_bias, midnorm_gain, midnorm_bias]),
        (attention_gain, feed_gain),
        jnp.concatenate([token_ids, targets], axis=1).reshape(2 * MB, LEN),
    )
    blocks = (first, second, third)
    whole_tiles = query_map.shape[0] % 16 == 0
    work = hyper_work(pieces, slot_count, hyper_feed, model_width) if whole_tiles else Work()
    first, second, third, gains, notes, own_one, own_two, *made = spread(
        1, wides, outer, blocks, (gains, notes), columns, work
    )
    first = first.reshape(hyper_width, -1)
    second = second.reshape(hyper_width, -1)
    third = third.reshape(hyper_feed, hyper_width)
    if whole_tiles:
        vectors, table_shard, *hyper_stored = made
        params = (first, second, third, vectors)
    else:
        vectors = second[:, model_width : model_width + 8].astype(jnp.float32).T
        params = (first, second, third, vectors)
        table_shard, hyper_stored = hyper_forward(pieces, slot_count, params)

    if outer > 1:
        gains = lax.all_gather(gains, "wide", axis=1, axis_index_groups=groups)
        gains = gains.reshape(-1, gains.shape[2], gains.shape[3])
        output_weight, down_weight = (
            lax.all_gather(item, "wide", axis=1, axis_index_groups=groups, tiled=True)
            for item in (output_weight, down_weight)
        )
    gains = gains.transpose(1, 0, 2).reshape(-1, model_width)
    final_scale = final_gain.astype(jnp.float32).reshape(1, model_width)
    gains = jnp.concatenate([gains[:4], final_scale, gains[:3]], axis=0)
    notes = lax.dynamic_slice_in_dim(notes, section_index * 2, 2, 0)
    ids, wanted = notes[:, 0].reshape(-1), notes[:, 1].reshape(-1)

    table_rows = section_gather(3, table_shard)
    if outer > 1:
        table_rows = lax.all_gather(table_rows, "wide", axis=1, axis_index_groups=groups)
    table_rows = table_rows.reshape(-1, model_width)
    wide_rows = rank * outer + jnp.arange(outer, dtype=jnp.int32)
    row_starts = (
        jnp.arange(SECTIONS, dtype=jnp.int32)[:, None] * wides + wide_rows[None, :]
    ) * entries
    own_rows = row_starts[:, :, None] + jnp.arange(entries, dtype=jnp.int32)[None, None, :]
    own_rows = own_rows.reshape(-1)
    own_rows = own_rows.reshape(-1, 1)

    def by_halves(numbers):
        return jnp.pad(numbers.reshape(2, -1), ((0, 6), (0, 0)))

    normed, grads, logit_grad, loss_block = decode(
        outer,
        4,
        total_tokens,
        all_teams((own_one, own_two), outer, groups),
        output_weight,
        down_weight,
        gains,
        (turn_tables(False), turn_tables(True)),
        table_rows,
        own_rows,
        by_halves(ids),
        by_halves(wanted),
    )

    hits = (own_rows == ids[None, :]).astype(jnp.bfloat16)
    table_part = matmul(logit_grad, normed.reshape(ROWS, model_width)) + matmul(
        hits, grads.reshape(ROWS, model_width)
    )
    table_part = table_part.astype(jnp.bfloat16).reshape(SECTIONS, outer, entries, model_width)
    if outer > 1:
        table_part = lax.psum_scatter(
            table_part.astype(jnp.float32),
            "wide",
            scatter_dimension=1,
            axis_index_groups=groups,
        ).astype(jnp.bfloat16)
        loss_block = lax.psum(loss_block, "wide", axis_index_groups=groups)
    table_grad, loss_block = section_sum(
        11, table_part.reshape(SECTIONS, entries, model_width), loss_block
    )
    mean_loss = loss_block[0, 0]
    if whole_tiles:
        grad_embed, grad_expand, grad_reduce, front, rear = hyper_collect(
            12, wides, pieces, slot_count, params, hyper_stored, table_grad
        )
    else:
        grads = hyper_backward(pieces, slot_count, params, hyper_stored, table_grad)
        grads = [item.reshape(SECTIONS, wides, -1, item.shape[1]) for item in grads]
        first, second, grad_reduce = collect(12, grads)
        grad_embed, grad_expand = second[:, :model_width], first[:, 4 * hyper_width :]
        front = first[:, : 2 * hyper_width]
        rear = jnp.concatenate(
            [first[:, 2 * hyper_width : 4 * hyper_width], second[:, model_width:]], axis=1
        )
    if whole_tiles:
        outs = deliver(grad_embed, grad_expand, grad_reduce, front, rear)
    else:
        vectors = rear[:, 2 * hyper_width : 2 * hyper_width + 4]
        outs = [vectors[:, n] for n in range(4)]
        outs += [front[:, :hyper_width], front[:, hyper_width:]]
        outs += [rear[:, :hyper_width], rear[:, hyper_width : 2 * hyper_width]]
        outs += [grad_expand, grad_reduce, grad_embed]
    prescale, prebias, midscale, midshift, *maps = outs
    return (mean_loss, prescale, prebias, *maps[:4], midscale, midshift, *maps[4:])


def solution(mesh):
    placed = (
        P("wide", None, None),
        P("wide", None, None),
        P(("section", "wide"), None),
        P(("section", "wide")),
        P(),
        P(),
        P(("section", "wide")),
        P(("section", "wide")),
        P(("section", "wide"), None),
        P(("section", "wide"), None),
        P(("section", "wide"), None),
        P(("section", "wide"), None),
        P(("section", "wide")),
        P(("section", "wide")),
        P(("section", "wide"), None),
        P(("section", "wide"), None),
        P(("section", "wide"), None),
        P(None, "wide"),
        P(None, "wide", None),
        P(None, "wide", None),
        P(None, "wide", None),
        P(None, "wide", None),
        P(None, "wide"),
        P(None, "wide", None),
        P(None, "wide", None),
        P(None, "wide", None),
        P(),
    )
    return jax.shard_map(
        shards,
        mesh=mesh,
        in_specs=placed,
        out_specs=(
            P(),
            P(("section", "wide")),
            P(("section", "wide")),
            P(("section", "wide"), None),
            P(("section", "wide"), None),
            P(("section", "wide"), None),
            P(("section", "wide"), None),
            P(("section", "wide")),
            P(("section", "wide")),
            P(("section", "wide"), None),
            P(("section", "wide"), None),
            P(("section", "wide"), None),
        ),
        check_vma=False,
    )
```

```python
import functools

import jax
import jax.numpy as jnp
from jax import lax
from jax.experimental import pallas as pl
from jax.experimental.pallas import tpu as pltpu
from jax.sharding import PartitionSpec as P

HEAD_DIM = 64
HYPER_HEAD_COUNT = 8
MB = 2
LEN = 64
TEAM = 8
SECTIONS = 4
ROWS = MB * LEN * TEAM // SECTIONS
HALF = ROWS // 2
EACH = HALF // TEAM
LINES = TEAM // 2
FIRST, SECOND = 0, 1
LANES = 128
MESH_IDS = pl.DeviceIdType.MESH
ANYWHERE = pl.BlockSpec(memory_space=pl.ANY)
IN_VMEM = pl.BlockSpec(memory_space=pltpu.VMEM)
VMEM_LIMIT = 56 * 1024 * 1024

norm_eps = 1e-05
inv_root_two = 0.7071067811865476
inv_root_tau = 0.3989422804014327


def matmul(former, latter):
    return jnp.dot(former, latter, preferred_element_type=jnp.float32)


def times_trans(former, latter):
    return lax.dot_general(
        former, latter, (((1,), (1,)), ((), ())), preferred_element_type=jnp.float32
    )


def trans_times(former, latter):
    return lax.dot_general(
        former, latter, (((0,), (0,)), ((), ())), preferred_element_type=jnp.float32
    )


def center_norm(values):
    center = values - jnp.mean(values, axis=-1, keepdims=True)
    inverse = lax.rsqrt(jnp.mean(center * center, axis=-1, keepdims=True) + norm_eps)
    return (center * inverse, inverse)


def center_back(normed, inverse, normed_grad):
    mean_grad = jnp.mean(normed_grad, axis=-1, keepdims=True)
    mean_mix = jnp.mean(normed_grad * normed, axis=-1, keepdims=True)
    return inverse * (normed_grad - mean_grad - normed * mean_mix)


def root_inverse(values):
    return lax.rsqrt(jnp.mean(values * values, axis=-1, keepdims=True) + norm_eps)


def reciprocal_root_backward(values, inverse, gain_vec, outer_grad):
    scaled = outer_grad * gain_vec
    mixing = jnp.mean(scaled * values, axis=-1, keepdims=True)
    return inverse * scaled - values * inverse * inverse * inverse * mixing


def rope_tables(positions, head_width):
    halfway = head_width // 2
    frequency = jnp.exp(
        -jnp.log(10000.0) * (2.0 * jnp.arange(halfway, dtype=jnp.float32) / head_width)
    )
    angles = jnp.arange(positions, dtype=jnp.float32)[:, None] * frequency[None, :]
    angles = jnp.concatenate([angles, angles], axis=1)
    return (jnp.cos(angles), jnp.sin(angles))


def greet(peers):
    barrier = pltpu.get_barrier_semaphore()
    for peer in peers:
        pl.semaphore_signal(barrier, inc=1, device_id=peer, device_id_type=MESH_IDS)
    pl.semaphore_wait(barrier, len(peers))


def remote(source, target, send, recv, peer):
    return pltpu.make_async_remote_copy(
        src_ref=source,
        dst_ref=target,
        send_sem=send,
        recv_sem=recv,
        device_id=peer,
        device_id_type=MESH_IDS,
    )


def settings(collective_id):
    return pltpu.CompilerParams(
        collective_id=collective_id, has_side_effects=True, vmem_limit_bytes=VMEM_LIMIT
    )


def dma_sems(*shape):
    return pltpu.SemaphoreType.DMA(shape)


def section_places():
    section = lax.axis_index("section")
    core = section % 2
    partner = section + 1 - 2 * core
    across = (section + 2) % SECTIONS
    return section, partner, across


def section_gather_kernel(block, gathered, keep_sem, send, recv):
    section, partner, across = section_places()
    greet([{"section": partner}, {"section": across}])
    keep = pltpu.make_async_copy(block, gathered.at[section], keep_sem)
    near = remote(block, gathered.at[section], send.at[0], recv.at[0], {"section": partner})
    far = remote(block, gathered.at[section], send.at[1], recv.at[1], {"section": across})
    on = remote(
        gathered.at[across], gathered.at[across], send.at[2], recv.at[2], {"section": partner}
    )
    far.start()
    near.start()
    keep.start()
    far.wait_recv()
    on.start()
    near.wait()
    on.wait()
    far.wait_send()
    keep.wait()


def section_gather(collective_id, block):
    return pl.pallas_call(
        section_gather_kernel,
        out_shape=jax.ShapeDtypeStruct((SECTIONS,) + block.shape, block.dtype),
        in_specs=[ANYWHERE],
        out_specs=ANYWHERE,
        scratch_shapes=[pltpu.SemaphoreType.DMA, dma_sems(3), dma_sems(3)],
        compiler_params=settings(collective_id),
        name="section_gather",
    )(block)


def section_sum_kernel(partial, loss, summed, loss_sum, own, near, pair, far, loss_near, loss_pair, loss_far, load_sem, send, recv):
    section, partner, across = section_places()
    beyond = (partner + 2) % SECTIONS
    greet([{"section": partner}, {"section": across}])
    loads = [
        pltpu.make_async_copy(partial.at[section], own.at[0], load_sem.at[0]),
        pltpu.make_async_copy(partial.at[across], own.at[1], load_sem.at[1]),
    ]
    nears = [
        remote(partial.at[partner], near.at[0], send.at[0], recv.at[0], {"section": partner}),
        remote(partial.at[beyond], near.at[1], send.at[1], recv.at[1], {"section": partner}),
        remote(loss, loss_near, send.at[2], recv.at[2], {"section": partner}),
    ]
    fars = [
        remote(pair, far, send.at[3], recv.at[3], {"section": across}),
        remote(loss_pair, loss_far, send.at[4], recv.at[4], {"section": across}),
    ]
    for j in (1, 2, 0):
        nears[j].start()
    loads[1].start()
    loads[0].start()
    loads[1].wait()
    nears[1].wait_recv()
    pair[...] = (own[1].astype(jnp.float32) + near[1].astype(jnp.float32)).astype(jnp.bfloat16)
    fars[0].start()
    nears[2].wait_recv()
    loss_pair[...] = loss[...] + loss_near[...]
    fars[1].start()
    loads[0].wait()
    nears[0].wait_recv()
    total = own[0].astype(jnp.float32) + near[0].astype(jnp.float32)
    fars[0].wait_recv()
    summed[...] = total + far[...].astype(jnp.float32)
    fars[1].wait_recv()
    loss_sum[...] = loss_pair[...] + loss_far[...]
    for copy in nears + fars:
        copy.wait_send()


def section_sum(collective_id, partial, loss):
    shape = partial.shape[1:]
    low, low_two = pltpu.VMEM(shape, jnp.bfloat16), pltpu.VMEM((2,) + shape, jnp.bfloat16)
    number = pltpu.VMEM(loss.shape, jnp.float32)
    return pl.pallas_call(
        section_sum_kernel,
        out_shape=(
            jax.ShapeDtypeStruct(shape, jnp.float32),
            jax.ShapeDtypeStruct(loss.shape, jnp.float32),
        ),
        in_specs=[ANYWHERE, IN_VMEM],
        out_specs=(IN_VMEM, IN_VMEM),
        scratch_shapes=[low_two, low_two, low, low, number, number, number]
        + [dma_sems(2), dma_sems(5), dma_sems(5)],
        compiler_params=settings(collective_id),
        name="section_sum",
    )(partial, loss)


def all_places(halves):
    section, partner, across = section_places()
    wide = lax.axis_index("wide")
    line, column = wide // 2, wide % 2

    def wide_at(j):
        return ((line + j) % halves) * 2 + column

    return section, partner, across, wide, wide_at


def steps_of(x_first, section, partner, across, wide):
    column_flip = wide + 1 - 2 * (wide % 2)
    x_step = ({"wide": column_flip}, False, True)
    y_step = ({"section": across}, True, False)
    return (x_step, y_step) if x_first else (y_step, x_step)


def owner_of(home, flips_y, flips_x, wide_block):
    section = (home + 2) % SECTIONS if flips_y else home
    return section, (wide_block + 1 - 2 * (wide_block % 2) if flips_x else wide_block)


def spread_kernel(count, halves, outer, work, *refs):
    blocks, notes, columns = refs[:count], refs[count : count + 2], refs[count + 2 : count + 4]
    refs = refs[count + 4 :]
    extra, refs = refs[: work.inputs], refs[work.inputs :]
    outs, notes_out, columns_out = refs[:count], refs[count : count + 2], refs[count + 2 : count + 4]
    refs = refs[count + 4 :]
    extra, refs = extra + refs[: work.outputs], refs[work.outputs :]
    gathereds = outs
    if work.body is not None:
        gathereds, refs = refs[:count], refs[count:]
    (
        keep_sem,
        note_keep,
        note_send,
        note_recv,
        z_send,
        a_send,
        b_send,
        c_send,
        z_recv,
        a_recv,
        b_recv,
        c_recv,
    ) = refs[:12]
    section, partner, across, wide, wide_at = all_places(halves)
    rank, team = wide // outer, wide % outer
    members = [None] + [{"wide": (rank + k) % TEAM * outer + team} for k in range(1, TEAM)]
    beside = wide + 1 - 2 * (wide % 2)
    barrier = pltpu.get_barrier_semaphore()
    for peer in ({"section": partner}, {"section": across}, {"wide": beside}):
        pl.semaphore_signal(barrier, inc=1, device_id=peer, device_id_type=MESH_IDS)

    def hello(j, carry):
        peer = {"wide": wide_at(j)}
        pl.semaphore_signal(barrier, inc=1, device_id=peer, device_id_type=MESH_IDS)
        return carry

    lax.fori_loop(1, halves, hello, 0)
    for peer in members[1:]:
        pl.semaphore_signal(barrier, inc=1, device_id=peer, device_id_type=MESH_IDS)
    pl.semaphore_wait(barrier, 3 + halves - 1 + TEAM - 1)
    note_keeps = [
        pltpu.make_async_copy(notes[m], notes_out[m].at[rank], note_keep.at[m]) for m in range(2)
    ]
    note_copies = [
        remote(notes[m], notes_out[m].at[rank], note_send.at[m, k], note_recv.at[m, k], members[k])
        for m in range(2)
        for k in range(1, TEAM)
    ]
    column_copies = []
    for layer in range(2):
        column_copies.append(
            pltpu.make_async_copy(
                columns[layer].at[rank], columns_out[layer].at[rank], note_keep.at[2 + layer]
            )
        )
        column_copies += [
            remote(
                columns[layer].at[(rank + k) % TEAM],
                columns_out[layer].at[rank],
                note_send.at[2 + layer, k],
                note_recv.at[2 + layer, k],
                members[k],
            )
            for k in (4, 3, 5, 2, 6, 1, 7)
        ]
    for copy in note_keeps + note_copies:
        copy.start()

    keeps = [
        pltpu.make_async_copy(blocks[n], gathereds[n].at[section, wide], keep_sem.at[n])
        for n in range(count)
    ]

    def z_copy(n, j):
        return remote(
            blocks[n],
            gathereds[n].at[section, wide],
            z_send.at[n, j],
            z_recv.at[n, j],
            {"wide": wide_at(j)},
        )

    def a_copy(n, j):
        (peer, _, _), _ = steps_of(n == 0, section, partner, across, wide)
        block = gathereds[n].at[section, wide_at(-j)]
        return remote(block, block, a_send.at[n, j], a_recv.at[n, j], peer)

    def b_copy(n, flip, j):
        (_, y_a, x_a), (peer, _, _) = steps_of(n == 0, section, partner, across, wide)
        place = owner_of(section, y_a and flip, x_a and flip, wide_at(-j))
        block = gathereds[n].at[place[0], place[1]]
        slot = j + (halves if flip else 0)
        return remote(block, block, b_send.at[n, slot], b_recv.at[n, slot], peer)

    def c_copy(n, which):
        home = (section + 2) % SECTIONS if which else section
        block = gathereds[n].at[home]
        return remote(
            block, block, c_send.at[n, which], c_recv.at[n, which], {"section": partner}
        )

    for keep in keeps:
        keep.start()

    def start_z(j, carry):
        for n in range(count):
            z_copy(n, j).start()
        return carry

    lax.fori_loop(1, halves, start_z, 0)
    work.begin(extra + refs[12:])
    for n in range(count):
        keeps[n].wait()
        a_copy(n, 0).start()
        b_copy(n, False, 0).start()

    def pass_z(j, carry):
        for n in range(count):
            z_copy(n, j).wait_recv()
            a_copy(n, j).start()
            b_copy(n, False, j).start()
        return carry

    lax.fori_loop(1, halves, pass_z, 0)
    for copy in column_copies:
        copy.start()

    def pass_a(j, carry):
        for n in range(count):
            a_copy(n, j).wait_recv()
            b_copy(n, True, j).start()
        return carry

    lax.fori_loop(0, halves, pass_a, 0)

    def settle_b(j, carry):
        for n in range(count):
            for flip in (False, True):
                b_copy(n, flip, j).wait_recv()
        return carry

    c_copy(0, 0).start()
    lax.fori_loop(0, halves, settle_b, 0)
    c_copy(0, 1).start()
    for n in range(1, count):
        c_copy(n, 0).start()
        c_copy(n, 1).start()
    for n in range(count):
        c_copy(n, 0).wait()
        c_copy(n, 1).wait()

    def drain(j, carry):
        for n in range(count):
            a_copy(n, j).wait_send()
            b_copy(n, False, j).wait_send()
            b_copy(n, True, j).wait_send()
        return carry

    lax.fori_loop(0, halves, drain, 0)

    def drain_z(j, carry):
        for n in range(count):
            z_copy(n, j).wait_send()
        return carry

    lax.fori_loop(1, halves, drain_z, 0)
    copies = []
    if work.body is not None:
        copies = [
            pltpu.make_async_copy(gathereds[n], outs[n], keep_sem.at[n]) for n in range(count)
        ]
    for copy in copies:
        copy.start()
    work.run(gathereds, extra + refs[12:])
    for copy in copies:
        copy.wait()
    for copy in note_keeps + note_copies + column_copies:
        copy.wait()


class Work:
    def __init__(self, early=None, body=None, operands=(), outs=(), scratch=()):
        self.early, self.body = early, body
        self.operands, self.outs, self.scratch = operands, outs, scratch
        self.inputs, self.outputs = len(operands), len(outs)

    def begin(self, refs):
        if self.early is not None:
            self.early(*refs)

    def run(self, gathereds, refs):
        if self.body is not None:
            self.body(gathereds, *refs)


def spread(collective_id, wides, outer, blocks, notes, columns, work):
    count, halves = len(blocks), wides // 2
    held = [] if work.body is None else blocks
    return pl.pallas_call(
        functools.partial(spread_kernel, count, halves, outer, work),
        out_shape=tuple(
            jax.ShapeDtypeStruct((SECTIONS, wides) + block.shape, block.dtype) for block in blocks
        )
        + tuple(jax.ShapeDtypeStruct((TEAM,) + note.shape, note.dtype) for note in notes)
        + tuple(jax.ShapeDtypeStruct(item.shape, item.dtype) for item in columns)
        + tuple(jax.ShapeDtypeStruct(shape, kind) for shape, kind, _ in work.outs),
        in_specs=[ANYWHERE] * (count + 4) + [place for _, place in work.operands],
        out_specs=(ANYWHERE,) * (count + 4) + tuple(place for _, _, place in work.outs),
        scratch_shapes=[
            pltpu.VMEM((SECTIONS, wides) + block.shape, block.dtype) for block in held
        ]
        + [dma_sems(count), dma_sems(4), dma_sems(4, TEAM), dma_sems(4, TEAM)]
        + [
            dma_sems(count, halves),
            dma_sems(count, halves),
            dma_sems(count, 2 * halves),
            dma_sems(count, 2),
        ]
        * 2
        + list(work.scratch),
        compiler_params=settings(collective_id),
        name="spread",
    )(*blocks, *notes, *columns, *(item for item, _ in work.operands))


def collect_kernel(count, halves, *refs):
    partials, sums = refs[:count], refs[count : 2 * count]
    keeps, c_in, b_in, a_in, z_in = (refs[(2 + k) * count : (3 + k) * count] for k in range(5))
    load_sem, c_send, b_send, a_send, z_send, c_recv, b_recv, a_recv, z_recv = refs[7 * count :]
    section, partner, across, wide, wide_at = all_places(halves)
    beside = wide + 1 - 2 * (wide % 2)
    barrier = pltpu.get_barrier_semaphore()
    for peer in ({"section": partner}, {"section": across}, {"wide": beside}):
        pl.semaphore_signal(barrier, inc=1, device_id=peer, device_id_type=MESH_IDS)

    def hello(j, carry):
        peer = {"wide": wide_at(j)}
        pl.semaphore_signal(barrier, inc=1, device_id=peer, device_id_type=MESH_IDS)
        return carry

    lax.fori_loop(1, halves, hello, 0)
    pl.semaphore_wait(barrier, 3 + halves - 1)

    def place(n, home, flip_b, flip_a, j):
        (_, y_a, x_a), (_, y_b, x_b) = steps_of(n == 0, section, partner, across, wide)
        flips_y = (y_a and flip_a) or (y_b and flip_b)
        flips_x = (x_a and flip_a) or (x_b and flip_b)
        return owner_of(home, flips_y, flips_x, wide_at(j))

    def load(n, fb, fa, j):
        owner = place(n, section, fb, fa, j)
        slot = (fb * 2 + fa) * halves + j
        return pltpu.make_async_copy(
            partials[n].at[owner[0], owner[1]], keeps[n].at[slot], load_sem.at[n, slot]
        )

    def c_copy(n, fb, fa, j):
        owner = place(n, partner, fb, fa, j)
        slot = (fb * 2 + fa) * halves + j
        return remote(
            partials[n].at[owner[0], owner[1]],
            c_in[n].at[slot],
            c_send.at[n, slot],
            c_recv.at[n, slot],
            {"section": partner},
        )

    def b_copy(n, fa, j):
        _, (peer, _, _) = steps_of(n == 0, section, partner, across, wide)
        slot = fa * halves + j
        return remote(
            keeps[n].at[2 * halves + slot],
            b_in[n].at[slot],
            b_send.at[n, slot],
            b_recv.at[n, slot],
            peer,
        )

    def a_copy(n, j):
        (peer, _, _), _ = steps_of(n == 0, section, partner, across, wide)
        return remote(
            keeps[n].at[halves + j], a_in[n].at[j], a_send.at[n, j], a_recv.at[n, j], peer
        )

    def z_copy(n, j):
        return remote(
            keeps[n].at[j],
            z_in[n].at[j],
            z_send.at[n, j],
            z_recv.at[n, j],
            {"wide": wide_at(j)},
        )

    def add(n, slot, more):
        keeps[n][slot] = (
            keeps[n][slot].astype(jnp.float32) + more.astype(jnp.float32)
        ).astype(jnp.bfloat16)

    groups = ((1, 1), (1, 0), (0, 1), (0, 0))
    for fb, fa in groups:

        def start_c(j, carry):
            for n in range(count):
                c_copy(n, fb, fa, j).start()
                load(n, fb, fa, j).start()
            return carry

        lax.fori_loop(0, halves, start_c, 0)

    for fb, fa in groups:

        def sum_c(j, carry):
            for n in range(count):
                slot = (fb * 2 + fa) * halves + j
                load(n, fb, fa, j).wait()
                c_copy(n, fb, fa, j).wait_recv()
                add(n, slot, c_in[n][slot])
                if fb:
                    b_copy(n, fa, j).start()
            return carry

        lax.fori_loop(0, halves, sum_c, 0)

    for fa in (1, 0):

        def sum_b(j, carry):
            for n in range(count):
                slot = fa * halves + j
                b_copy(n, fa, j).wait_recv()
                add(n, slot, b_in[n][slot])
                if fa:
                    a_copy(n, j).start()
            return carry

        lax.fori_loop(0, halves, sum_b, 0)

    def sum_a(j, carry):
        for n in range(count):
            a_copy(n, j).wait_recv()
            add(n, j, a_in[n][j])
            z_copy(n, j).start()
        return carry

    lax.fori_loop(1, halves, sum_a, 0)
    for n in range(count):
        a_copy(n, 0).wait_recv()
        sums[n][...] = keeps[n][0].astype(jnp.float32) + a_in[n][0].astype(jnp.float32)

    def sum_z(j, carry):
        for n in range(count):
            z_copy(n, j).wait_recv()
            sums[n][...] += z_in[n][j].astype(jnp.float32)
        return carry

    lax.fori_loop(1, halves, sum_z, 0)

    def drain(j, carry):
        for n in range(count):
            for fb, fa in groups:
                c_copy(n, fb, fa, j).wait_send()
            b_copy(n, 0, j).wait_send()
            b_copy(n, 1, j).wait_send()
            a_copy(n, j).wait_send()
        return carry

    lax.fori_loop(0, halves, drain, 0)

    def drain_z(j, carry):
        for n in range(count):
            z_copy(n, j).wait_send()
        return carry

    lax.fori_loop(1, halves, drain_z, 0)


def collect(collective_id, partials):
    count, halves = len(partials), partials[0].shape[1] // 2
    shapes = [partial.shape[2:] for partial in partials]

    def slots(number):
        return [pltpu.VMEM((number,) + shape, jnp.bfloat16) for shape in shapes]

    return pl.pallas_call(
        functools.partial(collect_kernel, count, halves),
        out_shape=tuple(jax.ShapeDtypeStruct(shape, jnp.float32) for shape in shapes),
        in_specs=[ANYWHERE] * count,
        out_specs=(IN_VMEM,) * count,
        scratch_shapes=slots(4 * halves)
        + slots(4 * halves)
        + slots(2 * halves)
        + slots(halves)
        + slots(halves)
        + [dma_sems(count, 4 * halves)]
        + [
            dma_sems(count, 4 * halves),
            dma_sems(count, 2 * halves),
            dma_sems(count, halves),
            dma_sems(count, halves),
        ]
        * 2,
        compiler_params=settings(collective_id),
        name="collect",
    )(*partials)


TILE = 256


def causal_blocks(count, length):
    row = lax.broadcasted_iota(jnp.int32, (count, count), 0)
    column = lax.broadcasted_iota(jnp.int32, (count, count), 1)
    return (row // length == column // length) & (column <= row)


def turn(values, tables):
    cosines, upper, lower = tables
    parts = []
    for start in range(0, values.shape[1], LANES):
        part = values[:, start : start + LANES]
        ahead = pltpu.roll(part, LANES - HEAD_DIM // 2, 1)
        behind = pltpu.roll(part, HEAD_DIM // 2, 1)
        parts.append(part * cosines + ahead * upper + behind * lower)
    return parts[0] if len(parts) == 1 else jnp.concatenate(parts, axis=1)


def turn_tables(back):
    cosines, sines = rope_tables(LEN, HEAD_DIM)
    sines = -sines if back else sines
    first = jnp.arange(HEAD_DIM) < HEAD_DIM // 2
    upper, lower = jnp.where(first, -sines, 0.0), jnp.where(first, 0.0, sines)
    blank = jnp.zeros_like(cosines)
    pairs = [(cosines, cosines), (upper, upper), (lower, lower)]
    pairs += [(cosines, blank + 1.0), (upper, blank), (lower, blank)]
    tables = jnp.stack([jnp.concatenate(pair, axis=1) for pair in pairs])
    return jnp.tile(tables, (1, HALF // LEN, 1))


def attend(queries, key, mask, scale):
    scores = times_trans(queries, key) * scale
    scores = jnp.where(mask, scores, -1e30)
    peak = jnp.max(scores, axis=1, keepdims=True)
    mass = jnp.exp(scores - peak)
    return mass / jnp.sum(mass, axis=1, keepdims=True)


def local(kernel, operands, outs, scratch, name):
    return pl.pallas_call(
        kernel,
        out_shape=tuple(jax.ShapeDtypeStruct(shape, kind) for shape, kind in outs),
        in_specs=[IN_VMEM] * len(operands),
        out_specs=(IN_VMEM,) * len(outs),
        scratch_shapes=list(scratch),
        compiler_params=pltpu.CompilerParams(vmem_limit_bytes=VMEM_LIMIT),
        name=name,
    )(*operands)


CHUNK = 128


def same_entry(count, slots):
    entry = lax.broadcasted_iota(jnp.int32, (count // slots, slots, count), 0)
    column = lax.broadcasted_iota(jnp.int32, (count // slots, slots, count), 2)
    return entry == column // slots


def gathered_slots(products, mask):
    return jnp.sum(jnp.where(mask, products.reshape(mask.shape), 0.0), axis=0)


def spread_slots(values, mask):
    spread = jnp.where(mask, values[None], 0.0)
    return spread.reshape(mask.shape[0] * mask.shape[1], mask.shape[2])


def slot_weights(query, key, mask, scale):
    scores = gathered_slots(times_trans(key, query), mask) * scale
    mass = jnp.exp(scores - jnp.max(scores, axis=0, keepdims=True))
    return mass / jnp.sum(mass, axis=0, keepdims=True)


def gelu(values):
    return 0.5 * values * (1.0 + lax.erf(values * inv_root_two))


def hyper_kernel(
    slots,
    pieces,
    first,
    second,
    third,
    vectors,
    table,
    heads_out,
    mixed_out,
    middle_out,
    expanded_out,
    pooled_out,
    entered,
    outcome,
    done=lambda *names: None,
):
    width = pieces.shape[1]
    count, feed = pieces.shape[0], third.shape[0]
    head = width // HYPER_HEAD_COUNT
    flat = pieces[...].astype(jnp.float32)
    normed, _ = center_norm(flat)
    entered[...] = (normed * vectors[0:1] + vectors[1:2]).astype(jnp.bfloat16)

    @pl.loop(0, 3 * width // TILE)
    def _(n):
        columns = pl.ds(pl.multiple_of(n * TILE, TILE), TILE)
        heads_out[:, columns] = matmul(entered[...], first[:, columns]).astype(jnp.bfloat16)

    mask = same_entry(CHUNK, slots)

    @pl.loop(0, count // CHUNK)
    def _(n):
        rows = pl.ds(pl.multiple_of(n * CHUNK, CHUNK), CHUNK)
        block = heads_out[rows, :]
        mixed = []
        for start in range(0, width, head):
            query, key, value = (
                block[:, part * width + start : part * width + start + head] for part in range(3)
            )
            weights = slot_weights(query, key, mask, head ** (-0.5))
            weights = spread_slots(weights, mask).astype(jnp.bfloat16)
            mixed.append(trans_times(weights, value))
        mixed_out[rows, :] = jnp.concatenate(mixed, axis=1).astype(jnp.bfloat16)

    done("heads", "mixed")
    for start in range(0, width, TILE):
        columns = pl.ds(start, TILE)
        middle_out[:, columns] = pieces[:, columns].astype(jnp.float32) + matmul(
            mixed_out[...], first[:, pl.ds(3 * width + start, TILE)]
        )
    done("middle")
    normed, _ = center_norm(middle_out[...])
    entered[...] = (normed * vectors[2:3] + vectors[3:4]).astype(jnp.bfloat16)
    outcome[...] = middle_out[...]

    @pl.loop(0, feed // TILE)
    def _(n):
        start = pl.multiple_of(n * TILE, TILE)
        columns = pl.ds(pl.multiple_of(4 * width + start, TILE), TILE)
        expanded = matmul(entered[...], first[:, columns])
        expanded_out[:, pl.ds(start, TILE)] = expanded
        outcome[...] += matmul(gelu(expanded).astype(jnp.bfloat16), third[pl.ds(start, TILE), :])

    done("expanded")
    pooled = jnp.mean(outcome[...].reshape(count // slots, slots, width), axis=1)
    pooled_out[...] = pooled.astype(jnp.bfloat16)

    @pl.loop(0, table.shape[1] // TILE)
    def _(n):
        columns = pl.ds(pl.multiple_of(n * TILE, TILE), TILE)
        table[:, columns] = matmul(pooled_out[...], second[:, columns]).astype(jnp.bfloat16)


class Rows:
    def __init__(self, blocks):
        self.blocks = blocks
        sections, wides, rows, columns = blocks.shape
        self.wides, self.rows, self.shape = wides, rows, (sections * wides * rows, columns)

    def __getitem__(self, index):
        rows, columns = index
        if rows == slice(None):
            values = self.blocks[:, :, :, columns]
        else:
            first = rows.start // self.rows
            owners = pl.ds(first % self.wides, rows.size // self.rows)
            values = self.blocks[first // self.wides, owners]
        return values.reshape(-1, values.shape[-1])


def hyper_outs(count, slots, width, feed, depth):
    entries = count // slots
    return [
        ((entries, depth), jnp.bfloat16),
        ((count, 3 * width), jnp.bfloat16),
        ((count, width), jnp.bfloat16),
        ((count, width), jnp.float32),
        ((count, feed), jnp.float32),
        ((entries, width), jnp.bfloat16),
    ]


def hyper_scratch(count, width):
    return [pltpu.VMEM((count, width), jnp.bfloat16), pltpu.VMEM((count, width), jnp.float32)]


def hyper_work(piece_rows, piece_table, slots, feed, depth):
    count, width = piece_rows.shape[0], piece_table.shape[1]
    table, heads, mixed, middle, expanded, pooled = hyper_outs(count, slots, width, feed, depth)
    far = dict(heads=heads, mixed=mixed, middle=middle, expanded=expanded)

    def unpack(refs):
        rows, source, vectors, pieces, table_out, pooled_out, *refs = refs
        outs, held = dict(zip(far, refs[:4])), dict(zip(far, refs[4:8]))
        held_table, entered, outcome, sem = refs[8:]
        return rows, source, vectors, pieces, table_out, pooled_out, outs, held, held_table, entered, outcome, sem

    def early(*refs):
        rows, source, _, pieces, *_, held_table, _, outcome, sem = unpack(refs)
        load = pltpu.make_async_copy(source, held_table, sem.at[4])
        load.start()
        outcome[...] = jnp.zeros_like(outcome)
        load.wait()

        @pl.loop(0, held_table.shape[0] // TILE)
        def _(n):
            start = pl.multiple_of(n * TILE, TILE)
            column = lax.broadcasted_iota(jnp.int32, (count, TILE), 1) + start
            ones = jnp.where(rows[...] == column, 1.0, 0.0).astype(jnp.bfloat16)
            outcome[...] += matmul(ones, held_table[pl.ds(start, TILE), :])

        pieces[...] = outcome[...].astype(jnp.bfloat16)

    def body(gathereds, *refs):
        _, _, vectors, pieces, table_out, pooled_out, outs, held, _, entered, outcome, sem = unpack(refs)
        first, second, third = (Rows(blocks) for blocks in gathereds)
        turned = jnp.transpose(second[:, pl.ds(depth, LANES)].astype(jnp.float32))
        vectors[...] = turned[: vectors.shape[0]]
        copies = {
            name: pltpu.make_async_copy(held[name], outs[name], sem.at[n])
            for n, name in enumerate(far)
        }

        def done(*names):
            for name in names:
                copies[name].start()

        hyper_kernel(
            slots,
            pieces,
            first,
            second,
            third,
            vectors,
            table_out,
            held["heads"],
            held["mixed"],
            held["middle"],
            held["expanded"],
            pooled_out,
            entered,
            outcome,
            done,
        )
        for name in far:
            copies[name].wait()

    near = [((8, width), jnp.float32), ((count, width), jnp.bfloat16), table, pooled]
    return Work(
        early,
        body,
        ((piece_rows, IN_VMEM), (piece_table, ANYWHERE)),
        [(*item, IN_VMEM) for item in near] + [(*item, ANYWHERE) for item in far.values()],
        [pltpu.VMEM(*item) for item in far.values()]
        + [pltpu.VMEM(piece_table.shape, jnp.bfloat16)]
        + hyper_scratch(count, width)
        + [dma_sems(5)],
    )


def hyper_forward(pieces, slots, params):
    count, width = pieces.shape
    _, second, third, _ = params
    table, *stored = local(
        functools.partial(hyper_kernel, slots),
        (pieces, *params),
        hyper_outs(count, slots, width, third.shape[0], second.shape[1] - LANES),
        hyper_scratch(count, width),
        "hyper",
    )
    return table, stored


def hyper_back_kernel(
    slots,
    table_grad,
    pieces,
    first,
    second,
    third,
    vectors,
    heads,
    mixed,
    middle,
    expanded,
    pooled,
    first_grad,
    second_grad,
    third_grad,
    entered,
    outcome_low,
    feed_grad,
    heads_grad,
    mixed_grad,
):
    width = pieces.shape[1]
    count, feed = pieces.shape[0], third.shape[0]
    depth = table_grad.shape[1]
    head = width // HYPER_HEAD_COUNT
    scale = head ** (-0.5)
    grad_low = table_grad[...].astype(jnp.bfloat16)
    pooled_turned = jnp.transpose(pooled[...].astype(jnp.float32)).astype(jnp.bfloat16)

    for start in range(0, depth, TILE):
        columns = pl.ds(start, TILE)
        second_grad[:, columns] = matmul(
            pooled_turned, grad_low[:, start : start + TILE]
        ).astype(jnp.bfloat16)
    pooled_grad = times_trans(grad_low, second[:, pl.ds(0, depth)]) / slots
    outcome_grad = jnp.broadcast_to(pooled_grad[:, None, :], (count // slots, slots, width))
    outcome_grad = outcome_grad.reshape(count, width)
    outcome_low[...] = outcome_grad.astype(jnp.bfloat16)
    normed, inverse = center_norm(middle[...])
    entered[...] = jnp.transpose(normed * vectors[2:3] + vectors[3:4]).astype(jnp.bfloat16)
    feed_grad[...] = jnp.zeros_like(feed_grad)

    @pl.loop(0, feed // TILE)
    def _(n):
        start = pl.multiple_of(n * TILE, TILE)
        tile = pl.ds(start, TILE)
        columns = pl.ds(pl.multiple_of(4 * width + start, TILE), TILE)
        values = expanded[:, tile]
        erf = 0.5 * (1.0 + lax.erf(values * inv_root_two))
        active = (values * erf).astype(jnp.bfloat16)
        third_grad[tile, :] = trans_times(active, outcome_low[...]).astype(jnp.bfloat16)
        active_grad = times_trans(outcome_low[...], third[tile, :])
        slope = erf + values * jnp.exp(-0.5 * values * values) * inv_root_tau
        low = (active_grad * slope).astype(jnp.bfloat16)
        first_grad[:, columns] = matmul(entered[...], low).astype(jnp.bfloat16)
        feed_grad[...] += times_trans(low, first[:, columns])

    grad = feed_grad[...]
    scale_two = jnp.sum(grad * normed, axis=0, keepdims=True)
    shift_two = jnp.sum(grad, axis=0, keepdims=True)
    middle_grad = outcome_grad + center_back(normed, inverse, grad * vectors[2:3])
    middle_low = middle_grad.astype(jnp.bfloat16)
    out_columns = pl.ds(3 * width, width)
    first_grad[:, out_columns] = trans_times(mixed[...], middle_low).astype(jnp.bfloat16)
    mixed_grad[...] = times_trans(middle_low, first[:, out_columns]).astype(jnp.bfloat16)
    mask = same_entry(CHUNK, slots)

    @pl.loop(0, count // CHUNK)
    def _(n):
        rows = pl.ds(pl.multiple_of(n * CHUNK, CHUNK), CHUNK)
        block = heads[rows, :]
        outer_block = mixed_grad[rows, :]
        grads = [[], [], []]
        for start in range(0, width, head):
            query, key, value = (
                block[:, part * width + start : part * width + start + head] for part in range(3)
            )
            outer = outer_block[:, start : start + head]
            weights = slot_weights(query, key, mask, scale)
            weight_grad = gathered_slots(times_trans(value, outer), mask)
            score_grad = weights * (
                weight_grad - jnp.sum(weights * weight_grad, axis=0, keepdims=True)
            )
            score_grad = spread_slots(score_grad, mask).astype(jnp.bfloat16)
            weights = spread_slots(weights, mask).astype(jnp.bfloat16)
            grads[0].append(trans_times(score_grad, key) * scale)
            grads[1].append(matmul(score_grad, query) * scale)
            grads[2].append(matmul(weights, outer))
        for part in range(3):
            heads_grad[rows, pl.ds(part * width, width)] = jnp.concatenate(
                grads[part], axis=1
            ).astype(jnp.bfloat16)

    normed, _ = center_norm(pieces[...].astype(jnp.float32))
    entered[...] = jnp.transpose(normed * vectors[0:1] + vectors[1:2]).astype(jnp.bfloat16)
    feed_grad[...] = jnp.zeros_like(feed_grad)

    @pl.loop(0, 3 * width // TILE)
    def _(n):
        columns = pl.ds(pl.multiple_of(n * TILE, TILE), TILE)
        low = heads_grad[:, columns]
        first_grad[:, columns] = matmul(entered[...], low).astype(jnp.bfloat16)
        feed_grad[...] += times_trans(low, first[:, columns])

    grad = feed_grad[...]
    scale_one = jnp.sum(grad * normed, axis=0, keepdims=True)
    shift_one = jnp.sum(grad, axis=0, keepdims=True)
    row = lax.broadcasted_iota(jnp.int32, (LANES, width), 0)
    summed = jnp.zeros((LANES, width), jnp.float32)
    for n, item in enumerate((scale_one, shift_one, scale_two, shift_two)):
        summed = jnp.where(row == n, item, summed)
    second_grad[:, pl.ds(depth, LANES)] = jnp.transpose(summed).astype(jnp.bfloat16)


def hyper_backward(pieces, slots, params, stored, table_grad):
    count, width = pieces.shape
    first, second, third, _ = params
    return local(
        functools.partial(hyper_back_kernel, slots),
        (table_grad, pieces, *params, *stored),
        [(item.shape, jnp.bfloat16) for item in (first, second, third)],
        [
            pltpu.VMEM((width, count), jnp.bfloat16),
            pltpu.VMEM((count, width), jnp.bfloat16),
            pltpu.VMEM((count, width), jnp.float32),
            pltpu.VMEM((count, 3 * width), jnp.bfloat16),
            pltpu.VMEM((count, width), jnp.bfloat16),
        ],
        "hyper_back",
    )


def column_plan(q_columns, kv_columns, ff_columns):
    share = ff_columns // TEAM
    edge = share // LANES * LANES
    tail = share - edge
    heads = kv_columns // HEAD_DIM
    q_share = q_columns // TEAM
    plan = []
    for rank in range(TEAM):
        kv = rank * heads // TEAM * HEAD_DIM
        widths = [
            (0, rank * q_share, q_share),
            (1, kv, HEAD_DIM),
            (2, kv, HEAD_DIM),
            (3, rank * share, edge),
            (4, rank * share, edge),
            (3, rank * share + edge, tail),
            (4, rank * share + edge, tail),
        ]
        moves, start = [], 0
        for item, source, size in widths:
            moves.append((item, source, start, size))
            start += size
        plan.append(moves)
    return plan, start


def pack_kernel(plan, rows, *refs):
    sources, maps, targets = refs[:5], refs[5:16], refs[16:23]
    blocks, sem, square = refs[23:28], refs[28], refs[29]
    section = lax.axis_index("section")
    mine = pl.ds(pl.multiple_of(section * rows, rows), rows)
    copies = [
        [
            pltpu.make_async_copy(source.at[layer, mine], block.at[layer], sem.at[layer, n])
            for n, (source, block) in enumerate(zip(sources, blocks))
        ]
        for layer in range(2)
    ]
    for layer in range(2):
        for copy in copies[layer]:
            copy.start()
    *heads, expand, embed, reduce, vectors, norms, feeds, tokens = maps
    first, second, third, gains, notes = targets[2:]
    width = heads[0].shape[1]
    for n, item in enumerate(heads):
        first[:, n * width : (n + 1) * width] = item[...].astype(jnp.bfloat16)
    first[:, 4 * width :] = expand[...].astype(jnp.bfloat16)
    depth = embed.shape[1]
    second[:, :depth] = embed[...].astype(jnp.bfloat16)
    square[...] = jnp.zeros_like(square)
    square[: vectors.shape[0], : vectors.shape[1]] = vectors[...]
    second[:, depth:] = jnp.transpose(square[...])[: second.shape[0]].astype(jnp.bfloat16)
    third[...] = reduce[...].astype(jnp.bfloat16)
    gains[...] = jnp.zeros_like(gains)
    gains[0:2, :] = norms[...].astype(jnp.float32)
    gains[2:4, :] = feeds[...].astype(jnp.float32)
    notes[...] = jnp.zeros_like(notes)
    for n in range(2):
        for batch in range(MB):
            own = pl.ds(n * MB + batch, 1)
            notes[n : n + 1, batch * LEN : (batch + 1) * LEN] = tokens[own, :]
    for layer in range(2):
        for copy in copies[layer]:
            copy.wait()
        for rank, moves in enumerate(plan):
            parts = [
                blocks[item][layer, :, source : source + size] for item, source, _, size in moves
            ]
            heads = jnp.concatenate(parts[1:3], axis=1)
            ends = jnp.concatenate(parts[5:7], axis=1)
            for part, start in zip(
                (parts[0], heads, parts[3], parts[4], ends),
                (moves[0][2], moves[1][2], moves[3][2], moves[4][2], moves[5][2]),
            ):
                if part.shape[1]:
                    targets[layer][rank, :, start : start + part.shape[1]] = part


def pack(weights, maps, vectors, norms, tokens):
    rows = weights[0].shape[1] // SECTIONS
    plan, width = column_plan(weights[0].shape[2], weights[1].shape[2], weights[3].shape[2])
    low = jnp.bfloat16
    owned, hyper_width = maps[0].shape
    feed, depth = maps[4].shape[1], maps[5].shape[1]
    if rows % 16 or owned % 16:
        section = lax.axis_index("section")
        mine = [lax.dynamic_slice_in_dim(item, section * rows, rows, 1) for item in weights]
        columns = tuple(
            jnp.stack(
                [
                    jnp.concatenate(
                        [mine[item][layer, :, at : at + size] for item, at, _, size in moves], axis=1
                    )
                    for moves in plan
                ]
            )
            for layer in range(2)
        )
        first = jnp.concatenate(maps[:5], axis=1).astype(low)
        padded = jnp.pad(vectors.T, ((0, 0), (0, LANES - vectors.shape[0])))
        second = jnp.concatenate([maps[5], padded], axis=1).astype(low)
        gains = jnp.pad(jnp.concatenate(norms, axis=0).astype(jnp.float32), ((0, 4), (0, 0)))
        notes = jnp.pad(tokens.reshape(2, -1), ((0, 6), (0, 0)))
        return (*columns, first, second, maps[6].astype(low), gains, notes)
    shapes = [((TEAM, rows, width), low)] * 2 + [
        ((owned, 4 * hyper_width + feed), low),
        ((owned, depth + LANES), low),
        (maps[6].shape, low),
        ((8, norms[0].shape[1]), jnp.float32),
        ((8, MB * LEN), jnp.int32),
    ]
    return pl.pallas_call(
        functools.partial(pack_kernel, plan, rows),
        out_shape=tuple(jax.ShapeDtypeStruct(shape, kind) for shape, kind in shapes),
        in_specs=[ANYWHERE] * 5 + [IN_VMEM] * 11,
        out_specs=(IN_VMEM,) * 7,
        scratch_shapes=[pltpu.VMEM((2, rows, item.shape[2]), low) for item in weights]
        + [dma_sems(2, 5), pltpu.VMEM((LANES, LANES), jnp.float32)],
        compiler_params=pltpu.CompilerParams(vmem_limit_bytes=VMEM_LIMIT),
        name="pack",
    )(*weights, *maps, vectors, *norms, tokens)


def deliver_kernel(embed, expand, reduce, front, rear, *refs):
    outs, square = refs[:11], refs[11]
    width = front.shape[1] // 2
    square[...] = jnp.zeros_like(square)
    square[: rear.shape[0], :] = rear[:, 2 * width :]
    vectors = jnp.transpose(square[...])
    for n in range(4):
        outs[n][...] = vectors[n, : rear.shape[0]]
    outs[4][...] = front[:, :width]
    outs[5][...] = front[:, width:]
    outs[6][...] = rear[:, :width]
    outs[7][...] = rear[:, width : 2 * width]
    outs[8][...] = expand[...]
    outs[9][...] = reduce[...]
    outs[10][...] = embed[...]


def deliver(embed, expand, reduce, front, rear):
    rows, width = front.shape[0], front.shape[1] // 2
    shapes = [(rows,)] * 4 + [(rows, width)] * 4 + [expand.shape, reduce.shape, embed.shape]
    return local(
        deliver_kernel,
        (embed, expand, reduce, front, rear),
        [(shape, jnp.float32) for shape in shapes],
        [pltpu.VMEM((LANES, LANES), jnp.float32)],
        "deliver",
    )


ORDER = "grgrrgg"


def finish(*steps):
    steps = list(steps)
    while steps:
        steps = [step for step in steps if next(step, steps) is not steps]


class Decoder:
    def __init__(self, shape, refs):
        self.outer, self.tokens, self.share, self.q_width, self.depth = shape
        for name, ref in refs.items():
            setattr(self, name, ref)
        self.section, self.partner, self.across = section_places()
        wide = lax.axis_index("wide")
        self.rank, self.team = wide // self.outer, wide % self.outer
        self.line, self.column = self.rank // 2, self.rank % 2
        self.mine = self.rank
        self.beside = self.member(self.line, 1 - self.column)
        self.edge = self.share // LANES * LANES
        self.tail = self.share - self.edge

    def at(self, line, column):
        return (line % LINES) * 2 + column

    def member(self, line, column):
        return {"wide": self.at(line, column) * self.outer + self.team}

    def ranked(self, step):
        return {"wide": (self.rank + step) % TEAM * self.outer + self.team}

    def greet(self):
        sections = [{"section": place} for place in (self.partner, self.across)]
        greet(sections + [self.ranked(k) for k in range(1, TEAM)])

    def share_copy(self, layer, part, kind):
        split = self.q_width + LANES
        columns = pl.ds(split, 2 * self.share) if part else pl.ds(0, split)
        weight = self.feed_weight if part else self.head_weight
        source = self.own[layer].at[:, :, columns]
        target = weight.at[layer, :, self.section]
        if kind == "keep":
            return pltpu.make_async_copy(source, target, self.load_sem.at[layer, part, 0])
        if kind == "whole":
            source = self.down_source if part else self.out_source
            target = self.down_weight if part else self.out_weight
            return pltpu.make_async_copy(
                source.at[layer], target.at[layer], self.load_sem.at[layer, part, 1]
            )
        n = ("far", "near", "on").index(kind)
        if kind == "on":
            source = target = weight.at[layer, :, self.across]
        return remote(
            source,
            target,
            self.share_send.at[layer, part, n],
            self.share_recv.at[layer, part, n],
            {"section": self.across if kind == "far" else self.partner},
        )

    def share_start(self, layer):
        for part in range(2):
            for kind in ("far", "near", "keep", "whole"):
                self.share_copy(layer, part, kind).start()

    def share_on(self, layer, part):
        self.share_copy(layer, part, "far").wait_recv()
        self.share_copy(layer, part, "on").start()

    def share_end(self, layer, part):
        for kind in ("keep", "whole", "near", "on"):
            self.share_copy(layer, part, kind).wait()
        self.share_copy(layer, part, "far").wait_send()

    def send(self, half):
        self.sides = getattr(self, "sides", {})
        self.sides[half] = [
            remote(
                self.partial.at[half, self.at(self.line + j, 1 - self.column)],
                self.side.at[half, j],
                self.side_send.at[half, j],
                self.side_recv.at[half, j],
                self.beside,
            )
            for j in range(LINES)
        ]
        for j in (2, 1, 3, 0):
            self.sides[half][j].start()

    def reduce(self, half, close):
        sides = self.sides[half]
        fars = [None] + [
            remote(
                self.pair.at[half, j],
                self.far.at[half, j],
                self.far_send.at[half, j],
                self.far_recv.at[half, j],
                self.member(self.line + j, self.column),
            )
            for j in range(1, LINES)
        ]

        def pair_sum(j):
            sides[j].wait_recv()
            own = self.partial[half, self.at(self.line + j, self.column)]
            return own.astype(jnp.float32) + self.side[half, j].astype(jnp.float32)

        for j in (2, 1, 3):
            self.pair[half, j] = pair_sum(j).astype(jnp.bfloat16)
            fars[j].start()
            yield
        total = pair_sum(0)
        for j in (1, 3, 2):
            fars[j].wait_recv()
            total = total + self.far[half, j].astype(jnp.float32)
        self.gathered[half, self.mine] = close(half, total)
        for j in range(LINES):
            sides[j].wait_send()
            if j:
                fars[j].wait_send()
        pushes = [None] + [
            remote(
                self.gathered.at[half, self.mine],
                self.gathered.at[half, self.mine],
                self.out_send.at[half, j],
                self.out_recv.at[half, j],
                self.member(self.line + j, self.column),
            )
            for j in range(1, LINES)
        ]
        overs = []
        for j in range(LINES):
            block = self.gathered.at[half, self.at(self.line - j, self.column)]
            overs.append(
                remote(
                    block, block, self.over_send.at[half, j], self.over_recv.at[half, j], self.beside
                )
            )
        for j in (2, 1, 3):
            pushes[j].start()
        overs[0].start()
        self.moving[half] = (pushes, overs)
        yield

    def gather(self, half):
        pushes, overs = self.moving[half]
        for j in (1, 3, 2):
            pushes[j].wait_recv()
            overs[j].start()
            yield
        for j in range(LINES):
            overs[j].wait()
            if j:
                pushes[j].wait_send()
        yield

    def rows(self, half):
        return self.gathered[half].reshape(HALF, self.depth)

    def store_partial(self, half, columns, values):
        self.partial[half, :, :, columns] = values.astype(jnp.bfloat16).reshape(
            TEAM, EACH, values.shape[1]
        )

    def tiles(self, count, parts):
        bounds = [count * n // parts for n in range(parts + 1)]
        return [(low, high) for low, high in zip(bounds[:-1], bounds[1:]) if high > low]

    def inject(self, half):
        hits = self.own_rows[...] == self.ids[half : half + 1, :]
        hits = jnp.where(hits, 1.0, 0.0).astype(jnp.bfloat16)

        @pl.loop(0, self.depth // TILE)
        def _(n):
            columns = pl.ds(pl.multiple_of(n * TILE, TILE), TILE)
            self.store_partial(half, columns, trans_times(hits, self.table[:, columns]))

        if half == SECOND:
            self.share_on(0, 0)
        yield

    def attention(self, layer, half):
        if half == FIRST:
            self.share_end(layer, 0)
        own = pl.ds(half * HALF, HALF)
        width = self.q_width + LANES
        projected = matmul(self.rows(half), self.head_weight[layer].reshape(self.depth, width))
        yield
        queries = turn(projected[:, : self.q_width], [self.tables[n] for n in range(3)])
        pairs = turn(projected[:, self.q_width :], [self.tables[n] for n in range(3, 6)])
        queries, pairs = queries.astype(jnp.bfloat16), pairs.astype(jnp.bfloat16)
        self.queries[layer, own, :] = queries
        self.pairs[layer, own, :] = pairs
        key, value = pairs[:, :HEAD_DIM], pairs[:, HEAD_DIM:]
        mask = causal_blocks(HALF, LEN)
        mixed = []
        for start in range(0, self.q_width, HEAD_DIM):
            weights = attend(queries[:, start : start + HEAD_DIM], key, mask, HEAD_DIM ** (-0.5))
            mixed.append(matmul(weights.astype(jnp.bfloat16), value))
        mixed = jnp.concatenate(mixed, axis=1).astype(jnp.bfloat16)
        yield

        @pl.loop(0, self.depth // TILE)
        def _(n):
            columns = pl.ds(pl.multiple_of(n * TILE, TILE), TILE)
            self.store_partial(half, columns, matmul(mixed, self.out_weight[layer, :, columns]))

        if half == SECOND:
            self.share_on(layer, 1)
            if layer == 0:
                self.share_start(1)
        yield

    def feed(self, layer, half):
        if half == FIRST:
            self.share_end(layer, 1)
        own = pl.ds(half * HALF, HALF)
        edge, tail = self.edge, self.tail
        def project(columns, width):
            block = self.feed_weight[layer, :, :, :, columns].reshape(self.depth, width)
            self.kept[layer, own, columns] = matmul(self.rows(half), block)

        full, rest = 2 * self.share // TILE, 2 * self.share % TILE
        for low, high in self.tiles(full, 3):

            @pl.loop(low, high)
            def _(n):
                project(pl.ds(pl.multiple_of(n * TILE, TILE), TILE), TILE)

            if high == full and rest:
                project(pl.ds(full * TILE, rest), rest)
            yield

        def activate(gate, up):
            return (jax.nn.silu(gate) * up).astype(jnp.bfloat16)

        self.active[:, :edge] = activate(
            self.kept[layer, own, :edge], self.kept[layer, own, edge : 2 * edge]
        )
        if tail:
            last = self.kept[layer, own, 2 * edge :]
            self.active[:, edge:] = activate(last[:, :tail], last[:, tail:])
        for low, high in self.tiles(self.depth // TILE, 2):

            @pl.loop(low, high)
            def _(n):
                columns = pl.ds(pl.multiple_of(n * TILE, TILE), TILE)
                block = self.down_weight[layer, :, columns]
                self.store_partial(half, columns, matmul(self.active[...], block))

            if half == SECOND and layer == 0 and low:
                self.share_on(1, 0)
            yield

    def head(self, half):
        keep = pltpu.make_async_copy(
            self.gathered.at[half], self.normed_out.at[half], self.keep_sem.at[half]
        )
        keep.start()
        logits = times_trans(self.table[...], self.rows(half))
        peak = jnp.max(logits, axis=0, keepdims=True)
        mass = jnp.sum(jnp.exp(logits - peak), axis=0, keepdims=True)
        wanted = self.own_rows[...] == self.wanted[half : half + 1, :]
        chosen = jnp.sum(jnp.where(wanted, logits, 0.0), axis=0, keepdims=True)
        row = lax.broadcasted_iota(jnp.int32, (8, HALF), 0)
        stats = jnp.where(row == 0, peak, jnp.where(row == 1, mass, chosen))
        self.stats[half, self.rank] = stats
        copies = [
            remote(
                self.stats.at[half, self.rank],
                self.stats.at[half, self.rank],
                self.stats_send.at[half, k],
                self.stats_recv.at[half, k],
                self.ranked(k),
            )
            for k in range(1, TEAM)
        ]
        for copy in copies:
            copy.start()
        yield
        yield
        for copy in copies:
            copy.wait()
        peaks = [self.stats[half, n, 0:1, :] for n in range(TEAM)]
        top = functools.reduce(jnp.maximum, peaks)
        mass = sum(self.stats[half, n, 1:2, :] * jnp.exp(peaks[n] - top) for n in range(TEAM))
        chosen = sum(self.stats[half, n, 2:3, :] for n in range(TEAM))
        log_norm = top + jnp.log(mass)
        loss = jnp.sum(log_norm - chosen, axis=1, keepdims=True) / self.tokens
        loss = jnp.broadcast_to(loss, self.loss_out.shape)
        if half == FIRST:
            self.loss_out[...] = loss
        else:
            self.loss_out[...] += loss
        grad = (jnp.exp(logits - log_norm) - jnp.where(wanted, 1.0, 0.0)) / self.tokens
        grad = grad.astype(jnp.bfloat16)
        self.logit_grad[:, pl.ds(half * HALF, HALF)] = grad
        yield

        @pl.loop(0, self.depth // TILE)
        def _(n):
            columns = pl.ds(pl.multiple_of(n * TILE, TILE), TILE)
            self.store_partial(half, columns, trans_times(grad, self.table[:, columns]))

        keep.wait()
        yield

    def feed_back(self, layer, half):
        own = pl.ds(half * HALF, HALF)
        edge, tail = self.edge, self.tail
        active_grad = times_trans(self.rows(half), self.down_weight[layer])
        yield

        def back(outer, gate, up):
            sigmoid = jax.nn.sigmoid(gate)
            gate_grad = outer * up * sigmoid * (1.0 + gate * (1.0 - sigmoid))
            return gate_grad.astype(jnp.bfloat16), (outer * gate * sigmoid).astype(jnp.bfloat16)

        gate_grad, up_grad = back(
            active_grad[:, :edge],
            self.kept[layer, own, :edge],
            self.kept[layer, own, edge : 2 * edge],
        )
        self.both[:, :edge] = gate_grad
        self.both[:, edge : 2 * edge] = up_grad
        if tail:
            last = self.kept[layer, own, 2 * edge :]
            gate_grad, up_grad = back(active_grad[:, edge:], last[:, :tail], last[:, tail:])
            self.both[:, 2 * edge :] = jnp.concatenate([gate_grad, up_grad], axis=1)
        yield
        tiles = self.depth // TILE
        each = self.feed_weight.shape[1] // tiles
        for low, high in self.tiles(tiles, 3):

            @pl.loop(low, high)
            def _(n):
                columns = pl.ds(pl.multiple_of(n * TILE, TILE), TILE)
                block = self.feed_weight[layer, pl.ds(n * each, each)].reshape(TILE, -1)
                self.store_partial(half, columns, times_trans(self.both[...], block))

            yield

    def attention_back(self, layer, half):
        own = pl.ds(half * HALF, HALF)
        scale = HEAD_DIM ** (-0.5)
        mixed_grad = times_trans(self.rows(half), self.out_weight[layer]).astype(jnp.bfloat16)
        yield
        queries, pairs = self.queries[layer, own, :], self.pairs[layer, own, :]
        key, value = pairs[:, :HEAD_DIM], pairs[:, HEAD_DIM:]
        mask = causal_blocks(HALF, LEN)
        query_grads, key_grad, value_grad = [], 0.0, 0.0
        for start in range(0, self.q_width, HEAD_DIM):
            query = queries[:, start : start + HEAD_DIM]
            outer = mixed_grad[:, start : start + HEAD_DIM]
            weights = attend(query, key, mask, scale)
            weight_grad = times_trans(outer, value)
            score_grad = weights * (
                weight_grad - jnp.sum(weights * weight_grad, axis=1, keepdims=True)
            )
            score_grad = score_grad.astype(jnp.bfloat16)
            query_grads.append(matmul(score_grad, key) * scale)
            key_grad = key_grad + trans_times(score_grad, query) * scale
            value_grad = value_grad + trans_times(weights.astype(jnp.bfloat16), outer)
        query_grad = jnp.concatenate(query_grads, axis=1)
        query_grad = turn(query_grad, [self.back_tables[n] for n in range(3)])
        pair_grad = jnp.concatenate([key_grad, value_grad], axis=1)
        pair_grad = turn(pair_grad, [self.back_tables[n] for n in range(3, 6)])
        both = jnp.concatenate([query_grad, pair_grad], axis=1).astype(jnp.bfloat16)
        yield
        tiles = self.depth // TILE
        each = self.head_weight.shape[1] // tiles

        @pl.loop(0, tiles)
        def _(n):
            columns = pl.ds(pl.multiple_of(n * TILE, TILE), TILE)
            block = self.head_weight[layer, pl.ds(n * each, each)].reshape(TILE, -1)
            self.store_partial(half, columns, times_trans(both, block))

        yield

    def normed(self, values, gain):
        return (values * root_inverse(values) * gain[...]).astype(jnp.bfloat16)

    def close_inject(self, half, total):
        hidden = total.astype(jnp.bfloat16)
        self.hidden[0, half] = hidden
        return self.normed(hidden.astype(jnp.float32), self.gains[0])

    def close_attention(self, layer):
        def close(half, total):
            middle = self.hidden[layer, half].astype(jnp.float32) + total
            self.middle[layer, half] = middle
            return self.normed(middle, self.gains[2 + layer])

        return close

    def close_feed(self, layer):
        def close(half, total):
            hidden = (self.middle[layer, half] + total).astype(jnp.bfloat16)
            self.hidden[layer + 1, half] = hidden
            gain = self.gains[4] if layer else self.gains[1]
            return self.normed(hidden.astype(jnp.float32), gain)

        return close

    def close_head(self, half, total):
        hidden = self.hidden[2, half].astype(jnp.float32)
        grad = reciprocal_root_backward(hidden, root_inverse(hidden), self.gains[4][...], total)
        grad = grad.astype(jnp.bfloat16)
        self.grad[half] = grad.astype(jnp.float32)
        return grad

    def close_feed_back(self, layer):
        def close(half, total):
            middle = self.middle[layer, half]
            grad = self.grad[half] + reciprocal_root_backward(
                middle, root_inverse(middle), self.gains[2 + layer][...], total
            )
            self.grad[half] = grad
            return grad.astype(jnp.bfloat16)

        return close

    def close_attention_back(self, layer):
        def close(half, total):
            hidden = self.hidden[layer, half].astype(jnp.float32)
            grad = self.grad[half] + reciprocal_root_backward(
                hidden, root_inverse(hidden), self.gains[layer][...], total
            )
            grad = grad.astype(jnp.bfloat16)
            self.grad[half] = grad.astype(jnp.float32)
            return grad

        return close


def decode_kernel(shape, names, *refs):
    refs = dict(zip(names, refs))
    refs["own"] = [refs.pop(name) for name in ("own_one", "own_two")]
    refs["gains"] = [refs["gain_rows"].at[pl.ds(n, 1)] for n in range(5)]
    this = Decoder(shape, refs)
    this.greet()
    this.moving = {}
    this.share_start(0)
    phases = [(this.inject, this.close_inject, 1)]
    for layer in range(2):
        phases.append((functools.partial(this.attention, layer), this.close_attention(layer), 1))
        phases.append((functools.partial(this.feed, layer), this.close_feed(layer), 2))
    phases.append((this.head, this.close_head, 2))
    for layer in (1, 0):
        phases.append((functools.partial(this.feed_back, layer), this.close_feed_back(layer), 2))
        phases.append(
            (functools.partial(this.attention_back, layer), this.close_attention_back(layer), 1)
        )
    gathers = {}
    sent = None
    for work, close, parts in phases:
        for half in (FIRST, SECOND):
            gather = gathers.pop(half, iter(()))
            reduce = sent or iter(())
            for kind in ORDER:
                next(gather if kind == "g" else reduce, None)
            for count, _ in enumerate(work(half)):
                if count + 1 == parts:
                    finish(reduce)
            finish(reduce)
            if sent is not None:
                gathers[1 - half] = this.gather(1 - half)
            this.send(half)
            sent = this.reduce(half, close)
    finish(gathers.pop(FIRST), sent)
    finish(this.gather(SECOND))
    outs = [
        pltpu.make_async_copy(
            this.gathered.at[half], this.grad_out.at[half], this.keep_sem.at[half]
        )
        for half in (FIRST, SECOND)
    ]
    for copy in outs:
        copy.start()
    for copy in outs:
        copy.wait()


def decode(outer, collective_id, tokens, weights, out_source, down_source, gains, tables, table, own_rows, ids, wanted):
    q_width, depth = out_source.shape[1:]
    share = down_source.shape[1]
    groups, quarter = weights[0].shape[:2]
    entries = table.shape[0]
    low, full = jnp.bfloat16, jnp.float32
    block = (2, TEAM, EACH, depth)
    slots = pltpu.VMEM((2, LINES, EACH, depth), low)
    inputs = dict(
        own_rows=own_rows,
        ids=ids,
        wanted=wanted,
        table=table,
        gain_rows=gains,
        tables=tables[0],
        back_tables=tables[1],
    )
    far_inputs = dict(
        zip(("own_one", "own_two"), weights),
        out_source=out_source,
        down_source=down_source,
    )
    outputs = dict(
        normed_out=(jax.ShapeDtypeStruct(block, low), ANYWHERE),
        grad_out=(jax.ShapeDtypeStruct(block, low), ANYWHERE),
        logit_grad=(jax.ShapeDtypeStruct((entries, ROWS), low), IN_VMEM),
        loss_out=(jax.ShapeDtypeStruct((8, LANES), full), IN_VMEM),
    )
    scratch = dict(
        head_weight=pltpu.VMEM((2, groups, SECTIONS, quarter, q_width + LANES), low),
        feed_weight=pltpu.VMEM((2, groups, SECTIONS, quarter, 2 * share), low),
        out_weight=pltpu.VMEM((2, q_width, depth), low),
        down_weight=pltpu.VMEM((2, share, depth), low),
        gathered=pltpu.VMEM(block, low),
        partial=pltpu.VMEM(block, low),
        side=slots,
        pair=slots,
        far=slots,
        kept=pltpu.VMEM((2, ROWS, 2 * share), full),
        queries=pltpu.VMEM((2, ROWS, q_width), low),
        pairs=pltpu.VMEM((2, ROWS, LANES), low),
        active=pltpu.VMEM((HALF, share), low),
        both=pltpu.VMEM((HALF, 2 * share), low),
        hidden=pltpu.VMEM((3, 2, EACH, depth), low),
        middle=pltpu.VMEM((2, 2, EACH, depth), full),
        grad=pltpu.VMEM((2, EACH, depth), full),
        stats=pltpu.VMEM((2, TEAM, 8, HALF), full),
        load_sem=dma_sems(2, 2, 2),
        share_send=dma_sems(2, 2, 3),
        share_recv=dma_sems(2, 2, 3),
        stats_send=dma_sems(2, TEAM),
        stats_recv=dma_sems(2, TEAM),
        keep_sem=dma_sems(2),
    )
    for name in ("side", "far", "out", "over"):
        scratch[name + "_send"] = dma_sems(2, LINES)
        scratch[name + "_recv"] = dma_sems(2, LINES)
    names = (*inputs, *far_inputs, *outputs, *scratch)
    return pl.pallas_call(
        functools.partial(decode_kernel, (outer, tokens, share, q_width, depth), names),
        out_shape=tuple(shape for shape, _ in outputs.values()),
        in_specs=[IN_VMEM] * len(inputs) + [ANYWHERE] * len(far_inputs),
        out_specs=tuple(spec for _, spec in outputs.values()),
        scratch_shapes=list(scratch.values()),
        compiler_params=settings(collective_id),
        name="decode",
    )(*inputs.values(), *far_inputs.values())


class Collector:
    def __init__(self, halves, refs):
        for name, ref in refs.items():
            setattr(self, name, ref)
        self.halves = halves
        self.section, self.partner, self.across, self.wide, self.wide_at = all_places(halves)
        self.groups = ((1, 1), (1, 0), (0, 1), (0, 0))

    def greet(self):
        beside = self.wide + 1 - 2 * (self.wide % 2)
        peers = [{"section": self.partner}, {"section": self.across}, {"wide": beside}]
        greet(peers + [{"wide": self.wide_at(j)} for j in range(1, self.halves)])

    def steps(self, n):
        return steps_of(n % 2 == 0, self.section, self.partner, self.across, self.wide)

    def lines(self, n, home, flip_b, flip_a):
        (_, y_a, x_a), (_, y_b, x_b) = self.steps(n)
        flips_y = (y_a and flip_a) or (y_b and flip_b)
        flips_x = (x_a and flip_a) or (x_b and flip_b)
        section, wide = owner_of(home, flips_y, flips_x, self.wide)
        return self.partials[n].at[section, :, wide % 2]

    def line_block(self, n, j):
        return self.partials[n].at[self.section, (self.wide // 2 + j) % self.halves, self.wide % 2]

    def core_copy(self, n, fb, fa):
        return remote(
            self.lines(n, self.partner, fb, fa),
            self.core_in[n].at[fb, fa],
            self.core_send.at[n, fb, fa],
            self.core_recv.at[n, fb, fa],
            {"section": self.partner},
        )

    def b_copy(self, n, fa):
        _, (peer, _, _) = self.steps(n)
        return remote(
            self.lines(n, self.section, 1, fa),
            self.b_in[n].at[fa],
            self.b_send.at[n, fa],
            self.b_recv.at[n, fa],
            peer,
        )

    def a_copy(self, n):
        (peer, _, _), _ = self.steps(n)
        return remote(
            self.lines(n, self.section, 0, 1),
            self.a_in[n],
            self.a_send.at[n],
            self.a_recv.at[n],
            peer,
        )

    def z_copy(self, n, j):
        return remote(
            self.line_block(n, j),
            self.z_in[n].at[j],
            self.z_send.at[n, j],
            self.z_recv.at[n, j],
            {"wide": self.wide_at(j)},
        )

    def add(self, block, more):
        block[...] = (block[...].astype(jnp.float32) + more.astype(jnp.float32)).astype(jnp.bfloat16)

    def start(self, n):
        for fb, fa in self.groups:
            self.core_copy(n, fb, fa).start()

    def sum_core(self, n):
        for fb, fa in self.groups:
            self.core_copy(n, fb, fa).wait_recv()
            self.add(self.lines(n, self.section, fb, fa), self.core_in[n][fb, fa])
            if fb:
                self.b_copy(n, fa).start()

    def sum_b(self, n):
        for fa in (1, 0):
            self.b_copy(n, fa).wait_recv()
            self.add(self.lines(n, self.section, 0, fa), self.b_in[n][fa])
            if fa:
                self.a_copy(n).start()

    def sum_a(self, n):
        self.a_copy(n).wait_recv()
        self.add(self.lines(n, self.section, 0, 0), self.a_in[n][...])
        for j in range(1, self.halves):
            self.z_copy(n, j).start()

    def sum_lines(self, n):
        total = self.line_block(n, 0)[...].astype(jnp.float32)
        for j in range(1, self.halves):
            self.z_copy(n, j).wait_recv()
            total = total + self.z_in[n][j].astype(jnp.float32)
        self.sums[n][...] = total

    def drain(self, n):
        for fb, fa in self.groups:
            self.core_copy(n, fb, fa).wait_send()
        for fa in (0, 1):
            self.b_copy(n, fa).wait_send()
        self.a_copy(n).wait_send()
        for j in range(1, self.halves):
            self.z_copy(n, j).wait_send()


EMBED, REDUCE, EXPAND, FRONT, REAR = range(5)
FAR = ("middle", "expanded", "third", "first", "mixed", "heads", "pieces")


def hyper_collect_kernel(slots, halves, names, *refs):
    refs = dict(zip(names, refs))
    for name in ("sums", "partials", "core_in", "b_in", "a_in", "z_in"):
        refs[name] = [refs.pop(f"{name}{n}") for n in range(5)]
    this = Collector(halves, refs)
    first, second, third, vectors = this.first, this.second, this.third, this.vectors
    entered, outcome_low, feed_grad = this.entered, this.outcome_low, this.feed_grad
    width = this.pieces.shape[1]
    count, feed = this.pieces.shape[0], third.shape[0]
    depth = this.table_grad.shape[1]
    head = width // HYPER_HEAD_COUNT
    scale = head ** (-0.5)
    loads = {
        name: pltpu.make_async_copy(getattr(this, "far_" + name), getattr(this, name), this.load_sem.at[n])
        for n, name in enumerate(FAR)
    }
    for name in FAR:
        loads[name].start()
    this.greet()

    def store(n, columns, values):
        block = this.partials[n]
        block[:, :, :, :, columns] = values.astype(jnp.bfloat16).reshape(
            block.shape[:4] + (values.shape[1],)
        )

    grad_low = this.table_grad[...].astype(jnp.bfloat16)
    pooled_turned = jnp.transpose(this.pooled[...].astype(jnp.float32)).astype(jnp.bfloat16)
    for start in range(0, depth, TILE):
        store(EMBED, pl.ds(start, TILE), matmul(pooled_turned, grad_low[:, start : start + TILE]))
    this.start(EMBED)
    pooled_grad = times_trans(grad_low, second[:, pl.ds(0, depth)]) / slots
    outcome_grad = jnp.broadcast_to(pooled_grad[:, None, :], (count // slots, slots, width))
    outcome_grad = outcome_grad.reshape(count, width)
    outcome_low[...] = outcome_grad.astype(jnp.bfloat16)
    loads["middle"].wait()
    normed, inverse = center_norm(this.middle[...])
    entered[...] = jnp.transpose(normed * vectors[2:3] + vectors[3:4]).astype(jnp.bfloat16)
    feed_grad[...] = jnp.zeros_like(feed_grad)
    this.sum_core(EMBED)

    for name in FAR[1:]:
        loads[name].wait()
    tiles = feed // TILE

    @pl.loop(0, tiles)
    def _(n):
        tile = pl.ds(pl.multiple_of(n * TILE, TILE), TILE)
        values = this.expanded[:, tile]
        erf = 0.5 * (1.0 + lax.erf(values * inv_root_two))
        active = (values * erf).astype(jnp.bfloat16)
        this.expanded[:, tile] = erf + values * jnp.exp(-0.5 * values * values) * inv_root_tau
        block = this.partials[REDUCE]
        owned = block.shape[3]
        lines = TILE // (2 * owned)
        at = n * lines
        turned = trans_times(active, outcome_low[...]).astype(jnp.bfloat16)
        block[at // halves, pl.ds(at % halves, lines)] = turned.reshape(lines, 2, owned, width)

    this.start(REDUCE)

    def feed_tiles(low, high):
        @pl.loop(low, high)
        def _(n):
            start = pl.multiple_of(n * TILE, TILE)
            tile = pl.ds(start, TILE)
            columns = pl.ds(pl.multiple_of(4 * width + start, TILE), TILE)
            active_grad = times_trans(outcome_low[...], third[tile, :])
            low_grad = (active_grad * this.expanded[:, tile]).astype(jnp.bfloat16)
            store(EXPAND, tile, matmul(entered[...], low_grad))
            feed_grad[...] += times_trans(low_grad, first[:, columns])

    feed_tiles(0, tiles // 2)
    this.sum_core(REDUCE)
    this.sum_b(EMBED)
    feed_tiles(tiles // 2, tiles)
    this.start(EXPAND)

    grad = feed_grad[...]
    scale_two = jnp.sum(grad * normed, axis=0, keepdims=True)
    shift_two = jnp.sum(grad, axis=0, keepdims=True)
    middle_grad = outcome_grad + center_back(normed, inverse, grad * vectors[2:3])
    middle_low = middle_grad.astype(jnp.bfloat16)
    out_columns = pl.ds(3 * width, width)
    store(REAR, pl.ds(width, width), trans_times(this.mixed[...], middle_low))
    this.mixed_grad[...] = times_trans(middle_low, first[:, out_columns]).astype(jnp.bfloat16)
    mask = same_entry(CHUNK, slots)
    this.sum_core(EXPAND)
    this.sum_a(EMBED)

    def attention_chunks(low, high):
        @pl.loop(low, high)
        def _(n):
            rows = pl.ds(pl.multiple_of(n * CHUNK, CHUNK), CHUNK)
            block = this.heads[rows, :]
            outer_block = this.mixed_grad[rows, :]
            grads = [[], [], []]
            for start in range(0, width, head):
                query, key, value = (
                    block[:, part * width + start : part * width + start + head]
                    for part in range(3)
                )
                outer = outer_block[:, start : start + head]
                weights = slot_weights(query, key, mask, scale)
                weight_grad = gathered_slots(times_trans(value, outer), mask)
                score_grad = weights * (
                    weight_grad - jnp.sum(weights * weight_grad, axis=0, keepdims=True)
                )
                score_grad = spread_slots(score_grad, mask).astype(jnp.bfloat16)
                weights = spread_slots(weights, mask).astype(jnp.bfloat16)
                grads[0].append(trans_times(score_grad, key) * scale)
                grads[1].append(matmul(score_grad, query) * scale)
                grads[2].append(matmul(weights, outer))
            for part in range(3):
                this.heads_grad[rows, pl.ds(part * width, width)] = jnp.concatenate(
                    grads[part], axis=1
                ).astype(jnp.bfloat16)

    chunks = count // CHUNK
    attention_chunks(0, chunks // 2)
    this.sum_b(REDUCE)
    attention_chunks(chunks // 2, chunks)
    this.sum_b(EXPAND)
    this.sum_a(REDUCE)

    normed, _ = center_norm(this.pieces[...].astype(jnp.float32))
    entered[...] = jnp.transpose(normed * vectors[0:1] + vectors[1:2]).astype(jnp.bfloat16)
    feed_grad[...] = jnp.zeros_like(feed_grad)
    for start in range(0, 3 * width, TILE):
        columns = pl.ds(start, TILE)
        low_grad = this.heads_grad[:, columns]
        target = (FRONT, start) if start < 2 * width else (REAR, start - 2 * width)
        store(target[0], pl.ds(target[1], TILE), matmul(entered[...], low_grad))
        feed_grad[...] += times_trans(low_grad, first[:, columns])
        if start + TILE == 2 * width:
            this.start(FRONT)

    grad = feed_grad[...]
    scale_one = jnp.sum(grad * normed, axis=0, keepdims=True)
    shift_one = jnp.sum(grad, axis=0, keepdims=True)
    row = lax.broadcasted_iota(jnp.int32, (LANES, width), 0)
    summed = jnp.zeros((LANES, width), jnp.float32)
    for n, item in enumerate((scale_one, shift_one, scale_two, shift_two)):
        summed = jnp.where(row == n, item, summed)
    store(REAR, pl.ds(2 * width, LANES), jnp.transpose(summed))
    this.start(REAR)
    this.sum_core(FRONT)
    this.sum_core(REAR)
    this.sum_a(EXPAND)
    this.sum_lines(EMBED)
    this.sum_b(FRONT)
    this.sum_b(REAR)
    this.sum_lines(REDUCE)
    this.sum_a(FRONT)
    this.sum_a(REAR)
    this.sum_lines(EXPAND)
    this.sum_lines(FRONT)
    this.sum_lines(REAR)
    for n in range(5):
        this.drain(n)


def hyper_collect(collective_id, wides, pieces, slots, params, stored, table_grad):
    count, width = pieces.shape
    first, second, third, vectors = params
    depth, feed = table_grad.shape[1], third.shape[0]
    devices, halves = SECTIONS * wides, wides // 2
    low, full = jnp.bfloat16, jnp.float32
    rows = width // devices
    shapes = [
        (rows, depth),
        (feed // devices, width),
        (rows, feed),
        (rows, 2 * width),
        (rows, 2 * width + LANES),
    ]
    heads, mixed, middle, expanded, pooled = stored
    inputs = dict(table_grad=table_grad, second=second, vectors=vectors, pooled=pooled)
    far = dict(
        middle=middle,
        expanded=expanded,
        third=third,
        first=first,
        mixed=mixed,
        heads=heads,
        pieces=pieces,
    )
    inputs.update({"far_" + name: far[name] for name in FAR})
    outputs = {f"sums{n}": jax.ShapeDtypeStruct(shape, full) for n, shape in enumerate(shapes)}
    scratch = {name: pltpu.VMEM(far[name].shape, far[name].dtype) for name in FAR}
    scratch.update(
        load_sem=dma_sems(len(FAR)),
        entered=pltpu.VMEM((width, count), low),
        outcome_low=pltpu.VMEM((count, width), low),
        feed_grad=pltpu.VMEM((count, width), full),
        heads_grad=pltpu.VMEM((count, 3 * width), low),
        mixed_grad=pltpu.VMEM((count, width), low),
    )
    for name, slots_of in (
        ("partials", (SECTIONS, halves, 2)),
        ("core_in", (2, 2, halves)),
        ("b_in", (2, halves)),
        ("a_in", (halves,)),
        ("z_in", (halves,)),
    ):
        for n, shape in enumerate(shapes):
            scratch[f"{name}{n}"] = pltpu.VMEM(slots_of + shape, low)
    for name, numbers in (("core", (2, 2)), ("b", (2,)), ("a", ()), ("z", (halves,))):
        scratch[name + "_send"] = dma_sems(5, *numbers)
        scratch[name + "_recv"] = dma_sems(5, *numbers)
    return pl.pallas_call(
        functools.partial(hyper_collect_kernel, slots, halves, (*inputs, *outputs, *scratch)),
        out_shape=tuple(outputs.values()),
        in_specs=[IN_VMEM] * (len(inputs) - len(FAR)) + [ANYWHERE] * len(FAR),
        out_specs=(IN_VMEM,) * len(outputs),
        scratch_shapes=list(scratch.values()),
        compiler_params=settings(collective_id),
        name="hyper_collect",
    )(*inputs.values())


def team_groups(wides, outer):
    return [[rank * outer + team for team in range(outer)] for rank in range(wides // outer)]


def all_teams(pieces, outer, groups):
    if outer == 1:
        return pieces
    pieces = [
        lax.all_gather(piece, "wide", axis=1, axis_index_groups=groups) for piece in pieces
    ]
    return [piece.reshape((-1,) + piece.shape[2:]) for piece in pieces]


def shards(
    token_ids,
    targets,
    slot_ids,
    group_ids,
    group_offsets,
    piece_table,
    prenorm_gain,
    prenorm_bias,
    query_map,
    key_map,
    value_map,
    output_map,
    midnorm_gain,
    midnorm_bias,
    expand_map,
    reduce_map,
    embed_map,
    attention_gain,
    query_weight,
    key_weight,
    value_weight,
    output_weight,
    feed_gain,
    gate_weight,
    up_weight,
    down_weight,
    final_gain,
):
    wides = lax.axis_size("wide")
    outer = wides // TEAM
    groups = team_groups(wides, outer)
    section_index = lax.axis_index("section")
    wide_index = lax.axis_index("wide")
    rank = wide_index // outer
    hyper_width, hyper_feed = piece_table.shape[1], expand_map.shape[1]
    model_width = embed_map.shape[1]
    total_tokens = wides * MB * LEN

    entries, slot_count = slot_ids.shape
    group_hits = (
        group_ids[:, None] == jnp.arange(group_offsets.shape[0], dtype=jnp.int32)[None, :]
    ).astype(jnp.int32)
    row_start = jnp.sum(group_hits * group_offsets[None, :], axis=1)
    piece_rows = (row_start[:, None] + slot_ids).reshape(-1)
    *columns, first, second, third, gains, notes = pack(
        (query_weight, key_weight, value_weight, gate_weight, up_weight),
        (query_map, key_map, value_map, output_map, expand_map, embed_map, reduce_map),
        jnp.stack([prenorm_gain, prenorm_bias, midnorm_gain, midnorm_bias]),
        (attention_gain, feed_gain),
        jnp.concatenate([token_ids, targets], axis=1).reshape(2 * MB, LEN),
    )
    blocks = (first, second, third)
    whole_tiles = query_map.shape[0] % 16 == 0
    work = Work()
    if whole_tiles:
        work = hyper_work(
            piece_rows.reshape(-1, 1), piece_table, slot_count, hyper_feed, model_width
        )
    first, second, third, gains, notes, own_one, own_two, *made = spread(
        1, wides, outer, blocks, (gains, notes), columns, work
    )
    first = first.reshape(hyper_width, -1)
    second = second.reshape(hyper_width, -1)
    third = third.reshape(hyper_feed, hyper_width)
    if whole_tiles:
        vectors, pieces, table_shard, pooled, *hyper_stored = made
        hyper_stored = (*hyper_stored, pooled)
        params = (first, second, third, vectors)
    else:
        vectors = second[:, model_width : model_width + 8].astype(jnp.float32).T
        params = (first, second, third, vectors)
        pieces = jnp.take(piece_table, piece_rows, axis=0)
        table_shard, hyper_stored = hyper_forward(pieces, slot_count, params)

    if outer > 1:
        gains = lax.all_gather(gains, "wide", axis=1, axis_index_groups=groups)
        gains = gains.reshape(-1, gains.shape[2], gains.shape[3])
        output_weight, down_weight = (
            lax.all_gather(item, "wide", axis=1, axis_index_groups=groups, tiled=True)
            for item in (output_weight, down_weight)
        )
    gains = gains.transpose(1, 0, 2).reshape(-1, model_width)
    final_scale = final_gain.astype(jnp.float32).reshape(1, model_width)
    gains = jnp.concatenate([gains[:4], final_scale, gains[:3]], axis=0)
    notes = lax.dynamic_slice_in_dim(notes, section_index * 2, 2, 0)
    ids, wanted = notes[:, 0].reshape(-1), notes[:, 1].reshape(-1)

    table_rows = section_gather(3, table_shard)
    if outer > 1:
        table_rows = lax.all_gather(table_rows, "wide", axis=1, axis_index_groups=groups)
    table_rows = table_rows.reshape(-1, model_width)
    wide_rows = rank * outer + jnp.arange(outer, dtype=jnp.int32)
    row_starts = (
        jnp.arange(SECTIONS, dtype=jnp.int32)[:, None] * wides + wide_rows[None, :]
    ) * entries
    own_rows = row_starts[:, :, None] + jnp.arange(entries, dtype=jnp.int32)[None, None, :]
    own_rows = own_rows.reshape(-1)
    own_rows = own_rows.reshape(-1, 1)

    def by_halves(numbers):
        return jnp.pad(numbers.reshape(2, -1), ((0, 6), (0, 0)))

    normed, grads, logit_grad, loss_block = decode(
        outer,
        4,
        total_tokens,
        all_teams((own_one, own_two), outer, groups),
        output_weight,
        down_weight,
        gains,
        (turn_tables(False), turn_tables(True)),
        table_rows,
        own_rows,
        by_halves(ids),
        by_halves(wanted),
    )

    hits = (own_rows == ids[None, :]).astype(jnp.bfloat16)
    table_part = matmul(logit_grad, normed.reshape(ROWS, model_width)) + matmul(
        hits, grads.reshape(ROWS, model_width)
    )
    table_part = table_part.astype(jnp.bfloat16).reshape(SECTIONS, outer, entries, model_width)
    if outer > 1:
        table_part = lax.psum_scatter(
            table_part.astype(jnp.float32),
            "wide",
            scatter_dimension=1,
            axis_index_groups=groups,
        ).astype(jnp.bfloat16)
        loss_block = lax.psum(loss_block, "wide", axis_index_groups=groups)
    table_grad, loss_block = section_sum(
        11, table_part.reshape(SECTIONS, entries, model_width), loss_block
    )
    mean_loss = loss_block[0, 0]
    if whole_tiles:
        grad_embed, grad_reduce, grad_expand, front, rear = hyper_collect(
            12, wides, pieces, slot_count, params, hyper_stored, table_grad
        )
    else:
        grads = hyper_backward(pieces, slot_count, params, hyper_stored, table_grad)
        grads = [item.reshape(SECTIONS, wides, -1, item.shape[1]) for item in grads]
        first, second, grad_reduce = collect(12, grads)
        grad_embed, grad_expand = second[:, :model_width], first[:, 4 * hyper_width :]
        front = first[:, : 2 * hyper_width]
        rear = jnp.concatenate(
            [first[:, 2 * hyper_width : 4 * hyper_width], second[:, model_width:]], axis=1
        )
    if whole_tiles:
        outs = deliver(grad_embed, grad_expand, grad_reduce, front, rear)
    else:
        vectors = rear[:, 2 * hyper_width : 2 * hyper_width + 4]
        outs = [vectors[:, n] for n in range(4)]
        outs += [front[:, :hyper_width], front[:, hyper_width:]]
        outs += [rear[:, :hyper_width], rear[:, hyper_width : 2 * hyper_width]]
        outs += [grad_expand, grad_reduce, grad_embed]
    prescale, prebias, midscale, midshift, *maps = outs
    return (mean_loss, prescale, prebias, *maps[:4], midscale, midshift, *maps[4:])


def solution(mesh):
    placed = (
        P("wide", None, None),
        P("wide", None, None),
        P(("section", "wide"), None),
        P(("section", "wide")),
        P(),
        P(),
        P(("section", "wide")),
        P(("section", "wide")),
        P(("section", "wide"), None),
        P(("section", "wide"), None),
        P(("section", "wide"), None),
        P(("section", "wide"), None),
        P(("section", "wide")),
        P(("section", "wide")),
        P(("section", "wide"), None),
        P(("section", "wide"), None),
        P(("section", "wide"), None),
        P(None, "wide"),
        P(None, "wide", None),
        P(None, "wide", None),
        P(None, "wide", None),
        P(None, "wide", None),
        P(None, "wide"),
        P(None, "wide", None),
        P(None, "wide", None),
        P(None, "wide", None),
        P(),
    )
    return jax.shard_map(
        shards,
        mesh=mesh,
        in_specs=placed,
        out_specs=(
            P(),
            P(("section", "wide")),
            P(("section", "wide")),
            P(("section", "wide"), None),
            P(("section", "wide"), None),
            P(("section", "wide"), None),
            P(("section", "wide"), None),
            P(("section", "wide")),
            P(("section", "wide")),
            P(("section", "wide"), None),
            P(("section", "wide"), None),
            P(("section", "wide"), None),
        ),
        check_vma=False,
    )
```

```python
import functools

import jax
import jax.numpy as jnp
from jax import lax
from jax.experimental import pallas as pl
from jax.experimental.pallas import tpu as pltpu
from jax.sharding import PartitionSpec as P

HEAD_DIM = 64
HYPER_HEAD_COUNT = 8
MB = 2
LEN = 64
TEAM = 8
SECTIONS = 4
ROWS = MB * LEN * TEAM // SECTIONS
HALF = ROWS // 2
EACH = HALF // TEAM
LINES = TEAM // 2
FIRST, SECOND = 0, 1
LANES = 128
MESH_IDS = pl.DeviceIdType.MESH
ANYWHERE = pl.BlockSpec(memory_space=pl.ANY)
IN_VMEM = pl.BlockSpec(memory_space=pltpu.VMEM)
VMEM_LIMIT = 56 * 1024 * 1024

norm_eps = 1e-05
inv_root_two = 0.7071067811865476
inv_root_tau = 0.3989422804014327


def matmul(former, latter):
    return jnp.dot(former, latter, preferred_element_type=jnp.float32)


def times_trans(former, latter):
    return lax.dot_general(
        former, latter, (((1,), (1,)), ((), ())), preferred_element_type=jnp.float32
    )


def trans_times(former, latter):
    return lax.dot_general(
        former, latter, (((0,), (0,)), ((), ())), preferred_element_type=jnp.float32
    )


def center_norm(values):
    center = values - jnp.mean(values, axis=-1, keepdims=True)
    inverse = lax.rsqrt(jnp.mean(center * center, axis=-1, keepdims=True) + norm_eps)
    return (center * inverse, inverse)


def center_back(normed, inverse, normed_grad):
    mean_grad = jnp.mean(normed_grad, axis=-1, keepdims=True)
    mean_mix = jnp.mean(normed_grad * normed, axis=-1, keepdims=True)
    return inverse * (normed_grad - mean_grad - normed * mean_mix)


def root_inverse(values):
    return lax.rsqrt(jnp.mean(values * values, axis=-1, keepdims=True) + norm_eps)


def reciprocal_root_backward(values, inverse, gain_vec, outer_grad):
    scaled = outer_grad * gain_vec
    mixing = jnp.mean(scaled * values, axis=-1, keepdims=True)
    return inverse * scaled - values * inverse * inverse * inverse * mixing


def rope_tables(positions, head_width):
    halfway = head_width // 2
    frequency = jnp.exp(
        -jnp.log(10000.0) * (2.0 * jnp.arange(halfway, dtype=jnp.float32) / head_width)
    )
    angles = jnp.arange(positions, dtype=jnp.float32)[:, None] * frequency[None, :]
    angles = jnp.concatenate([angles, angles], axis=1)
    return (jnp.cos(angles), jnp.sin(angles))


def greet(peers):
    barrier = pltpu.get_barrier_semaphore()
    for peer in peers:
        pl.semaphore_signal(barrier, inc=1, device_id=peer, device_id_type=MESH_IDS)
    pl.semaphore_wait(barrier, len(peers))


def remote(source, target, send, recv, peer):
    return pltpu.make_async_remote_copy(
        src_ref=source,
        dst_ref=target,
        send_sem=send,
        recv_sem=recv,
        device_id=peer,
        device_id_type=MESH_IDS,
    )


def settings(collective_id):
    return pltpu.CompilerParams(
        collective_id=collective_id, has_side_effects=True, vmem_limit_bytes=VMEM_LIMIT
    )


def dma_sems(*shape):
    return pltpu.SemaphoreType.DMA(shape)


def section_places():
    section = lax.axis_index("section")
    core = section % 2
    partner = section + 1 - 2 * core
    across = (section + 2) % SECTIONS
    return section, partner, across


def section_gather_kernel(block, gathered, keep_sem, send, recv):
    section, partner, across = section_places()
    greet([{"section": partner}, {"section": across}])
    keep = pltpu.make_async_copy(block, gathered.at[section], keep_sem)
    near = remote(block, gathered.at[section], send.at[0], recv.at[0], {"section": partner})
    far = remote(block, gathered.at[section], send.at[1], recv.at[1], {"section": across})
    on = remote(
        gathered.at[across], gathered.at[across], send.at[2], recv.at[2], {"section": partner}
    )
    far.start()
    near.start()
    keep.start()
    far.wait_recv()
    on.start()
    near.wait()
    on.wait()
    far.wait_send()
    keep.wait()


def section_gather(collective_id, block):
    return pl.pallas_call(
        section_gather_kernel,
        out_shape=jax.ShapeDtypeStruct((SECTIONS,) + block.shape, block.dtype),
        in_specs=[ANYWHERE],
        out_specs=ANYWHERE,
        scratch_shapes=[pltpu.SemaphoreType.DMA, dma_sems(3), dma_sems(3)],
        compiler_params=settings(collective_id),
        name="section_gather",
    )(block)


def section_sum_kernel(partial, loss, summed, loss_sum, own, near, pair, far, loss_near, loss_pair, loss_far, load_sem, send, recv):
    section, partner, across = section_places()
    beyond = (partner + 2) % SECTIONS
    greet([{"section": partner}, {"section": across}])
    loads = [
        pltpu.make_async_copy(partial.at[section], own.at[0], load_sem.at[0]),
        pltpu.make_async_copy(partial.at[across], own.at[1], load_sem.at[1]),
    ]
    nears = [
        remote(partial.at[partner], near.at[0], send.at[0], recv.at[0], {"section": partner}),
        remote(partial.at[beyond], near.at[1], send.at[1], recv.at[1], {"section": partner}),
        remote(loss, loss_near, send.at[2], recv.at[2], {"section": partner}),
    ]
    fars = [
        remote(pair, far, send.at[3], recv.at[3], {"section": across}),
        remote(loss_pair, loss_far, send.at[4], recv.at[4], {"section": across}),
    ]
    for j in (1, 2, 0):
        nears[j].start()
    loads[1].start()
    loads[0].start()
    loads[1].wait()
    nears[1].wait_recv()
    pair[...] = (own[1].astype(jnp.float32) + near[1].astype(jnp.float32)).astype(jnp.bfloat16)
    fars[0].start()
    nears[2].wait_recv()
    loss_pair[...] = loss[...] + loss_near[...]
    fars[1].start()
    loads[0].wait()
    nears[0].wait_recv()
    total = own[0].astype(jnp.float32) + near[0].astype(jnp.float32)
    fars[0].wait_recv()
    summed[...] = total + far[...].astype(jnp.float32)
    fars[1].wait_recv()
    loss_sum[...] = loss_pair[...] + loss_far[...]
    for copy in nears + fars:
        copy.wait_send()


def section_sum(collective_id, partial, loss):
    shape = partial.shape[1:]
    low, low_two = pltpu.VMEM(shape, jnp.bfloat16), pltpu.VMEM((2,) + shape, jnp.bfloat16)
    number = pltpu.VMEM(loss.shape, jnp.float32)
    return pl.pallas_call(
        section_sum_kernel,
        out_shape=(
            jax.ShapeDtypeStruct(shape, jnp.float32),
            jax.ShapeDtypeStruct(loss.shape, jnp.float32),
        ),
        in_specs=[ANYWHERE, IN_VMEM],
        out_specs=(IN_VMEM, IN_VMEM),
        scratch_shapes=[low_two, low_two, low, low, number, number, number]
        + [dma_sems(2), dma_sems(5), dma_sems(5)],
        compiler_params=settings(collective_id),
        name="section_sum",
    )(partial, loss)


def all_places(halves):
    section, partner, across = section_places()
    wide = lax.axis_index("wide")
    line, column = wide // 2, wide % 2

    def wide_at(j):
        return ((line + j) % halves) * 2 + column

    return section, partner, across, wide, wide_at


def steps_of(x_first, section, partner, across, wide):
    column_flip = wide + 1 - 2 * (wide % 2)
    x_step = ({"wide": column_flip}, False, True)
    y_step = ({"section": across}, True, False)
    return (x_step, y_step) if x_first else (y_step, x_step)


def owner_of(home, flips_y, flips_x, wide_block):
    section = (home + 2) % SECTIONS if flips_y else home
    return section, (wide_block + 1 - 2 * (wide_block % 2) if flips_x else wide_block)


def spread_kernel(count, halves, outer, work, *refs):
    blocks, notes, columns = refs[:count], refs[count : count + 2], refs[count + 2 : count + 4]
    refs = refs[count + 4 :]
    extra, refs = refs[: work.inputs], refs[work.inputs :]
    outs, notes_out, columns_out = refs[:count], refs[count : count + 2], refs[count + 2 : count + 4]
    refs = refs[count + 4 :]
    extra, refs = extra + refs[: work.outputs], refs[work.outputs :]
    gathereds = outs
    if work.body is not None:
        gathereds, refs = refs[:count], refs[count:]
    (
        keep_sem,
        note_keep,
        note_send,
        note_recv,
        z_send,
        a_send,
        b_send,
        c_send,
        z_recv,
        a_recv,
        b_recv,
        c_recv,
    ) = refs[:12]
    section, partner, across, wide, wide_at = all_places(halves)
    rank, team = wide // outer, wide % outer
    members = [None] + [{"wide": (rank + k) % TEAM * outer + team} for k in range(1, TEAM)]
    beside = wide + 1 - 2 * (wide % 2)
    barrier = pltpu.get_barrier_semaphore()
    for peer in ({"section": partner}, {"section": across}, {"wide": beside}):
        pl.semaphore_signal(barrier, inc=1, device_id=peer, device_id_type=MESH_IDS)

    def hello(j, carry):
        peer = {"wide": wide_at(j)}
        pl.semaphore_signal(barrier, inc=1, device_id=peer, device_id_type=MESH_IDS)
        return carry

    lax.fori_loop(1, halves, hello, 0)
    for peer in members[1:]:
        pl.semaphore_signal(barrier, inc=1, device_id=peer, device_id_type=MESH_IDS)
    pl.semaphore_wait(barrier, 3 + halves - 1 + TEAM - 1)
    note_keeps = [
        pltpu.make_async_copy(notes[m], notes_out[m].at[rank], note_keep.at[m]) for m in range(2)
    ]
    note_copies = [
        remote(notes[m], notes_out[m].at[rank], note_send.at[m, k], note_recv.at[m, k], members[k])
        for m in range(2)
        for k in range(1, TEAM)
    ]
    column_copies = []
    for layer in range(2):
        column_copies.append(
            pltpu.make_async_copy(
                columns[layer].at[rank], columns_out[layer].at[rank], note_keep.at[2 + layer]
            )
        )
        column_copies += [
            remote(
                columns[layer].at[(rank + k) % TEAM],
                columns_out[layer].at[rank],
                note_send.at[2 + layer, k],
                note_recv.at[2 + layer, k],
                members[k],
            )
            for k in (4, 3, 5, 2, 6, 1, 7)
        ]
    for copy in note_keeps + note_copies:
        copy.start()

    keeps = [
        pltpu.make_async_copy(blocks[n], gathereds[n].at[section, wide], keep_sem.at[n])
        for n in range(count)
    ]

    def z_copy(n, j):
        return remote(
            blocks[n],
            gathereds[n].at[section, wide],
            z_send.at[n, j],
            z_recv.at[n, j],
            {"wide": wide_at(j)},
        )

    def a_copy(n, j):
        (peer, _, _), _ = steps_of(n == 0, section, partner, across, wide)
        block = gathereds[n].at[section, wide_at(-j)]
        return remote(block, block, a_send.at[n, j], a_recv.at[n, j], peer)

    def b_copy(n, flip, j):
        (_, y_a, x_a), (peer, _, _) = steps_of(n == 0, section, partner, across, wide)
        place = owner_of(section, y_a and flip, x_a and flip, wide_at(-j))
        block = gathereds[n].at[place[0], place[1]]
        slot = j + (halves if flip else 0)
        return remote(block, block, b_send.at[n, slot], b_recv.at[n, slot], peer)

    def c_copy(n, which):
        home = (section + 2) % SECTIONS if which else section
        block = gathereds[n].at[home]
        return remote(
            block, block, c_send.at[n, which], c_recv.at[n, which], {"section": partner}
        )

    for keep in keeps:
        keep.start()

    def start_z(j, carry):
        for n in range(count):
            z_copy(n, j).start()
        return carry

    lax.fori_loop(1, halves, start_z, 0)
    work.begin(extra + refs[12:])
    for n in range(count):
        keeps[n].wait()
        a_copy(n, 0).start()
        b_copy(n, False, 0).start()

    def pass_z(j, carry):
        for n in range(count):
            z_copy(n, j).wait_recv()
            a_copy(n, j).start()
            b_copy(n, False, j).start()
        return carry

    lax.fori_loop(1, halves, pass_z, 0)
    for copy in column_copies:
        copy.start()

    def pass_a(j, carry):
        for n in range(count):
            a_copy(n, j).wait_recv()
            b_copy(n, True, j).start()
        return carry

    lax.fori_loop(0, halves, pass_a, 0)

    def settle_b(j, carry):
        for n in range(count):
            for flip in (False, True):
                b_copy(n, flip, j).wait_recv()
        return carry

    c_copy(0, 0).start()
    lax.fori_loop(0, halves, settle_b, 0)
    c_copy(0, 1).start()
    for n in range(1, count):
        c_copy(n, 0).start()
        c_copy(n, 1).start()
    for n in range(count):
        c_copy(n, 0).wait()
        c_copy(n, 1).wait()

    def drain(j, carry):
        for n in range(count):
            a_copy(n, j).wait_send()
            b_copy(n, False, j).wait_send()
            b_copy(n, True, j).wait_send()
        return carry

    lax.fori_loop(0, halves, drain, 0)

    def drain_z(j, carry):
        for n in range(count):
            z_copy(n, j).wait_send()
        return carry

    lax.fori_loop(1, halves, drain_z, 0)
    copies = []
    if work.body is not None:
        copies = [
            pltpu.make_async_copy(gathereds[n], outs[n], keep_sem.at[n]) for n in range(count)
        ]
    for copy in copies:
        copy.start()
    work.run(gathereds, extra + refs[12:])
    for copy in copies:
        copy.wait()
    for copy in note_keeps + note_copies + column_copies:
        copy.wait()


class Work:
    def __init__(self, early=None, body=None, operands=(), outs=(), scratch=()):
        self.early, self.body = early, body
        self.operands, self.outs, self.scratch = operands, outs, scratch
        self.inputs, self.outputs = len(operands), len(outs)

    def begin(self, refs):
        if self.early is not None:
            self.early(*refs)

    def run(self, gathereds, refs):
        if self.body is not None:
            self.body(gathereds, *refs)


def spread(collective_id, wides, outer, blocks, notes, columns, work):
    count, halves = len(blocks), wides // 2
    held = [] if work.body is None else blocks
    return pl.pallas_call(
        functools.partial(spread_kernel, count, halves, outer, work),
        out_shape=tuple(
            jax.ShapeDtypeStruct((SECTIONS, wides) + block.shape, block.dtype) for block in blocks
        )
        + tuple(jax.ShapeDtypeStruct((TEAM,) + note.shape, note.dtype) for note in notes)
        + tuple(jax.ShapeDtypeStruct(item.shape, item.dtype) for item in columns)
        + tuple(jax.ShapeDtypeStruct(shape, kind) for shape, kind, _ in work.outs),
        in_specs=[ANYWHERE] * (count + 4) + [place for _, place in work.operands],
        out_specs=(ANYWHERE,) * (count + 4) + tuple(place for _, _, place in work.outs),
        scratch_shapes=[
            pltpu.VMEM((SECTIONS, wides) + block.shape, block.dtype) for block in held
        ]
        + [dma_sems(count), dma_sems(4), dma_sems(4, TEAM), dma_sems(4, TEAM)]
        + [
            dma_sems(count, halves),
            dma_sems(count, halves),
            dma_sems(count, 2 * halves),
            dma_sems(count, 2),
        ]
        * 2
        + list(work.scratch),
        compiler_params=settings(collective_id),
        name="spread",
    )(*blocks, *notes, *columns, *(item for item, _ in work.operands))


def collect_kernel(count, halves, *refs):
    partials, sums = refs[:count], refs[count : 2 * count]
    keeps, c_in, b_in, a_in, z_in = (refs[(2 + k) * count : (3 + k) * count] for k in range(5))
    load_sem, c_send, b_send, a_send, z_send, c_recv, b_recv, a_recv, z_recv = refs[7 * count :]
    section, partner, across, wide, wide_at = all_places(halves)
    beside = wide + 1 - 2 * (wide % 2)
    barrier = pltpu.get_barrier_semaphore()
    for peer in ({"section": partner}, {"section": across}, {"wide": beside}):
        pl.semaphore_signal(barrier, inc=1, device_id=peer, device_id_type=MESH_IDS)

    def hello(j, carry):
        peer = {"wide": wide_at(j)}
        pl.semaphore_signal(barrier, inc=1, device_id=peer, device_id_type=MESH_IDS)
        return carry

    lax.fori_loop(1, halves, hello, 0)
    pl.semaphore_wait(barrier, 3 + halves - 1)

    def place(n, home, flip_b, flip_a, j):
        (_, y_a, x_a), (_, y_b, x_b) = steps_of(n == 0, section, partner, across, wide)
        flips_y = (y_a and flip_a) or (y_b and flip_b)
        flips_x = (x_a and flip_a) or (x_b and flip_b)
        return owner_of(home, flips_y, flips_x, wide_at(j))

    def load(n, fb, fa, j):
        owner = place(n, section, fb, fa, j)
        slot = (fb * 2 + fa) * halves + j
        return pltpu.make_async_copy(
            partials[n].at[owner[0], owner[1]], keeps[n].at[slot], load_sem.at[n, slot]
        )

    def c_copy(n, fb, fa, j):
        owner = place(n, partner, fb, fa, j)
        slot = (fb * 2 + fa) * halves + j
        return remote(
            partials[n].at[owner[0], owner[1]],
            c_in[n].at[slot],
            c_send.at[n, slot],
            c_recv.at[n, slot],
            {"section": partner},
        )

    def b_copy(n, fa, j):
        _, (peer, _, _) = steps_of(n == 0, section, partner, across, wide)
        slot = fa * halves + j
        return remote(
            keeps[n].at[2 * halves + slot],
            b_in[n].at[slot],
            b_send.at[n, slot],
            b_recv.at[n, slot],
            peer,
        )

    def a_copy(n, j):
        (peer, _, _), _ = steps_of(n == 0, section, partner, across, wide)
        return remote(
            keeps[n].at[halves + j], a_in[n].at[j], a_send.at[n, j], a_recv.at[n, j], peer
        )

    def z_copy(n, j):
        return remote(
            keeps[n].at[j],
            z_in[n].at[j],
            z_send.at[n, j],
            z_recv.at[n, j],
            {"wide": wide_at(j)},
        )

    def add(n, slot, more):
        keeps[n][slot] = (
            keeps[n][slot].astype(jnp.float32) + more.astype(jnp.float32)
        ).astype(jnp.bfloat16)

    groups = ((1, 1), (1, 0), (0, 1), (0, 0))
    for fb, fa in groups:

        def start_c(j, carry):
            for n in range(count):
                c_copy(n, fb, fa, j).start()
                load(n, fb, fa, j).start()
            return carry

        lax.fori_loop(0, halves, start_c, 0)

    for fb, fa in groups:

        def sum_c(j, carry):
            for n in range(count):
                slot = (fb * 2 + fa) * halves + j
                load(n, fb, fa, j).wait()
                c_copy(n, fb, fa, j).wait_recv()
                add(n, slot, c_in[n][slot])
                if fb:
                    b_copy(n, fa, j).start()
            return carry

        lax.fori_loop(0, halves, sum_c, 0)

    for fa in (1, 0):

        def sum_b(j, carry):
            for n in range(count):
                slot = fa * halves + j
                b_copy(n, fa, j).wait_recv()
                add(n, slot, b_in[n][slot])
                if fa:
                    a_copy(n, j).start()
            return carry

        lax.fori_loop(0, halves, sum_b, 0)

    def sum_a(j, carry):
        for n in range(count):
            a_copy(n, j).wait_recv()
            add(n, j, a_in[n][j])
            z_copy(n, j).start()
        return carry

    lax.fori_loop(1, halves, sum_a, 0)
    for n in range(count):
        a_copy(n, 0).wait_recv()
        sums[n][...] = keeps[n][0].astype(jnp.float32) + a_in[n][0].astype(jnp.float32)

    def sum_z(j, carry):
        for n in range(count):
            z_copy(n, j).wait_recv()
            sums[n][...] += z_in[n][j].astype(jnp.float32)
        return carry

    lax.fori_loop(1, halves, sum_z, 0)

    def drain(j, carry):
        for n in range(count):
            for fb, fa in groups:
                c_copy(n, fb, fa, j).wait_send()
            b_copy(n, 0, j).wait_send()
            b_copy(n, 1, j).wait_send()
            a_copy(n, j).wait_send()
        return carry

    lax.fori_loop(0, halves, drain, 0)

    def drain_z(j, carry):
        for n in range(count):
            z_copy(n, j).wait_send()
        return carry

    lax.fori_loop(1, halves, drain_z, 0)


def collect(collective_id, partials):
    count, halves = len(partials), partials[0].shape[1] // 2
    shapes = [partial.shape[2:] for partial in partials]

    def slots(number):
        return [pltpu.VMEM((number,) + shape, jnp.bfloat16) for shape in shapes]

    return pl.pallas_call(
        functools.partial(collect_kernel, count, halves),
        out_shape=tuple(jax.ShapeDtypeStruct(shape, jnp.float32) for shape in shapes),
        in_specs=[ANYWHERE] * count,
        out_specs=(IN_VMEM,) * count,
        scratch_shapes=slots(4 * halves)
        + slots(4 * halves)
        + slots(2 * halves)
        + slots(halves)
        + slots(halves)
        + [dma_sems(count, 4 * halves)]
        + [
            dma_sems(count, 4 * halves),
            dma_sems(count, 2 * halves),
            dma_sems(count, halves),
            dma_sems(count, halves),
        ]
        * 2,
        compiler_params=settings(collective_id),
        name="collect",
    )(*partials)


TILE = 256


def causal_blocks(count, length):
    row = lax.broadcasted_iota(jnp.int32, (count, count), 0)
    column = lax.broadcasted_iota(jnp.int32, (count, count), 1)
    return (row // length == column // length) & (row <= column)


def turn(values, tables):
    cosines, upper, lower = tables
    parts = []
    for start in range(0, values.shape[1], LANES):
        part = values[:, start : start + LANES]
        ahead = pltpu.roll(part, LANES - HEAD_DIM // 2, 1)
        behind = pltpu.roll(part, HEAD_DIM // 2, 1)
        parts.append(part * cosines + ahead * upper + behind * lower)
    return parts[0] if len(parts) == 1 else jnp.concatenate(parts, axis=1)


def turn_tables(back):
    cosines, sines = rope_tables(LEN, HEAD_DIM)
    sines = -sines if back else sines
    first = jnp.arange(HEAD_DIM) < HEAD_DIM // 2
    upper, lower = jnp.where(first, -sines, 0.0), jnp.where(first, 0.0, sines)
    blank = jnp.zeros_like(cosines)
    pairs = [(cosines, cosines), (upper, upper), (lower, lower)]
    pairs += [(cosines, blank + 1.0), (upper, blank), (lower, blank)]
    tables = jnp.stack([jnp.concatenate(pair, axis=1) for pair in pairs])
    return jnp.tile(tables, (1, HALF // LEN, 1))


def attend(queries, key, mask, scale):
    scores = jnp.where(mask, times_trans(key, queries) * scale, -1e30)
    mass = jnp.exp(scores - jnp.max(scores, axis=0, keepdims=True))
    return mass / jnp.sum(mass, axis=0, keepdims=True)


def local(kernel, operands, outs, scratch, name):
    return pl.pallas_call(
        kernel,
        out_shape=tuple(jax.ShapeDtypeStruct(shape, kind) for shape, kind in outs),
        in_specs=[IN_VMEM] * len(operands),
        out_specs=(IN_VMEM,) * len(outs),
        scratch_shapes=list(scratch),
        compiler_params=pltpu.CompilerParams(vmem_limit_bytes=VMEM_LIMIT),
        name=name,
    )(*operands)


CHUNK = 128


def same_entry(count, slots):
    entry = lax.broadcasted_iota(jnp.int32, (count // slots, slots, count), 0)
    column = lax.broadcasted_iota(jnp.int32, (count // slots, slots, count), 2)
    return entry == column // slots


def gathered_slots(products, mask):
    return jnp.sum(jnp.where(mask, products.reshape(mask.shape), 0.0), axis=0)


def spread_slots(values, mask):
    spread = jnp.where(mask, values[None], 0.0)
    return spread.reshape(mask.shape[0] * mask.shape[1], mask.shape[2])


def slot_weights(query, key, mask, scale):
    scores = gathered_slots(times_trans(key, query), mask) * scale
    mass = jnp.exp(scores - jnp.max(scores, axis=0, keepdims=True))
    return mass / jnp.sum(mass, axis=0, keepdims=True)


def gelu(values):
    return 0.5 * values * (1.0 + lax.erf(values * inv_root_two))


def hyper_kernel(
    slots,
    pieces,
    first,
    second,
    third,
    vectors,
    table,
    heads_out,
    mixed_out,
    middle_out,
    expanded_out,
    pooled_out,
    entered,
    outcome,
    done=lambda *names: None,
):
    width = pieces.shape[1]
    count, feed = pieces.shape[0], third.shape[0]
    head = width // HYPER_HEAD_COUNT
    flat = pieces[...].astype(jnp.float32)
    normed, _ = center_norm(flat)
    entered[...] = (normed * vectors[0:1] + vectors[1:2]).astype(jnp.bfloat16)

    @pl.loop(0, 3 * width // TILE)
    def _(n):
        columns = pl.ds(pl.multiple_of(n * TILE, TILE), TILE)
        heads_out[:, columns] = matmul(entered[...], first[:, columns]).astype(jnp.bfloat16)

    mask = same_entry(CHUNK, slots)

    @pl.loop(0, count // CHUNK)
    def _(n):
        rows = pl.ds(pl.multiple_of(n * CHUNK, CHUNK), CHUNK)
        block = heads_out[rows, :]
        mixed = []
        for start in range(0, width, head):
            query, key, value = (
                block[:, part * width + start : part * width + start + head] for part in range(3)
            )
            weights = slot_weights(query, key, mask, head ** (-0.5))
            weights = spread_slots(weights, mask).astype(jnp.bfloat16)
            mixed.append(trans_times(weights, value))
        mixed_out[rows, :] = jnp.concatenate(mixed, axis=1).astype(jnp.bfloat16)

    done("heads", "mixed")
    for start in range(0, width, TILE):
        columns = pl.ds(start, TILE)
        middle_out[:, columns] = pieces[:, columns].astype(jnp.float32) + matmul(
            mixed_out[...], first[:, pl.ds(3 * width + start, TILE)]
        )
    done("middle")
    normed, _ = center_norm(middle_out[...])
    entered[...] = (normed * vectors[2:3] + vectors[3:4]).astype(jnp.bfloat16)
    outcome[...] = middle_out[...]

    @pl.loop(0, feed // TILE)
    def _(n):
        start = pl.multiple_of(n * TILE, TILE)
        columns = pl.ds(pl.multiple_of(4 * width + start, TILE), TILE)
        expanded = matmul(entered[...], first[:, columns])
        expanded_out[:, pl.ds(start, TILE)] = expanded
        outcome[...] += matmul(gelu(expanded).astype(jnp.bfloat16), third[pl.ds(start, TILE), :])

    done("expanded")
    pooled = jnp.mean(outcome[...].reshape(count // slots, slots, width), axis=1)
    pooled_out[...] = pooled.astype(jnp.bfloat16)

    @pl.loop(0, table.shape[1] // TILE)
    def _(n):
        columns = pl.ds(pl.multiple_of(n * TILE, TILE), TILE)
        table[:, columns] = matmul(pooled_out[...], second[:, columns]).astype(jnp.bfloat16)


class Rows:
    def __init__(self, blocks):
        self.blocks = blocks
        sections, wides, rows, columns = blocks.shape
        self.wides, self.rows, self.shape = wides, rows, (sections * wides * rows, columns)

    def __getitem__(self, index):
        rows, columns = index
        if rows == slice(None):
            values = self.blocks[:, :, :, columns]
        else:
            first = rows.start // self.rows
            owners = pl.ds(first % self.wides, rows.size // self.rows)
            values = self.blocks[first // self.wides, owners]
        return values.reshape(-1, values.shape[-1])


def hyper_outs(count, slots, width, feed, depth):
    entries = count // slots
    return [
        ((entries, depth), jnp.bfloat16),
        ((count, 3 * width), jnp.bfloat16),
        ((count, width), jnp.bfloat16),
        ((count, width), jnp.float32),
        ((count, feed), jnp.float32),
        ((entries, width), jnp.bfloat16),
    ]


def hyper_scratch(count, width):
    return [pltpu.VMEM((count, width), jnp.bfloat16), pltpu.VMEM((count, width), jnp.float32)]


def hyper_work(piece_rows, piece_table, slots, feed, depth):
    count, width = piece_rows.shape[0], piece_table.shape[1]
    table, heads, mixed, middle, expanded, pooled = hyper_outs(count, slots, width, feed, depth)
    far = dict(heads=heads, mixed=mixed, middle=middle, expanded=expanded)

    def unpack(refs):
        rows, source, vectors, pieces, table_out, pooled_out, *refs = refs
        outs, held = dict(zip(far, refs[:4])), dict(zip(far, refs[4:8]))
        held_table, entered, outcome, sem = refs[8:]
        return rows, source, vectors, pieces, table_out, pooled_out, outs, held, held_table, entered, outcome, sem

    def early(*refs):
        rows, source, _, pieces, *_, held_table, _, outcome, sem = unpack(refs)
        load = pltpu.make_async_copy(source, held_table, sem.at[4])
        load.start()
        outcome[...] = jnp.zeros_like(outcome)
        load.wait()

        @pl.loop(0, held_table.shape[0] // TILE)
        def _(n):
            start = pl.multiple_of(n * TILE, TILE)
            column = lax.broadcasted_iota(jnp.int32, (count, TILE), 1) + start
            ones = jnp.where(rows[...] == column, 1.0, 0.0).astype(jnp.bfloat16)
            outcome[...] += matmul(ones, held_table[pl.ds(start, TILE), :])

        pieces[...] = outcome[...].astype(jnp.bfloat16)

    def body(gathereds, *refs):
        _, _, vectors, pieces, table_out, pooled_out, outs, held, _, entered, outcome, sem = unpack(refs)
        first, second, third = (Rows(blocks) for blocks in gathereds)
        turned = jnp.transpose(second[:, pl.ds(depth, LANES)].astype(jnp.float32))
        vectors[...] = turned[: vectors.shape[0]]
        copies = {
            name: pltpu.make_async_copy(held[name], outs[name], sem.at[n])
            for n, name in enumerate(far)
        }

        def done(*names):
            for name in names:
                copies[name].start()

        hyper_kernel(
            slots,
            pieces,
            first,
            second,
            third,
            vectors,
            table_out,
            held["heads"],
            held["mixed"],
            held["middle"],
            held["expanded"],
            pooled_out,
            entered,
            outcome,
            done,
        )
        for name in far:
            copies[name].wait()

    near = [((8, width), jnp.float32), ((count, width), jnp.bfloat16), table, pooled]
    return Work(
        early,
        body,
        ((piece_rows, IN_VMEM), (piece_table, ANYWHERE)),
        [(*item, IN_VMEM) for item in near] + [(*item, ANYWHERE) for item in far.values()],
        [pltpu.VMEM(*item) for item in far.values()]
        + [pltpu.VMEM(piece_table.shape, jnp.bfloat16)]
        + hyper_scratch(count, width)
        + [dma_sems(5)],
    )


def hyper_forward(pieces, slots, params):
    count, width = pieces.shape
    _, second, third, _ = params
    table, *stored = local(
        functools.partial(hyper_kernel, slots),
        (pieces, *params),
        hyper_outs(count, slots, width, third.shape[0], second.shape[1] - LANES),
        hyper_scratch(count, width),
        "hyper",
    )
    return table, stored


def hyper_back_kernel(
    slots,
    table_grad,
    pieces,
    first,
    second,
    third,
    vectors,
    heads,
    mixed,
    middle,
    expanded,
    pooled,
    first_grad,
    second_grad,
    third_grad,
    entered,
    outcome_low,
    feed_grad,
    heads_grad,
    mixed_grad,
):
    width = pieces.shape[1]
    count, feed = pieces.shape[0], third.shape[0]
    depth = table_grad.shape[1]
    head = width // HYPER_HEAD_COUNT
    scale = head ** (-0.5)
    grad_low = table_grad[...].astype(jnp.bfloat16)
    pooled_turned = jnp.transpose(pooled[...].astype(jnp.float32)).astype(jnp.bfloat16)

    for start in range(0, depth, TILE):
        columns = pl.ds(start, TILE)
        second_grad[:, columns] = matmul(
            pooled_turned, grad_low[:, start : start + TILE]
        ).astype(jnp.bfloat16)
    pooled_grad = times_trans(grad_low, second[:, pl.ds(0, depth)]) / slots
    outcome_grad = jnp.broadcast_to(pooled_grad[:, None, :], (count // slots, slots, width))
    outcome_grad = outcome_grad.reshape(count, width)
    outcome_low[...] = outcome_grad.astype(jnp.bfloat16)
    normed, inverse = center_norm(middle[...])
    entered[...] = jnp.transpose(normed * vectors[2:3] + vectors[3:4]).astype(jnp.bfloat16)
    feed_grad[...] = jnp.zeros_like(feed_grad)

    @pl.loop(0, feed // TILE)
    def _(n):
        start = pl.multiple_of(n * TILE, TILE)
        tile = pl.ds(start, TILE)
        columns = pl.ds(pl.multiple_of(4 * width + start, TILE), TILE)
        values = expanded[:, tile]
        erf = 0.5 * (1.0 + lax.erf(values * inv_root_two))
        active = (values * erf).astype(jnp.bfloat16)
        third_grad[tile, :] = trans_times(active, outcome_low[...]).astype(jnp.bfloat16)
        active_grad = times_trans(outcome_low[...], third[tile, :])
        slope = erf + values * jnp.exp(-0.5 * values * values) * inv_root_tau
        low = (active_grad * slope).astype(jnp.bfloat16)
        first_grad[:, columns] = matmul(entered[...], low).astype(jnp.bfloat16)
        feed_grad[...] += times_trans(low, first[:, columns])

    grad = feed_grad[...]
    scale_two = jnp.sum(grad * normed, axis=0, keepdims=True)
    shift_two = jnp.sum(grad, axis=0, keepdims=True)
    middle_grad = outcome_grad + center_back(normed, inverse, grad * vectors[2:3])
    middle_low = middle_grad.astype(jnp.bfloat16)
    out_columns = pl.ds(3 * width, width)
    first_grad[:, out_columns] = trans_times(mixed[...], middle_low).astype(jnp.bfloat16)
    mixed_grad[...] = times_trans(middle_low, first[:, out_columns]).astype(jnp.bfloat16)
    mask = same_entry(CHUNK, slots)

    @pl.loop(0, count // CHUNK)
    def _(n):
        rows = pl.ds(pl.multiple_of(n * CHUNK, CHUNK), CHUNK)
        block = heads[rows, :]
        outer_block = mixed_grad[rows, :]
        grads = [[], [], []]
        for start in range(0, width, head):
            query, key, value = (
                block[:, part * width + start : part * width + start + head] for part in range(3)
            )
            outer = outer_block[:, start : start + head]
            weights = slot_weights(query, key, mask, scale)
            weight_grad = gathered_slots(times_trans(value, outer), mask)
            score_grad = weights * (
                weight_grad - jnp.sum(weights * weight_grad, axis=0, keepdims=True)
            )
            score_grad = spread_slots(score_grad, mask).astype(jnp.bfloat16)
            weights = spread_slots(weights, mask).astype(jnp.bfloat16)
            grads[0].append(trans_times(score_grad, key) * scale)
            grads[1].append(matmul(score_grad, query) * scale)
            grads[2].append(matmul(weights, outer))
        for part in range(3):
            heads_grad[rows, pl.ds(part * width, width)] = jnp.concatenate(
                grads[part], axis=1
            ).astype(jnp.bfloat16)

    normed, _ = center_norm(pieces[...].astype(jnp.float32))
    entered[...] = jnp.transpose(normed * vectors[0:1] + vectors[1:2]).astype(jnp.bfloat16)
    feed_grad[...] = jnp.zeros_like(feed_grad)

    @pl.loop(0, 3 * width // TILE)
    def _(n):
        columns = pl.ds(pl.multiple_of(n * TILE, TILE), TILE)
        low = heads_grad[:, columns]
        first_grad[:, columns] = matmul(entered[...], low).astype(jnp.bfloat16)
        feed_grad[...] += times_trans(low, first[:, columns])

    grad = feed_grad[...]
    scale_one = jnp.sum(grad * normed, axis=0, keepdims=True)
    shift_one = jnp.sum(grad, axis=0, keepdims=True)
    row = lax.broadcasted_iota(jnp.int32, (LANES, width), 0)
    summed = jnp.zeros((LANES, width), jnp.float32)
    for n, item in enumerate((scale_one, shift_one, scale_two, shift_two)):
        summed = jnp.where(row == n, item, summed)
    second_grad[:, pl.ds(depth, LANES)] = jnp.transpose(summed).astype(jnp.bfloat16)


def hyper_backward(pieces, slots, params, stored, table_grad):
    count, width = pieces.shape
    first, second, third, _ = params
    return local(
        functools.partial(hyper_back_kernel, slots),
        (table_grad, pieces, *params, *stored),
        [(item.shape, jnp.bfloat16) for item in (first, second, third)],
        [
            pltpu.VMEM((width, count), jnp.bfloat16),
            pltpu.VMEM((count, width), jnp.bfloat16),
            pltpu.VMEM((count, width), jnp.float32),
            pltpu.VMEM((count, 3 * width), jnp.bfloat16),
            pltpu.VMEM((count, width), jnp.bfloat16),
        ],
        "hyper_back",
    )


def column_plan(q_columns, kv_columns, ff_columns):
    share = ff_columns // TEAM
    edge = share // LANES * LANES
    tail = share - edge
    heads = kv_columns // HEAD_DIM
    q_share = q_columns // TEAM
    plan = []
    for rank in range(TEAM):
        kv = rank * heads // TEAM * HEAD_DIM
        widths = [
            (0, rank * q_share, q_share),
            (1, kv, HEAD_DIM),
            (2, kv, HEAD_DIM),
            (3, rank * share, edge),
            (4, rank * share, edge),
            (3, rank * share + edge, tail),
            (4, rank * share + edge, tail),
        ]
        moves, start = [], 0
        for item, source, size in widths:
            moves.append((item, source, start, size))
            start += size
        plan.append(moves)
    return plan, start


def pack_kernel(plan, rows, *refs):
    sources, maps, targets = refs[:5], refs[5:16], refs[16:23]
    blocks, sem, square = refs[23:28], refs[28], refs[29]
    section = lax.axis_index("section")
    mine = pl.ds(pl.multiple_of(section * rows, rows), rows)
    copies = [
        [
            pltpu.make_async_copy(source.at[layer, mine], block.at[layer], sem.at[layer, n])
            for n, (source, block) in enumerate(zip(sources, blocks))
        ]
        for layer in range(2)
    ]
    for layer in range(2):
        for copy in copies[layer]:
            copy.start()
    *heads, expand, embed, reduce, vectors, norms, feeds, tokens = maps
    first, second, third, gains, notes = targets[2:]
    width = heads[0].shape[1]
    for n, item in enumerate(heads):
        first[:, n * width : (n + 1) * width] = item[...].astype(jnp.bfloat16)
    first[:, 4 * width :] = expand[...].astype(jnp.bfloat16)
    depth = embed.shape[1]
    second[:, :depth] = embed[...].astype(jnp.bfloat16)
    square[...] = jnp.zeros_like(square)
    square[: vectors.shape[0], : vectors.shape[1]] = vectors[...]
    second[:, depth:] = jnp.transpose(square[...])[: second.shape[0]].astype(jnp.bfloat16)
    third[...] = reduce[...].astype(jnp.bfloat16)
    gains[...] = jnp.zeros_like(gains)
    gains[0:2, :] = norms[...].astype(jnp.float32)
    gains[2:4, :] = feeds[...].astype(jnp.float32)
    notes[...] = jnp.zeros_like(notes)
    for n in range(2):
        for batch in range(MB):
            own = pl.ds(n * MB + batch, 1)
            notes[n : n + 1, batch * LEN : (batch + 1) * LEN] = tokens[own, :]
    for layer in range(2):
        for copy in copies[layer]:
            copy.wait()
        for rank, moves in enumerate(plan):
            parts = [
                blocks[item][layer, :, source : source + size] for item, source, _, size in moves
            ]
            heads = jnp.concatenate(parts[1:3], axis=1)
            ends = jnp.concatenate(parts[5:7], axis=1)
            for part, start in zip(
                (parts[0], heads, parts[3], parts[4], ends),
                (moves[0][2], moves[1][2], moves[3][2], moves[4][2], moves[5][2]),
            ):
                if part.shape[1]:
                    targets[layer][rank, :, start : start + part.shape[1]] = part


def pack(weights, maps, vectors, norms, tokens):
    rows = weights[0].shape[1] // SECTIONS
    plan, width = column_plan(weights[0].shape[2], weights[1].shape[2], weights[3].shape[2])
    low = jnp.bfloat16
    owned, hyper_width = maps[0].shape
    feed, depth = maps[4].shape[1], maps[5].shape[1]
    if rows % 16 or owned % 16:
        section = lax.axis_index("section")
        mine = [lax.dynamic_slice_in_dim(item, section * rows, rows, 1) for item in weights]
        columns = tuple(
            jnp.stack(
                [
                    jnp.concatenate(
                        [mine[item][layer, :, at : at + size] for item, at, _, size in moves], axis=1
                    )
                    for moves in plan
                ]
            )
            for layer in range(2)
        )
        first = jnp.concatenate(maps[:5], axis=1).astype(low)
        padded = jnp.pad(vectors.T, ((0, 0), (0, LANES - vectors.shape[0])))
        second = jnp.concatenate([maps[5], padded], axis=1).astype(low)
        gains = jnp.pad(jnp.concatenate(norms, axis=0).astype(jnp.float32), ((0, 4), (0, 0)))
        notes = jnp.pad(tokens.reshape(2, -1), ((0, 6), (0, 0)))
        return (*columns, first, second, maps[6].astype(low), gains, notes)
    shapes = [((TEAM, rows, width), low)] * 2 + [
        ((owned, 4 * hyper_width + feed), low),
        ((owned, depth + LANES), low),
        (maps[6].shape, low),
        ((8, norms[0].shape[1]), jnp.float32),
        ((8, MB * LEN), jnp.int32),
    ]
    return pl.pallas_call(
        functools.partial(pack_kernel, plan, rows),
        out_shape=tuple(jax.ShapeDtypeStruct(shape, kind) for shape, kind in shapes),
        in_specs=[ANYWHERE] * 5 + [IN_VMEM] * 11,
        out_specs=(IN_VMEM,) * 7,
        scratch_shapes=[pltpu.VMEM((2, rows, item.shape[2]), low) for item in weights]
        + [dma_sems(2, 5), pltpu.VMEM((LANES, LANES), jnp.float32)],
        compiler_params=pltpu.CompilerParams(vmem_limit_bytes=VMEM_LIMIT),
        name="pack",
    )(*weights, *maps, vectors, *norms, tokens)


def deliver_kernel(embed, expand, reduce, front, rear, *refs):
    outs, square = refs[:11], refs[11]
    width = front.shape[1] // 2
    square[...] = jnp.zeros_like(square)
    square[: rear.shape[0], :] = rear[:, 2 * width :]
    vectors = jnp.transpose(square[...])
    for n in range(4):
        outs[n][...] = vectors[n, : rear.shape[0]]
    outs[4][...] = front[:, :width]
    outs[5][...] = front[:, width:]
    outs[6][...] = rear[:, :width]
    outs[7][...] = rear[:, width : 2 * width]
    outs[8][...] = expand[...]
    outs[9][...] = reduce[...]
    outs[10][...] = embed[...]


def deliver(embed, expand, reduce, front, rear):
    rows, width = front.shape[0], front.shape[1] // 2
    shapes = [(rows,)] * 4 + [(rows, width)] * 4 + [expand.shape, reduce.shape, embed.shape]
    return local(
        deliver_kernel,
        (embed, expand, reduce, front, rear),
        [(shape, jnp.float32) for shape in shapes],
        [pltpu.VMEM((LANES, LANES), jnp.float32)],
        "deliver",
    )


ORDER = "grgrrgg"


def finish(*steps):
    steps = list(steps)
    while steps:
        steps = [step for step in steps if next(step, steps) is not steps]


class Decoder:
    def __init__(self, shape, refs):
        self.outer, self.tokens, self.share, self.q_width, self.depth = shape
        for name, ref in refs.items():
            setattr(self, name, ref)
        self.section, self.partner, self.across = section_places()
        wide = lax.axis_index("wide")
        self.rank, self.team = wide // self.outer, wide % self.outer
        self.line, self.column = self.rank // 2, self.rank % 2
        self.mine = self.rank
        self.beside = self.member(self.line, 1 - self.column)
        self.edge = self.share // LANES * LANES
        self.tail = self.share - self.edge

    def at(self, line, column):
        return (line % LINES) * 2 + column

    def member(self, line, column):
        return {"wide": self.at(line, column) * self.outer + self.team}

    def ranked(self, step):
        return {"wide": (self.rank + step) % TEAM * self.outer + self.team}

    def greet(self):
        sections = [{"section": place} for place in (self.partner, self.across)]
        greet(sections + [self.ranked(k) for k in range(1, TEAM)])

    def share_copy(self, layer, part, kind):
        split = self.q_width + LANES
        columns = pl.ds(split, 2 * self.share) if part else pl.ds(0, split)
        weight = self.feed_weight if part else self.head_weight
        source = self.own[layer].at[:, :, columns]
        target = weight.at[layer, :, self.section]
        if kind == "keep":
            return pltpu.make_async_copy(source, target, self.load_sem.at[layer, part, 0])
        if kind == "whole":
            source = self.down_source if part else self.out_source
            target = self.down_weight if part else self.out_weight
            return pltpu.make_async_copy(
                source.at[layer], target.at[layer], self.load_sem.at[layer, part, 1]
            )
        n = ("far", "near", "on").index(kind)
        if kind == "on":
            source = target = weight.at[layer, :, self.across]
        return remote(
            source,
            target,
            self.share_send.at[layer, part, n],
            self.share_recv.at[layer, part, n],
            {"section": self.across if kind == "far" else self.partner},
        )

    def share_start(self, layer):
        for part in range(2):
            for kind in ("far", "near", "keep", "whole"):
                self.share_copy(layer, part, kind).start()

    def share_on(self, layer, part):
        self.share_copy(layer, part, "far").wait_recv()
        self.share_copy(layer, part, "on").start()

    def share_end(self, layer, part):
        for kind in ("keep", "whole", "near", "on"):
            self.share_copy(layer, part, kind).wait()
        self.share_copy(layer, part, "far").wait_send()

    def send(self, half):
        self.sides = getattr(self, "sides", {})
        self.sides[half] = [
            remote(
                self.partial.at[half, self.at(self.line + j, 1 - self.column)],
                self.side.at[half, j],
                self.side_send.at[half, j],
                self.side_recv.at[half, j],
                self.beside,
            )
            for j in range(LINES)
        ]
        for j in (2, 1, 3, 0):
            self.sides[half][j].start()

    def reduce(self, half, close):
        sides = self.sides[half]
        fars = [None] + [
            remote(
                self.pair.at[half, j],
                self.far.at[half, j],
                self.far_send.at[half, j],
                self.far_recv.at[half, j],
                self.member(self.line + j, self.column),
            )
            for j in range(1, LINES)
        ]

        def pair_sum(j):
            sides[j].wait_recv()
            own = self.partial[half, self.at(self.line + j, self.column)]
            return own.astype(jnp.float32) + self.side[half, j].astype(jnp.float32)

        for j in (2, 1, 3):
            self.pair[half, j] = pair_sum(j).astype(jnp.bfloat16)
            fars[j].start()
            yield
        total = pair_sum(0)
        for j in (1, 3, 2):
            fars[j].wait_recv()
            total = total + self.far[half, j].astype(jnp.float32)
        self.gathered[half, self.mine] = close(half, total)
        for j in range(LINES):
            sides[j].wait_send()
            if j:
                fars[j].wait_send()
        pushes = [None] + [
            remote(
                self.gathered.at[half, self.mine],
                self.gathered.at[half, self.mine],
                self.out_send.at[half, j],
                self.out_recv.at[half, j],
                self.member(self.line + j, self.column),
            )
            for j in range(1, LINES)
        ]
        overs = []
        for j in range(LINES):
            block = self.gathered.at[half, self.at(self.line - j, self.column)]
            overs.append(
                remote(
                    block, block, self.over_send.at[half, j], self.over_recv.at[half, j], self.beside
                )
            )
        for j in (2, 1, 3):
            pushes[j].start()
        overs[0].start()
        self.moving[half] = (pushes, overs)
        yield

    def gather(self, half):
        pushes, overs = self.moving[half]
        for j in (1, 3, 2):
            pushes[j].wait_recv()
            overs[j].start()
            yield
        for j in range(LINES):
            overs[j].wait()
            if j:
                pushes[j].wait_send()
        yield

    def rows(self, half):
        return self.gathered[half].reshape(HALF, self.depth)

    def store_partial(self, half, columns, values):
        self.partial[half, :, :, columns] = values.astype(jnp.bfloat16).reshape(
            TEAM, EACH, values.shape[1]
        )

    def tiles(self, count, parts):
        bounds = [count * n // parts for n in range(parts + 1)]
        return [(low, high) for low, high in zip(bounds[:-1], bounds[1:]) if high > low]

    def inject(self, half):
        hits = self.own_rows[...] == self.ids[half : half + 1, :]
        hits = jnp.where(hits, 1.0, 0.0).astype(jnp.bfloat16)

        @pl.loop(0, self.depth // TILE)
        def _(n):
            columns = pl.ds(pl.multiple_of(n * TILE, TILE), TILE)
            self.store_partial(half, columns, trans_times(hits, self.table[:, columns]))

        if half == SECOND:
            self.share_on(0, 0)
        yield

    def attention(self, layer, half):
        if half == FIRST:
            self.share_end(layer, 0)
        own = pl.ds(half * HALF, HALF)
        width = self.q_width + LANES
        projected = matmul(self.rows(half), self.head_weight[layer].reshape(self.depth, width))
        yield
        queries = turn(projected[:, : self.q_width], [self.tables[n] for n in range(3)])
        pairs = turn(projected[:, self.q_width :], [self.tables[n] for n in range(3, 6)])
        queries, pairs = queries.astype(jnp.bfloat16), pairs.astype(jnp.bfloat16)
        self.queries[layer, own, :] = queries
        self.pairs[layer, own, :] = pairs
        key, value = pairs[:, :HEAD_DIM], pairs[:, HEAD_DIM:]
        mask = causal_blocks(HALF, LEN)
        mixed = []
        for start in range(0, self.q_width, HEAD_DIM):
            weights = attend(queries[:, start : start + HEAD_DIM], key, mask, HEAD_DIM ** (-0.5))
            mixed.append(trans_times(weights.astype(jnp.bfloat16), value))
        mixed = jnp.concatenate(mixed, axis=1).astype(jnp.bfloat16)
        yield

        @pl.loop(0, self.depth // TILE)
        def _(n):
            columns = pl.ds(pl.multiple_of(n * TILE, TILE), TILE)
            self.store_partial(half, columns, matmul(mixed, self.out_weight[layer, :, columns]))

        if half == SECOND:
            self.share_on(layer, 1)
            if layer == 0:
                self.share_start(1)
        yield

    def feed(self, layer, half):
        if half == FIRST:
            self.share_end(layer, 1)
        own = pl.ds(half * HALF, HALF)
        edge, tail = self.edge, self.tail
        def project(columns, width):
            block = self.feed_weight[layer, :, :, :, columns].reshape(self.depth, width)
            self.kept[layer, own, columns] = matmul(self.rows(half), block)

        full, rest = 2 * self.share // TILE, 2 * self.share % TILE
        for low, high in self.tiles(full, 3):

            @pl.loop(low, high)
            def _(n):
                project(pl.ds(pl.multiple_of(n * TILE, TILE), TILE), TILE)

            if high == full and rest:
                project(pl.ds(full * TILE, rest), rest)
            yield

        def activate(gate, up):
            return (jax.nn.silu(gate) * up).astype(jnp.bfloat16)

        self.active[:, :edge] = activate(
            self.kept[layer, own, :edge], self.kept[layer, own, edge : 2 * edge]
        )
        if tail:
            last = self.kept[layer, own, 2 * edge :]
            self.active[:, edge:] = activate(last[:, :tail], last[:, tail:])
        for low, high in self.tiles(self.depth // TILE, 2):

            @pl.loop(low, high)
            def _(n):
                columns = pl.ds(pl.multiple_of(n * TILE, TILE), TILE)
                block = self.down_weight[layer, :, columns]
                self.store_partial(half, columns, matmul(self.active[...], block))

            if half == SECOND and layer == 0 and low:
                self.share_on(1, 0)
            yield

    def head(self, half):
        keep = pltpu.make_async_copy(
            self.gathered.at[half], self.normed_out.at[half], self.keep_sem.at[half]
        )
        keep.start()
        logits = times_trans(self.table[...], self.rows(half))
        peak = jnp.max(logits, axis=0, keepdims=True)
        mass = jnp.sum(jnp.exp(logits - peak), axis=0, keepdims=True)
        wanted = self.own_rows[...] == self.wanted[half : half + 1, :]
        chosen = jnp.sum(jnp.where(wanted, logits, 0.0), axis=0, keepdims=True)
        row = lax.broadcasted_iota(jnp.int32, (8, HALF), 0)
        stats = jnp.where(row == 0, peak, jnp.where(row == 1, mass, chosen))
        self.stats[half, self.rank] = stats
        copies = [
            remote(
                self.stats.at[half, self.rank],
                self.stats.at[half, self.rank],
                self.stats_send.at[half, k],
                self.stats_recv.at[half, k],
                self.ranked(k),
            )
            for k in range(1, TEAM)
        ]
        for copy in copies:
            copy.start()
        yield
        yield
        for copy in copies:
            copy.wait()
        peaks = [self.stats[half, n, 0:1, :] for n in range(TEAM)]
        top = functools.reduce(jnp.maximum, peaks)
        mass = sum(self.stats[half, n, 1:2, :] * jnp.exp(peaks[n] - top) for n in range(TEAM))
        chosen = sum(self.stats[half, n, 2:3, :] for n in range(TEAM))
        log_norm = top + jnp.log(mass)
        loss = jnp.sum(log_norm - chosen, axis=1, keepdims=True) / self.tokens
        loss = jnp.broadcast_to(loss, self.loss_out.shape)
        if half == FIRST:
            self.loss_out[...] = loss
        else:
            self.loss_out[...] += loss
        grad = (jnp.exp(logits - log_norm) - jnp.where(wanted, 1.0, 0.0)) / self.tokens
        grad = grad.astype(jnp.bfloat16)
        self.logit_grad[:, pl.ds(half * HALF, HALF)] = grad
        yield

        @pl.loop(0, self.depth // TILE)
        def _(n):
            columns = pl.ds(pl.multiple_of(n * TILE, TILE), TILE)
            self.store_partial(half, columns, trans_times(grad, self.table[:, columns]))

        keep.wait()
        yield

    def feed_back(self, layer, half):
        own = pl.ds(half * HALF, HALF)
        edge, tail = self.edge, self.tail
        active_grad = times_trans(self.rows(half), self.down_weight[layer])
        yield

        def back(outer, gate, up):
            sigmoid = jax.nn.sigmoid(gate)
            gate_grad = outer * up * sigmoid * (1.0 + gate * (1.0 - sigmoid))
            return gate_grad.astype(jnp.bfloat16), (outer * gate * sigmoid).astype(jnp.bfloat16)

        gate_grad, up_grad = back(
            active_grad[:, :edge],
            self.kept[layer, own, :edge],
            self.kept[layer, own, edge : 2 * edge],
        )
        self.both[:, :edge] = gate_grad
        self.both[:, edge : 2 * edge] = up_grad
        if tail:
            last = self.kept[layer, own, 2 * edge :]
            gate_grad, up_grad = back(active_grad[:, edge:], last[:, :tail], last[:, tail:])
            self.both[:, 2 * edge :] = jnp.concatenate([gate_grad, up_grad], axis=1)
        yield
        tiles = self.depth // TILE
        each = self.feed_weight.shape[1] // tiles
        for low, high in self.tiles(tiles, 3):

            @pl.loop(low, high)
            def _(n):
                columns = pl.ds(pl.multiple_of(n * TILE, TILE), TILE)
                block = self.feed_weight[layer, pl.ds(n * each, each)].reshape(TILE, -1)
                self.store_partial(half, columns, times_trans(self.both[...], block))

            yield

    def attention_back(self, layer, half):
        own = pl.ds(half * HALF, HALF)
        scale = HEAD_DIM ** (-0.5)
        mixed_grad = times_trans(self.rows(half), self.out_weight[layer]).astype(jnp.bfloat16)
        yield
        queries, pairs = self.queries[layer, own, :], self.pairs[layer, own, :]
        key, value = pairs[:, :HEAD_DIM], pairs[:, HEAD_DIM:]
        mask = causal_blocks(HALF, LEN)
        query_grads, key_grad, value_grad = [], 0.0, 0.0
        for start in range(0, self.q_width, HEAD_DIM):
            query = queries[:, start : start + HEAD_DIM]
            outer = mixed_grad[:, start : start + HEAD_DIM]
            weights = attend(query, key, mask, scale)
            weight_grad = times_trans(value, outer)
            score_grad = weights * (
                weight_grad - jnp.sum(weights * weight_grad, axis=0, keepdims=True)
            )
            score_grad = score_grad.astype(jnp.bfloat16)
            query_grads.append(trans_times(score_grad, key) * scale)
            key_grad = key_grad + matmul(score_grad, query) * scale
            value_grad = value_grad + matmul(weights.astype(jnp.bfloat16), outer)
        query_grad = jnp.concatenate(query_grads, axis=1)
        query_grad = turn(query_grad, [self.back_tables[n] for n in range(3)])
        pair_grad = jnp.concatenate([key_grad, value_grad], axis=1)
        pair_grad = turn(pair_grad, [self.back_tables[n] for n in range(3, 6)])
        both = jnp.concatenate([query_grad, pair_grad], axis=1).astype(jnp.bfloat16)
        yield
        tiles = self.depth // TILE
        each = self.head_weight.shape[1] // tiles

        @pl.loop(0, tiles)
        def _(n):
            columns = pl.ds(pl.multiple_of(n * TILE, TILE), TILE)
            block = self.head_weight[layer, pl.ds(n * each, each)].reshape(TILE, -1)
            self.store_partial(half, columns, times_trans(both, block))

        yield

    def normed(self, values, gain):
        return (values * root_inverse(values) * gain[...]).astype(jnp.bfloat16)

    def close_inject(self, half, total):
        hidden = total.astype(jnp.bfloat16)
        self.hidden[0, half] = hidden
        return self.normed(hidden.astype(jnp.float32), self.gains[0])

    def close_attention(self, layer):
        def close(half, total):
            middle = self.hidden[layer, half].astype(jnp.float32) + total
            self.middle[layer, half] = middle
            return self.normed(middle, self.gains[2 + layer])

        return close

    def close_feed(self, layer):
        def close(half, total):
            hidden = (self.middle[layer, half] + total).astype(jnp.bfloat16)
            self.hidden[layer + 1, half] = hidden
            gain = self.gains[4] if layer else self.gains[1]
            return self.normed(hidden.astype(jnp.float32), gain)

        return close

    def close_head(self, half, total):
        hidden = self.hidden[2, half].astype(jnp.float32)
        grad = reciprocal_root_backward(hidden, root_inverse(hidden), self.gains[4][...], total)
        grad = grad.astype(jnp.bfloat16)
        self.grad[half] = grad.astype(jnp.float32)
        return grad

    def close_feed_back(self, layer):
        def close(half, total):
            middle = self.middle[layer, half]
            grad = self.grad[half] + reciprocal_root_backward(
                middle, root_inverse(middle), self.gains[2 + layer][...], total
            )
            self.grad[half] = grad
            return grad.astype(jnp.bfloat16)

        return close

    def close_attention_back(self, layer):
        def close(half, total):
            hidden = self.hidden[layer, half].astype(jnp.float32)
            grad = self.grad[half] + reciprocal_root_backward(
                hidden, root_inverse(hidden), self.gains[layer][...], total
            )
            grad = grad.astype(jnp.bfloat16)
            self.grad[half] = grad.astype(jnp.float32)
            return grad

        return close


def decode_kernel(shape, names, *refs):
    refs = dict(zip(names, refs))
    refs["own"] = [refs.pop(name) for name in ("own_one", "own_two")]
    refs["gains"] = [refs["gain_rows"].at[pl.ds(n, 1)] for n in range(5)]
    this = Decoder(shape, refs)
    this.greet()
    this.moving = {}
    this.share_start(0)
    phases = [(this.inject, this.close_inject, 1)]
    for layer in range(2):
        phases.append((functools.partial(this.attention, layer), this.close_attention(layer), 1))
        phases.append((functools.partial(this.feed, layer), this.close_feed(layer), 2))
    phases.append((this.head, this.close_head, 2))
    for layer in (1, 0):
        phases.append((functools.partial(this.feed_back, layer), this.close_feed_back(layer), 2))
        phases.append(
            (functools.partial(this.attention_back, layer), this.close_attention_back(layer), 1)
        )
    gathers = {}
    sent = None
    for work, close, parts in phases:
        for half in (FIRST, SECOND):
            gather = gathers.pop(half, iter(()))
            reduce = sent or iter(())
            for kind in ORDER:
                next(gather if kind == "g" else reduce, None)
            for count, _ in enumerate(work(half)):
                if count + 1 == parts:
                    finish(reduce)
            finish(reduce)
            if sent is not None:
                gathers[1 - half] = this.gather(1 - half)
            this.send(half)
            sent = this.reduce(half, close)
    finish(gathers.pop(FIRST), sent)
    finish(this.gather(SECOND))
    outs = [
        pltpu.make_async_copy(
            this.gathered.at[half], this.grad_out.at[half], this.keep_sem.at[half]
        )
        for half in (FIRST, SECOND)
    ]
    for copy in outs:
        copy.start()
    for copy in outs:
        copy.wait()


def decode(outer, collective_id, tokens, weights, out_source, down_source, gains, tables, table, own_rows, ids, wanted):
    q_width, depth = out_source.shape[1:]
    share = down_source.shape[1]
    groups, quarter = weights[0].shape[:2]
    entries = table.shape[0]
    low, full = jnp.bfloat16, jnp.float32
    block = (2, TEAM, EACH, depth)
    slots = pltpu.VMEM((2, LINES, EACH, depth), low)
    inputs = dict(
        own_rows=own_rows,
        ids=ids,
        wanted=wanted,
        table=table,
        gain_rows=gains,
        tables=tables[0],
        back_tables=tables[1],
    )
    far_inputs = dict(
        zip(("own_one", "own_two"), weights),
        out_source=out_source,
        down_source=down_source,
    )
    outputs = dict(
        normed_out=(jax.ShapeDtypeStruct(block, low), ANYWHERE),
        grad_out=(jax.ShapeDtypeStruct(block, low), ANYWHERE),
        logit_grad=(jax.ShapeDtypeStruct((entries, ROWS), low), IN_VMEM),
        loss_out=(jax.ShapeDtypeStruct((8, LANES), full), IN_VMEM),
    )
    scratch = dict(
        head_weight=pltpu.VMEM((2, groups, SECTIONS, quarter, q_width + LANES), low),
        feed_weight=pltpu.VMEM((2, groups, SECTIONS, quarter, 2 * share), low),
        out_weight=pltpu.VMEM((2, q_width, depth), low),
        down_weight=pltpu.VMEM((2, share, depth), low),
        gathered=pltpu.VMEM(block, low),
        partial=pltpu.VMEM(block, low),
        side=slots,
        pair=slots,
        far=slots,
        kept=pltpu.VMEM((2, ROWS, 2 * share), full),
        queries=pltpu.VMEM((2, ROWS, q_width), low),
        pairs=pltpu.VMEM((2, ROWS, LANES), low),
        active=pltpu.VMEM((HALF, share), low),
        both=pltpu.VMEM((HALF, 2 * share), low),
        hidden=pltpu.VMEM((3, 2, EACH, depth), low),
        middle=pltpu.VMEM((2, 2, EACH, depth), full),
        grad=pltpu.VMEM((2, EACH, depth), full),
        stats=pltpu.VMEM((2, TEAM, 8, HALF), full),
        load_sem=dma_sems(2, 2, 2),
        share_send=dma_sems(2, 2, 3),
        share_recv=dma_sems(2, 2, 3),
        stats_send=dma_sems(2, TEAM),
        stats_recv=dma_sems(2, TEAM),
        keep_sem=dma_sems(2),
    )
    for name in ("side", "far", "out", "over"):
        scratch[name + "_send"] = dma_sems(2, LINES)
        scratch[name + "_recv"] = dma_sems(2, LINES)
    names = (*inputs, *far_inputs, *outputs, *scratch)
    return pl.pallas_call(
        functools.partial(decode_kernel, (outer, tokens, share, q_width, depth), names),
        out_shape=tuple(shape for shape, _ in outputs.values()),
        in_specs=[IN_VMEM] * len(inputs) + [ANYWHERE] * len(far_inputs),
        out_specs=tuple(spec for _, spec in outputs.values()),
        scratch_shapes=list(scratch.values()),
        compiler_params=settings(collective_id),
        name="decode",
    )(*inputs.values(), *far_inputs.values())


class Collector:
    def __init__(self, halves, refs):
        for name, ref in refs.items():
            setattr(self, name, ref)
        self.halves = halves
        self.section, self.partner, self.across, self.wide, self.wide_at = all_places(halves)
        self.groups = ((1, 1), (1, 0), (0, 1), (0, 0))

    def greet(self):
        beside = self.wide + 1 - 2 * (self.wide % 2)
        peers = [{"section": self.partner}, {"section": self.across}, {"wide": beside}]
        greet(peers + [{"wide": self.wide_at(j)} for j in range(1, self.halves)])

    def steps(self, n):
        return steps_of(n % 2 == 0, self.section, self.partner, self.across, self.wide)

    def lines(self, n, home, flip_b, flip_a):
        (_, y_a, x_a), (_, y_b, x_b) = self.steps(n)
        flips_y = (y_a and flip_a) or (y_b and flip_b)
        flips_x = (x_a and flip_a) or (x_b and flip_b)
        section, wide = owner_of(home, flips_y, flips_x, self.wide)
        return self.partials[n].at[section, :, wide % 2]

    def line_block(self, n, j):
        return self.partials[n].at[self.section, (self.wide // 2 + j) % self.halves, self.wide % 2]

    def core_copy(self, n, fb, fa):
        return remote(
            self.lines(n, self.partner, fb, fa),
            self.core_in[n].at[fb, fa],
            self.core_send.at[n, fb, fa],
            self.core_recv.at[n, fb, fa],
            {"section": self.partner},
        )

    def b_copy(self, n, fa):
        _, (peer, _, _) = self.steps(n)
        return remote(
            self.lines(n, self.section, 1, fa),
            self.b_in[n].at[fa],
            self.b_send.at[n, fa],
            self.b_recv.at[n, fa],
            peer,
        )

    def a_copy(self, n):
        (peer, _, _), _ = self.steps(n)
        return remote(
            self.lines(n, self.section, 0, 1),
            self.a_in[n],
            self.a_send.at[n],
            self.a_recv.at[n],
            peer,
        )

    def z_copy(self, n, j):
        return remote(
            self.line_block(n, j),
            self.z_in[n].at[j],
            self.z_send.at[n, j],
            self.z_recv.at[n, j],
            {"wide": self.wide_at(j)},
        )

    def add(self, block, more):
        block[...] = (block[...].astype(jnp.float32) + more.astype(jnp.float32)).astype(jnp.bfloat16)

    def start(self, n):
        for fb, fa in self.groups:
            self.core_copy(n, fb, fa).start()

    def sum_core(self, n):
        for fb, fa in self.groups:
            self.core_copy(n, fb, fa).wait_recv()
            self.add(self.lines(n, self.section, fb, fa), self.core_in[n][fb, fa])
            if fb:
                self.b_copy(n, fa).start()

    def sum_b(self, n):
        for fa in (1, 0):
            self.b_copy(n, fa).wait_recv()
            self.add(self.lines(n, self.section, 0, fa), self.b_in[n][fa])
            if fa:
                self.a_copy(n).start()

    def sum_a(self, n):
        self.a_copy(n).wait_recv()
        self.add(self.lines(n, self.section, 0, 0), self.a_in[n][...])
        for j in range(1, self.halves):
            self.z_copy(n, j).start()

    def sum_lines(self, n):
        total = self.line_block(n, 0)[...].astype(jnp.float32)
        for j in range(1, self.halves):
            self.z_copy(n, j).wait_recv()
            total = total + self.z_in[n][j].astype(jnp.float32)
        self.sums[n][...] = total

    def drain(self, n):
        for fb, fa in self.groups:
            self.core_copy(n, fb, fa).wait_send()
        for fa in (0, 1):
            self.b_copy(n, fa).wait_send()
        self.a_copy(n).wait_send()
        for j in range(1, self.halves):
            self.z_copy(n, j).wait_send()


EMBED, REDUCE, EXPAND, FRONT, REAR = range(5)
FAR = ("middle", "expanded", "third", "first", "mixed", "heads", "pieces")


def hyper_collect_kernel(slots, halves, names, *refs):
    refs = dict(zip(names, refs))
    for name in ("sums", "partials", "core_in", "b_in", "a_in", "z_in"):
        refs[name] = [refs.pop(f"{name}{n}") for n in range(5)]
    this = Collector(halves, refs)
    first, second, third, vectors = this.first, this.second, this.third, this.vectors
    entered, outcome_low, feed_grad = this.entered, this.outcome_low, this.feed_grad
    width = this.pieces.shape[1]
    count, feed = this.pieces.shape[0], third.shape[0]
    depth = this.table_grad.shape[1]
    head = width // HYPER_HEAD_COUNT
    scale = head ** (-0.5)
    loads = {
        name: pltpu.make_async_copy(getattr(this, "far_" + name), getattr(this, name), this.load_sem.at[n])
        for n, name in enumerate(FAR)
    }
    for name in FAR:
        loads[name].start()
    this.greet()

    def store(n, columns, values):
        block = this.partials[n]
        block[:, :, :, :, columns] = values.astype(jnp.bfloat16).reshape(
            block.shape[:4] + (values.shape[1],)
        )

    grad_low = this.table_grad[...].astype(jnp.bfloat16)
    pooled_turned = jnp.transpose(this.pooled[...].astype(jnp.float32)).astype(jnp.bfloat16)
    for start in range(0, depth, TILE):
        store(EMBED, pl.ds(start, TILE), matmul(pooled_turned, grad_low[:, start : start + TILE]))
    this.start(EMBED)
    pooled_grad = times_trans(grad_low, second[:, pl.ds(0, depth)]) / slots
    outcome_grad = jnp.broadcast_to(pooled_grad[:, None, :], (count // slots, slots, width))
    outcome_grad = outcome_grad.reshape(count, width)
    outcome_low[...] = outcome_grad.astype(jnp.bfloat16)
    loads["middle"].wait()
    normed, inverse = center_norm(this.middle[...])
    entered[...] = jnp.transpose(normed * vectors[2:3] + vectors[3:4]).astype(jnp.bfloat16)
    feed_grad[...] = jnp.zeros_like(feed_grad)
    this.sum_core(EMBED)

    for name in FAR[1:]:
        loads[name].wait()
    tiles = feed // TILE

    @pl.loop(0, tiles)
    def _(n):
        tile = pl.ds(pl.multiple_of(n * TILE, TILE), TILE)
        values = this.expanded[:, tile]
        erf = 0.5 * (1.0 + lax.erf(values * inv_root_two))
        active = (values * erf).astype(jnp.bfloat16)
        this.expanded[:, tile] = erf + values * jnp.exp(-0.5 * values * values) * inv_root_tau
        block = this.partials[REDUCE]
        owned = block.shape[3]
        lines = TILE // (2 * owned)
        at = n * lines
        turned = trans_times(active, outcome_low[...]).astype(jnp.bfloat16)
        block[at // halves, pl.ds(at % halves, lines)] = turned.reshape(lines, 2, owned, width)

    this.start(REDUCE)

    def feed_tiles(low, high):
        @pl.loop(low, high)
        def _(n):
            start = pl.multiple_of(n * TILE, TILE)
            tile = pl.ds(start, TILE)
            columns = pl.ds(pl.multiple_of(4 * width + start, TILE), TILE)
            active_grad = times_trans(outcome_low[...], third[tile, :])
            low_grad = (active_grad * this.expanded[:, tile]).astype(jnp.bfloat16)
            store(EXPAND, tile, matmul(entered[...], low_grad))
            feed_grad[...] += times_trans(low_grad, first[:, columns])

    feed_tiles(0, tiles // 2)
    this.sum_core(REDUCE)
    this.sum_b(EMBED)
    feed_tiles(tiles // 2, tiles)
    this.start(EXPAND)

    grad = feed_grad[...]
    scale_two = jnp.sum(grad * normed, axis=0, keepdims=True)
    shift_two = jnp.sum(grad, axis=0, keepdims=True)
    middle_grad = outcome_grad + center_back(normed, inverse, grad * vectors[2:3])
    middle_low = middle_grad.astype(jnp.bfloat16)
    out_columns = pl.ds(3 * width, width)
    store(REAR, pl.ds(width, width), trans_times(this.mixed[...], middle_low))
    this.mixed_grad[...] = times_trans(middle_low, first[:, out_columns]).astype(jnp.bfloat16)
    mask = same_entry(CHUNK, slots)
    this.sum_core(EXPAND)
    this.sum_a(EMBED)

    def attention_chunks(low, high):
        @pl.loop(low, high)
        def _(n):
            rows = pl.ds(pl.multiple_of(n * CHUNK, CHUNK), CHUNK)
            block = this.heads[rows, :]
            outer_block = this.mixed_grad[rows, :]
            grads = [[], [], []]
            for start in range(0, width, head):
                query, key, value = (
                    block[:, part * width + start : part * width + start + head]
                    for part in range(3)
                )
                outer = outer_block[:, start : start + head]
                weights = slot_weights(query, key, mask, scale)
                weight_grad = gathered_slots(times_trans(value, outer), mask)
                score_grad = weights * (
                    weight_grad - jnp.sum(weights * weight_grad, axis=0, keepdims=True)
                )
                score_grad = spread_slots(score_grad, mask).astype(jnp.bfloat16)
                weights = spread_slots(weights, mask).astype(jnp.bfloat16)
                grads[0].append(trans_times(score_grad, key) * scale)
                grads[1].append(matmul(score_grad, query) * scale)
                grads[2].append(matmul(weights, outer))
            for part in range(3):
                this.heads_grad[rows, pl.ds(part * width, width)] = jnp.concatenate(
                    grads[part], axis=1
                ).astype(jnp.bfloat16)

    chunks = count // CHUNK
    attention_chunks(0, chunks // 2)
    this.sum_b(REDUCE)
    attention_chunks(chunks // 2, chunks)
    this.sum_b(EXPAND)
    this.sum_a(REDUCE)

    normed, _ = center_norm(this.pieces[...].astype(jnp.float32))
    entered[...] = jnp.transpose(normed * vectors[0:1] + vectors[1:2]).astype(jnp.bfloat16)
    feed_grad[...] = jnp.zeros_like(feed_grad)
    for start in range(0, 3 * width, TILE):
        columns = pl.ds(start, TILE)
        low_grad = this.heads_grad[:, columns]
        target = (FRONT, start) if start < 2 * width else (REAR, start - 2 * width)
        store(target[0], pl.ds(target[1], TILE), matmul(entered[...], low_grad))
        feed_grad[...] += times_trans(low_grad, first[:, columns])
        if start + TILE == 2 * width:
            this.start(FRONT)

    grad = feed_grad[...]
    scale_one = jnp.sum(grad * normed, axis=0, keepdims=True)
    shift_one = jnp.sum(grad, axis=0, keepdims=True)
    row = lax.broadcasted_iota(jnp.int32, (LANES, width), 0)
    summed = jnp.zeros((LANES, width), jnp.float32)
    for n, item in enumerate((scale_one, shift_one, scale_two, shift_two)):
        summed = jnp.where(row == n, item, summed)
    store(REAR, pl.ds(2 * width, LANES), jnp.transpose(summed))
    this.start(REAR)
    this.sum_core(FRONT)
    this.sum_a(EXPAND)
    this.sum_core(REAR)
    this.sum_lines(EMBED)
    this.sum_b(FRONT)
    this.sum_b(REAR)
    this.sum_lines(REDUCE)
    this.sum_a(FRONT)
    this.sum_a(REAR)
    this.sum_lines(EXPAND)
    this.sum_lines(FRONT)
    this.sum_lines(REAR)
    for n in range(5):
        this.drain(n)


def hyper_collect(collective_id, wides, pieces, slots, params, stored, table_grad):
    count, width = pieces.shape
    first, second, third, vectors = params
    depth, feed = table_grad.shape[1], third.shape[0]
    devices, halves = SECTIONS * wides, wides // 2
    low, full = jnp.bfloat16, jnp.float32
    rows = width // devices
    shapes = [
        (rows, depth),
        (feed // devices, width),
        (rows, feed),
        (rows, 2 * width),
        (rows, 2 * width + LANES),
    ]
    heads, mixed, middle, expanded, pooled = stored
    inputs = dict(table_grad=table_grad, second=second, vectors=vectors, pooled=pooled)
    far = dict(
        middle=middle,
        expanded=expanded,
        third=third,
        first=first,
        mixed=mixed,
        heads=heads,
        pieces=pieces,
    )
    inputs.update({"far_" + name: far[name] for name in FAR})
    outputs = {f"sums{n}": jax.ShapeDtypeStruct(shape, full) for n, shape in enumerate(shapes)}
    scratch = {name: pltpu.VMEM(far[name].shape, far[name].dtype) for name in FAR}
    scratch.update(
        load_sem=dma_sems(len(FAR)),
        entered=pltpu.VMEM((width, count), low),
        outcome_low=pltpu.VMEM((count, width), low),
        feed_grad=pltpu.VMEM((count, width), full),
        heads_grad=pltpu.VMEM((count, 3 * width), low),
        mixed_grad=pltpu.VMEM((count, width), low),
    )
    for name, slots_of in (
        ("partials", (SECTIONS, halves, 2)),
        ("core_in", (2, 2, halves)),
        ("b_in", (2, halves)),
        ("a_in", (halves,)),
        ("z_in", (halves,)),
    ):
        for n, shape in enumerate(shapes):
            scratch[f"{name}{n}"] = pltpu.VMEM(slots_of + shape, low)
    for name, numbers in (("core", (2, 2)), ("b", (2,)), ("a", ()), ("z", (halves,))):
        scratch[name + "_send"] = dma_sems(5, *numbers)
        scratch[name + "_recv"] = dma_sems(5, *numbers)
    return pl.pallas_call(
        functools.partial(hyper_collect_kernel, slots, halves, (*inputs, *outputs, *scratch)),
        out_shape=tuple(outputs.values()),
        in_specs=[IN_VMEM] * (len(inputs) - len(FAR)) + [ANYWHERE] * len(FAR),
        out_specs=(IN_VMEM,) * len(outputs),
        scratch_shapes=list(scratch.values()),
        compiler_params=settings(collective_id),
        name="hyper_collect",
    )(*inputs.values())


def team_groups(wides, outer):
    return [[rank * outer + team for team in range(outer)] for rank in range(wides // outer)]


def all_teams(pieces, outer, groups):
    if outer == 1:
        return pieces
    pieces = [
        lax.all_gather(piece, "wide", axis=1, axis_index_groups=groups) for piece in pieces
    ]
    return [piece.reshape((-1,) + piece.shape[2:]) for piece in pieces]


def shards(
    token_ids,
    targets,
    slot_ids,
    group_ids,
    group_offsets,
    piece_table,
    prenorm_gain,
    prenorm_bias,
    query_map,
    key_map,
    value_map,
    output_map,
    midnorm_gain,
    midnorm_bias,
    expand_map,
    reduce_map,
    embed_map,
    attention_gain,
    query_weight,
    key_weight,
    value_weight,
    output_weight,
    feed_gain,
    gate_weight,
    up_weight,
    down_weight,
    final_gain,
):
    wides = lax.axis_size("wide")
    outer = wides // TEAM
    groups = team_groups(wides, outer)
    section_index = lax.axis_index("section")
    wide_index = lax.axis_index("wide")
    rank = wide_index // outer
    hyper_width, hyper_feed = piece_table.shape[1], expand_map.shape[1]
    model_width = embed_map.shape[1]
    total_tokens = wides * MB * LEN

    entries, slot_count = slot_ids.shape
    group_hits = (
        group_ids[:, None] == jnp.arange(group_offsets.shape[0], dtype=jnp.int32)[None, :]
    ).astype(jnp.int32)
    row_start = jnp.sum(group_hits * group_offsets[None, :], axis=1)
    piece_rows = (row_start[:, None] + slot_ids).reshape(-1)
    *columns, first, second, third, gains, notes = pack(
        (query_weight, key_weight, value_weight, gate_weight, up_weight),
        (query_map, key_map, value_map, output_map, expand_map, embed_map, reduce_map),
        jnp.stack([prenorm_gain, prenorm_bias, midnorm_gain, midnorm_bias]),
        (attention_gain, feed_gain),
        jnp.concatenate([token_ids, targets], axis=1).reshape(2 * MB, LEN),
    )
    blocks = (first, second, third)
    whole_tiles = query_map.shape[0] % 16 == 0
    work = Work()
    if whole_tiles:
        work = hyper_work(
            piece_rows.reshape(-1, 1), piece_table, slot_count, hyper_feed, model_width
        )
    first, second, third, gains, notes, own_one, own_two, *made = spread(
        1, wides, outer, blocks, (gains, notes), columns, work
    )
    first = first.reshape(hyper_width, -1)
    second = second.reshape(hyper_width, -1)
    third = third.reshape(hyper_feed, hyper_width)
    if whole_tiles:
        vectors, pieces, table_shard, pooled, *hyper_stored = made
        hyper_stored = (*hyper_stored, pooled)
        params = (first, second, third, vectors)
    else:
        vectors = second[:, model_width : model_width + 8].astype(jnp.float32).T
        params = (first, second, third, vectors)
        pieces = jnp.take(piece_table, piece_rows, axis=0)
        table_shard, hyper_stored = hyper_forward(pieces, slot_count, params)

    if outer > 1:
        gains = lax.all_gather(gains, "wide", axis=1, axis_index_groups=groups)
        gains = gains.reshape(-1, gains.shape[2], gains.shape[3])
        output_weight, down_weight = (
            lax.all_gather(item, "wide", axis=1, axis_index_groups=groups, tiled=True)
            for item in (output_weight, down_weight)
        )
    gains = gains.transpose(1, 0, 2).reshape(-1, model_width)
    final_scale = final_gain.astype(jnp.float32).reshape(1, model_width)
    gains = jnp.concatenate([gains[:4], final_scale, gains[:3]], axis=0)
    notes = lax.dynamic_slice_in_dim(notes, section_index * 2, 2, 0)
    ids, wanted = notes[:, 0].reshape(-1), notes[:, 1].reshape(-1)

    table_rows = section_gather(3, table_shard)
    if outer > 1:
        table_rows = lax.all_gather(table_rows, "wide", axis=1, axis_index_groups=groups)
    table_rows = table_rows.reshape(-1, model_width)
    wide_rows = rank * outer + jnp.arange(outer, dtype=jnp.int32)
    row_starts = (
        jnp.arange(SECTIONS, dtype=jnp.int32)[:, None] * wides + wide_rows[None, :]
    ) * entries
    own_rows = row_starts[:, :, None] + jnp.arange(entries, dtype=jnp.int32)[None, None, :]
    own_rows = own_rows.reshape(-1)
    own_rows = own_rows.reshape(-1, 1)

    def by_halves(numbers):
        return jnp.pad(numbers.reshape(2, -1), ((0, 6), (0, 0)))

    normed, grads, logit_grad, loss_block = decode(
        outer,
        4,
        total_tokens,
        all_teams((own_one, own_two), outer, groups),
        output_weight,
        down_weight,
        gains,
        (turn_tables(False), turn_tables(True)),
        table_rows,
        own_rows,
        by_halves(ids),
        by_halves(wanted),
    )

    hits = (own_rows == ids[None, :]).astype(jnp.bfloat16)
    table_part = matmul(logit_grad, normed.reshape(ROWS, model_width)) + matmul(
        hits, grads.reshape(ROWS, model_width)
    )
    table_part = table_part.astype(jnp.bfloat16).reshape(SECTIONS, outer, entries, model_width)
    if outer > 1:
        table_part = lax.psum_scatter(
            table_part.astype(jnp.float32),
            "wide",
            scatter_dimension=1,
            axis_index_groups=groups,
        ).astype(jnp.bfloat16)
        loss_block = lax.psum(loss_block, "wide", axis_index_groups=groups)
    table_grad, loss_block = section_sum(
        11, table_part.reshape(SECTIONS, entries, model_width), loss_block
    )
    mean_loss = loss_block[0, 0]
    if whole_tiles:
        grad_embed, grad_reduce, grad_expand, front, rear = hyper_collect(
            12, wides, pieces, slot_count, params, hyper_stored, table_grad
        )
    else:
        grads = hyper_backward(pieces, slot_count, params, hyper_stored, table_grad)
        grads = [item.reshape(SECTIONS, wides, -1, item.shape[1]) for item in grads]
        first, second, grad_reduce = collect(12, grads)
        grad_embed, grad_expand = second[:, :model_width], first[:, 4 * hyper_width :]
        front = first[:, : 2 * hyper_width]
        rear = jnp.concatenate(
            [first[:, 2 * hyper_width : 4 * hyper_width], second[:, model_width:]], axis=1
        )
    if whole_tiles:
        outs = deliver(grad_embed, grad_expand, grad_reduce, front, rear)
    else:
        vectors = rear[:, 2 * hyper_width : 2 * hyper_width + 4]
        outs = [vectors[:, n] for n in range(4)]
        outs += [front[:, :hyper_width], front[:, hyper_width:]]
        outs += [rear[:, :hyper_width], rear[:, hyper_width : 2 * hyper_width]]
        outs += [grad_expand, grad_reduce, grad_embed]
    prescale, prebias, midscale, midshift, *maps = outs
    return (mean_loss, prescale, prebias, *maps[:4], midscale, midshift, *maps[4:])


def solution(mesh):
    placed = (
        P("wide", None, None),
        P("wide", None, None),
        P(("section", "wide"), None),
        P(("section", "wide")),
        P(),
        P(),
        P(("section", "wide")),
        P(("section", "wide")),
        P(("section", "wide"), None),
        P(("section", "wide"), None),
        P(("section", "wide"), None),
        P(("section", "wide"), None),
        P(("section", "wide")),
        P(("section", "wide")),
        P(("section", "wide"), None),
        P(("section", "wide"), None),
        P(("section", "wide"), None),
        P(None, "wide"),
        P(None, "wide", None),
        P(None, "wide", None),
        P(None, "wide", None),
        P(None, "wide", None),
        P(None, "wide"),
        P(None, "wide", None),
        P(None, "wide", None),
        P(None, "wide", None),
        P(),
    )
    return jax.shard_map(
        shards,
        mesh=mesh,
        in_specs=placed,
        out_specs=(
            P(),
            P(("section", "wide")),
            P(("section", "wide")),
            P(("section", "wide"), None),
            P(("section", "wide"), None),
            P(("section", "wide"), None),
            P(("section", "wide"), None),
            P(("section", "wide")),
            P(("section", "wide")),
            P(("section", "wide"), None),
            P(("section", "wide"), None),
            P(("section", "wide"), None),
        ),
        check_vma=False,
    )
```
